32 devices in a mesh: fsdp: 32 (over z, y, x, core).
Axes of the slice: x: 2, y: 2, z: 4, core: 2. Of those that a mesh axis runs over, the one named last changes fastest.
Arguments:
- tokens: bfloat16 [32768, 1024], P('fsdp'), may hold values from -6 to 6
- image_ids: int32 [32768], P('fsdp'), may hold values from 0 to 57, as said below
- cotangent: bfloat16 [32768, 1024], P('fsdp'), may hold values from -6 to 6
- norm1_gain: bfloat16 [1024], P('fsdp'), may hold values from 0.099609375 to 1.8984375
- norm1_shift: bfloat16 [1024], P('fsdp'), may hold values from -1.5 to 1.5
- qkv_weight: bfloat16 [1024, 3072], P('fsdp'), may hold values from -0.1875 to 0.1875
- query_bias: bfloat16 [1024], P('fsdp'), may hold values from -2.5 to 2.5
- value_bias: bfloat16 [1024], P('fsdp'), may hold values from -1 to 1
- out_weight: bfloat16 [1024, 1024], P('fsdp'), may hold values from -1.5 to 1.5
- out_bias: bfloat16 [1024], P('fsdp'), may hold values from -1 to 1
- norm2_gain: bfloat16 [1024], P('fsdp'), may hold values from 0.099609375 to 1.8984375
- norm2_shift: bfloat16 [1024], P('fsdp'), may hold values from -1.5 to 1.5
- up_weight: bfloat16 [1024, 4096], P('fsdp'), may hold values from -0.1875 to 0.1875
- up_bias: bfloat16 [4096], P('fsdp'), may hold values from -2.5 to 2.5
- down_weight: bfloat16 [4096, 1024], P('fsdp'), may hold values from -0.1875 to 0.1875
- down_bias: bfloat16 [1024], P('fsdp'), may hold values from -1 to 1
Outputs:
- layer_out: bfloat16 [32768, 1024], P('fsdp')
- grad_tokens: float32 [32768, 1024], P('fsdp')
- grad_norm1_gain: float32 [1024], P('fsdp')
- grad_norm1_shift: float32 [1024], P('fsdp')
- grad_qkv_weight: float32 [1024, 3072], P('fsdp')
- grad_query_bias: float32 [1024], P('fsdp')
- grad_value_bias: float32 [1024], P('fsdp')
- grad_out_weight: float32 [1024, 1024], P('fsdp')
- grad_out_bias: float32 [1024], P('fsdp')
- grad_norm2_gain: float32 [1024], P('fsdp')
- grad_norm2_shift: float32 [1024], P('fsdp')
- grad_up_weight: float32 [1024, 4096], P('fsdp')
- grad_up_bias: float32 [4096], P('fsdp')
- grad_down_weight: float32 [4096, 1024], P('fsdp')
- grad_down_bias: float32 [1024], P('fsdp')
The draws below stay inside these ranges and needn't reach their ends.
Inputs may be any that keep to these rules, and one draw needn't show every extreme that they name: `image_ids`: image numbers never fall along the tokens and rise by one from image to image; every image has 577 tokens except the first and the last, which have 1 to 577.
All inputs are finite; a program needn't handle non-finite values.
Results may differ from the reference program's by a relative error of at most 0.013.
Values may be sent and summed in bfloat16 or wider, within the bound.
A program may use at most 256 MiB of HBM per device.

```python
import math
import jax
import jax.numpy as jnp
from jax import lax

D = 1024
FF = 4096
HEADS = 16
HDIM = 64
IMG = 577
TOK_DEV = 1024
TOKENS = 32768


def draw_image_ids(key, part):
    key = jax.random.fold_in(key, 7)
    first_len = jax.random.randint(key, (), 1, IMG + 1, dtype=jnp.int32)
    position = jnp.arange(TOKENS, dtype=jnp.int32)
    return ((position + IMG - first_len) // IMG).astype(jnp.int32)


def spiked(entries, rng, source, target, blocks, factor):
    def block_of(axis_at):
        return (jnp.arange(entries.shape[axis_at]) // (entries.shape[axis_at] // blocks)).reshape((-1,) + (1,) * (entries.ndim - 1 - axis_at))

    near = jax.random.permutation(rng, blocks)[block_of(target)]
    second = (block_of(target) + blocks // 2) % blocks
    return jnp.where((block_of(source) == near) | (block_of(source) == second), factor * entries, entries)


def levels(stream_key, shape, split, smallest, largest):
    def one(axis_at, parts):
        steps = jax.random.uniform(jax.random.fold_in(jax.random.fold_in(stream_key, 6), axis_at), (parts,), jnp.float32, smallest / len(split), largest / len(split))
        return jnp.repeat(jnp.exp(steps), shape[axis_at] // parts).reshape((-1,) + (1,) * (len(shape) - axis_at - 1))

    factor_of = one(*split[0])
    for cut in split[1:]:
        factor_of = factor_of * one(*cut)
    return factor_of


def noise(key, extent, scale, bound, pieces=(), kind=jnp.bfloat16):
    array = jax.random.normal(key, extent, jnp.float32) * scale
    if len(pieces) > 0:
        array = levels(key, extent, pieces, -0.22, 0.18) * array
    return jnp.clip(array, min=-bound, max=bound).astype(kind)


def noise_with(rng, shape, scale, bound, split, heavy, kind=jnp.bfloat16):
    entries = scale * jax.random.normal(rng, shape, jnp.float32)
    if split:
        entries = entries * levels(rng, shape, split, -0.22, 0.18)
    return jnp.clip(spiked(entries, jax.random.fold_in(rng, 3), *heavy), -bound, bound).astype(kind)


def setup_inputs(seed: int = 0) -> dict:
    splits = jax.random.split(jax.random.key(seed), 17)
    return {
        "tokens": noise(splits[0], (TOKENS, D), 1.0, 6.0, ((0, 32),)),
        "image_ids": draw_image_ids(jax.random.fold_in(splits[16], 71), 0),
        "cotangent": noise_with(splits[2], (TOKENS, D), 1.0, 6.0, ((0, 32),), (0, 1, 32, 2.75)),
        "norm1_gain": jnp.clip(1.0 + 0.18 * jax.random.normal(splits[3], (D,), jnp.float32), 0.099609375, 1.8984375).astype(jnp.bfloat16),
        "norm1_shift": noise(splits[4], (D,), 0.3, 1.5, ((0, 32),)),
        "qkv_weight": noise(splits[5], (D, 3 * D), D ** -0.5, 0.1875, ((0, 32),)),
        "query_bias": noise(splits[6], (D,), 0.5, 2.5, ((0, 32),)),
        "value_bias": noise(splits[7], (D,), 0.2, 1.0, ((0, 32),)),
        "out_weight": noise(splits[8], (D, D), (D // 64) ** -0.5, 1.5, ((0, 32),)),
        "out_bias": noise(splits[9], (D,), 0.2, 1.0, ((0, 32),)),
        "norm2_gain": jnp.clip(1.0 + 0.18 * jax.random.normal(splits[10], (D,), jnp.float32), 0.099609375, 1.8984375).astype(jnp.bfloat16),
        "norm2_shift": noise(splits[11], (D,), 0.3, 1.5, ((0, 32),)),
        "up_weight": noise(splits[12], (D, FF), D ** -0.5, 0.1875, ((0, 32),)),
        "up_bias": noise(splits[13], (FF,), 0.5, 2.5, ((0, 32),)),
        "down_weight": noise(splits[14], (FF, D), (FF // 4) ** -0.5, 0.1875, ((0, 32),)),
        "down_bias": noise(splits[15], (D,), 0.2, 1.0, ((0, 32),)),
    }


@jax.custom_vjp
def low(v):
    return lax.optimization_barrier(v.astype(jnp.bfloat16)).astype(jnp.float32)

@jax.custom_vjp
def low_back(v):
    return v

def low_keep(v):
    return (low(v), None)

def low_pass(kept, grad):
    return (grad,)

def back_keep(v):
    return (v, None)

def back_low(kept, grad):
    return (low(grad),)
low.defvjp(low_keep, low_pass)
low_back.defvjp(back_keep, back_low)
EPS = 1e-06
HIGH = lax.Precision.HIGHEST

def product(left, right):
    return jnp.dot(left, right, precision=HIGH, preferred_element_type=jnp.float32)

def normalize(inputs, gain, shift):
    center = inputs - lax.optimization_barrier(jnp.mean(inputs, axis=1, keepdims=True))
    scaled = center * lax.rsqrt(lax.optimization_barrier(jnp.mean(center * center, axis=1, keepdims=True)) + EPS)
    return scaled * gain + shift

def attention(queries, key_rows, value_rows, image_ids):
    rim_rows = IMG - 1
    block_rows = min(512, TOK_DEV)
    window_rows = block_rows + 2 * rim_rows
    key_pad = jnp.pad(key_rows, ((rim_rows, rim_rows), (0, 0)))
    value_pad = jnp.pad(value_rows, ((rim_rows, rim_rows), (0, 0)))
    ids_pad = jnp.pad(image_ids, (rim_rows, rim_rows), constant_values=-1)
    score_scale = 1.0 / math.sqrt(HDIM)

    def one_block(block_idx):
        row_start = (block_idx * block_rows).astype(jnp.int32)
        query_block = lax.dynamic_slice_in_dim(queries, row_start, block_rows, 0).reshape(block_rows, HEADS, HDIM)
        key_block = lax.dynamic_slice_in_dim(key_pad, row_start, window_rows, 0).reshape(window_rows, HEADS, HDIM)
        value_block = lax.dynamic_slice_in_dim(value_pad, row_start, window_rows, 0).reshape(window_rows, HEADS, HDIM)
        own_ids = lax.dynamic_slice_in_dim(image_ids, row_start, block_rows, 0)
        near_ids = lax.dynamic_slice_in_dim(ids_pad, row_start, window_rows, 0)
        same_image = own_ids[:, None] == near_ids[None, :]
        logits = low_back(jnp.einsum('qhd,khd->hqk', query_block, key_block, precision=HIGH) * score_scale)
        logits = jnp.where(same_image[None], logits, -1e+30)
        exp_terms = jnp.exp(logits - lax.optimization_barrier(jnp.max(logits, axis=2, keepdims=True)))
        weights = low(exp_terms / lax.optimization_barrier(jnp.sum(exp_terms, axis=2, keepdims=True)))
        mixed = jnp.einsum('hqk,khd->qhd', weights, value_block, precision=HIGH)
        return mixed.reshape(block_rows, HEADS * HDIM)
    mixed_all = lax.map(jax.checkpoint(one_block), jnp.arange(TOKENS // block_rows, dtype=jnp.int32))
    return mixed_all.reshape(TOKENS, HEADS * HDIM)

def reference(tokens, image_ids, cotangent, norm1_gain, norm1_shift, qkv_weight, query_bias, value_bias, out_weight, out_bias, norm2_gain, norm2_shift, up_weight, up_bias, down_weight, down_bias):
    model_width = HEADS * HDIM
    inputs = tokens.astype(jnp.float32)
    params = (norm1_gain.astype(jnp.float32), norm1_shift.astype(jnp.float32), qkv_weight.astype(jnp.float32), query_bias.astype(jnp.float32), value_bias.astype(jnp.float32), out_weight.astype(jnp.float32), out_bias.astype(jnp.float32), norm2_gain.astype(jnp.float32), norm2_shift.astype(jnp.float32), up_weight.astype(jnp.float32), up_bias.astype(jnp.float32), down_weight.astype(jnp.float32), down_bias.astype(jnp.float32))

    def forward(layer_in, weights):
        gain_first, shift_first, qkv_mat, query_add, value_add, out_mat, out_add, gain_second, shift_second, up_mat, up_add, down_mat, down_add = weights
        normed = low(normalize(layer_in, gain_first, shift_first))
        bias_row = jnp.concatenate([query_add, jnp.zeros_like(query_add), value_add])
        projected = low_back(low(product(normed, qkv_mat) + bias_row))
        mixed = attention(projected[:, :model_width], projected[:, model_width:2 * model_width], projected[:, 2 * model_width:], image_ids)
        mixed = low_back(low(mixed))
        branch = low_back(product(mixed, out_mat) + out_add)
        resid = layer_in + branch
        normed_two = low(normalize(resid, gain_second, shift_second))
        upward = low_back(product(normed_two, up_mat) + up_add)
        activated = low(jax.nn.gelu(upward, approximate=False))
        return resid + (product(activated, down_mat) + down_add)
    layer_value, pull_back = jax.vjp(forward, inputs, params)
    grad_in, grad_params = pull_back(cotangent.astype(jnp.float32))
    return (layer_value.astype(jnp.bfloat16), grad_in, grad_params[0], grad_params[1], grad_params[2], grad_params[3], grad_params[4], grad_params[5], grad_params[6], grad_params[7], grad_params[8], grad_params[9], grad_params[10], grad_params[11], grad_params[12])
```

```python
import functools
import math

import jax
import jax.numpy as jnp
from jax import lax
from jax.experimental import pallas as pl
from jax.experimental.pallas import tpu as pltpu
from jax.sharding import PartitionSpec as P

HDIM = 64
IMG = 577
RIM = IMG - 1
WIN = 592
QB = 128
EPS = 1e-06
NEG = -1e30
AXIS = "fsdp"
BF = jnp.bfloat16
F32 = jnp.float32
NT = (((1,), (1,)), ((), ()))
TN = (((0,), (0,)), ((), ()))
NN = (((1,), (0,)), ((), ()))


def dot(a, b, dims=NN):
    return lax.dot_general(a, b, dims, preferred_element_type=F32)


def stacked(block):
    lane = lax.broadcasted_iota(jnp.int32, block.shape, 1)
    zero = jnp.zeros_like(block)
    return jnp.concatenate(
        [jnp.where(lane < HDIM, block, zero), jnp.where(lane >= HDIM, block, zero)], axis=0
    )


def unstacked(wide):
    return jnp.concatenate([wide[:HDIM, :QB], wide[HDIM:, QB:]], axis=0).T


def segments(meta, rows):
    n0, first, last = meta[0], meta[1], meta[2]
    limit = jnp.where(last == 1, RIM + rows, 2 * RIM + rows)
    start0 = jnp.where(first == 1, RIM, n0 - 1)
    start1 = RIM + n0
    start2 = start1 + IMG
    return (
        (start0, start1),
        (start1, jnp.minimum(start1 + IMG, limit)),
        (start2, jnp.minimum(start2 + IMG, limit)),
    )


def pick(seg, table):
    (a0, b0), (a1, b1), (a2, b2) = table
    start = jnp.where(seg == 0, a0, jnp.where(seg == 1, a1, a2))
    stop = jnp.where(seg == 0, b0, jnp.where(seg == 1, b1, b2))
    base = pl.multiple_of(start // 16 * 16, 16)
    return base, start - base, stop - base


def key_mask(low, high):
    row = lax.broadcasted_iota(jnp.int32, (WIN, 2 * QB), 0)
    return (row >= low) & (row < high)


def attend_kernel(meta, q_ref, k_ref, v_ref, out_ref, lse_ref):
    rows = q_ref.shape[0]
    n0 = meta[0]
    n1 = n0 + IMG
    table = segments(meta, rows)

    def one(queries, seg):
        base, low, high = pick(seg, table)
        keys = k_ref[pl.ds(base, WIN), :]
        values = v_ref[pl.ds(base, WIN), :]
        scores = jnp.where(key_mask(low, high), dot(keys, queries, NT), NEG)
        top = jnp.max(scores, axis=0, keepdims=True)
        terms = jnp.exp(scores - top)
        total = jnp.sum(terms, axis=0, keepdims=True)
        mixed = dot(values, terms.astype(BF), TN) / total
        return unstacked(mixed), top + jnp.log(total)

    @pl.loop(0, rows // QB)
    def _(blk):
        row0 = pl.multiple_of(blk * QB, QB)
        queries = stacked(q_ref[pl.ds(row0, QB), :]) * jnp.asarray(0.125, BF)
        seg_a = (row0 >= n0).astype(jnp.int32) + (row0 >= n1).astype(jnp.int32)
        end = row0 + QB - 1
        seg_b = (end >= n0).astype(jnp.int32) + (end >= n1).astype(jnp.int32)
        mixed, lse = one(queries, seg_a)
        out_ref[pl.ds(row0, QB), :] = mixed.astype(BF)
        lse_ref[0, pl.ds(blk, 1), :] = lse

        @pl.when(seg_b > seg_a)
        def _():
            split = jnp.where(seg_a == 0, n0, n1) - row0
            mixed_b, lse_b = one(queries, seg_b)
            here = lax.broadcasted_iota(jnp.int32, mixed.shape, 0) < split
            out_ref[pl.ds(row0, QB), :] = jnp.where(here, mixed, mixed_b).astype(BF)
            lane = lax.broadcasted_iota(jnp.int32, lse.shape, 1) % QB
            lse_ref[0, pl.ds(blk, 1), :] = jnp.where(lane < split, lse, lse_b)


def attend(meta, queries, key_value):
    rows, width = queries.shape
    pairs = width // (2 * HDIM)
    ext = key_value.shape[0]
    return pl.pallas_call(
        attend_kernel,
        grid_spec=pltpu.PrefetchScalarGridSpec(
            num_scalar_prefetch=1,
            grid=(pairs,),
            in_specs=[
                pl.BlockSpec((rows, 2 * HDIM), lambda p, m: (0, p)),
                pl.BlockSpec((ext, 2 * HDIM), lambda p, m: (0, p)),
                pl.BlockSpec((ext, 2 * HDIM), lambda p, m: (0, pairs + p)),
            ],
            out_specs=[
                pl.BlockSpec((rows, 2 * HDIM), lambda p, m: (0, p)),
                pl.BlockSpec((1, rows // QB, 2 * QB), lambda p, m: (p, 0, 0)),
            ],
        ),
        out_shape=[
            jax.ShapeDtypeStruct((rows, width), BF),
            jax.ShapeDtypeStruct((pairs, rows // QB, 2 * QB), F32),
        ],
        compiler_params=pltpu.CompilerParams(vmem_limit_bytes=48 * 2**20),
        name="attend",
    )(meta, queries, key_value, key_value)


def attend_back_kernel(meta, q_ref, k_ref, v_ref, up_ref, lse_ref, dq_ref, dk_ref, dv_ref):
    rows = q_ref.shape[0]
    n0 = meta[0]
    n1 = n0 + IMG
    table = segments(meta, rows)
    dk_ref[...] = jnp.zeros_like(dk_ref)
    dv_ref[...] = jnp.zeros_like(dv_ref)

    def one(queries, upstream, lse, seg):
        base, low, high = pick(seg, table)
        keys = k_ref[pl.ds(base, WIN), :]
        values = v_ref[pl.ds(base, WIN), :]
        scores = jnp.where(key_mask(low, high), dot(keys, queries, NT), NEG)
        probs = jnp.exp(scores - lse)
        dprobs = dot(values, upstream, NT)
        row_dot = jnp.sum(probs * dprobs, axis=0, keepdims=True)
        dscores = (probs * (dprobs - row_dot)).astype(BF)
        dv_ref[pl.ds(base, WIN), :] += dot(probs.astype(BF), upstream)
        dk_ref[pl.ds(base, WIN), :] += dot(dscores, queries)
        return unstacked(dot(keys, dscores, TN)) * 0.125

    @pl.loop(0, rows // QB)
    def _(blk):
        row0 = pl.multiple_of(blk * QB, QB)
        queries = stacked(q_ref[pl.ds(row0, QB), :]) * jnp.asarray(0.125, BF)
        upstream = stacked(up_ref[pl.ds(row0, QB), :])
        lse = lse_ref[0, pl.ds(blk, 1), :]
        seg_a = (row0 >= n0).astype(jnp.int32) + (row0 >= n1).astype(jnp.int32)
        end = row0 + QB - 1
        seg_b = (end >= n0).astype(jnp.int32) + (end >= n1).astype(jnp.int32)
        split = jnp.where(seg_b > seg_a, jnp.where(seg_a == 0, n0, n1) - row0, QB)
        lane = lax.broadcasted_iota(jnp.int32, lse.shape, 1) % QB
        dq = one(queries, upstream, jnp.where(lane < split, lse, -NEG), seg_a)
        dq_ref[pl.ds(row0, QB), :] = dq.astype(BF)

        @pl.when(seg_b > seg_a)
        def _():
            dq_b = one(queries, upstream, jnp.where(lane < split, -NEG, lse), seg_b)
            dq_ref[pl.ds(row0, QB), :] = (dq + dq_b).astype(BF)


def attend_back(meta, queries, key_value, upstream, lse):
    rows, width = queries.shape
    pairs = width // (2 * HDIM)
    ext = key_value.shape[0]
    own = pl.BlockSpec((rows, 2 * HDIM), lambda p, m: (0, p))
    wide = pl.BlockSpec((ext, 2 * HDIM), lambda p, m: (0, p))
    return pl.pallas_call(
        attend_back_kernel,
        grid_spec=pltpu.PrefetchScalarGridSpec(
            num_scalar_prefetch=1,
            grid=(pairs,),
            in_specs=[
                own,
                wide,
                pl.BlockSpec((ext, 2 * HDIM), lambda p, m: (0, pairs + p)),
                own,
                pl.BlockSpec((1, rows // QB, 2 * QB), lambda p, m: (p, 0, 0)),
            ],
            out_specs=[own, wide, wide],
        ),
        out_shape=[
            jax.ShapeDtypeStruct((rows, width), BF),
            jax.ShapeDtypeStruct((ext, width), F32),
            jax.ShapeDtypeStruct((ext, width), F32),
        ],
        compiler_params=pltpu.CompilerParams(vmem_limit_bytes=48 * 2**20),
        name="attend_back",
    )(meta, queries, key_value, key_value, upstream, lse)


def shifted(value, by):
    peers = lax.axis_size(AXIS)
    pairs = [(i, i + by) for i in range(peers) if 0 <= i + by < peers]
    return lax.ppermute(value, AXIS, pairs)


def gathered(value):
    return lax.all_gather(value, AXIS, axis=0, tiled=True)


def scattered(value):
    return lax.psum_scatter(value, AXIS, scatter_dimension=0, tiled=True)


def normalize(inputs, gain, shift):
    center = inputs - jnp.mean(inputs, axis=1, keepdims=True)
    inv_std = lax.rsqrt(jnp.mean(center * center, axis=1, keepdims=True) + EPS)
    scaled = center * inv_std
    return (scaled * gain + shift, scaled, inv_std)


def normalize_back(upstream, scaled, inv_std, gain):
    through = upstream * gain
    inner = (
        through
        - jnp.mean(through, axis=1, keepdims=True)
        - scaled * jnp.mean(through * scaled, axis=1, keepdims=True)
    )
    return (inv_std * inner, jnp.sum(upstream * scaled, axis=0), jnp.sum(upstream, axis=0))


def local(
    tokens,
    image_ids,
    cotangent,
    norm1_gain,
    norm1_shift,
    qkv_weight,
    query_bias,
    value_bias,
    out_weight,
    out_bias,
    norm2_gain,
    norm2_shift,
    up_weight,
    up_bias,
    down_weight,
    down_bias,
):
    rows, width = tokens.shape
    me = lax.axis_index(AXIS)
    peers = lax.axis_size(AXIS)
    meta = jnp.stack(
        [
            jnp.sum((image_ids == image_ids[0]).astype(jnp.int32)),
            (me == 0).astype(jnp.int32),
            (me == peers - 1).astype(jnp.int32),
        ]
    )
    ext = -(-(rows + 2 * RIM + 64) // 128) * 128
    vectors = gathered(
        jnp.concatenate(
            [norm1_gain, norm1_shift, query_bias, value_bias, out_bias, norm2_gain, norm2_shift,
             down_bias, up_bias]
        )[None]
    ).astype(F32)
    part = norm1_gain.shape[0]
    gain1, shift1, q_bias, v_bias, o_bias, gain2, shift2, d_bias = (
        vectors[:, i * part : (i + 1) * part].reshape(-1) for i in range(8)
    )
    u_bias = vectors[:, 8 * part :].reshape(-1)
    w_qkv, w_out, w_up, w_down = map(gathered, (qkv_weight, out_weight, up_weight, down_weight))

    low_rim = shifted(tokens[rows - RIM :], 1)
    high_rim = shifted(tokens[:RIM], -1)
    pad = jnp.zeros((ext - rows - 2 * RIM, width), BF)
    tokens_ext = jnp.concatenate([low_rim, tokens, high_rim, pad], axis=0).astype(F32)
    inputs = tokens.astype(F32)
    normed_ext = normalize(tokens_ext, gain1, shift1)[0].astype(BF)
    normed, scaled_one, inv_one = normalize(inputs, gain1, shift1)
    normed_low = normed.astype(BF)
    queries = (dot(normed_low, w_qkv[:, :width]) + q_bias).astype(BF)
    key_value = (
        dot(normed_ext, w_qkv[:, width:]) + jnp.concatenate([jnp.zeros_like(v_bias), v_bias])
    ).astype(BF)
    mixed_low, lse = attend(meta, queries, key_value)

    resid = inputs + dot(mixed_low, w_out) + o_bias
    normed_two, scaled_two, inv_two = normalize(resid, gain2, shift2)
    normed_two_low = normed_two.astype(BF)
    upward = dot(normed_two_low, w_up) + u_bias
    normal_cdf = 0.5 * (1.0 + lax.erf(upward * (1.0 / math.sqrt(2.0))))
    activated_low = (upward * normal_cdf).astype(BF)
    layer_out = (resid + dot(activated_low, w_down) + d_bias).astype(BF)

    upstream_out = cotangent.astype(F32)
    grad_down = dot(activated_low, cotangent, TN)
    grad_down_b = jnp.sum(upstream_out, axis=0)
    normal_pdf = jnp.exp(-0.5 * upward * upward) * (1.0 / math.sqrt(2.0 * math.pi))
    dupward_low = (dot(cotangent, w_down, NT) * (normal_cdf + upward * normal_pdf)).astype(BF)
    grad_up = dot(normed_two_low, dupward_low, TN)
    grad_up_b = jnp.sum(dupward_low.astype(F32), axis=0)
    dnormed_two = dot(dupward_low, w_up, NT)
    dresid_norm, grad_gain_two, grad_shift_two = normalize_back(
        dnormed_two, scaled_two, inv_two, gain2
    )
    dresid = upstream_out + dresid_norm
    dbranch_low = dresid.astype(BF)
    grad_out = dot(mixed_low, dbranch_low, TN)
    grad_out_b = jnp.sum(dbranch_low.astype(F32), axis=0)
    dmixed_low = dot(dbranch_low, w_out, NT).astype(BF)

    dquery_low, dkey_ext, dvalue_ext = attend_back(meta, queries, key_value, dmixed_low, lse)
    dkv_ext = jnp.concatenate([dkey_ext, dvalue_ext], axis=1)
    from_after = shifted(dkv_ext[:RIM].astype(BF), -1).astype(F32)
    from_before = shifted(dkv_ext[RIM + rows : 2 * RIM + rows].astype(BF), 1).astype(F32)
    own_grads = dkv_ext[RIM : RIM + rows]
    own_grads = own_grads.at[:RIM].add(from_before).at[rows - RIM :].add(from_after)
    dkv_low = own_grads.astype(BF)
    dproj_low = jnp.concatenate([dquery_low, dkv_low], axis=1)
    grad_qkv = dot(normed_low, dproj_low, TN)
    grad_query_b = jnp.sum(dquery_low.astype(F32), axis=0)
    grad_value_b = jnp.sum(dkv_low[:, width:].astype(F32), axis=0)
    dnormed = dot(dproj_low, w_qkv, NT)
    dinput_norm, grad_gain_one, grad_shift_one = normalize_back(
        dnormed, scaled_one, inv_one, gain1
    )
    grad_tokens = dresid + dinput_norm

    def small(value):
        return value.reshape(peers, -1)

    owned = scattered(
        jnp.concatenate(
            [
                small(v)
                for v in (
                    grad_gain_one, grad_shift_one, grad_query_b, grad_value_b, grad_out_b,
                    grad_gain_two, grad_shift_two, grad_down_b, grad_up_b,
                )
            ],
            axis=1,
        )
    )[0]
    g = [owned[i * part : (i + 1) * part] for i in range(8)] + [owned[8 * part :]]
    r_down, r_up, r_out, r_qkv = (
        scattered(v.astype(BF)).astype(F32) for v in (grad_down, grad_up, grad_out, grad_qkv)
    )
    return (
        layer_out, grad_tokens, g[0], g[1], r_qkv, g[2], g[3], r_out, g[4], g[5], g[6], r_up,
        g[8], r_down, g[7],
    )


def solution(mesh):
    row, vec = P(AXIS, None), P(AXIS)
    return jax.shard_map(
        local,
        mesh=mesh,
        in_specs=(
            row, vec, row, vec, vec, row, vec, vec, row, vec, vec, vec, row, vec, row, vec,
        ),
        out_specs=(
            row, row, vec, vec, row, vec, vec, row, vec, vec, vec, row, vec, row, vec,
        ),
        check_vma=False,
    )
```

```python
import functools
import math

import jax
import jax.numpy as jnp
from jax import lax
from jax.experimental import pallas as pl
from jax.experimental.pallas import tpu as pltpu
from jax.sharding import PartitionSpec as P

HDIM = 64
IMG = 577
RIM = IMG - 1
WIN = 592
QB = 128
EPS = 1e-06
NEG = -1e30
AXIS = "fsdp"
BF = jnp.bfloat16
F32 = jnp.float32
NT = (((1,), (1,)), ((), ()))
TN = (((0,), (0,)), ((), ()))
NN = (((1,), (0,)), ((), ()))


def dot(a, b, dims=NN):
    return lax.dot_general(a, b, dims, preferred_element_type=F32)


def stacked(block):
    lane = lax.broadcasted_iota(jnp.int32, block.shape, 1)
    zero = jnp.zeros_like(block)
    return jnp.concatenate(
        [jnp.where(lane < HDIM, block, zero), jnp.where(lane >= HDIM, block, zero)], axis=0
    )


def unstacked(wide):
    return jnp.concatenate([wide[:HDIM, :QB], wide[HDIM:, QB:]], axis=0).T


def key_mask(low, high):
    row = lax.broadcasted_iota(jnp.int32, (WIN, 2 * QB), 0)
    return (row >= low) & (row < high)


def mesh_copy(src, dst, send_sem, recv_sem, to):
    return pltpu.make_async_remote_copy(
        src_ref=src,
        dst_ref=dst,
        send_sem=send_sem,
        recv_sem=recv_sem,
        device_id=(to,),
        device_id_type=pl.DeviceIdType.MESH,
    )


class Place:
    def __init__(self):
        me = lax.axis_index(AXIS)
        self.c, self.x, self.y, self.z = me % 2, me // 2 % 2, me // 4 % 2, me // 8
        self.sib = self.at(self.z, self.y, self.x, 1 - self.c)
        self.xp = self.at(self.z, self.y, 1 - self.x, self.c)
        self.yp = self.at(self.z, 1 - self.y, self.x, self.c)
        self.zp = [self.at((self.z + k) % 4, self.y, self.x, self.c) for k in (1, 2, 3)]
        self.partners = [self.sib, self.xp, self.yp, *self.zp]

    @staticmethod
    def at(z, y, x, c):
        return ((z * 2 + y) * 2 + x) * 2 + c


def greet(partners, before=None, after=None):
    barrier = pltpu.get_barrier_semaphore()

    def hello(to):
        pl.semaphore_signal(
            barrier, inc=1, device_id=(to,), device_id_type=pl.DeviceIdType.MESH
        )

    for to in partners:
        hello(to)
    if before is None:
        pl.semaphore_wait(barrier, len(partners))
        return
    me = lax.axis_index(AXIS)
    pl.when(before)(lambda: hello(me - 1))
    pl.when(after)(lambda: hello(me + 1))
    pl.semaphore_wait(
        barrier, len(partners) + before.astype(jnp.int32) + after.astype(jnp.int32)
    )


class Gather:
    def __init__(self, place, shard, full, cols, send, recv, own):
        self.shard, self.own = shard.at[:, cols], own
        p, rows = place, shard.shape[0]
        half = rows // 2

        def block(y, x, part=slice(None)):
            return full.at[:, y, x, p.c, part, cols]

        mine = full.at[p.z, p.y, p.x, p.c, :, cols]
        self.local = lambda: pltpu.make_async_copy(self.shard, mine, own)

        def copy(i, src, dst, to):
            return lambda: mesh_copy(src, dst, send.at[i], recv.at[i], to)

        same = lambda i, ref, to: copy(i, ref, ref, to)
        first, second = pl.ds(0, half), pl.ds(half, half)
        self.z = [copy(i, self.shard, mine, to) for i, to in enumerate(p.zp)]
        self.xy = [same(3, block(p.y, p.x), p.xp), same(4, block(p.y, p.x), p.yp)]
        self.far = [
            same(5, block(p.y, 1 - p.x, first), p.yp),
            same(6, block(1 - p.y, p.x, second), p.xp),
        ]
        self.pair = [
            same(7, block(p.y, p.x), p.sib),
            same(8, block(p.y, 1 - p.x), p.sib),
            same(9, block(1 - p.y, p.x), p.sib),
            same(10, block(1 - p.y, 1 - p.x), p.sib),
        ]

    def stage(self, number):
        if number == 0:
            self.local().start()
            for c in self.z:
                c().start()
        elif number == 1:
            self.local().wait()
            for c in self.z:
                c().wait()
            for c in (*self.xy, self.pair[0]):
                c().start()
        elif number == 2:
            for c in self.xy:
                c().wait()
            for c in (*self.far, self.pair[1], self.pair[2]):
                c().start()
        elif number == 3:
            for c in self.far:
                c().wait()
            self.pair[3]().start()
        else:
            for c in self.pair:
                c().wait()


GATHER_SEMS = 11


def run_stages(pieces, tick, last):
    for at in range(last + 1):
        steps = [
            (s, piece)
            for k, piece in enumerate(pieces)
            for s in (4, 3, 2, 1, 0)
            if k + s == at
        ]
        if steps:
            @pl.when(tick == at)
            def _():
                for s, piece in steps:
                    piece.stage(s)


class Scatter:
    def __init__(self, place, grad, held, from_pair, far, side, line, out, sems):
        self.p, self.out = place, out
        self.held, self.from_pair, self.far, self.side, self.line = held, from_pair, far, side, line
        p, rows = place, held.shape[3]
        self.half = rows // 2
        own, send, recv = sems
        first, second = pl.ds(0, self.half), pl.ds(self.half, self.half)

        def copy(i, src, dst, to):
            return lambda: mesh_copy(src, dst, send.at[i], recv.at[i], to)

        self.load = lambda: pltpu.make_async_copy(grad.at[:, :, :, p.c], held, own)
        self.to_pair = copy(0, grad.at[:, :, :, 1 - p.c], from_pair, p.sib)
        self.to_far = [
            copy(1, held.at[:, 1 - p.y, 1 - p.x, first], far.at[0], p.xp),
            copy(2, held.at[:, 1 - p.y, 1 - p.x, second], far.at[1], p.yp),
        ]
        self.to_side = [
            copy(3, held.at[:, p.y, 1 - p.x], side.at[0], p.xp),
            copy(4, held.at[:, 1 - p.y, p.x], side.at[1], p.yp),
        ]
        self.to_line = [
            copy(5 + k, held.at[(p.z + k + 1) % 4, p.y, p.x], line.at[k], to)
            for k, to in enumerate(p.zp)
        ]

    def stage(self, number):
        p, half = self.p, self.half
        held, far, side, line = self.held, self.far, self.side, self.line
        if number == 0:
            self.load().start()
            self.to_pair().start()
        elif number == 1:
            self.load().wait()
            self.to_pair().wait()

            @pl.loop(0, 4)
            def _(z):
                for y in range(2):
                    for x in range(2):
                        held[z, y, x] = (
                            held[z, y, x].astype(F32) + self.from_pair[z, y, x].astype(F32)
                        ).astype(held.dtype)

            for c in self.to_far:
                c().start()
        elif number == 2:
            for c in self.to_far:
                c().wait()

            @pl.loop(0, 4)
            def _(z):
                held[z, 1 - p.y, p.x, :half] = (
                    held[z, 1 - p.y, p.x, :half].astype(F32) + far[0, z].astype(F32)
                ).astype(held.dtype)
                held[z, p.y, 1 - p.x, half:] = (
                    held[z, p.y, 1 - p.x, half:].astype(F32) + far[1, z].astype(F32)
                ).astype(held.dtype)

            for c in self.to_side:
                c().start()
        elif number == 3:
            for c in self.to_side:
                c().wait()

            @pl.loop(0, 4)
            def _(z):
                held[z, p.y, p.x] = (
                    held[z, p.y, p.x].astype(F32)
                    + side[0, z].astype(F32)
                    + side[1, z].astype(F32)
                ).astype(held.dtype)

            for c in self.to_line:
                c().start()
        else:
            for c in self.to_line:
                c().wait()
            self.out[...] = (
                held[p.z, p.y, p.x].astype(F32)
                + line[0].astype(F32)
                + line[1].astype(F32)
                + line[2].astype(F32)
            )


SCATTER_SEMS = 8
UNIT = 1024


def scatter_scratch(rows, cols, dtype=BF):
    return [
        pltpu.VMEM((4, 2, 2, rows, cols), dtype),
        pltpu.VMEM((4, 2, 2, rows, cols), dtype),
        pltpu.VMEM((2, 4, rows // 2, cols), dtype),
        pltpu.VMEM((2, 4, rows, cols), dtype),
        pltpu.VMEM((3, rows, cols), dtype),
        pltpu.SemaphoreType.DMA,
        pltpu.SemaphoreType.DMA((SCATTER_SEMS,)),
        pltpu.SemaphoreType.DMA((SCATTER_SEMS,)),
    ]


def blocks(value):
    return value.reshape(4, 2, 2, 2, value.shape[0] // 32, value.shape[1])


def gather_kernel(wide, vec, wide_out, vec_out, send, recv, own):
    place = Place()
    greet(place.partners)
    pieces = [Gather(place, vec, vec_out, pl.ds(0, vec.shape[1]), send.at[0], recv.at[0], own.at[0])]
    for k in range(wide.shape[1] // UNIT):
        pieces.append(
            Gather(
                place, wide, wide_out, pl.ds(k * UNIT, UNIT), send.at[k + 1], recv.at[k + 1],
                own.at[k + 1],
            )
        )
    for at in range(len(pieces) + 4):
        for s in (4, 3, 2, 1, 0):
            if 0 <= at - s < len(pieces):
                pieces[at - s].stage(s)


def gather_blocks(wide, vec):
    count = wide.shape[1] // UNIT + 1
    out = [
        jax.ShapeDtypeStruct((4, 2, 2, 2, *v.shape), v.dtype) for v in (wide, vec)
    ]
    hbm = pl.BlockSpec(memory_space=pl.ANY)
    full, small = pl.pallas_call(
        gather_kernel,
        out_shape=out,
        in_specs=[hbm, hbm],
        out_specs=[hbm, hbm],
        scratch_shapes=[
            pltpu.SemaphoreType.DMA((count, GATHER_SEMS)),
            pltpu.SemaphoreType.DMA((count, GATHER_SEMS)),
            pltpu.SemaphoreType.DMA((count,)),
        ],
        compiler_params=pltpu.CompilerParams(collective_id=0, has_side_effects=True),
        name="gather_qkv",
    )(wide, vec)
    return full.reshape(-1, wide.shape[1]), small.reshape(32, -1)


def scatter_kernel(g_q, g_k, g_v, small, out, small_out, *scratch):
    place = Place()
    greet(place.partners)
    size = 8
    pieces = []
    for k, grad in enumerate((g_q, g_k, g_v, small)):
        bufs = scratch[k * size : (k + 1) * size]
        to = small_out if k == 3 else out.at[:, pl.ds(k * UNIT, UNIT)]
        pieces.append(Scatter(place, grad, *bufs[:5], to, bufs[5:]))
    for at in range(len(pieces) + 4):
        for s in (4, 3, 2, 1, 0):
            if 0 <= at - s < len(pieces):
                pieces[at - s].stage(s)


def scatter_blocks(grads, small):
    hbm = pl.BlockSpec(memory_space=pl.ANY)
    vmem = pl.BlockSpec(memory_space=pltpu.VMEM)
    rows = grads[0].shape[0] // 32
    small = blocks(small)
    return pl.pallas_call(
        scatter_kernel,
        out_shape=[
            jax.ShapeDtypeStruct((rows, 3 * UNIT), F32),
            jax.ShapeDtypeStruct(small.shape[4:], F32),
        ],
        in_specs=[hbm] * 4,
        out_specs=[vmem] * 2,
        scratch_shapes=scatter_scratch(rows, UNIT) * 3
        + scatter_scratch(*small.shape[4:], F32),
        compiler_params=pltpu.CompilerParams(
            collective_id=3, has_side_effects=True, vmem_limit_bytes=40 * 2**20
        ),
        name="scatter_qkv",
    )(*map(blocks, grads), small)


ITEMS = 10


class Images:
    def __init__(self, n0, rows, ext):
        self.n0, self.n1, self.rows, self.ext = n0, n0 + IMG, rows, ext
        me, peers = lax.axis_index(AXIS), lax.axis_size(AXIS)
        limit = jnp.where(me == peers - 1, RIM + rows, 2 * RIM + rows)
        start0 = jnp.where(me == 0, RIM, n0 - 1)
        start1 = RIM + n0
        start2 = start1 + IMG
        self.spans = (
            (start0, start1),
            (start1, jnp.minimum(start1 + IMG, limit)),
            (start2, jnp.minimum(start2 + IMG, limit)),
        )
        one = lambda flag: jnp.where(flag, 1, 0)
        self.b0, self.b1 = lax.div(n0, QB), lax.div(self.n1, QB)
        self.d0 = one(self.b0 * QB != n0)
        self.d1 = one((self.n1 < rows) & (self.b1 * QB != self.n1))
        self.third = self.n1 < rows
        self.end0 = lax.div(n0 - 1, QB)
        self.end1 = lax.div(self.n1 - 1, QB) + self.d0
        self.one = one

    def base(self, start):
        return jnp.minimum(lax.div(start, 16), (self.ext - WIN) // 16)

    def segment(self, item):
        return self.one(item > self.end0) + self.one(item > self.end1)

    def item(self, item):
        blk = (
            item
            - self.d0 * self.one(item > self.b0)
            - self.d1 * self.one(item > self.b1 + self.d0)
        )
        used = blk < self.rows // QB
        blk = jnp.minimum(blk, self.rows // QB - 1)
        seg = self.segment(item)
        choose = lambda i: jnp.where(
            seg == 0, self.spans[0][i], jnp.where(seg == 1, self.spans[1][i], self.spans[2][i])
        )
        start, stop = choose(0), choose(1)
        base = self.base(start) * 16
        row0 = blk * QB
        low = jnp.maximum(start - RIM - row0, 0)
        high = jnp.where(used, jnp.minimum(stop - RIM - row0, QB), 0)
        return blk, row0, base, start - base, stop - base, low, high

    def of_block(self, blk):
        at0 = self.d0 * self.one(blk == self.b0)
        at1 = self.d1 * self.one(blk == self.b1)
        first = blk + self.d0 * self.one(blk > self.b0) + self.d1 * self.one(blk > self.b1)
        split = jnp.where(at0 == 1, self.n0, jnp.where(at1 == 1, self.n1, self.rows)) - blk * QB
        return first, first + at0 + at1, split


def attend_body(n0_ref, q_ref, k_ref, v_ref, out_ref, lse_ref, parts, parts_lse):
    rows = q_ref.shape[0]
    images = Images(n0_ref[0], rows, k_ref.shape[0])

    @pl.loop(0, ITEMS)
    def _(item):
        _, row0, base, low, high, _, _ = images.item(item)
        queries = stacked(q_ref[pl.ds(row0, QB), :]) * jnp.asarray(0.125, BF)
        keys = k_ref[pl.ds(base, WIN), :]
        values = v_ref[pl.ds(base, WIN), :]
        scores = jnp.where(key_mask(low, high), dot(keys, queries, NT), NEG)
        top = jnp.max(scores, axis=0, keepdims=True)
        terms = jnp.exp(scores - top)
        total = jnp.sum(terms, axis=0, keepdims=True)
        mixed = dot(values, terms.astype(BF), TN) / total
        parts[item] = unstacked(mixed)
        parts_lse[item] = jnp.broadcast_to(top + jnp.log(total), parts_lse.shape[1:])

    for blk in range(rows // QB):
        first, last, split = images.of_block(blk)
        row = lax.broadcasted_iota(jnp.int32, (QB, 2 * HDIM), 0)
        out_ref[pl.ds(blk * QB, QB), :] = jnp.where(
            row < split, parts[first], parts[last]
        ).astype(BF)
        lane = lax.broadcasted_iota(jnp.int32, parts_lse.shape[1:], 1) % QB
        lse_ref[0, pl.ds(blk, 1), :] = jnp.where(
            lane < split, parts_lse[first], parts_lse[last]
        )[:1]


def attend_kernel(n0_ref, q_ref, k_ref, v_ref, out_ref, lse_ref, parts, parts_lse):
    attend_body(n0_ref, q_ref, k_ref, v_ref, out_ref, lse_ref, parts, parts_lse)


def attend_gather_kernel(
    n0_ref, q_ref, k_ref, v_ref, w_out, w_up, out_ref, lse_ref, full_out, full_up,
    parts, parts_lse, send, recv, own,
):
    tick = pl.program_id(0)
    place = Place()
    pl.when(tick == 0)(lambda: greet(place.partners))
    pieces = []
    for shard, full in ((w_out, full_out), (w_up, full_up)):
        for k in range(shard.shape[1] // UNIT):
            i = len(pieces)
            pieces.append(
                Gather(
                    place, shard, full, pl.ds(k * UNIT, UNIT), send.at[i], recv.at[i], own.at[i]
                )
            )
    run_stages(pieces, tick, 7)
    attend_body(n0_ref, q_ref, k_ref, v_ref, out_ref, lse_ref, parts, parts_lse)

    @pl.when(tick == 7)
    def _():
        pieces[-1].stage(4)


def attend(n0, queries, key_value, shards=None):
    rows, width = queries.shape
    pairs = width // (2 * HDIM)
    ext = key_value.shape[0]
    hbm = pl.BlockSpec(memory_space=pl.ANY)
    in_specs = [
        pl.BlockSpec(memory_space=pltpu.SMEM),
        pl.BlockSpec((rows, 2 * HDIM), lambda p: (0, p)),
        pl.BlockSpec((ext, 2 * HDIM), lambda p: (0, p)),
        pl.BlockSpec((ext, 2 * HDIM), lambda p: (0, pairs + p)),
    ]
    out_specs = [
        pl.BlockSpec((rows, 2 * HDIM), lambda p: (0, p)),
        pl.BlockSpec((1, rows // QB, 2 * QB), lambda p: (p, 0, 0)),
    ]
    out_shape = [
        jax.ShapeDtypeStruct((rows, width), BF),
        jax.ShapeDtypeStruct((pairs, rows // QB, 2 * QB), F32),
    ]
    scratch = [
        pltpu.VMEM((ITEMS, QB, 2 * HDIM), F32),
        pltpu.VMEM((ITEMS, 8, 2 * QB), F32),
    ]
    params = dict(vmem_limit_bytes=48 * 2**20)
    args = [n0, queries, key_value, key_value]
    kernel = attend_kernel
    if shards is not None:
        kernel = attend_gather_kernel
        in_specs += [hbm] * 2
        out_specs += [hbm] * 2
        out_shape += [jax.ShapeDtypeStruct((4, 2, 2, 2, *v.shape), BF) for v in shards]
        count = sum(v.shape[1] // UNIT for v in shards)
        scratch += [
            pltpu.SemaphoreType.DMA((count, GATHER_SEMS)),
            pltpu.SemaphoreType.DMA((count, GATHER_SEMS)),
            pltpu.SemaphoreType.DMA((count,)),
        ]
        params |= dict(collective_id=1, has_side_effects=True)
        args += shards
    return pl.pallas_call(
        kernel,
        grid=(pairs,),
        in_specs=in_specs,
        out_specs=out_specs,
        out_shape=out_shape,
        scratch_shapes=scratch,
        compiler_params=pltpu.CompilerParams(**params),
        name="attend",
    )(*args)


TILE = 64


def attend_back_body(
    pair, pairs, n0_ref, q_ref, k_ref, v_ref, up_ref, lse_ref, dq_ref, dk_ref, dv_ref,
    slots, parts, padded, outgoing, incoming, send, recv,
):
    rows = q_ref.shape[0]
    images = Images(n0_ref[0], rows, k_ref.shape[0])
    me, peers = lax.axis_index(AXIS), lax.axis_size(AXIS)
    wide = slice(TILE, TILE + WIN)

    def halo(p, way):
        return mesh_copy(
            outgoing.at[p, way], incoming.at[p, way], send.at[p, way], recv.at[p, way],
            me - 1 if way == 0 else me + 1,
        )

    @pl.when(pair == 0)
    def _():
        slots[0] = jnp.zeros(slots.shape[1:], F32)
        padded[...] = jnp.zeros(padded.shape, F32)

        @pl.when(me == 0)
        def _():
            incoming[:, 1] = jnp.zeros((pairs, WIN, 4 * HDIM), BF)

        @pl.when(me == peers - 1)
        def _():
            incoming[:, 0] = jnp.zeros((pairs, WIN, 4 * HDIM), BF)

    @pl.when(pair < pairs)
    def _():
        @pl.loop(0, ITEMS)
        def _(item):
            blk, row0, base, low, high, first, stop = images.item(item)
            queries = stacked(q_ref[pl.ds(row0, QB), :]) * jnp.asarray(0.125, BF)
            upstream = stacked(up_ref[pl.ds(row0, QB), :])
            lane = lax.broadcasted_iota(jnp.int32, (1, 2 * QB), 1) % QB
            here = (lane >= first) & (lane < stop)
            lse = jnp.where(here, lse_ref[0, pl.ds(blk, 1), :], -NEG)
            keys = k_ref[pl.ds(base, WIN), :]
            values = v_ref[pl.ds(base, WIN), :]
            scores = jnp.where(key_mask(low, high), dot(keys, queries, NT), NEG)
            probs = jnp.exp(scores - lse)
            dprobs = dot(values, upstream, NT)
            row_dot = jnp.sum(probs * dprobs, axis=0, keepdims=True)
            dscores = (probs * (dprobs - row_dot)).astype(BF)
            same = images.segment(item) == images.segment(item - 1)
            keep = (item > 0) & same
            old = jnp.where(keep, slots[item], jnp.zeros(slots.shape[1:], F32))
            slots[item + 1, :, : 2 * HDIM] = old[:, : 2 * HDIM] + dot(dscores, queries)
            slots[item + 1, :, 2 * HDIM :] = old[:, 2 * HDIM :] + dot(probs.astype(BF), upstream)
            parts[item] = unstacked(dot(keys, dscores, TN)) * 0.125

        for blk in range(rows // QB):
            first, last, split = images.of_block(blk)
            row = lax.broadcasted_iota(jnp.int32, (QB, 2 * HDIM), 0)
            dq_ref[pl.ds(blk * QB, QB), :] = jnp.where(
                row < split, parts[first], parts[last]
            ).astype(BF)

    @pl.when(pair > 0)
    def _():
        done = pair - 1

        @pl.when(me > 0)
        def _():
            halo(done, 0).wait_send()

        @pl.when(me < peers - 1)
        def _():
            halo(done, 0).wait_recv()
            halo(done, 1).wait_send()

        @pl.when(me > 0)
        def _():
            halo(done, 1).wait_recv()

        none = jnp.zeros((WIN, 4 * HDIM), F32)
        last = jnp.where(images.third, 2, 1)
        stop = jnp.where(images.third, images.spans[2][1], images.spans[1][1])
        cut = (stop > RIM + rows) & (me < peers - 1)
        after = jnp.where(cut, incoming[done, 0].astype(F32), none)
        before = jnp.where(images.spans[0][0] < RIM, incoming[done, 1].astype(F32), none)
        padded[0, wide] = padded[0, wide] + before
        padded[1, wide] = padded[1, wide] + jnp.where(last == 1, after, none)
        padded[2, wide] = padded[2, wide] + jnp.where(last == 2, after, none)
        bases = [images.base(span[0]) for span in images.spans]

        @pl.loop(0, rows // TILE)
        def _(tile):
            row = pl.multiple_of(tile * TILE, TILE)
            total = None
            for seg, base in enumerate(bases):
                off = jnp.maximum((RIM + TILE) // 16 + tile * (TILE // 16) - base, 0)
                off = jnp.minimum(off, (WIN + TILE) // 16) * 16
                term = padded[seg, pl.ds(off, TILE), :]
                total = term if total is None else total + term
            dk_ref[pl.ds(row, TILE), :] = total[:, : 2 * HDIM].astype(BF)
            dv_ref[pl.ds(row, TILE), :] = total[:, 2 * HDIM :].astype(BF)

    @pl.when(pair < pairs)
    def _():
        ends = (
            images.end0 + 1,
            jnp.minimum(images.end1, (rows - 1) // QB + images.d0) + 1,
            jnp.where(images.third, ITEMS, 0),
        )
        for seg, end in enumerate(ends):
            padded[seg, wide] = slots[end]
        outgoing[pair, 0] = padded[0, wide].astype(BF)
        outgoing[pair, 1] = jnp.where(images.third, padded[2, wide], padded[1, wide]).astype(BF)

        @pl.when(me > 0)
        def _():
            halo(pair, 0).start()

        @pl.when(me < peers - 1)
        def _():
            halo(pair, 1).start()


def attend_back_kernel(pairs, *refs):
    me, peers = lax.axis_index(AXIS), lax.axis_size(AXIS)
    pair = pl.program_id(0)
    pl.when(pair == 0)(lambda: greet([], me > 0, me < peers - 1))
    attend_back_body(pair, pairs, *refs)


def attend_back_scatter_kernel(pairs, *refs):
    base, (g_out, g_up), rest = refs[:6], refs[6:8], refs[8:]
    outs, (r_out, r_up), scratch = rest[:3], rest[3:5], rest[5:]
    mine, comm = scratch[:7], scratch[7:]
    me, peers = lax.axis_index(AXIS), lax.axis_size(AXIS)
    pair = pl.program_id(0)
    place = Place()
    pl.when(pair == 0)(lambda: greet(place.partners, me > 0, me < peers - 1))
    pieces = []
    for grad, out in ((g_out, r_out), (g_up, r_up)):
        for k in range(grad.shape[5] // UNIT):
            cols = pl.ds(k * UNIT, UNIT)
            bufs = comm[len(pieces) * 8 : len(pieces) * 8 + 8]
            pieces.append(
                Scatter(
                    place, grad.at[:, :, :, :, :, cols], *bufs[:5], out.at[:, cols], bufs[5:]
                )
            )
    run_stages(pieces, pair, pairs)
    attend_back_body(pair, pairs, *base, *outs, *mine)


def attend_back(n0, queries, key_value, upstream, lse, grads=None):
    rows, width = queries.shape
    pairs = width // (2 * HDIM)
    ext = key_value.shape[0]
    hbm, vmem = pl.BlockSpec(memory_space=pl.ANY), pl.BlockSpec(memory_space=pltpu.VMEM)
    here = lambda p: jnp.minimum(p, pairs - 1)
    own = pl.BlockSpec((rows, 2 * HDIM), lambda p: (0, here(p)))
    late = pl.BlockSpec((rows, 2 * HDIM), lambda p: (0, jnp.maximum(p - 1, 0)))
    in_specs = [
        pl.BlockSpec(memory_space=pltpu.SMEM),
        own,
        pl.BlockSpec((ext, 2 * HDIM), lambda p: (0, here(p))),
        pl.BlockSpec((ext, 2 * HDIM), lambda p: (0, pairs + here(p))),
        own,
        pl.BlockSpec((1, rows // QB, 2 * QB), lambda p: (here(p), 0, 0)),
    ]
    out_specs = [own, late, late]
    out_shape = [jax.ShapeDtypeStruct((rows, width), BF)] * 3
    scratch = [
        pltpu.VMEM((ITEMS + 1, WIN, 4 * HDIM), F32),
        pltpu.VMEM((ITEMS, QB, 2 * HDIM), F32),
        pltpu.VMEM((3, WIN + 2 * TILE, 4 * HDIM), F32),
        pltpu.VMEM((pairs, 2, WIN, 4 * HDIM), BF),
        pltpu.VMEM((pairs, 2, WIN, 4 * HDIM), BF),
        pltpu.SemaphoreType.DMA((pairs, 2)),
        pltpu.SemaphoreType.DMA((pairs, 2)),
    ]
    args = [n0, queries, key_value, key_value, upstream, lse]
    kernel, collective = attend_back_kernel, 4
    if grads is not None:
        kernel, collective = attend_back_scatter_kernel, 2
        args += map(blocks, grads)
        in_specs += [hbm] * 2
        out_specs += [vmem] * 2
        out_shape += [jax.ShapeDtypeStruct((v.shape[0] // 32, v.shape[1]), F32) for v in grads]
        for v in grads:
            scratch += scatter_scratch(v.shape[0] // 32, UNIT) * (v.shape[1] // UNIT)
    return pl.pallas_call(
        functools.partial(kernel, pairs),
        grid=(pairs + 1,),
        in_specs=in_specs,
        out_specs=out_specs,
        out_shape=out_shape,
        scratch_shapes=scratch,
        compiler_params=pltpu.CompilerParams(
            vmem_limit_bytes=58 * 2**20, collective_id=collective, has_side_effects=True
        ),
        name="attend_back",
    )(*args)


def shifted(value, by):
    peers = lax.axis_size(AXIS)
    pairs = [(i, i + by) for i in range(peers) if 0 <= i + by < peers]
    return lax.ppermute(value, AXIS, pairs)


def gathered(value):
    return lax.all_gather(value, AXIS, axis=0, tiled=True)


def scattered(value):
    return lax.psum_scatter(value, AXIS, scatter_dimension=0, tiled=True)


def normalize(inputs, gain, shift):
    center = inputs - jnp.mean(inputs, axis=1, keepdims=True)
    inv_std = lax.rsqrt(jnp.mean(center * center, axis=1, keepdims=True) + EPS)
    scaled = center * inv_std
    return (scaled * gain + shift, scaled, inv_std)


def normalize_back(upstream, scaled, inv_std, gain):
    through = upstream * gain
    inner = (
        through
        - jnp.mean(through, axis=1, keepdims=True)
        - scaled * jnp.mean(through * scaled, axis=1, keepdims=True)
    )
    return (inv_std * inner, jnp.sum(upstream * scaled, axis=0), jnp.sum(upstream, axis=0))


def local(
    tokens,
    image_ids,
    cotangent,
    norm1_gain,
    norm1_shift,
    qkv_weight,
    query_bias,
    value_bias,
    out_weight,
    out_bias,
    norm2_gain,
    norm2_shift,
    up_weight,
    up_bias,
    down_weight,
    down_bias,
):
    rows, width = tokens.shape
    me = lax.axis_index(AXIS)
    peers = lax.axis_size(AXIS)
    n0 = jnp.sum((image_ids == image_ids[0]).astype(jnp.int32)).reshape(1)
    ext = -(-(rows + 2 * RIM + 64) // 128) * 128
    packed = jnp.concatenate(
        [norm1_gain, norm1_shift, query_bias, value_bias, out_bias, norm2_gain, norm2_shift,
         down_bias, up_bias]
    )
    block_plan = peers == 32
    if block_plan:
        count = packed.shape[0]
        packed = jnp.pad(packed, (0, 32 * 128 - count)).reshape(32, 128)
        w_qkv, vectors = gather_blocks(qkv_weight, packed)
        vectors = vectors[:, :count].astype(F32)
    else:
        w_qkv, vectors = gathered(qkv_weight), gathered(packed[None]).astype(F32)
        w_out, w_up = gathered(out_weight), gathered(up_weight)
    w_down = gathered(down_weight)
    part = norm1_gain.shape[0]
    gain1, shift1, q_bias, v_bias, o_bias, gain2, shift2, d_bias = (
        vectors[:, i * part : (i + 1) * part].reshape(-1) for i in range(8)
    )
    u_bias = vectors[:, 8 * part :].reshape(-1)

    low_rim = shifted(tokens[rows - RIM :], 1)
    high_rim = shifted(tokens[:RIM], -1)
    pad = jnp.zeros((ext - rows - 2 * RIM, width), BF)
    tokens_ext = jnp.concatenate([low_rim, tokens, high_rim, pad], axis=0).astype(F32)
    inputs = tokens.astype(F32)
    normed_ext = normalize(tokens_ext, gain1, shift1)[0].astype(BF)
    normed, scaled_one, inv_one = normalize(inputs, gain1, shift1)
    normed_low = normed.astype(BF)
    queries = (dot(normed_low, w_qkv[:, :width]) + q_bias).astype(BF)
    key_value = (
        dot(normed_ext, w_qkv[:, width:]) + jnp.concatenate([jnp.zeros_like(v_bias), v_bias])
    ).astype(BF)
    if block_plan:
        mixed_low, lse, w_out, w_up = attend(
            n0, queries, key_value, (out_weight, up_weight)
        )
        w_out, w_up = w_out.reshape(width, -1), w_up.reshape(width, -1)
    else:
        mixed_low, lse = attend(n0, queries, key_value)

    resid = inputs + dot(mixed_low, w_out) + o_bias
    normed_two, scaled_two, inv_two = normalize(resid, gain2, shift2)
    normed_two_low = normed_two.astype(BF)
    upward = dot(normed_two_low, w_up) + u_bias
    normal_cdf = 0.5 * (1.0 + lax.erf(upward * (1.0 / math.sqrt(2.0))))
    activated_low = (upward * normal_cdf).astype(BF)
    layer_out = (resid + dot(activated_low, w_down) + d_bias).astype(BF)

    upstream_out = cotangent.astype(F32)
    grad_down = dot(activated_low, cotangent, TN)
    grad_down_b = jnp.sum(upstream_out, axis=0)
    normal_pdf = jnp.exp(-0.5 * upward * upward) * (1.0 / math.sqrt(2.0 * math.pi))
    dupward_low = (dot(cotangent, w_down, NT) * (normal_cdf + upward * normal_pdf)).astype(BF)
    grad_up = dot(normed_two_low, dupward_low, TN)
    grad_up_b = jnp.sum(dupward_low.astype(F32), axis=0)
    dnormed_two = dot(dupward_low, w_up, NT)
    dresid_norm, grad_gain_two, grad_shift_two = normalize_back(
        dnormed_two, scaled_two, inv_two, gain2
    )
    dresid = upstream_out + dresid_norm
    dbranch_low = dresid.astype(BF)
    grad_out = dot(mixed_low, dbranch_low, TN)
    grad_out_b = jnp.sum(dbranch_low.astype(F32), axis=0)
    dmixed_low = dot(dbranch_low, w_out, NT).astype(BF)

    grad_out, grad_up = grad_out.astype(BF), grad_up.astype(BF)
    r_down = scattered(grad_down.astype(BF)).astype(F32)
    if block_plan:
        dquery, dkey, dvalue, r_out, r_up = attend_back(
            n0, queries, key_value, dmixed_low, lse, (grad_out, grad_up)
        )
    else:
        dquery, dkey, dvalue = attend_back(n0, queries, key_value, dmixed_low, lse)
        r_out, r_up = (scattered(v).astype(F32) for v in (grad_out, grad_up))
    dproj = (dquery, dkey, dvalue)
    grad_qkv = [dot(normed_low, v, TN).astype(BF) for v in dproj]
    grad_query_b = jnp.sum(dquery.astype(F32), axis=0)
    grad_value_b = jnp.sum(dvalue.astype(F32), axis=0)
    dnormed = sum(
        dot(v, w_qkv[:, i * width : (i + 1) * width], NT) for i, v in enumerate(dproj)
    )
    dinput_norm, grad_gain_one, grad_shift_one = normalize_back(
        dnormed, scaled_one, inv_one, gain1
    )
    grad_tokens = dresid + dinput_norm

    def small(value):
        return value.reshape(peers, -1)

    smalls = jnp.concatenate(
        [
            small(v)
            for v in (
                grad_gain_one, grad_shift_one, grad_query_b, grad_value_b, grad_out_b,
                grad_gain_two, grad_shift_two, grad_down_b, grad_up_b,
            )
        ],
        axis=1,
    )
    if block_plan:
        count = smalls.shape[1]
        smalls = jnp.pad(smalls, ((0, 0), (0, 16 * 128 - count))).reshape(peers * 16, 128)
        r_qkv, owned = scatter_blocks(grad_qkv, smalls)
        owned = owned.reshape(-1)[:count]
    else:
        owned = scattered(smalls)[0]
        r_qkv = jnp.concatenate([scattered(v) for v in grad_qkv], axis=1).astype(F32)
    g = [owned[i * part : (i + 1) * part] for i in range(8)] + [owned[8 * part :]]
    return (
        layer_out, grad_tokens, g[0], g[1], r_qkv, g[2], g[3], r_out, g[4], g[5], g[6], r_up,
        g[8], r_down, g[7],
    )


def solution(mesh):
    row, vec = P(AXIS, None), P(AXIS)
    return jax.shard_map(
        local,
        mesh=mesh,
        in_specs=(
            row, vec, row, vec, vec, row, vec, vec, row, vec, vec, vec, row, vec, row, vec,
        ),
        out_specs=(
            row, row, vec, vec, row, vec, vec, row, vec, vec, vec, row, vec, row, vec,
        ),
        check_vma=False,
    )
```

```python
import functools
import math

import jax
import jax.numpy as jnp
from jax import lax
from jax.experimental import pallas as pl
from jax.experimental.pallas import tpu as pltpu
from jax.sharding import PartitionSpec as P

HDIM = 64
IMG = 577
RIM = IMG - 1
WIN = 592
QB = 128
EPS = 1e-06
NEG = -1e30
AXIS = "fsdp"
BF = jnp.bfloat16
F32 = jnp.float32
NT = (((1,), (1,)), ((), ()))
TN = (((0,), (0,)), ((), ()))
NN = (((1,), (0,)), ((), ()))


def dot(a, b, dims=NN):
    return lax.dot_general(a, b, dims, preferred_element_type=F32)


def stacked(block):
    lane = lax.broadcasted_iota(jnp.int32, block.shape, 1)
    zero = jnp.zeros_like(block)
    return jnp.concatenate(
        [jnp.where(lane < HDIM, block, zero), jnp.where(lane >= HDIM, block, zero)], axis=0
    )


def unstacked(wide):
    return jnp.concatenate([wide[:HDIM, :QB], wide[HDIM:, QB:]], axis=0).T


def key_mask(low, high):
    row = lax.broadcasted_iota(jnp.int32, (WIN, 2 * QB), 0)
    return (row >= low) & (row < high)


def mesh_copy(src, dst, send_sem, recv_sem, to):
    return pltpu.make_async_remote_copy(
        src_ref=src,
        dst_ref=dst,
        send_sem=send_sem,
        recv_sem=recv_sem,
        device_id=(to,),
        device_id_type=pl.DeviceIdType.MESH,
    )


class Place:
    def __init__(self):
        me = lax.axis_index(AXIS)
        self.c, self.x, self.y, self.z = me % 2, me // 2 % 2, me // 4 % 2, me // 8
        self.sib = self.at(self.z, self.y, self.x, 1 - self.c)
        self.xp = self.at(self.z, self.y, 1 - self.x, self.c)
        self.yp = self.at(self.z, 1 - self.y, self.x, self.c)
        self.zp = [self.at((self.z + k) % 4, self.y, self.x, self.c) for k in (1, 2, 3)]
        self.partners = [self.sib, self.xp, self.yp, *self.zp]

    @staticmethod
    def at(z, y, x, c):
        return ((z * 2 + y) * 2 + x) * 2 + c


def greet(partners, before=None, after=None):
    barrier = pltpu.get_barrier_semaphore()

    def hello(to):
        pl.semaphore_signal(
            barrier, inc=1, device_id=(to,), device_id_type=pl.DeviceIdType.MESH
        )

    for to in partners:
        hello(to)
    if before is None:
        pl.semaphore_wait(barrier, len(partners))
        return
    me = lax.axis_index(AXIS)
    pl.when(before)(lambda: hello(me - 1))
    pl.when(after)(lambda: hello(me + 1))
    pl.semaphore_wait(
        barrier, len(partners) + before.astype(jnp.int32) + after.astype(jnp.int32)
    )


class Gather:
    def __init__(self, place, shard, full, cols, send, recv, own):
        self.shard, self.own = shard.at[:, cols], own
        p, rows = place, shard.shape[0]
        half = rows // 2

        def block(y, x, part=slice(None)):
            return full.at[:, y, x, p.c, part, cols]

        mine = full.at[p.z, p.y, p.x, p.c, :, cols]
        self.local = lambda: pltpu.make_async_copy(self.shard, mine, own)

        def copy(i, src, dst, to):
            return lambda: mesh_copy(src, dst, send.at[i], recv.at[i], to)

        same = lambda i, ref, to: copy(i, ref, ref, to)
        first, second = pl.ds(0, half), pl.ds(half, half)
        self.z = [copy(i, self.shard, mine, to) for i, to in enumerate(p.zp)]
        self.xy = [same(3, block(p.y, p.x), p.xp), same(4, block(p.y, p.x), p.yp)]
        self.far = [
            same(5, block(p.y, 1 - p.x, first), p.yp),
            same(6, block(1 - p.y, p.x, second), p.xp),
        ]
        self.pair = [
            same(7, block(p.y, p.x), p.sib),
            same(8, block(p.y, 1 - p.x), p.sib),
            same(9, block(1 - p.y, p.x), p.sib),
            same(10, block(1 - p.y, 1 - p.x), p.sib),
        ]

    def stage(self, number):
        if number == 0:
            self.local().start()
            for c in self.z:
                c().start()
        elif number == 1:
            self.local().wait()
            for c in self.z:
                c().wait()
            for c in (*self.xy, self.pair[0]):
                c().start()
        elif number == 2:
            for c in self.xy:
                c().wait()
            for c in (*self.far, self.pair[1], self.pair[2]):
                c().start()
        elif number == 3:
            for c in self.far:
                c().wait()
            self.pair[3]().start()
        else:
            for c in self.pair:
                c().wait()


GATHER_SEMS = 11


def run_stages(pieces, step, steps):
    for at in sorted(set(steps)):
        todo = [
            (q, piece)
            for tick, when in enumerate(steps)
            if when == at
            for k, piece in enumerate(pieces)
            for q in (4, 3, 2, 1, 0)
            if k + q == tick
        ]

        @pl.when(step == at)
        def _():
            for q, piece in todo:
                piece.stage(q)


class Scatter:
    def __init__(self, place, grad, held, from_pair, far, side, line, out, sems):
        self.p, self.out = place, out
        self.held, self.from_pair, self.far, self.side, self.line = held, from_pair, far, side, line
        p, rows = place, held.shape[3]
        self.half = rows // 2
        own, send, recv = sems
        first, second = pl.ds(0, self.half), pl.ds(self.half, self.half)

        def copy(i, src, dst, to):
            return lambda: mesh_copy(src, dst, send.at[i], recv.at[i], to)

        self.load = lambda: pltpu.make_async_copy(grad.at[:, :, :, p.c], held, own)
        self.to_pair = copy(0, grad.at[:, :, :, 1 - p.c], from_pair, p.sib)
        self.to_far = [
            copy(1, held.at[:, 1 - p.y, 1 - p.x, first], far.at[0], p.xp),
            copy(2, held.at[:, 1 - p.y, 1 - p.x, second], far.at[1], p.yp),
        ]
        self.to_side = [
            copy(3, held.at[:, p.y, 1 - p.x], side.at[0], p.xp),
            copy(4, held.at[:, 1 - p.y, p.x], side.at[1], p.yp),
        ]
        self.to_line = [
            copy(5 + k, held.at[(p.z + k + 1) % 4, p.y, p.x], line.at[k], to)
            for k, to in enumerate(p.zp)
        ]

    def stage(self, number):
        p, half = self.p, self.half
        held, far, side, line = self.held, self.far, self.side, self.line
        if number == 0:
            self.load().start()
            self.to_pair().start()
        elif number == 1:
            self.load().wait()
            self.to_pair().wait()

            @pl.loop(0, 4)
            def _(z):
                for y in range(2):
                    for x in range(2):
                        held[z, y, x] = (
                            held[z, y, x].astype(F32) + self.from_pair[z, y, x].astype(F32)
                        ).astype(held.dtype)

            for c in self.to_far:
                c().start()
        elif number == 2:
            for c in self.to_far:
                c().wait()

            @pl.loop(0, 4)
            def _(z):
                held[z, 1 - p.y, p.x, :half] = (
                    held[z, 1 - p.y, p.x, :half].astype(F32) + far[0, z].astype(F32)
                ).astype(held.dtype)
                held[z, p.y, 1 - p.x, half:] = (
                    held[z, p.y, 1 - p.x, half:].astype(F32) + far[1, z].astype(F32)
                ).astype(held.dtype)

            for c in self.to_side:
                c().start()
        elif number == 3:
            for c in self.to_side:
                c().wait()

            @pl.loop(0, 4)
            def _(z):
                held[z, p.y, p.x] = (
                    held[z, p.y, p.x].astype(F32)
                    + side[0, z].astype(F32)
                    + side[1, z].astype(F32)
                ).astype(held.dtype)

            for c in self.to_line:
                c().start()
        else:
            for c in self.to_line:
                c().wait()
            self.out[...] = (
                held[p.z, p.y, p.x].astype(F32)
                + line[0].astype(F32)
                + line[1].astype(F32)
                + line[2].astype(F32)
            )


SCATTER_SEMS = 8
UNIT = 1024


def scatter_scratch(rows, cols, dtype=BF):
    return [
        pltpu.VMEM((4, 2, 2, rows, cols), dtype),
        pltpu.VMEM((4, 2, 2, rows, cols), dtype),
        pltpu.VMEM((2, 4, rows // 2, cols), dtype),
        pltpu.VMEM((2, 4, rows, cols), dtype),
        pltpu.VMEM((3, rows, cols), dtype),
        pltpu.SemaphoreType.DMA,
        pltpu.SemaphoreType.DMA((SCATTER_SEMS,)),
        pltpu.SemaphoreType.DMA((SCATTER_SEMS,)),
    ]


def blocks(value):
    return value.reshape(4, 2, 2, 2, value.shape[0] // 32, value.shape[1])


def gather_kernel(wide, vec, wide_out, vec_out, send, recv, own):
    place = Place()
    greet(place.partners)
    pieces = [Gather(place, vec, vec_out, pl.ds(0, vec.shape[1]), send.at[0], recv.at[0], own.at[0])]
    for k in range(wide.shape[1] // UNIT):
        pieces.append(
            Gather(
                place, wide, wide_out, pl.ds(k * UNIT, UNIT), send.at[k + 1], recv.at[k + 1],
                own.at[k + 1],
            )
        )
    for at in range(len(pieces) + 4):
        for s in (4, 3, 2, 1, 0):
            if 0 <= at - s < len(pieces):
                pieces[at - s].stage(s)


def gather_blocks(wide, vec):
    count = wide.shape[1] // UNIT + 1
    out = [
        jax.ShapeDtypeStruct((4, 2, 2, 2, *v.shape), v.dtype) for v in (wide, vec)
    ]
    hbm = pl.BlockSpec(memory_space=pl.ANY)
    full, small = pl.pallas_call(
        gather_kernel,
        out_shape=out,
        in_specs=[hbm, hbm],
        out_specs=[hbm, hbm],
        scratch_shapes=[
            pltpu.SemaphoreType.DMA((count, GATHER_SEMS)),
            pltpu.SemaphoreType.DMA((count, GATHER_SEMS)),
            pltpu.SemaphoreType.DMA((count,)),
        ],
        compiler_params=pltpu.CompilerParams(collective_id=0, has_side_effects=True),
        name="gather_qkv",
    )(wide, vec)
    return full.reshape(-1, wide.shape[1]), small.reshape(32, -1)


def scatter_kernel(g_q, g_k, g_v, small, out, small_out, *scratch):
    place = Place()
    greet(place.partners)
    size = 8
    pieces = []
    for k, grad in enumerate((g_q, g_k, g_v, small)):
        bufs = scratch[k * size : (k + 1) * size]
        to = small_out if k == 3 else out.at[:, pl.ds(k * UNIT, UNIT)]
        pieces.append(Scatter(place, grad, *bufs[:5], to, bufs[5:]))
    for at in range(len(pieces) + 4):
        for s in (4, 3, 2, 1, 0):
            if 0 <= at - s < len(pieces):
                pieces[at - s].stage(s)


def scatter_blocks(grads, small):
    hbm = pl.BlockSpec(memory_space=pl.ANY)
    vmem = pl.BlockSpec(memory_space=pltpu.VMEM)
    rows = grads[0].shape[0] // 32
    small = blocks(small)
    return pl.pallas_call(
        scatter_kernel,
        out_shape=[
            jax.ShapeDtypeStruct((rows, 3 * UNIT), F32),
            jax.ShapeDtypeStruct(small.shape[4:], F32),
        ],
        in_specs=[hbm] * 4,
        out_specs=[vmem] * 2,
        scratch_shapes=scatter_scratch(rows, UNIT) * 3
        + scatter_scratch(*small.shape[4:], F32),
        compiler_params=pltpu.CompilerParams(
            collective_id=3, has_side_effects=True, vmem_limit_bytes=40 * 2**20
        ),
        name="scatter_qkv",
    )(*map(blocks, grads), small)


ITEMS = 10


class Images:
    def __init__(self, n0, rows, ext):
        self.n0, self.n1, self.rows, self.ext = n0, n0 + IMG, rows, ext
        me, peers = lax.axis_index(AXIS), lax.axis_size(AXIS)
        limit = jnp.where(me == peers - 1, RIM + rows, 2 * RIM + rows)
        start0 = jnp.where(me == 0, RIM, n0 - 1)
        start1 = RIM + n0
        start2 = start1 + IMG
        self.spans = (
            (start0, start1),
            (start1, jnp.minimum(start1 + IMG, limit)),
            (start2, jnp.minimum(start2 + IMG, limit)),
        )
        one = lambda flag: jnp.where(flag, 1, 0)
        self.b0, self.b1 = lax.div(n0, QB), lax.div(self.n1, QB)
        self.d0 = one(self.b0 * QB != n0)
        self.d1 = one((self.n1 < rows) & (self.b1 * QB != self.n1))
        self.third = self.n1 < rows
        self.end0 = lax.div(n0 - 1, QB)
        self.end1 = lax.div(self.n1 - 1, QB) + self.d0
        self.one = one

    def base(self, start):
        return jnp.minimum(lax.div(start, 16), (self.ext - WIN) // 16)

    def segment(self, item):
        return self.one(item > self.end0) + self.one(item > self.end1)

    def item(self, item):
        blk = (
            item
            - self.d0 * self.one(item > self.b0)
            - self.d1 * self.one(item > self.b1 + self.d0)
        )
        used = blk < self.rows // QB
        blk = jnp.minimum(blk, self.rows // QB - 1)
        seg = self.segment(item)
        choose = lambda i: jnp.where(
            seg == 0, self.spans[0][i], jnp.where(seg == 1, self.spans[1][i], self.spans[2][i])
        )
        start, stop = choose(0), choose(1)
        base = self.base(start) * 16
        row0 = blk * QB
        low = jnp.maximum(start - RIM - row0, 0)
        high = jnp.where(used, jnp.minimum(stop - RIM - row0, QB), 0)
        return blk, row0, base, start - base, stop - base, low, high

    def of_block(self, blk):
        at0 = self.d0 * self.one(blk == self.b0)
        at1 = self.d1 * self.one(blk == self.b1)
        first = blk + self.d0 * self.one(blk > self.b0) + self.d1 * self.one(blk > self.b1)
        split = jnp.where(at0 == 1, self.n0, jnp.where(at1 == 1, self.n1, self.rows)) - blk * QB
        return first, first + at0 + at1, split


def attend_body(n0_ref, q_ref, k_ref, v_ref, out_ref, lse_ref, parts, parts_lse):
    rows = q_ref.shape[0]
    images = Images(n0_ref[0], rows, k_ref.shape[0])

    @pl.loop(0, ITEMS)
    def _(item):
        _, row0, base, low, high, _, _ = images.item(item)
        queries = stacked(q_ref[pl.ds(row0, QB), :]) * jnp.asarray(0.125, BF)
        keys = k_ref[pl.ds(base, WIN), :]
        values = v_ref[pl.ds(base, WIN), :]
        scores = jnp.where(key_mask(low, high), dot(keys, queries, NT), NEG)
        top = jnp.max(scores, axis=0, keepdims=True)
        terms = jnp.exp(scores - top)
        total = jnp.sum(terms, axis=0, keepdims=True)
        mixed = dot(values, terms.astype(BF), TN) / total
        parts[item] = unstacked(mixed)
        parts_lse[item] = jnp.broadcast_to(top + jnp.log(total), parts_lse.shape[1:])

    for blk in range(rows // QB):
        first, last, split = images.of_block(blk)
        row = lax.broadcasted_iota(jnp.int32, (QB, 2 * HDIM), 0)
        out_ref[pl.ds(blk * QB, QB), :] = jnp.where(
            row < split, parts[first], parts[last]
        ).astype(BF)
        lane = lax.broadcasted_iota(jnp.int32, parts_lse.shape[1:], 1) % QB
        lse_ref[0, pl.ds(blk, 1), :] = jnp.where(
            lane < split, parts_lse[first], parts_lse[last]
        )[:1]


def attend_kernel(n0_ref, q_ref, k_ref, v_ref, out_ref, lse_ref, parts, parts_lse):
    attend_body(n0_ref, q_ref, k_ref, v_ref, out_ref, lse_ref, parts, parts_lse)


def attend_gather_kernel(
    n0_ref, q_ref, k_ref, v_ref, w_out, w_up, out_ref, lse_ref, full_out, full_up,
    parts, parts_lse, send, recv, own,
):
    tick = pl.program_id(0)
    place = Place()
    pl.when(tick == 0)(lambda: greet(place.partners))
    pieces = []
    for shard, full in ((w_out, full_out), (w_up, full_up)):
        for k in range(shard.shape[1] // UNIT):
            i = len(pieces)
            pieces.append(
                Gather(
                    place, shard, full, pl.ds(k * UNIT, UNIT), send.at[i], recv.at[i], own.at[i]
                )
            )
    run_stages(pieces, tick, range(8))
    attend_body(n0_ref, q_ref, k_ref, v_ref, out_ref, lse_ref, parts, parts_lse)

    @pl.when(tick == 7)
    def _():
        pieces[-1].stage(4)


def attend(n0, queries, key_value, shards=None):
    rows, width = queries.shape
    pairs = width // (2 * HDIM)
    ext = key_value.shape[0]
    hbm = pl.BlockSpec(memory_space=pl.ANY)
    in_specs = [
        pl.BlockSpec(memory_space=pltpu.SMEM),
        pl.BlockSpec((rows, 2 * HDIM), lambda p: (0, p)),
        pl.BlockSpec((ext, 2 * HDIM), lambda p: (0, p)),
        pl.BlockSpec((ext, 2 * HDIM), lambda p: (0, pairs + p)),
    ]
    out_specs = [
        pl.BlockSpec((rows, 2 * HDIM), lambda p: (0, p)),
        pl.BlockSpec((1, rows // QB, 2 * QB), lambda p: (p, 0, 0)),
    ]
    out_shape = [
        jax.ShapeDtypeStruct((rows, width), BF),
        jax.ShapeDtypeStruct((pairs, rows // QB, 2 * QB), F32),
    ]
    scratch = [
        pltpu.VMEM((ITEMS, QB, 2 * HDIM), F32),
        pltpu.VMEM((ITEMS, 8, 2 * QB), F32),
    ]
    params = dict(vmem_limit_bytes=48 * 2**20)
    args = [n0, queries, key_value, key_value]
    kernel = attend_kernel
    if shards is not None:
        kernel = attend_gather_kernel
        in_specs += [hbm] * 2
        out_specs += [hbm] * 2
        out_shape += [jax.ShapeDtypeStruct((4, 2, 2, 2, *v.shape), BF) for v in shards]
        count = sum(v.shape[1] // UNIT for v in shards)
        scratch += [
            pltpu.SemaphoreType.DMA((count, GATHER_SEMS)),
            pltpu.SemaphoreType.DMA((count, GATHER_SEMS)),
            pltpu.SemaphoreType.DMA((count,)),
        ]
        params |= dict(collective_id=1, has_side_effects=True)
        args += shards
    return pl.pallas_call(
        kernel,
        grid=(pairs,),
        in_specs=in_specs,
        out_specs=out_specs,
        out_shape=out_shape,
        scratch_shapes=scratch,
        compiler_params=pltpu.CompilerParams(**params),
        name="attend",
    )(*args)


TILE = 64


def attend_back_body(
    pair, pairs, n0_ref, q_ref, k_ref, v_ref, up_ref, lse_ref, dq_ref, dk_ref, dv_ref,
    slots, parts, padded, outgoing, incoming, send, recv,
):
    rows = q_ref.shape[0]
    images = Images(n0_ref[0], rows, k_ref.shape[0])
    me, peers = lax.axis_index(AXIS), lax.axis_size(AXIS)
    wide = slice(TILE, TILE + WIN)

    def halo(p, way):
        return mesh_copy(
            outgoing.at[p, way], incoming.at[p, way], send.at[p, way], recv.at[p, way],
            me - 1 if way == 0 else me + 1,
        )

    @pl.when(pair == 0)
    def _():
        slots[0] = jnp.zeros(slots.shape[1:], F32)
        padded[...] = jnp.zeros(padded.shape, F32)

        @pl.when(me == 0)
        def _():
            incoming[:, 1] = jnp.zeros((pairs, WIN, 4 * HDIM), BF)

        @pl.when(me == peers - 1)
        def _():
            incoming[:, 0] = jnp.zeros((pairs, WIN, 4 * HDIM), BF)

    @pl.when(pair < pairs)
    def _():
        @pl.loop(0, ITEMS)
        def _(item):
            blk, row0, base, low, high, first, stop = images.item(item)
            queries = stacked(q_ref[pl.ds(row0, QB), :]) * jnp.asarray(0.125, BF)
            upstream = stacked(up_ref[pl.ds(row0, QB), :])
            lane = lax.broadcasted_iota(jnp.int32, (1, 2 * QB), 1) % QB
            here = (lane >= first) & (lane < stop)
            lse = jnp.where(here, lse_ref[0, pl.ds(blk, 1), :], -NEG)
            keys = k_ref[pl.ds(base, WIN), :]
            values = v_ref[pl.ds(base, WIN), :]
            scores = jnp.where(key_mask(low, high), dot(keys, queries, NT), NEG)
            probs = jnp.exp(scores - lse)
            dprobs = dot(values, upstream, NT)
            row_dot = jnp.sum(probs * dprobs, axis=0, keepdims=True)
            dscores = (probs * (dprobs - row_dot)).astype(BF)
            same = images.segment(item) == images.segment(item - 1)
            keep = (item > 0) & same
            old = jnp.where(keep, slots[item], jnp.zeros(slots.shape[1:], F32))
            slots[item + 1, :, : 2 * HDIM] = old[:, : 2 * HDIM] + dot(dscores, queries)
            slots[item + 1, :, 2 * HDIM :] = old[:, 2 * HDIM :] + dot(probs.astype(BF), upstream)
            parts[item] = unstacked(dot(keys, dscores, TN)) * 0.125

        for blk in range(rows // QB):
            first, last, split = images.of_block(blk)
            row = lax.broadcasted_iota(jnp.int32, (QB, 2 * HDIM), 0)
            dq_ref[pl.ds(blk * QB, QB), :] = jnp.where(
                row < split, parts[first], parts[last]
            ).astype(BF)

    @pl.when(pair > 0)
    def _():
        done = pair - 1

        @pl.when(me > 0)
        def _():
            halo(done, 0).wait_send()

        @pl.when(me < peers - 1)
        def _():
            halo(done, 0).wait_recv()
            halo(done, 1).wait_send()

        @pl.when(me > 0)
        def _():
            halo(done, 1).wait_recv()

        none = jnp.zeros((WIN, 4 * HDIM), F32)
        last = jnp.where(images.third, 2, 1)
        stop = jnp.where(images.third, images.spans[2][1], images.spans[1][1])
        cut = (stop > RIM + rows) & (me < peers - 1)
        after = jnp.where(cut, incoming[done, 0].astype(F32), none)
        before = jnp.where(images.spans[0][0] < RIM, incoming[done, 1].astype(F32), none)
        padded[0, wide] = padded[0, wide] + before
        padded[1, wide] = padded[1, wide] + jnp.where(last == 1, after, none)
        padded[2, wide] = padded[2, wide] + jnp.where(last == 2, after, none)
        bases = [images.base(span[0]) for span in images.spans]

        @pl.loop(0, rows // TILE)
        def _(tile):
            row = pl.multiple_of(tile * TILE, TILE)
            total = None
            for seg, base in enumerate(bases):
                off = jnp.maximum((RIM + TILE) // 16 + tile * (TILE // 16) - base, 0)
                off = jnp.minimum(off, (WIN + TILE) // 16) * 16
                term = padded[seg, pl.ds(off, TILE), :]
                total = term if total is None else total + term
            dk_ref[pl.ds(row, TILE), :] = total[:, : 2 * HDIM].astype(BF)
            dv_ref[pl.ds(row, TILE), :] = total[:, 2 * HDIM :].astype(BF)

    @pl.when(pair < pairs)
    def _():
        ends = (
            images.end0 + 1,
            jnp.minimum(images.end1, (rows - 1) // QB + images.d0) + 1,
            jnp.where(images.third, ITEMS, 0),
        )
        for seg, end in enumerate(ends):
            padded[seg, wide] = slots[end]
        outgoing[pair, 0] = padded[0, wide].astype(BF)
        outgoing[pair, 1] = jnp.where(images.third, padded[2, wide], padded[1, wide]).astype(BF)

        @pl.when(me > 0)
        def _():
            halo(pair, 0).start()

        @pl.when(me < peers - 1)
        def _():
            halo(pair, 1).start()


def attend_back_kernel(pairs, *refs):
    me, peers = lax.axis_index(AXIS), lax.axis_size(AXIS)
    pair = pl.program_id(0)
    pl.when(pair == 0)(lambda: greet([], me > 0, me < peers - 1))
    attend_back_body(pair, pairs, *refs)


def attend_back_scatter_kernel(pairs, *refs):
    base, (g_out, g_up), rest = refs[:6], refs[6:8], refs[8:]
    outs, (r_out, r_up), scratch = rest[:3], rest[3:5], rest[5:]
    mine, comm = scratch[:7], scratch[7:]
    me, peers = lax.axis_index(AXIS), lax.axis_size(AXIS)
    pair = pl.program_id(0)
    place = Place()
    pl.when(pair == 0)(lambda: greet(place.partners, me > 0, me < peers - 1))
    pieces = []
    for grad, out in ((g_out, r_out), (g_up, r_up)):
        for k in range(grad.shape[5] // UNIT):
            cols = pl.ds(k * UNIT, UNIT)
            bufs = comm[len(pieces) * 8 : len(pieces) * 8 + 8]
            pieces.append(
                Scatter(
                    place, grad.at[:, :, :, :, :, cols], *bufs[:5], out.at[:, cols], bufs[5:]
                )
            )
    run_stages(pieces, pair, range(9))
    attend_back_body(pair, pairs, *base, *outs, *mine)


def attend_back(n0, queries, key_value, upstream, lse, grads=None):
    rows, width = queries.shape
    pairs = width // (2 * HDIM)
    ext = key_value.shape[0]
    hbm, vmem = pl.BlockSpec(memory_space=pl.ANY), pl.BlockSpec(memory_space=pltpu.VMEM)
    here = lambda p: jnp.minimum(p, pairs - 1)
    own = pl.BlockSpec((rows, 2 * HDIM), lambda p: (0, here(p)))
    late = pl.BlockSpec((rows, 2 * HDIM), lambda p: (0, jnp.maximum(p - 1, 0)))
    in_specs = [
        pl.BlockSpec(memory_space=pltpu.SMEM),
        own,
        pl.BlockSpec((ext, 2 * HDIM), lambda p: (0, here(p))),
        pl.BlockSpec((ext, 2 * HDIM), lambda p: (0, pairs + here(p))),
        own,
        pl.BlockSpec((1, rows // QB, 2 * QB), lambda p: (here(p), 0, 0)),
    ]
    out_specs = [own, late, late]
    out_shape = [jax.ShapeDtypeStruct((rows, width), BF)] * 3
    scratch = [
        pltpu.VMEM((ITEMS + 1, WIN, 4 * HDIM), F32),
        pltpu.VMEM((ITEMS, QB, 2 * HDIM), F32),
        pltpu.VMEM((3, WIN + 2 * TILE, 4 * HDIM), F32),
        pltpu.VMEM((pairs, 2, WIN, 4 * HDIM), BF),
        pltpu.VMEM((pairs, 2, WIN, 4 * HDIM), BF),
        pltpu.SemaphoreType.DMA((pairs, 2)),
        pltpu.SemaphoreType.DMA((pairs, 2)),
    ]
    args = [n0, queries, key_value, key_value, upstream, lse]
    kernel, collective = attend_back_kernel, 4
    if grads is not None:
        kernel, collective = attend_back_scatter_kernel, 2
        args += map(blocks, grads)
        in_specs += [hbm] * 2
        out_specs += [vmem] * 2
        out_shape += [jax.ShapeDtypeStruct((v.shape[0] // 32, v.shape[1]), F32) for v in grads]
        for v in grads:
            scratch += scatter_scratch(v.shape[0] // 32, UNIT) * (v.shape[1] // UNIT)
    return pl.pallas_call(
        functools.partial(kernel, pairs),
        grid=(pairs + 1,),
        in_specs=in_specs,
        out_specs=out_specs,
        out_shape=out_shape,
        scratch_shapes=scratch,
        compiler_params=pltpu.CompilerParams(
            vmem_limit_bytes=58 * 2**20, collective_id=collective, has_side_effects=True
        ),
        name="attend_back",
    )(*args)


ROW_TILE = 256
FF_TILE = 512
ROOT_HALF = 1.0 / math.sqrt(2.0)
PDF_SCALE = 1.0 / math.sqrt(2.0 * math.pi)


def row_stats(value):
    mean = jnp.mean(value, axis=1, keepdims=True)
    center = value - mean
    inv_std = lax.rsqrt(jnp.mean(center * center, axis=1, keepdims=True) + EPS)
    return center * inv_std, inv_std


def mlp_up_body(
    step, row_steps, mixed, tokens, w_out, vecs, w_up, up_bias, cot, resid, normed, act, slope,
    g_down, held,
):
    @pl.when(step < row_steps)
    def _():
        value = tokens[...].astype(F32) + dot(mixed[...], w_out[...]) + vecs[0:1]
        resid[...] = value
        low = (row_stats(value)[0] * vecs[1:2] + vecs[2:3]).astype(BF)
        normed[...] = low
        held[pl.ds(step * ROW_TILE, ROW_TILE), :] = low

    @pl.when(step >= row_steps)
    def _():
        rows = held.shape[0]

        for row in range(0, rows, ROW_TILE):
            part = pl.ds(row, ROW_TILE)
            upward = dot(held[part, :], w_up[...]) + up_bias[...]
            cdf = 0.5 * (1.0 + lax.erf(upward * ROOT_HALF))
            pdf = jnp.exp(-0.5 * upward * upward) * PDF_SCALE
            act[part, :] = (upward * cdf).astype(BF)
            slope[part, :] = (cdf + upward * pdf).astype(BF)
        g_down[...] = dot(act[...], cot[...], TN).astype(BF)


def mlp_up_kernel(row_steps, *refs):
    mlp_up_body(pl.program_id(0), row_steps, *refs)


def mlp_up_gather_kernel(row_steps, *refs):
    ins, shard, outs, full = refs[:7], refs[7], refs[8:13], refs[13]
    held, send, recv, own = refs[14:]
    step = pl.program_id(0)
    place = Place()
    pl.when(step == 0)(lambda: greet(place.partners))
    cols = shard.shape[1] // 4
    pieces = [
        Gather(place, shard, full, pl.ds(k * cols, cols), send.at[k], recv.at[k], own.at[k])
        for k in range(4)
    ]
    run_stages(pieces, step, (0, 2, 4, 5, 7, 9, 11))
    mlp_up_body(step, row_steps, *ins, *outs, held)

    @pl.when(step == pl.num_programs(0) - 1)
    def _():
        pieces[3].stage(4)


def mlp_up(mixed, tokens, w_out, vecs, w_up, up_bias, cot, shard=None):
    rows, width = tokens.shape
    hidden = w_up.shape[1]
    row_steps, ff_steps = rows // ROW_TILE, hidden // FF_TILE
    at_row = lambda s: (jnp.minimum(s, row_steps - 1), 0)
    at_col = lambda s: (0, jnp.maximum(s - row_steps, 0))
    at_ff = lambda s: (jnp.maximum(s - row_steps, 0), 0)
    const = lambda s: (0, 0)
    hbm = pl.BlockSpec(memory_space=pl.ANY)
    tall = pl.BlockSpec((rows, FF_TILE), at_col)
    in_specs = [
        pl.BlockSpec((ROW_TILE, width), at_row),
        pl.BlockSpec((ROW_TILE, width), at_row),
        pl.BlockSpec((width, width), const),
        pl.BlockSpec((8, width), const),
        pl.BlockSpec((width, FF_TILE), at_col),
        pl.BlockSpec((1, FF_TILE), at_col),
        pl.BlockSpec((rows, width), const),
    ]
    out_specs = [
        pl.BlockSpec((ROW_TILE, width), at_row),
        pl.BlockSpec((ROW_TILE, width), at_row),
        tall,
        tall,
        pl.BlockSpec((FF_TILE, width), at_ff),
    ]
    out_shape = [
        jax.ShapeDtypeStruct((rows, width), F32),
        jax.ShapeDtypeStruct((rows, width), BF),
        jax.ShapeDtypeStruct((rows, hidden), BF),
        jax.ShapeDtypeStruct((rows, hidden), BF),
        jax.ShapeDtypeStruct((hidden, width), BF),
    ]
    scratch = [pltpu.VMEM((rows, width), BF)]
    params = dict(vmem_limit_bytes=58 * 2**20)
    args = [mixed, tokens, w_out, vecs, w_up, up_bias, cot]
    kernel = mlp_up_kernel
    if shard is not None:
        kernel = mlp_up_gather_kernel
        in_specs += [hbm]
        out_specs += [hbm]
        out_shape += [jax.ShapeDtypeStruct((4, 2, 2, 2, *shard.shape), BF)]
        scratch += [
            pltpu.SemaphoreType.DMA((4, GATHER_SEMS)),
            pltpu.SemaphoreType.DMA((4, GATHER_SEMS)),
            pltpu.SemaphoreType.DMA((4,)),
        ]
        params |= dict(collective_id=5, has_side_effects=True)
        args += [shard]
    return pl.pallas_call(
        functools.partial(kernel, row_steps),
        grid=(row_steps + ff_steps,),
        in_specs=in_specs,
        out_specs=out_specs,
        out_shape=out_shape,
        scratch_shapes=scratch,
        compiler_params=pltpu.CompilerParams(**params),
        name="mlp_up",
    )(*args)


def mlp_back_body(
    step, ff_steps, act, slope, w_up, w_down, cot, normed, resid, mixed, w_out, vecs,
    g_up, up_sums, layer_out, dresid, dmixed, g_out, sums, total, dnormed, branches, dup,
):
    rows, width = cot.shape

    @pl.when(step == 0)
    def _():
        total[...] = jnp.zeros(total.shape, F32)
        dnormed[...] = jnp.zeros(dnormed.shape, F32)
        sums[...] = jnp.zeros(sums.shape, F32)

    @pl.when(step < ff_steps)
    def _():
        count = jnp.zeros(up_sums.shape, F32)
        for row in range(0, rows, ROW_TILE):
            part = pl.ds(row, ROW_TILE)
            total[part, :] += dot(act[part, :], w_down[...])
            dact = dot(cot[part, :], w_down[...], NT)
            low = (dact * slope[part, :].astype(F32)).astype(BF)
            dup[part, :] = low
            count += jnp.sum(low.astype(F32), axis=0, keepdims=True)
            dnormed[part, :] += dot(low, w_up[...], NT)
        up_sums[...] = count
        g_up[...] = dot(normed[...], dup[...], TN).astype(BF)

    @pl.when(step >= ff_steps)
    def _():
        part = pl.ds((step - ff_steps) * ROW_TILE, ROW_TILE)
        value = resid[...]
        scaled, inv_std = row_stats(value)
        upstream = dnormed[part, :]
        above = cot[part, :].astype(F32)
        through = upstream * vecs[1:2]
        inner = (
            through
            - jnp.mean(through, axis=1, keepdims=True)
            - scaled * jnp.mean(through * scaled, axis=1, keepdims=True)
        )
        grad = above + inv_std * inner
        dresid[...] = grad
        low = grad.astype(BF)
        branches[part, :] = low
        dmixed[...] = dot(low, w_out[...], NT).astype(BF)
        layer_out[...] = (value + total[part, :] + vecs[3:4]).astype(BF)
        sums[0:1] += jnp.sum(low.astype(F32), axis=0, keepdims=True)
        sums[1:2] += jnp.sum(upstream * scaled, axis=0, keepdims=True)
        sums[2:3] += jnp.sum(upstream, axis=0, keepdims=True)
        sums[3:4] += jnp.sum(above, axis=0, keepdims=True)

    @pl.when(step == pl.num_programs(0) - 1)
    def _():
        g_out[...] = dot(mixed[...], branches[...], TN).astype(BF)


def mlp_back_kernel(ff_steps, *refs):
    mlp_back_body(pl.program_id(0), ff_steps, *refs)


def mlp_back_scatter_kernel(ff_steps, *refs):
    ins, grad, outs, reduced, scratch, comm = (
        refs[:10], refs[10], refs[11:18], refs[18], refs[19:23], refs[23:],
    )
    step = pl.program_id(0)
    place = Place()
    pl.when(step == 0)(lambda: greet(place.partners))
    cols = reduced.shape[1] // 4
    pieces = []
    for k in range(4):
        here = pl.ds(k * cols, cols)
        bufs = comm[k * 8 : k * 8 + 8]
        pieces.append(
            Scatter(
                place, grad.at[:, :, :, :, :, here], *bufs[:5], reduced.at[:, here], bufs[5:]
            )
        )
    run_stages(pieces, step, (0, 1, 2, 4, 5, 7, 9))
    mlp_back_body(step, ff_steps, *ins, *outs, *scratch)

    @pl.when(step == pl.num_programs(0) - 1)
    def _():
        pieces[3].stage(4)


def mlp_back(act, slope, w_up, w_down, cot, normed, resid, mixed, w_out, vecs, grad=None):
    rows, width = cot.shape
    hidden = w_up.shape[1]
    row_steps, ff_steps = rows // ROW_TILE, hidden // FF_TILE
    at_row = lambda s: (jnp.maximum(s - ff_steps, 0), 0)
    at_col = lambda s: (0, jnp.minimum(s, ff_steps - 1))
    at_ff = lambda s: (jnp.minimum(s, ff_steps - 1), 0)
    const = lambda s: (0, 0)
    hbm, vmem = pl.BlockSpec(memory_space=pl.ANY), pl.BlockSpec(memory_space=pltpu.VMEM)
    once = lambda *shape: pl.BlockSpec(shape, const, pipeline_mode=pl.Buffered(1))
    tall = pl.BlockSpec((rows, FF_TILE), at_col)
    tile = pl.BlockSpec((ROW_TILE, width), at_row)
    in_specs = [
        tall, tall, pl.BlockSpec((width, FF_TILE), at_col), pl.BlockSpec((FF_TILE, width), at_ff),
        once(rows, width), once(rows, width), tile, once(rows, width), once(width, width),
        once(8, width),
    ]
    out_specs = [
        pl.BlockSpec((width, FF_TILE), at_col), pl.BlockSpec((1, FF_TILE), at_col), tile, tile,
        tile, once(width, width), once(8, width),
    ]
    out_shape = [
        jax.ShapeDtypeStruct((width, hidden), BF),
        jax.ShapeDtypeStruct((1, hidden), F32),
        jax.ShapeDtypeStruct((rows, width), BF),
        jax.ShapeDtypeStruct((rows, width), F32),
        jax.ShapeDtypeStruct((rows, width), BF),
        jax.ShapeDtypeStruct((width, width), BF),
        jax.ShapeDtypeStruct((8, width), F32),
    ]
    scratch = [
        pltpu.VMEM((rows, width), F32),
        pltpu.VMEM((rows, width), F32),
        pltpu.VMEM((rows, width), BF),
        pltpu.VMEM((rows, FF_TILE), BF),
    ]
    params = dict(vmem_limit_bytes=60 * 2**20)
    args = [act, slope, w_up, w_down, cot, normed, resid, mixed, w_out, vecs]
    kernel = mlp_back_kernel
    if grad is not None:
        kernel = mlp_back_scatter_kernel
        part = grad.shape[0] // 32
        in_specs += [hbm]
        out_specs += [vmem]
        out_shape += [jax.ShapeDtypeStruct((part, width), F32)]
        scratch += scatter_scratch(part, width // 4) * 4
        params |= dict(collective_id=6, has_side_effects=True)
        args += [blocks(grad)]
    return pl.pallas_call(
        functools.partial(kernel, ff_steps),
        grid=(row_steps + ff_steps,),
        in_specs=in_specs,
        out_specs=out_specs,
        out_shape=out_shape,
        scratch_shapes=scratch,
        compiler_params=pltpu.CompilerParams(**params),
        name="mlp_back",
    )(*args)


def shifted(value, by):
    peers = lax.axis_size(AXIS)
    pairs = [(i, i + by) for i in range(peers) if 0 <= i + by < peers]
    return lax.ppermute(value, AXIS, pairs)


def gathered(value):
    return lax.all_gather(value, AXIS, axis=0, tiled=True)


def scattered(value):
    return lax.psum_scatter(value, AXIS, scatter_dimension=0, tiled=True)


def normalize(inputs, gain, shift):
    center = inputs - jnp.mean(inputs, axis=1, keepdims=True)
    inv_std = lax.rsqrt(jnp.mean(center * center, axis=1, keepdims=True) + EPS)
    scaled = center * inv_std
    return (scaled * gain + shift, scaled, inv_std)


def normalize_back(upstream, scaled, inv_std, gain):
    through = upstream * gain
    inner = (
        through
        - jnp.mean(through, axis=1, keepdims=True)
        - scaled * jnp.mean(through * scaled, axis=1, keepdims=True)
    )
    return (inv_std * inner, jnp.sum(upstream * scaled, axis=0), jnp.sum(upstream, axis=0))


def local(
    tokens,
    image_ids,
    cotangent,
    norm1_gain,
    norm1_shift,
    qkv_weight,
    query_bias,
    value_bias,
    out_weight,
    out_bias,
    norm2_gain,
    norm2_shift,
    up_weight,
    up_bias,
    down_weight,
    down_bias,
):
    rows, width = tokens.shape
    me = lax.axis_index(AXIS)
    peers = lax.axis_size(AXIS)
    n0 = jnp.sum((image_ids == image_ids[0]).astype(jnp.int32)).reshape(1)
    ext = -(-(rows + 2 * RIM + 64) // 128) * 128
    packed = jnp.concatenate(
        [norm1_gain, norm1_shift, query_bias, value_bias, out_bias, norm2_gain, norm2_shift,
         down_bias, up_bias]
    )
    block_plan = peers == 32
    if block_plan:
        count = packed.shape[0]
        packed = jnp.pad(packed, (0, 32 * 128 - count)).reshape(32, 128)
        w_qkv, vectors = gather_blocks(qkv_weight, packed)
        vectors = vectors[:, :count].astype(F32)
    else:
        w_qkv, vectors = gathered(qkv_weight), gathered(packed[None]).astype(F32)
        w_out, w_up, w_down = map(gathered, (out_weight, up_weight, down_weight))
    part = norm1_gain.shape[0]
    gain1, shift1, q_bias, v_bias, o_bias, gain2, shift2, d_bias = (
        vectors[:, i * part : (i + 1) * part].reshape(-1) for i in range(8)
    )
    u_bias = vectors[:, 8 * part :].reshape(-1)

    low_rim = shifted(tokens[rows - RIM :], 1)
    high_rim = shifted(tokens[:RIM], -1)
    pad = jnp.zeros((ext - rows - 2 * RIM, width), BF)
    tokens_ext = jnp.concatenate([low_rim, tokens, high_rim, pad], axis=0).astype(F32)
    inputs = tokens.astype(F32)
    normed_ext = normalize(tokens_ext, gain1, shift1)[0].astype(BF)
    normed, scaled_one, inv_one = normalize(inputs, gain1, shift1)
    normed_low = normed.astype(BF)
    queries = (dot(normed_low, w_qkv[:, :width]) + q_bias).astype(BF)
    key_value = (
        dot(normed_ext, w_qkv[:, width:]) + jnp.concatenate([jnp.zeros_like(v_bias), v_bias])
    ).astype(BF)
    if block_plan:
        mixed_low, lse, w_out, w_up = attend(
            n0, queries, key_value, (out_weight, up_weight)
        )
        w_out, w_up = w_out.reshape(width, -1), w_up.reshape(width, -1)
    else:
        mixed_low, lse = attend(n0, queries, key_value)

    vecs = jnp.stack([o_bias, gain2, shift2, d_bias] + [jnp.zeros_like(d_bias)] * 4)
    args = (mixed_low, tokens, w_out, vecs, w_up, u_bias[None], cotangent)
    if block_plan:
        resid, normed_two, act, slope, grad_down, w_down = mlp_up(*args, down_weight)
        w_down = w_down.reshape(-1, width)
    else:
        resid, normed_two, act, slope, grad_down = mlp_up(*args)
    args = (act, slope, w_up, w_down, cotangent, normed_two, resid, mixed_low, w_out, vecs)
    if block_plan:
        grad_up, up_sums, layer_out, dresid, dmixed_low, grad_out, sums, r_down = mlp_back(
            *args, grad_down
        )
    else:
        grad_up, up_sums, layer_out, dresid, dmixed_low, grad_out, sums = mlp_back(*args)
        r_down = scattered(grad_down).astype(F32)
    grad_out_b, grad_gain_two, grad_shift_two, grad_down_b = sums[:4]
    grad_up_b = up_sums[0]

    if block_plan:
        dquery, dkey, dvalue, r_out, r_up = attend_back(
            n0, queries, key_value, dmixed_low, lse, (grad_out, grad_up)
        )
    else:
        dquery, dkey, dvalue = attend_back(n0, queries, key_value, dmixed_low, lse)
        r_out, r_up = (scattered(v).astype(F32) for v in (grad_out, grad_up))
    dproj = (dquery, dkey, dvalue)
    grad_qkv = [dot(normed_low, v, TN).astype(BF) for v in dproj]
    grad_query_b = jnp.sum(dquery.astype(F32), axis=0)
    grad_value_b = jnp.sum(dvalue.astype(F32), axis=0)
    dnormed = sum(
        dot(v, w_qkv[:, i * width : (i + 1) * width], NT) for i, v in enumerate(dproj)
    )
    dinput_norm, grad_gain_one, grad_shift_one = normalize_back(
        dnormed, scaled_one, inv_one, gain1
    )
    grad_tokens = dresid + dinput_norm

    def small(value):
        return value.reshape(peers, -1)

    smalls = jnp.concatenate(
        [
            small(v)
            for v in (
                grad_gain_one, grad_shift_one, grad_query_b, grad_value_b, grad_out_b,
                grad_gain_two, grad_shift_two, grad_down_b, grad_up_b,
            )
        ],
        axis=1,
    )
    if block_plan:
        count = smalls.shape[1]
        smalls = jnp.pad(smalls, ((0, 0), (0, 16 * 128 - count))).reshape(peers * 16, 128)
        r_qkv, owned = scatter_blocks(grad_qkv, smalls)
        owned = owned.reshape(-1)[:count]
    else:
        owned = scattered(smalls)[0]
        r_qkv = jnp.concatenate([scattered(v) for v in grad_qkv], axis=1).astype(F32)
    g = [owned[i * part : (i + 1) * part] for i in range(8)] + [owned[8 * part :]]
    return (
        layer_out, grad_tokens, g[0], g[1], r_qkv, g[2], g[3], r_out, g[4], g[5], g[6], r_up,
        g[8], r_down, g[7],
    )


def solution(mesh):
    row, vec = P(AXIS, None), P(AXIS)
    return jax.shard_map(
        local,
        mesh=mesh,
        in_specs=(
            row, vec, row, vec, vec, row, vec, vec, row, vec, vec, vec, row, vec, row, vec,
        ),
        out_specs=(
            row, row, vec, vec, row, vec, vec, row, vec, vec, vec, row, vec, row, vec,
        ),
        check_vma=False,
    )
```

```python
import functools
import math

import jax
import jax.numpy as jnp
from jax import lax
from jax.experimental import pallas as pl
from jax.experimental.pallas import tpu as pltpu
from jax.sharding import PartitionSpec as P

HDIM = 64
IMG = 577
RIM = IMG - 1
WIN = 592
QB = 128
EPS = 1e-06
NEG = -1e30
AXIS = "fsdp"
BF = jnp.bfloat16
F32 = jnp.float32
NT = (((1,), (1,)), ((), ()))
TN = (((0,), (0,)), ((), ()))
NN = (((1,), (0,)), ((), ()))


def dot(a, b, dims=NN):
    return lax.dot_general(a, b, dims, preferred_element_type=F32)


def stacked(block):
    lane = lax.broadcasted_iota(jnp.int32, block.shape, 1)
    zero = jnp.zeros_like(block)
    return jnp.concatenate(
        [jnp.where(lane < HDIM, block, zero), jnp.where(lane >= HDIM, block, zero)], axis=0
    )


def unstacked(wide):
    return jnp.concatenate([wide[:HDIM, :QB], wide[HDIM:, QB:]], axis=0).T


def key_mask(low, high):
    row = lax.broadcasted_iota(jnp.int32, (WIN, QB), 0)
    bias = jnp.where((row >= low) & (row < high), 0.0, NEG)
    return jnp.concatenate([bias, bias], axis=1)


def mesh_copy(src, dst, send_sem, recv_sem, to):
    return pltpu.make_async_remote_copy(
        src_ref=src,
        dst_ref=dst,
        send_sem=send_sem,
        recv_sem=recv_sem,
        device_id=(to,),
        device_id_type=pl.DeviceIdType.MESH,
    )


class Place:
    def __init__(self):
        me = lax.axis_index(AXIS)
        self.c, self.x, self.y, self.z = me % 2, me // 2 % 2, me // 4 % 2, me // 8
        self.sib = self.at(self.z, self.y, self.x, 1 - self.c)
        self.xp = self.at(self.z, self.y, 1 - self.x, self.c)
        self.yp = self.at(self.z, 1 - self.y, self.x, self.c)
        self.zp = [self.at((self.z + k) % 4, self.y, self.x, self.c) for k in (1, 2, 3)]
        self.partners = [self.sib, self.xp, self.yp, *self.zp]

    @staticmethod
    def at(z, y, x, c):
        return ((z * 2 + y) * 2 + x) * 2 + c


def greet(partners, before=None, after=None):
    barrier = pltpu.get_barrier_semaphore()

    def hello(to):
        pl.semaphore_signal(
            barrier, inc=1, device_id=(to,), device_id_type=pl.DeviceIdType.MESH
        )

    for to in partners:
        hello(to)
    if before is None:
        pl.semaphore_wait(barrier, len(partners))
        return
    me = lax.axis_index(AXIS)
    pl.when(before)(lambda: hello(me - 1))
    pl.when(after)(lambda: hello(me + 1))
    pl.semaphore_wait(
        barrier, len(partners) + before.astype(jnp.int32) + after.astype(jnp.int32)
    )


class Gather:
    def __init__(self, place, shard, full, cols, send, recv, own):
        self.shard, self.own = shard.at[:, cols], own
        p, rows = place, shard.shape[0]
        half = rows // 2

        def block(y, x, part=slice(None)):
            return full.at[:, y, x, p.c, part, cols]

        mine = full.at[p.z, p.y, p.x, p.c, :, cols]
        self.local = lambda: pltpu.make_async_copy(self.shard, mine, own)

        def copy(i, src, dst, to):
            return lambda: mesh_copy(src, dst, send.at[i], recv.at[i], to)

        same = lambda i, ref, to: copy(i, ref, ref, to)
        first, second = pl.ds(0, half), pl.ds(half, half)
        self.z = [copy(i, self.shard, mine, to) for i, to in enumerate(p.zp)]
        self.xy = [same(3, block(p.y, p.x), p.xp), same(4, block(p.y, p.x), p.yp)]
        self.far = [
            same(5, block(p.y, 1 - p.x, first), p.yp),
            same(6, block(1 - p.y, p.x, second), p.xp),
        ]
        self.pair = [
            same(7, block(p.y, p.x), p.sib),
            same(8, block(p.y, 1 - p.x), p.sib),
            same(9, block(1 - p.y, p.x), p.sib),
            same(10, block(1 - p.y, 1 - p.x), p.sib),
        ]

    def stage(self, number):
        if number == 0:
            self.local().start()
            for c in self.z:
                c().start()
        elif number == 1:
            self.local().wait()
            for c in self.z:
                c().wait()
            for c in (*self.xy, self.pair[0]):
                c().start()
        elif number == 2:
            for c in self.xy:
                c().wait()
            for c in (*self.far, self.pair[1], self.pair[2]):
                c().start()
        elif number == 3:
            for c in self.far:
                c().wait()
            self.pair[3]().start()
        else:
            for c in self.pair:
                c().wait()


GATHER_SEMS = 11


def run_stages(pieces, step, steps):
    for at in sorted(set(steps)):
        todo = [
            (q, piece)
            for tick, when in enumerate(steps)
            if when == at
            for k, piece in enumerate(pieces)
            for q in (4, 3, 2, 1, 0)
            if k + q == tick
        ]

        @pl.when(step == at)
        def _():
            for q, piece in todo:
                piece.stage(q)


class Scatter:
    def __init__(self, place, grad, held, from_pair, far, side, line, out, sems):
        self.p, self.out = place, out
        self.held, self.from_pair, self.far, self.side, self.line = held, from_pair, far, side, line
        p, rows = place, held.shape[3]
        self.half = rows // 2
        own, send, recv = sems
        first, second = pl.ds(0, self.half), pl.ds(self.half, self.half)

        def copy(i, src, dst, to):
            return lambda: mesh_copy(src, dst, send.at[i], recv.at[i], to)

        self.load = lambda: pltpu.make_async_copy(grad.at[:, :, :, p.c], held, own)
        self.to_pair = copy(0, grad.at[:, :, :, 1 - p.c], from_pair, p.sib)
        self.to_far = [
            copy(1, held.at[:, 1 - p.y, 1 - p.x, first], far.at[0], p.xp),
            copy(2, held.at[:, 1 - p.y, 1 - p.x, second], far.at[1], p.yp),
        ]
        self.to_side = [
            copy(3, held.at[:, p.y, 1 - p.x], side.at[0], p.xp),
            copy(4, held.at[:, 1 - p.y, p.x], side.at[1], p.yp),
        ]
        self.to_line = [
            copy(5 + k, held.at[(p.z + k + 1) % 4, p.y, p.x], line.at[k], to)
            for k, to in enumerate(p.zp)
        ]

    def stage(self, number):
        p, half = self.p, self.half
        held, far, side, line = self.held, self.far, self.side, self.line
        if number == 0:
            self.load().start()
            self.to_pair().start()
        elif number == 1:
            self.load().wait()
            self.to_pair().wait()

            @pl.loop(0, 4)
            def _(z):
                for y in range(2):
                    for x in range(2):
                        held[z, y, x] = (
                            held[z, y, x].astype(F32) + self.from_pair[z, y, x].astype(F32)
                        ).astype(held.dtype)

            for c in self.to_far:
                c().start()
        elif number == 2:
            for c in self.to_far:
                c().wait()

            @pl.loop(0, 4)
            def _(z):
                held[z, 1 - p.y, p.x, :half] = (
                    held[z, 1 - p.y, p.x, :half].astype(F32) + far[0, z].astype(F32)
                ).astype(held.dtype)
                held[z, p.y, 1 - p.x, half:] = (
                    held[z, p.y, 1 - p.x, half:].astype(F32) + far[1, z].astype(F32)
                ).astype(held.dtype)

            for c in self.to_side:
                c().start()
        elif number == 3:
            for c in self.to_side:
                c().wait()

            @pl.loop(0, 4)
            def _(z):
                held[z, p.y, p.x] = (
                    held[z, p.y, p.x].astype(F32)
                    + side[0, z].astype(F32)
                    + side[1, z].astype(F32)
                ).astype(held.dtype)

            for c in self.to_line:
                c().start()
        else:
            for c in self.to_line:
                c().wait()
            self.out[...] = (
                held[p.z, p.y, p.x].astype(F32)
                + line[0].astype(F32)
                + line[1].astype(F32)
                + line[2].astype(F32)
            )


SCATTER_SEMS = 8
UNIT = 1024


def scatter_scratch(rows, cols, dtype=BF):
    return [
        pltpu.VMEM((4, 2, 2, rows, cols), dtype),
        pltpu.VMEM((4, 2, 2, rows, cols), dtype),
        pltpu.VMEM((2, 4, rows // 2, cols), dtype),
        pltpu.VMEM((2, 4, rows, cols), dtype),
        pltpu.VMEM((3, rows, cols), dtype),
        pltpu.SemaphoreType.DMA,
        pltpu.SemaphoreType.DMA((SCATTER_SEMS,)),
        pltpu.SemaphoreType.DMA((SCATTER_SEMS,)),
    ]


def blocks(value):
    return value.reshape(4, 2, 2, 2, value.shape[0] // 32, value.shape[1])


def gather_kernel(wide, vec, wide_out, vec_out, send, recv, own):
    place = Place()
    greet(place.partners)
    pieces = [Gather(place, vec, vec_out, pl.ds(0, vec.shape[1]), send.at[0], recv.at[0], own.at[0])]
    for k in range(wide.shape[1] // UNIT):
        pieces.append(
            Gather(
                place, wide, wide_out, pl.ds(k * UNIT, UNIT), send.at[k + 1], recv.at[k + 1],
                own.at[k + 1],
            )
        )
    for at in range(len(pieces) + 4):
        for s in (4, 3, 2, 1, 0):
            if 0 <= at - s < len(pieces):
                pieces[at - s].stage(s)


def gather_blocks(wide, vec):
    count = wide.shape[1] // UNIT + 1
    out = [
        jax.ShapeDtypeStruct((4, 2, 2, 2, *v.shape), v.dtype) for v in (wide, vec)
    ]
    hbm = pl.BlockSpec(memory_space=pl.ANY)
    full, small = pl.pallas_call(
        gather_kernel,
        out_shape=out,
        in_specs=[hbm, hbm],
        out_specs=[hbm, hbm],
        scratch_shapes=[
            pltpu.SemaphoreType.DMA((count, GATHER_SEMS)),
            pltpu.SemaphoreType.DMA((count, GATHER_SEMS)),
            pltpu.SemaphoreType.DMA((count,)),
        ],
        compiler_params=pltpu.CompilerParams(collective_id=0, has_side_effects=True),
        name="gather_qkv",
    )(wide, vec)
    return full.reshape(-1, wide.shape[1]), small.reshape(32, -1)


ITEMS = 10
BACK_GROUP = 2
GROUP = 5


class Images:
    def __init__(self, n0, rows, ext):
        self.n0, self.n1, self.rows, self.ext = n0, n0 + IMG, rows, ext
        me, peers = lax.axis_index(AXIS), lax.axis_size(AXIS)
        limit = jnp.where(me == peers - 1, RIM + rows, 2 * RIM + rows)
        start0 = jnp.where(me == 0, RIM, n0 - 1)
        start1 = RIM + n0
        start2 = start1 + IMG
        self.spans = (
            (start0, start1),
            (start1, jnp.minimum(start1 + IMG, limit)),
            (start2, jnp.minimum(start2 + IMG, limit)),
        )
        one = lambda flag: jnp.where(flag, 1, 0)
        self.b0, self.b1 = lax.div(n0, QB), lax.div(self.n1, QB)
        self.d0 = one(self.b0 * QB != n0)
        self.d1 = one((self.n1 < rows) & (self.b1 * QB != self.n1))
        self.third = self.n1 < rows
        self.end0 = lax.div(n0 - 1, QB)
        self.end1 = lax.div(self.n1 - 1, QB) + self.d0
        self.one = one

    def base(self, start):
        return jnp.minimum(lax.div(start, 16), (self.ext - WIN) // 16)

    def segment(self, item):
        return self.one(item > self.end0) + self.one(item > self.end1)

    def item(self, item):
        blk = (
            item
            - self.d0 * self.one(item > self.b0)
            - self.d1 * self.one(item > self.b1 + self.d0)
        )
        used = blk < self.rows // QB
        blk = jnp.minimum(blk, self.rows // QB - 1)
        seg = self.segment(item)
        choose = lambda i: jnp.where(
            seg == 0, self.spans[0][i], jnp.where(seg == 1, self.spans[1][i], self.spans[2][i])
        )
        start, stop = choose(0), choose(1)
        base = self.base(start) * 16
        row0 = blk * QB
        low = jnp.maximum(start - RIM - row0, 0)
        high = jnp.where(used, jnp.minimum(stop - RIM - row0, QB), 0)
        return blk, row0, base, start - base, stop - base, low, high

    def of_block(self, blk):
        at0 = self.d0 * self.one(blk == self.b0)
        at1 = self.d1 * self.one(blk == self.b1)
        first = blk + self.d0 * self.one(blk > self.b0) + self.d1 * self.one(blk > self.b1)
        split = jnp.where(at0 == 1, self.n0, jnp.where(at1 == 1, self.n1, self.rows)) - blk * QB
        return first, first + at0 + at1, split


def attend_body(n0_ref, q_ref, k_ref, v_ref, out_ref, lse_ref, parts, parts_lse):
    rows = q_ref.shape[0]
    images = Images(n0_ref[0], rows, k_ref.shape[0])

    def scores_of(item):
        _, row0, base, low, high, _, _ = images.item(item)
        queries = stacked(q_ref[pl.ds(row0, QB), :]) * jnp.asarray(0.125, BF)
        scores = dot(k_ref[pl.ds(base, WIN), :], queries, NT)
        return scores + key_mask(low, high), base

    def softmax_of(scores):
        top = jnp.max(scores, axis=0, keepdims=True)
        terms = jnp.exp(scores - top)
        total = jnp.sum(terms, axis=0, keepdims=True)
        return terms.astype(BF), top, total

    @pl.loop(0, ITEMS // GROUP)
    def _(step):
        items = [step * GROUP + g for g in range(GROUP)]
        scored = [scores_of(item) for item in items]
        soft = [softmax_of(scores) for scores, _ in scored]
        mixed = [
            dot(v_ref[pl.ds(base, WIN), :], terms, TN) / total
            for (_, base), (terms, _, total) in zip(scored, soft)
        ]
        for item, value, (_, top, total) in zip(items, mixed, soft):
            parts[item] = unstacked(value)
            parts_lse[item] = jnp.broadcast_to(top + jnp.log(total), parts_lse.shape[1:])

    for blk in range(rows // QB):
        first, last, split = images.of_block(blk)
        row = lax.broadcasted_iota(jnp.int32, (QB, 2 * HDIM), 0)
        out_ref[pl.ds(blk * QB, QB), :] = jnp.where(
            row < split, parts[first], parts[last]
        ).astype(BF)
        lane = lax.broadcasted_iota(jnp.int32, parts_lse.shape[1:], 1) % QB
        lse_ref[0, pl.ds(blk, 1), :] = jnp.where(
            lane < split, parts_lse[first], parts_lse[last]
        )[:1]


def attend_kernel(n0_ref, q_ref, k_ref, v_ref, out_ref, lse_ref, parts, parts_lse):
    attend_body(n0_ref, q_ref, k_ref, v_ref, out_ref, lse_ref, parts, parts_lse)


def attend_gather_kernel(
    n0_ref, q_ref, k_ref, v_ref, w_out, w_up, out_ref, lse_ref, full_out, full_up,
    parts, parts_lse, send, recv, own,
):
    tick = pl.program_id(0)
    place = Place()
    pl.when(tick == 0)(lambda: greet(place.partners))
    pieces = []
    for shard, full in ((w_out, full_out), (w_up, full_up)):
        for k in range(shard.shape[1] // UNIT):
            i = len(pieces)
            pieces.append(
                Gather(
                    place, shard, full, pl.ds(k * UNIT, UNIT), send.at[i], recv.at[i], own.at[i]
                )
            )
    run_stages(pieces, tick, range(8))
    attend_body(n0_ref, q_ref, k_ref, v_ref, out_ref, lse_ref, parts, parts_lse)

    @pl.when(tick == 7)
    def _():
        pieces[-1].stage(4)


def attend(n0, queries, key_value, shards=None):
    rows, width = queries.shape
    pairs = width // (2 * HDIM)
    ext = key_value.shape[0]
    hbm = pl.BlockSpec(memory_space=pl.ANY)
    in_specs = [
        pl.BlockSpec(memory_space=pltpu.SMEM),
        pl.BlockSpec((rows, 2 * HDIM), lambda p: (0, p)),
        pl.BlockSpec((ext, 2 * HDIM), lambda p: (0, p)),
        pl.BlockSpec((ext, 2 * HDIM), lambda p: (0, pairs + p)),
    ]
    out_specs = [
        pl.BlockSpec((rows, 2 * HDIM), lambda p: (0, p)),
        pl.BlockSpec((1, rows // QB, 2 * QB), lambda p: (p, 0, 0)),
    ]
    out_shape = [
        jax.ShapeDtypeStruct((rows, width), BF),
        jax.ShapeDtypeStruct((pairs, rows // QB, 2 * QB), F32),
    ]
    scratch = [
        pltpu.VMEM((ITEMS, QB, 2 * HDIM), F32),
        pltpu.VMEM((ITEMS, 8, 2 * QB), F32),
    ]
    params = dict(vmem_limit_bytes=48 * 2**20)
    args = [n0, queries, key_value, key_value]
    kernel = attend_kernel
    if shards is not None:
        kernel = attend_gather_kernel
        in_specs += [hbm] * 2
        out_specs += [hbm] * 2
        out_shape += [jax.ShapeDtypeStruct((4, 2, 2, 2, *v.shape), BF) for v in shards]
        count = sum(v.shape[1] // UNIT for v in shards)
        scratch += [
            pltpu.SemaphoreType.DMA((count, GATHER_SEMS)),
            pltpu.SemaphoreType.DMA((count, GATHER_SEMS)),
            pltpu.SemaphoreType.DMA((count,)),
        ]
        params |= dict(collective_id=1, has_side_effects=True)
        args += shards
    return pl.pallas_call(
        kernel,
        grid=(pairs,),
        in_specs=in_specs,
        out_specs=out_specs,
        out_shape=out_shape,
        scratch_shapes=scratch,
        compiler_params=pltpu.CompilerParams(**params),
        name="attend",
    )(*args)


def attend_back_body(
    pair, n0_ref, q_ref, k_ref, v_ref, up_ref, lse_ref, dq_ref, dk_ref, dv_ref, slots, parts
):
    rows = q_ref.shape[0]
    images = Images(n0_ref[0], rows, k_ref.shape[0])
    pl.when(pair == 0)(lambda: slots.__setitem__(0, jnp.zeros(slots.shape[1:], F32)))
    lane = lax.broadcasted_iota(jnp.int32, (1, 2 * QB), 1) % QB

    def begin(item):
        blk, row0, base, low, high, first, stop = images.item(item)
        queries = stacked(q_ref[pl.ds(row0, QB), :]) * jnp.asarray(0.125, BF)
        upstream = stacked(up_ref[pl.ds(row0, QB), :])
        here = (lane >= first) & (lane < stop)
        lse = jnp.where(here, lse_ref[0, pl.ds(blk, 1), :], -NEG)
        scores = dot(k_ref[pl.ds(base, WIN), :], queries, NT)
        dprobs = dot(v_ref[pl.ds(base, WIN), :], upstream, NT)
        return base, queries, upstream, scores + key_mask(low, high), lse, dprobs

    def middle(scores, lse, dprobs):
        probs = jnp.exp(scores - lse)
        row_dot = jnp.sum(probs * dprobs, axis=0, keepdims=True)
        return probs.astype(BF), (probs * (dprobs - row_dot)).astype(BF)

    def finish(item, base, queries, upstream, probs, dscores):
        keep = (item > 0) & (images.segment(item) == images.segment(item - 1))
        old = jnp.where(keep, slots[item], jnp.zeros(slots.shape[1:], F32))
        slots[item + 1, :, : 2 * HDIM] = old[:, : 2 * HDIM] + dot(dscores, queries)
        slots[item + 1, :, 2 * HDIM :] = old[:, 2 * HDIM :] + dot(probs, upstream)
        parts[item] = unstacked(dot(k_ref[pl.ds(base, WIN), :], dscores, TN)) * 0.125

    @pl.loop(0, ITEMS // BACK_GROUP)
    def _(step):
        items = [step * BACK_GROUP + g for g in range(BACK_GROUP)]
        begun = [begin(items[0])]
        done = []
        for g in range(BACK_GROUP + 1):
            if g + 1 < BACK_GROUP:
                begun.append(begin(items[g + 1]))
            if g < BACK_GROUP:
                done.append(middle(*begun[g][3:]))
            if g > 0:
                finish(items[g - 1], *begun[g - 1][:3], *done[g - 1])

    for blk in range(rows // QB):
        first, last, split = images.of_block(blk)
        row = lax.broadcasted_iota(jnp.int32, (QB, 2 * HDIM), 0)
        dq_ref[pl.ds(blk * QB, QB), :] = jnp.where(
            row < split, parts[first], parts[last]
        ).astype(BF)
    ends = (
        images.end0 + 1,
        jnp.minimum(images.end1, (rows - 1) // QB + images.d0) + 1,
        jnp.where(images.third, ITEMS, 0),
    )
    for seg, end in enumerate(ends):
        dk_ref[seg] = slots[end, :, : 2 * HDIM].astype(BF)
        dv_ref[seg] = slots[end, :, 2 * HDIM :].astype(BF)


def attend_back_kernel(*refs):
    attend_back_body(pl.program_id(0), *refs)


def attend_back_scatter_kernel(*refs):
    base, (g_out, g_up), rest = refs[:6], refs[6:8], refs[8:]
    outs, (r_out, r_up), scratch = rest[:3], rest[3:5], rest[5:]
    mine, comm = scratch[:2], scratch[2:]
    pair = pl.program_id(0)
    place = Place()
    pl.when(pair == 0)(lambda: greet(place.partners))
    pieces = []
    for grad, out in ((g_out, r_out), (g_up, r_up)):
        for k in range(grad.shape[5] // UNIT):
            cols = pl.ds(k * UNIT, UNIT)
            bufs = comm[len(pieces) * 8 : len(pieces) * 8 + 8]
            pieces.append(
                Scatter(
                    place, grad.at[:, :, :, :, :, cols], *bufs[:5], out.at[:, cols], bufs[5:]
                )
            )
    run_stages(pieces, pair, range(8))
    attend_back_body(pair, *base, *outs, *mine)

    @pl.when(pair == pl.num_programs(0) - 1)
    def _():
        pieces[-1].stage(4)


def attend_back(n0, queries, key_value, upstream, lse, grads=None):
    rows, width = queries.shape
    pairs = width // (2 * HDIM)
    ext = key_value.shape[0]
    hbm, vmem = pl.BlockSpec(memory_space=pl.ANY), pl.BlockSpec(memory_space=pltpu.VMEM)
    own = pl.BlockSpec((rows, 2 * HDIM), lambda p: (0, p))
    windows = pl.BlockSpec((3, WIN, 2 * HDIM), lambda p: (0, 0, p))
    in_specs = [
        pl.BlockSpec(memory_space=pltpu.SMEM),
        own,
        pl.BlockSpec((ext, 2 * HDIM), lambda p: (0, p)),
        pl.BlockSpec((ext, 2 * HDIM), lambda p: (0, pairs + p)),
        own,
        pl.BlockSpec((1, rows // QB, 2 * QB), lambda p: (p, 0, 0)),
    ]
    out_specs = [own, windows, windows]
    out_shape = [jax.ShapeDtypeStruct((rows, width), BF)]
    out_shape += [jax.ShapeDtypeStruct((3, WIN, width), BF)] * 2
    scratch = [
        pltpu.VMEM((ITEMS + 1, WIN, 4 * HDIM), F32),
        pltpu.VMEM((ITEMS, QB, 2 * HDIM), F32),
    ]
    args = [n0, queries, key_value, key_value, upstream, lse]
    kernel, params = attend_back_kernel, dict(vmem_limit_bytes=58 * 2**20)
    if grads is not None:
        kernel = attend_back_scatter_kernel
        params |= dict(collective_id=2, has_side_effects=True)
        args += map(blocks, grads)
        in_specs += [hbm] * 2
        out_specs += [vmem] * 2
        out_shape += [jax.ShapeDtypeStruct((v.shape[0] // 32, v.shape[1]), F32) for v in grads]
        for v in grads:
            scratch += scatter_scratch(v.shape[0] // 32, UNIT) * (v.shape[1] // UNIT)
    return pl.pallas_call(
        kernel,
        grid=(pairs,),
        in_specs=in_specs,
        out_specs=out_specs,
        out_shape=out_shape,
        scratch_shapes=scratch,
        compiler_params=pltpu.CompilerParams(**params),
        name="attend_back",
    )(*args)


ROW_TILE = 256
FF_TILE = 512
ROOT_HALF = 1.0 / math.sqrt(2.0)
PDF_SCALE = 1.0 / math.sqrt(2.0 * math.pi)


def row_stats(value):
    mean = jnp.mean(value, axis=1, keepdims=True)
    center = value - mean
    inv_std = lax.rsqrt(jnp.mean(center * center, axis=1, keepdims=True) + EPS)
    return center * inv_std, inv_std


def mlp_up_body(
    step, row_steps, mixed, tokens, w_out, vecs, w_up, up_bias, cot, resid, normed, act, slope,
    g_down, held,
):
    @pl.when(step < row_steps)
    def _():
        value = tokens[...].astype(F32) + dot(mixed[...], w_out[...]) + vecs[0:1]
        resid[...] = value
        low = (row_stats(value)[0] * vecs[1:2] + vecs[2:3]).astype(BF)
        normed[...] = low
        held[pl.ds(step * ROW_TILE, ROW_TILE), :] = low

    @pl.when(step >= row_steps)
    def _():
        rows = held.shape[0]

        for row in range(0, rows, ROW_TILE):
            part = pl.ds(row, ROW_TILE)
            upward = dot(held[part, :], w_up[...]) + up_bias[...]
            cdf = 0.5 * (1.0 + lax.erf(upward * ROOT_HALF))
            pdf = jnp.exp(-0.5 * upward * upward) * PDF_SCALE
            act[part, :] = (upward * cdf).astype(BF)
            slope[part, :] = (cdf + upward * pdf).astype(BF)
        g_down[...] = dot(act[...], cot[...], TN).astype(BF)


def mlp_up_kernel(row_steps, *refs):
    mlp_up_body(pl.program_id(0), row_steps, *refs)


def mlp_up_gather_kernel(row_steps, *refs):
    ins, shard, outs, full = refs[:7], refs[7], refs[8:13], refs[13]
    held, send, recv, own = refs[14:]
    step = pl.program_id(0)
    place = Place()
    pl.when(step == 0)(lambda: greet(place.partners))
    cols = shard.shape[1] // 4
    pieces = [
        Gather(place, shard, full, pl.ds(k * cols, cols), send.at[k], recv.at[k], own.at[k])
        for k in range(4)
    ]
    run_stages(pieces, step, (0, 2, 4, 5, 7, 9, 11))
    mlp_up_body(step, row_steps, *ins, *outs, held)

    @pl.when(step == pl.num_programs(0) - 1)
    def _():
        pieces[3].stage(4)


def mlp_up(mixed, tokens, w_out, vecs, w_up, up_bias, cot, shard=None):
    rows, width = tokens.shape
    hidden = w_up.shape[1]
    row_steps, ff_steps = rows // ROW_TILE, hidden // FF_TILE
    at_row = lambda s: (jnp.minimum(s, row_steps - 1), 0)
    at_col = lambda s: (0, jnp.maximum(s - row_steps, 0))
    at_ff = lambda s: (jnp.maximum(s - row_steps, 0), 0)
    const = lambda s: (0, 0)
    hbm = pl.BlockSpec(memory_space=pl.ANY)
    tall = pl.BlockSpec((rows, FF_TILE), at_col)
    in_specs = [
        pl.BlockSpec((ROW_TILE, width), at_row),
        pl.BlockSpec((ROW_TILE, width), at_row),
        pl.BlockSpec((width, width), const),
        pl.BlockSpec((8, width), const),
        pl.BlockSpec((width, FF_TILE), at_col),
        pl.BlockSpec((1, FF_TILE), at_col),
        pl.BlockSpec((rows, width), const),
    ]
    out_specs = [
        pl.BlockSpec((ROW_TILE, width), at_row),
        pl.BlockSpec((ROW_TILE, width), at_row),
        tall,
        tall,
        pl.BlockSpec((FF_TILE, width), at_ff),
    ]
    out_shape = [
        jax.ShapeDtypeStruct((rows, width), F32),
        jax.ShapeDtypeStruct((rows, width), BF),
        jax.ShapeDtypeStruct((rows, hidden), BF),
        jax.ShapeDtypeStruct((rows, hidden), BF),
        jax.ShapeDtypeStruct((hidden, width), BF),
    ]
    scratch = [pltpu.VMEM((rows, width), BF)]
    params = dict(vmem_limit_bytes=58 * 2**20)
    args = [mixed, tokens, w_out, vecs, w_up, up_bias, cot]
    kernel = mlp_up_kernel
    if shard is not None:
        kernel = mlp_up_gather_kernel
        in_specs += [hbm]
        out_specs += [hbm]
        out_shape += [jax.ShapeDtypeStruct((4, 2, 2, 2, *shard.shape), BF)]
        scratch += [
            pltpu.SemaphoreType.DMA((4, GATHER_SEMS)),
            pltpu.SemaphoreType.DMA((4, GATHER_SEMS)),
            pltpu.SemaphoreType.DMA((4,)),
        ]
        params |= dict(collective_id=5, has_side_effects=True)
        args += [shard]
    return pl.pallas_call(
        functools.partial(kernel, row_steps),
        grid=(row_steps + ff_steps,),
        in_specs=in_specs,
        out_specs=out_specs,
        out_shape=out_shape,
        scratch_shapes=scratch,
        compiler_params=pltpu.CompilerParams(**params),
        name="mlp_up",
    )(*args)


def mlp_back_body(
    step, ff_steps, act, slope, w_up, w_down, cot, normed, resid, mixed, w_out, vecs,
    g_up, up_sums, layer_out, dresid, dmixed, g_out, sums, total, dnormed, branches, dup,
):
    rows, width = cot.shape

    @pl.when(step == 0)
    def _():
        total[...] = jnp.zeros(total.shape, F32)
        dnormed[...] = jnp.zeros(dnormed.shape, F32)
        sums[...] = jnp.zeros(sums.shape, F32)

    @pl.when(step < ff_steps)
    def _():
        count = jnp.zeros(up_sums.shape, F32)
        for row in range(0, rows, ROW_TILE):
            part = pl.ds(row, ROW_TILE)
            total[part, :] += dot(act[part, :], w_down[...])
            dact = dot(cot[part, :], w_down[...], NT)
            low = (dact * slope[part, :].astype(F32)).astype(BF)
            dup[part, :] = low
            count += jnp.sum(low.astype(F32), axis=0, keepdims=True)
            dnormed[part, :] += dot(low, w_up[...], NT)
        up_sums[...] = count
        g_up[...] = dot(normed[...], dup[...], TN).astype(BF)

    @pl.when(step >= ff_steps)
    def _():
        part = pl.ds((step - ff_steps) * ROW_TILE, ROW_TILE)
        value = resid[...]
        scaled, inv_std = row_stats(value)
        upstream = dnormed[part, :]
        above = cot[part, :].astype(F32)
        through = upstream * vecs[1:2]
        inner = (
            through
            - jnp.mean(through, axis=1, keepdims=True)
            - scaled * jnp.mean(through * scaled, axis=1, keepdims=True)
        )
        grad = above + inv_std * inner
        dresid[...] = grad
        low = grad.astype(BF)
        branches[part, :] = low
        dmixed[...] = dot(low, w_out[...], NT).astype(BF)
        layer_out[...] = (value + total[part, :] + vecs[3:4]).astype(BF)
        sums[0:1] += jnp.sum(low.astype(F32), axis=0, keepdims=True)
        sums[1:2] += jnp.sum(upstream * scaled, axis=0, keepdims=True)
        sums[2:3] += jnp.sum(upstream, axis=0, keepdims=True)
        sums[3:4] += jnp.sum(above, axis=0, keepdims=True)

    @pl.when(step == pl.num_programs(0) - 1)
    def _():
        g_out[...] = dot(mixed[...], branches[...], TN).astype(BF)


def mlp_back_kernel(ff_steps, *refs):
    mlp_back_body(pl.program_id(0), ff_steps, *refs)


def mlp_back_scatter_kernel(ff_steps, *refs):
    ins, grad, outs, reduced, scratch, comm = (
        refs[:10], refs[10], refs[11:18], refs[18], refs[19:23], refs[23:],
    )
    step = pl.program_id(0)
    place = Place()
    pl.when(step == 0)(lambda: greet(place.partners))
    cols = reduced.shape[1] // 4
    pieces = []
    for k in range(4):
        here = pl.ds(k * cols, cols)
        bufs = comm[k * 8 : k * 8 + 8]
        pieces.append(
            Scatter(
                place, grad.at[:, :, :, :, :, here], *bufs[:5], reduced.at[:, here], bufs[5:]
            )
        )
    run_stages(pieces, step, (0, 1, 2, 4, 5, 7, 9))
    mlp_back_body(step, ff_steps, *ins, *outs, *scratch)

    @pl.when(step == pl.num_programs(0) - 1)
    def _():
        pieces[3].stage(4)


def mlp_back(act, slope, w_up, w_down, cot, normed, resid, mixed, w_out, vecs, grad=None):
    rows, width = cot.shape
    hidden = w_up.shape[1]
    row_steps, ff_steps = rows // ROW_TILE, hidden // FF_TILE
    at_row = lambda s: (jnp.maximum(s - ff_steps, 0), 0)
    at_col = lambda s: (0, jnp.minimum(s, ff_steps - 1))
    at_ff = lambda s: (jnp.minimum(s, ff_steps - 1), 0)
    const = lambda s: (0, 0)
    hbm, vmem = pl.BlockSpec(memory_space=pl.ANY), pl.BlockSpec(memory_space=pltpu.VMEM)
    once = lambda *shape: pl.BlockSpec(shape, const, pipeline_mode=pl.Buffered(1))
    tall = pl.BlockSpec((rows, FF_TILE), at_col)
    tile = pl.BlockSpec((ROW_TILE, width), at_row)
    in_specs = [
        tall, tall, pl.BlockSpec((width, FF_TILE), at_col), pl.BlockSpec((FF_TILE, width), at_ff),
        once(rows, width), once(rows, width), tile, once(rows, width), once(width, width),
        once(8, width),
    ]
    out_specs = [
        pl.BlockSpec((width, FF_TILE), at_col), pl.BlockSpec((1, FF_TILE), at_col), tile, tile,
        tile, once(width, width), once(8, width),
    ]
    out_shape = [
        jax.ShapeDtypeStruct((width, hidden), BF),
        jax.ShapeDtypeStruct((1, hidden), F32),
        jax.ShapeDtypeStruct((rows, width), BF),
        jax.ShapeDtypeStruct((rows, width), F32),
        jax.ShapeDtypeStruct((rows, width), BF),
        jax.ShapeDtypeStruct((width, width), BF),
        jax.ShapeDtypeStruct((8, width), F32),
    ]
    scratch = [
        pltpu.VMEM((rows, width), F32),
        pltpu.VMEM((rows, width), F32),
        pltpu.VMEM((rows, width), BF),
        pltpu.VMEM((rows, FF_TILE), BF),
    ]
    params = dict(vmem_limit_bytes=60 * 2**20)
    args = [act, slope, w_up, w_down, cot, normed, resid, mixed, w_out, vecs]
    kernel = mlp_back_kernel
    if grad is not None:
        kernel = mlp_back_scatter_kernel
        part = grad.shape[0] // 32
        in_specs += [hbm]
        out_specs += [vmem]
        out_shape += [jax.ShapeDtypeStruct((part, width), F32)]
        scratch += scatter_scratch(part, width // 4) * 4
        params |= dict(collective_id=6, has_side_effects=True)
        args += [blocks(grad)]
    return pl.pallas_call(
        functools.partial(kernel, ff_steps),
        grid=(row_steps + ff_steps,),
        in_specs=in_specs,
        out_specs=out_specs,
        out_shape=out_shape,
        scratch_shapes=scratch,
        compiler_params=pltpu.CompilerParams(**params),
        name="mlp_back",
    )(*args)


TILE = 64


class Total:
    def __init__(self, place, value, arrived, send, recv):
        p = place
        near = p.z + 1 - 2 * (p.z % 2)
        self.to = [p.sib, p.xp, p.yp, p.at(near, p.y, p.x, p.c), p.zp[1]]
        self.value, self.arrived, self.send, self.recv = value, arrived, send, recv

    def run(self):
        for i, to in enumerate(self.to):
            copy = mesh_copy(
                self.value.at[i], self.arrived.at[i], self.send.at[i], self.recv.at[i], to
            )
            copy.start()
            copy.wait()
            self.value[i + 1] = self.value[i] + self.arrived[i]


def last_body(
    step, n0_ref, normed, dq, dk, dv, w_qkv, tokens, dresid, vecs, sums, up_sums, out, grads,
    padded, outgoing, incoming, send, recv, vector_out,
):
    rows = dq.shape[0]
    ext, width = normed.shape
    images = Images(n0_ref[0], rows, ext)
    bases = [images.base(span[0]) for span in images.spans]
    me, peers = lax.axis_index(AXIS), lax.axis_size(AXIS)
    wide = slice(TILE, TILE + WIN)

    def halo(way):
        return mesh_copy(
            outgoing.at[way], incoming.at[way], send.at[way], recv.at[way],
            me - 1 if way == 0 else me + 1,
        )

    def column_sums(value):
        return jnp.sum(value.astype(F32), axis=0, keepdims=True)

    @pl.when(step == 0)
    def _():
        vector_out[...] = jnp.zeros(vector_out.shape, F32)
        vector_out[4:8] = sums[0:4]
        for k in range(up_sums.shape[1] // width):
            vector_out[8 + k : 9 + k] = up_sums[:, k * width : (k + 1) * width]
        vector_out[2:3] = column_sums(dq[...])
        padded[...] = jnp.zeros(padded.shape, F32)

        @pl.when(me == 0)
        def _():
            incoming[1] = jnp.zeros(incoming.shape[1:], BF)

        @pl.when(me == peers - 1)
        def _():
            incoming[0] = jnp.zeros(incoming.shape[1:], BF)

        for col in range(0, width, ROW_TILE):
            cols = pl.ds(col, ROW_TILE)
            grads[0, cols, :] = dot(normed[pl.ds(RIM, rows), cols], dq[...], TN).astype(BF)

    for which, part in ((1, dk), (2, dv)):
        @pl.when(step == which)
        def _():
            for col in range(0, width, ROW_TILE):
                cols = pl.ds(col, ROW_TILE)
                total = None
                for seg, base in enumerate(bases):
                    term = dot(normed[pl.ds(base * 16, WIN), cols], part[seg], TN)
                    total = term if total is None else total + term
                grads[which, cols, :] = total.astype(BF)
            if which == 2:
                vector_out[3:4] = (
                    column_sums(dv[0]) + column_sums(dv[1]) + column_sums(dv[2])
                )

    @pl.when(step == 3)
    def _():
        for seg in range(3):
            padded[seg, wide] = dot(dk[seg], w_qkv[...], NT)

    @pl.when(step == 4)
    def _():
        for seg in (0, 2, 1):
            padded[seg, wide] += dot(dv[seg], w_qkv[...], NT)
        outgoing[0] = padded[0, wide].astype(BF)
        outgoing[1] = jnp.where(images.third, padded[2, wide], padded[1, wide]).astype(BF)
        pl.when(me > 0)(lambda: halo(0).start())
        pl.when(me < peers - 1)(lambda: halo(1).start())

    @pl.when(step == 5)
    def _():
        @pl.when(me > 0)
        def _():
            halo(0).wait_send()
            halo(1).wait_recv()

        @pl.when(me < peers - 1)
        def _():
            halo(1).wait_send()
            halo(0).wait_recv()

        none = jnp.zeros((WIN, width), F32)
        stop = jnp.where(images.third, images.spans[2][1], images.spans[1][1])
        cut = (stop > RIM + rows) & (me < peers - 1)
        after = jnp.where(cut, incoming[0].astype(F32), none)
        padded[0, wide] += jnp.where(images.spans[0][0] < RIM, incoming[1].astype(F32), none)
        padded[1, wide] += jnp.where(images.third, none, after)
        padded[2, wide] += jnp.where(images.third, after, none)

    @pl.when(step >= 5)
    def _():
        first = (step - 5) * ROW_TILE
        upstream = dot(dq[pl.ds(first, ROW_TILE), :], w_qkv[...], NT)
        places = []
        for k in range(ROW_TILE // TILE):
            total = upstream[k * TILE : (k + 1) * TILE]
            for seg, base in enumerate(bases):
                off = jnp.maximum(
                    (RIM + TILE) // 16 + (step - 5) * (ROW_TILE // 16) + k * (TILE // 16) - base, 0
                )
                off = jnp.minimum(off, (WIN + TILE) // 16) * 16
                total = total + padded[seg, pl.ds(off, TILE), :]
            places.append(total)
        upstream = jnp.concatenate(places, axis=0)
        scaled, inv_std = row_stats(tokens[...].astype(F32))
        through = upstream * vecs[0:1]
        inner = (
            through
            - jnp.mean(through, axis=1, keepdims=True)
            - scaled * jnp.mean(through * scaled, axis=1, keepdims=True)
        )
        out[...] = dresid[...] + inv_std * inner
        vector_out[0:1] += jnp.sum(upstream * scaled, axis=0, keepdims=True)
        vector_out[1:2] += jnp.sum(upstream, axis=0, keepdims=True)


LAST_STEPS = 9


def last_kernel(*refs):
    step = pl.program_id(0)
    me, peers = lax.axis_index(AXIS), lax.axis_size(AXIS)
    ins, (out, vector_out, grads_out), scratch = refs[:11], refs[11:14], refs[14:]
    grads, padded, outgoing, incoming, send, recv = scratch
    pl.when(step == 0)(lambda: greet([], me > 0, me < peers - 1))
    last_body(step, *ins, out, grads, padded, outgoing, incoming, send, recv, vector_out)

    @pl.when(step == LAST_STEPS - 1)
    def _():
        grads_out[...] = grads[...]


def last_scatter_kernel(*refs):
    step = pl.program_id(0)
    me, peers = lax.axis_index(AXIS), lax.axis_size(AXIS)
    ins, (out, vector_out, reduced), scratch = refs[:11], refs[11:14], refs[14:]
    grads, padded, outgoing, incoming, send, recv = scratch[:6]
    vectors, arrived, vec_send, vec_recv = scratch[6:10]
    comm = scratch[10:]
    place = Place()
    pl.when(step == 0)(lambda: greet(place.partners, me > 0, me < peers - 1))
    pieces = [
        Scatter(
            place, grads.at[k], *comm[k * 8 : k * 8 + 5], reduced.at[:, pl.ds(k * UNIT, UNIT)],
            comm[k * 8 + 5 : k * 8 + 8],
        )
        for k in range(3)
    ]
    run_stages(pieces, step, (1, 2, 3, 4, 5, 6))
    last_body(
        step, *ins, out, Flat(grads), padded, outgoing, incoming, send, recv, vectors.at[0]
    )

    @pl.when(step == LAST_STEPS - 1)
    def _():
        pieces[2].stage(4)
        Total(place, vectors, arrived, vec_send, vec_recv).run()
        vector_out[...] = vectors[5]


class Flat:
    def __init__(self, ref):
        self.ref = ref

    def __setitem__(self, index, value):
        k, rows, _ = index
        part = self.ref.shape[5]
        count = rows.size // part
        first = rows.start // part
        for i in range(0, count, 8):
            block = value[i * part : (i + 8) * part].reshape(2, 2, 2, part, value.shape[1])
            self.ref[k, (first + i) // 8] = block


def last(n0, normed, dq, dk, dv, w_qkv, tokens, dresid, vecs, sums, up_sums, plan):
    rows, width = dq.shape
    ext = normed.shape[0]
    peers = lax.axis_size(AXIS)
    const = lambda s: (0, 0)
    once = lambda *shape: pl.BlockSpec(
        shape, lambda s: (0,) * len(shape), pipeline_mode=pl.Buffered(1)
    )
    tile = pl.BlockSpec((ROW_TILE, width), lambda s: (jnp.maximum(s - 5, 0), 0))
    third = lambda s: (0, jnp.where(s <= 3, 1, jnp.where(s == 4, 2, 0)))
    vmem = pl.BlockSpec(memory_space=pltpu.VMEM)
    in_specs = [
        pl.BlockSpec(memory_space=pltpu.SMEM),
        once(ext, width), once(rows, width), once(3, WIN, width), once(3, WIN, width),
        pl.BlockSpec((width, width), third), tile, tile, once(8, width), once(8, width),
        once(*up_sums.shape),
    ]
    vector_rows = 16
    shared = [
        pltpu.VMEM((3, WIN + 2 * TILE, width), F32),
        pltpu.VMEM((2, WIN, width), BF),
        pltpu.VMEM((2, WIN, width), BF),
        pltpu.SemaphoreType.DMA((2,)),
        pltpu.SemaphoreType.DMA((2,)),
    ]
    if plan:
        part = width // peers
        kernel, collective = last_scatter_kernel, 3
        scratch = [pltpu.VMEM((3, 4, 2, 2, 2, part, width), BF)] + shared + [
            pltpu.VMEM((6, vector_rows, width), F32),
            pltpu.VMEM((5, vector_rows, width), F32),
            pltpu.SemaphoreType.DMA((5,)),
            pltpu.SemaphoreType.DMA((5,)),
        ] + scatter_scratch(part, UNIT) * 3
        third_out = jax.ShapeDtypeStruct((part, 3 * width), F32)
    else:
        kernel, collective = last_kernel, 4
        scratch = [pltpu.VMEM((3, width, width), BF)] + shared
        third_out = jax.ShapeDtypeStruct((3, width, width), BF)
    return pl.pallas_call(
        kernel,
        grid=(LAST_STEPS,),
        in_specs=in_specs,
        out_specs=[tile, once(vector_rows, width), once(*third_out.shape)],
        out_shape=[
            jax.ShapeDtypeStruct((rows, width), F32),
            jax.ShapeDtypeStruct((vector_rows, width), F32),
            third_out,
        ],
        scratch_shapes=scratch,
        compiler_params=pltpu.CompilerParams(
            vmem_limit_bytes=61 * 2**20, collective_id=collective, has_side_effects=True
        ),
        name="last",
    )(n0, normed, dq, dk, dv, w_qkv, tokens, dresid, vecs, sums, up_sums)


def shifted(value, by):
    peers = lax.axis_size(AXIS)
    pairs = [(i, i + by) for i in range(peers) if 0 <= i + by < peers]
    return lax.ppermute(value, AXIS, pairs)


def gathered(value):
    return lax.all_gather(value, AXIS, axis=0, tiled=True)


def scattered(value):
    return lax.psum_scatter(value, AXIS, scatter_dimension=0, tiled=True)


def normalize(inputs, gain, shift):
    center = inputs - jnp.mean(inputs, axis=1, keepdims=True)
    inv_std = lax.rsqrt(jnp.mean(center * center, axis=1, keepdims=True) + EPS)
    scaled = center * inv_std
    return (scaled * gain + shift, scaled, inv_std)


def local(
    tokens,
    image_ids,
    cotangent,
    norm1_gain,
    norm1_shift,
    qkv_weight,
    query_bias,
    value_bias,
    out_weight,
    out_bias,
    norm2_gain,
    norm2_shift,
    up_weight,
    up_bias,
    down_weight,
    down_bias,
):
    rows, width = tokens.shape
    me = lax.axis_index(AXIS)
    peers = lax.axis_size(AXIS)
    n0 = jnp.sum((image_ids == image_ids[0]).astype(jnp.int32)).reshape(1)
    ext = -(-(rows + 2 * RIM + 64) // 128) * 128
    packed = jnp.concatenate(
        [norm1_gain, norm1_shift, query_bias, value_bias, out_bias, norm2_gain, norm2_shift,
         down_bias, up_bias]
    )
    block_plan = peers == 32
    if block_plan:
        count = packed.shape[0]
        packed = jnp.pad(packed, (0, 32 * 128 - count)).reshape(32, 128)
        w_qkv, vectors = gather_blocks(qkv_weight, packed)
        vectors = vectors[:, :count].astype(F32)
    else:
        w_qkv, vectors = gathered(qkv_weight), gathered(packed[None]).astype(F32)
        w_out, w_up, w_down = map(gathered, (out_weight, up_weight, down_weight))
    part = norm1_gain.shape[0]
    gain1, shift1, q_bias, v_bias, o_bias, gain2, shift2, d_bias = (
        vectors[:, i * part : (i + 1) * part].reshape(-1) for i in range(8)
    )
    u_bias = vectors[:, 8 * part :].reshape(-1)

    low_rim = shifted(tokens[rows - RIM :], 1)
    high_rim = shifted(tokens[:RIM], -1)
    pad = jnp.zeros((ext - rows - 2 * RIM, width), BF)
    tokens_ext = jnp.concatenate([low_rim, tokens, high_rim, pad], axis=0).astype(F32)
    normed_ext = normalize(tokens_ext, gain1, shift1)[0].astype(BF)
    normed_low = normed_ext[RIM : RIM + rows]
    queries = (dot(normed_low, w_qkv[:, :width]) + q_bias).astype(BF)
    key_value = (
        dot(normed_ext, w_qkv[:, width:]) + jnp.concatenate([jnp.zeros_like(v_bias), v_bias])
    ).astype(BF)
    if block_plan:
        mixed_low, lse, w_out, w_up = attend(
            n0, queries, key_value, (out_weight, up_weight)
        )
        w_out, w_up = w_out.reshape(width, -1), w_up.reshape(width, -1)
    else:
        mixed_low, lse = attend(n0, queries, key_value)

    vecs = jnp.stack([o_bias, gain2, shift2, d_bias] + [jnp.zeros_like(d_bias)] * 4)
    args = (mixed_low, tokens, w_out, vecs, w_up, u_bias[None], cotangent)
    if block_plan:
        resid, normed_two, act, slope, grad_down, w_down = mlp_up(*args, down_weight)
        w_down = w_down.reshape(-1, width)
    else:
        resid, normed_two, act, slope, grad_down = mlp_up(*args)
    args = (act, slope, w_up, w_down, cotangent, normed_two, resid, mixed_low, w_out, vecs)
    if block_plan:
        grad_up, up_sums, layer_out, dresid, dmixed_low, grad_out, sums, r_down = mlp_back(
            *args, grad_down
        )
    else:
        grad_up, up_sums, layer_out, dresid, dmixed_low, grad_out, sums = mlp_back(*args)
        r_down = scattered(grad_down).astype(F32)
    if block_plan:
        dquery, dkey, dvalue, r_out, r_up = attend_back(
            n0, queries, key_value, dmixed_low, lse, (grad_out, grad_up)
        )
    else:
        dquery, dkey, dvalue = attend_back(n0, queries, key_value, dmixed_low, lse)
        r_out, r_up = (scattered(v).astype(F32) for v in (grad_out, grad_up))
    vecs = jnp.concatenate([gain1[None], jnp.zeros((7, width), F32)])
    grad_tokens, totals, r_qkv = last(
        n0, normed_ext, dquery, dkey, dvalue, w_qkv, tokens, dresid, vecs, sums, up_sums,
        block_plan,
    )
    if not block_plan:
        totals = lax.psum(totals, AXIS)
        r_qkv = jnp.concatenate([scattered(v) for v in r_qkv], axis=1).astype(F32)
    owned = lax.dynamic_slice_in_dim(totals[:8], me * part, part, 1)
    size = u_bias.shape[0] // peers
    up_own = lax.dynamic_slice_in_dim(totals[8 : 8 + u_bias.shape[0] // width].reshape(-1), me * size, size)
    g = [owned[i] for i in range(8)] + [up_own]
    return (
        layer_out, grad_tokens, g[0], g[1], r_qkv, g[2], g[3], r_out, g[4], g[5], g[6], r_up,
        g[8], r_down, g[7],
    )


def solution(mesh):
    row, vec = P(AXIS, None), P(AXIS)
    return jax.shard_map(
        local,
        mesh=mesh,
        in_specs=(
            row, vec, row, vec, vec, row, vec, vec, row, vec, vec, vec, row, vec, row, vec,
        ),
        out_specs=(
            row, row, vec, vec, row, vec, vec, row, vec, vec, vec, row, vec, row, vec,
        ),
        check_vma=False,
    )
```

```python
import functools
import math

import jax
import jax.numpy as jnp
from jax import lax
from jax.experimental import pallas as pl
from jax.experimental.pallas import tpu as pltpu
from jax.sharding import PartitionSpec as P

HDIM = 64
IMG = 577
RIM = IMG - 1
WIN = 592
QB = 128
EPS = 1e-06
NEG = -1e30
AXIS = "fsdp"
BF = jnp.bfloat16
F32 = jnp.float32
NT = (((1,), (1,)), ((), ()))
TN = (((0,), (0,)), ((), ()))
NN = (((1,), (0,)), ((), ()))


def dot(a, b, dims=NN):
    return lax.dot_general(a, b, dims, preferred_element_type=F32)


def stacked(block):
    lane = lax.broadcasted_iota(jnp.int32, block.shape, 1)
    zero = jnp.zeros_like(block)
    return jnp.concatenate(
        [jnp.where(lane < HDIM, block, zero), jnp.where(lane >= HDIM, block, zero)], axis=0
    )


def unstacked(wide):
    return jnp.concatenate([wide[:HDIM, :QB], wide[HDIM:, QB:]], axis=0).T


def key_mask(low, high):
    row = lax.broadcasted_iota(jnp.int32, (WIN, QB), 0)
    bias = jnp.where((row >= low) & (row < high), 0.0, NEG)
    return jnp.concatenate([bias, bias], axis=1)


def mesh_copy(src, dst, send_sem, recv_sem, to):
    return pltpu.make_async_remote_copy(
        src_ref=src,
        dst_ref=dst,
        send_sem=send_sem,
        recv_sem=recv_sem,
        device_id=(to,),
        device_id_type=pl.DeviceIdType.MESH,
    )


class Place:
    def __init__(self):
        me = lax.axis_index(AXIS)
        self.c, self.x, self.y, self.z = me % 2, me // 2 % 2, me // 4 % 2, me // 8
        self.sib = self.at(self.z, self.y, self.x, 1 - self.c)
        self.xp = self.at(self.z, self.y, 1 - self.x, self.c)
        self.yp = self.at(self.z, 1 - self.y, self.x, self.c)
        self.zp = [self.at((self.z + k) % 4, self.y, self.x, self.c) for k in (1, 2, 3)]
        self.far = self.at(self.z, 1 - self.y, 1 - self.x, self.c)
        self.partners = [self.sib, self.xp, self.yp, *self.zp]

    @staticmethod
    def at(z, y, x, c):
        return ((z * 2 + y) * 2 + x) * 2 + c


def greet(partners, before=None, after=None):
    barrier = pltpu.get_barrier_semaphore()

    def hello(to):
        pl.semaphore_signal(
            barrier, inc=1, device_id=(to,), device_id_type=pl.DeviceIdType.MESH
        )

    for to in partners:
        hello(to)
    if before is None:
        pl.semaphore_wait(barrier, len(partners))
        return
    me = lax.axis_index(AXIS)
    pl.when(before)(lambda: hello(me - 1))
    pl.when(after)(lambda: hello(me + 1))
    pl.semaphore_wait(
        barrier, len(partners) + before.astype(jnp.int32) + after.astype(jnp.int32)
    )


class Gather:
    def __init__(self, place, shard, full, cols, send, recv, own, tilt=False):
        self.shard, self.own = shard.at[:, cols], own
        p, rows = place, shard.shape[0]
        half = rows // 2

        def block(y, x, part=slice(None)):
            return full.at[:, y, x, p.c, part, cols]

        mine = full.at[p.z, p.y, p.x, p.c, :, cols]
        self.local = lambda: pltpu.make_async_copy(self.shard, mine, own)

        def copy(i, src, dst, to):
            return lambda: mesh_copy(src, dst, send.at[i], recv.at[i], to)

        same = lambda i, ref, to: copy(i, ref, ref, to)
        first, second = pl.ds(0, half), pl.ds(half, half)
        self.z = [copy(i, self.shard, mine, to) for i, to in enumerate(p.zp)]
        self.xy = [same(3, block(p.y, p.x), p.xp), same(4, block(p.y, p.x), p.yp)]
        self.far = [
            same(5, block(p.y, 1 - p.x, first), p.yp),
            same(6, block(1 - p.y, p.x, second), p.xp),
        ]
        if tilt:
            self.far = [same(5, block(p.y, 1 - p.x), p.yp)]
        self.pair = [
            same(7, block(p.y, p.x), p.sib),
            same(8, block(p.y, 1 - p.x), p.sib),
            same(9, block(1 - p.y, p.x), p.sib),
            same(10, block(1 - p.y, 1 - p.x), p.sib),
        ]

    def stage(self, number):
        if number == 0:
            self.local().start()
            for c in self.z:
                c().start()
        elif number == 1:
            self.local().wait()
            for c in self.z:
                c().wait()
            for c in (*self.xy, self.pair[0]):
                c().start()
        elif number == 2:
            for c in self.xy:
                c().wait()
            for c in (*self.far, self.pair[1], self.pair[2]):
                c().start()
        elif number == 3:
            for c in self.far:
                c().wait()
            self.pair[3]().start()
        else:
            for c in self.pair:
                c().wait()


GATHER_SEMS = 11


def run_stages(pieces, step, steps):
    for at in sorted(set(steps)):
        todo = [
            (q, piece)
            for tick, when in enumerate(steps)
            if when == at
            for k, piece in enumerate(pieces)
            for q in (4, 3, 2, 1, 0)
            if k + q == tick
        ][::-1]

        @pl.when(step == at)
        def _():
            for q, piece in todo:
                piece.stage(q)


class Scatter:
    def __init__(self, place, grad, held, from_pair, far, side, line, out, sems, tilt=False):
        self.tilt = tilt
        self.p, self.out = place, out
        self.held, self.from_pair, self.far, self.side, self.line = held, from_pair, far, side, line
        p, rows = place, held.shape[3]
        self.half = rows // 2
        own, send, recv = sems
        first, second = pl.ds(0, self.half), pl.ds(self.half, self.half)

        def copy(i, src, dst, to):
            return lambda: mesh_copy(src, dst, send.at[i], recv.at[i], to)

        self.load = lambda: pltpu.make_async_copy(grad.at[:, :, :, p.c], held, own)
        self.to_pair = copy(0, grad.at[:, :, :, 1 - p.c], from_pair, p.sib)
        self.to_far = [
            copy(1, held.at[:, 1 - p.y, 1 - p.x, first], far.at[0], p.xp),
            copy(2, held.at[:, 1 - p.y, 1 - p.x, second], far.at[1], p.yp),
        ]
        if tilt:
            self.to_far = [copy(1, held.at[:, 1 - p.y, 1 - p.x], far, p.yp)]
        self.to_side = [
            copy(3, held.at[:, p.y, 1 - p.x], side.at[0], p.xp),
            copy(4, held.at[:, 1 - p.y, p.x], side.at[1], p.yp),
        ]
        self.to_line = [
            copy(5 + k, held.at[(p.z + k + 1) % 4, p.y, p.x], line.at[k], to)
            for k, to in enumerate(p.zp)
        ]

    def stage(self, number):
        p, half = self.p, self.half
        held, far, side, line = self.held, self.far, self.side, self.line
        if number == 0:
            self.load().start()
            self.to_pair().start()
        elif number == 1:
            self.load().wait()
            self.to_pair().wait()

            @pl.loop(0, 4)
            def _(z):
                for y in range(2):
                    for x in range(2):
                        held[z, y, x] = (
                            held[z, y, x].astype(F32) + self.from_pair[z, y, x].astype(F32)
                        ).astype(held.dtype)

            for c in self.to_far:
                c().start()
        elif number == 2:
            for c in self.to_far:
                c().wait()

            @pl.loop(0, 4)
            def _(z):
                if self.tilt:
                    held[z, p.y, 1 - p.x] = (
                        held[z, p.y, 1 - p.x].astype(F32) + far[z].astype(F32)
                    ).astype(held.dtype)
                    return
                held[z, 1 - p.y, p.x, :half] = (
                    held[z, 1 - p.y, p.x, :half].astype(F32) + far[0, z].astype(F32)
                ).astype(held.dtype)
                held[z, p.y, 1 - p.x, half:] = (
                    held[z, p.y, 1 - p.x, half:].astype(F32) + far[1, z].astype(F32)
                ).astype(held.dtype)

            for c in self.to_side:
                c().start()
        elif number == 3:
            for c in self.to_side:
                c().wait()

            @pl.loop(0, 4)
            def _(z):
                held[z, p.y, p.x] = (
                    held[z, p.y, p.x].astype(F32)
                    + side[0, z].astype(F32)
                    + side[1, z].astype(F32)
                ).astype(held.dtype)

            for c in self.to_line:
                c().start()
        else:
            for c in self.to_line:
                c().wait()
            self.out[...] = (
                held[p.z, p.y, p.x].astype(F32)
                + line[0].astype(F32)
                + line[1].astype(F32)
                + line[2].astype(F32)
            )


SCATTER_SEMS = 8
UNIT = 1024


def scatter_scratch(rows, cols, dtype=BF, tilt=False):
    return [
        pltpu.VMEM((4, 2, 2, rows, cols), dtype),
        pltpu.VMEM((4, 2, 2, rows, cols), dtype),
        pltpu.VMEM((4, rows, cols) if tilt else (2, 4, rows // 2, cols), dtype),
        pltpu.VMEM((2, 4, rows, cols), dtype),
        pltpu.VMEM((3, rows, cols), dtype),
        pltpu.SemaphoreType.DMA,
        pltpu.SemaphoreType.DMA((SCATTER_SEMS,)),
        pltpu.SemaphoreType.DMA((SCATTER_SEMS,)),
    ]


def blocks(value):
    return value.reshape(4, 2, 2, 2, value.shape[0] // 32, value.shape[1])


VEC_ROWS = 16


def first_body(
    rows, tokens, wide, vec, q_out, kv_out, normed_out, w_out, vecs_out, bias_out,
    near, normed, weights, gathered_vec, queries, pairs, send, recv, own, halo_send, halo_recv,
    load, store,
):
    place = Place()
    me, peers = lax.axis_index(AXIS), lax.axis_size(AXIS)
    greet(place.partners, me > 0, me < peers - 1)
    width = near.shape[1]
    mine = pl.ds(RIM, rows)

    def halo(way):
        if way == 0:
            src, dst, to = tokens.at[pl.ds(0, RIM)], near.at[pl.ds(RIM + rows, RIM)], me - 1
        else:
            src, dst, to = tokens.at[pl.ds(rows - RIM, RIM)], near.at[pl.ds(0, RIM)], me + 1
        return mesh_copy(src, dst, halo_send.at[way], halo_recv.at[way], to)

    pieces = [
        Gather(
            place, vec, gathered_vec, pl.ds(0, vec.shape[1]), send.at[0], recv.at[0], own.at[0],
            True,
        )
    ]
    for i, k in enumerate((1, 2, 0)):
        pieces.append(
            Gather(
                place, wide, weights, pl.ds(k * UNIT, UNIT), send.at[i + 1], recv.at[i + 1],
                own.at[i + 1], i == 2,
            )
        )
    g_vec, g_k, g_v, g_q = pieces
    own_copy = pltpu.make_async_copy(tokens, near.at[mine], load)
    own_copy.start()
    g_vec.stage(0)
    g_k.stage(0)
    pl.when(me > 0)(lambda: halo(0).start())
    pl.when(me < peers - 1)(lambda: halo(1).start())
    near[pl.ds(2 * RIM + rows, near.shape[0] - rows - 2 * RIM), :] = jnp.zeros(
        (near.shape[0] - rows - 2 * RIM, width), BF
    )

    @pl.when(me == 0)
    def _():
        near[pl.ds(0, RIM), :] = jnp.zeros((RIM, width), BF)

    @pl.when(me == peers - 1)
    def _():
        near[pl.ds(RIM + rows, RIM), :] = jnp.zeros((RIM, width), BF)

    g_vec.stage(1)
    g_k.stage(1)
    g_v.stage(0)
    g_vec.stage(2)
    g_vec.stage(3)
    g_vec.stage(4)
    table = []
    for z in range(4):
        for y in range(2):
            group = [gathered_vec[z, y, x, c].astype(F32) for x in range(2) for c in range(2)]
            table.append(group[0] + group[1] + group[2] + group[3])
            for x in range(2):
                for c in range(2):
                    at = ((z * 2 + y) * 2 + x) * 2 + c
                    bias_out[:, at * 128 : (at + 1) * 128] = group[x * 2 + c][8:9]
    vecs = jnp.concatenate(table, axis=1)
    vecs_out[...] = vecs
    gain, shift = vecs[0:1], vecs[1:2]
    q_bias, v_bias = vecs[2:3], vecs[3:4]

    def norm(first, count):
        part = pl.ds(first, count)
        scaled = row_stats(near[part, :].astype(F32))[0]
        normed[part, :] = (scaled * gain + shift).astype(BF)

    own_copy.wait()
    for row in range(RIM, RIM + rows, 256):
        norm(row, 256)
    g_k.stage(2)
    g_v.stage(1)
    g_q.stage(0)
    g_k.stage(3)
    g_v.stage(2)
    g_q.stage(1)
    g_k.stage(4)

    def full(k):
        return weights[:, :, :, :, :, pl.ds(k * UNIT, UNIT)].reshape(width, UNIT)

    def project(target, k, first, stop, bias, at):
        matrix = full(k)
        for row in range(first, stop, 256):
            size = min(256, stop - row)
            value = dot(normed[pl.ds(row, size), :], matrix)
            value = value if bias is None else value + bias
            target[pl.ds(row - at[0], size), pl.ds(at[1], UNIT)] = value.astype(BF)

    last_row = near.shape[0]
    project(pairs, 1, RIM, RIM + rows, None, (0, 0))
    g_v.stage(3)
    g_q.stage(2)

    @pl.when(me > 0)
    def _():
        halo(0).wait_send()
        halo(1).wait_recv()

    @pl.when(me < peers - 1)
    def _():
        halo(1).wait_send()
        halo(0).wait_recv()

    for row in range(0, RIM, 192):
        norm(row, 192)
    for row in range(RIM + rows, last_row, 176):
        norm(row, 176)
    normed_copy = pltpu.make_async_copy(normed, normed_out, store.at[0])
    normed_copy.start()
    project(pairs, 1, 0, RIM, None, (0, 0))
    project(pairs, 1, RIM + rows, last_row, None, (0, 0))
    k_copy = pltpu.make_async_copy(
        pairs.at[:, pl.ds(0, UNIT)], kv_out.at[:, pl.ds(0, UNIT)], store.at[1]
    )
    k_copy.start()
    g_v.stage(4)
    g_q.stage(3)
    project(pairs, 2, 0, last_row, v_bias, (0, UNIT))
    v_copy = pltpu.make_async_copy(
        pairs.at[:, pl.ds(UNIT, UNIT)], kv_out.at[:, pl.ds(UNIT, UNIT)], store.at[2]
    )
    v_copy.start()
    g_q.stage(4)
    w_copy = pltpu.make_async_copy(weights, w_out, store.at[3])
    w_copy.start()
    project(queries, 0, RIM, RIM + rows, q_bias, (RIM, 0))
    q_copy = pltpu.make_async_copy(queries, q_out, store.at[4])
    q_copy.start()
    for copy in (normed_copy, k_copy, v_copy, w_copy, q_copy):
        copy.wait()


def first(tokens, wide, vec, ext):
    rows, width = tokens.shape
    part = wide.shape[0]
    hbm, vmem = pl.BlockSpec(memory_space=pl.ANY), pl.BlockSpec(memory_space=pltpu.VMEM)
    queries, key_value, normed, w_qkv, vecs, bias = pl.pallas_call(
        functools.partial(first_body, rows),
        in_specs=[hbm] * 3,
        out_specs=[hbm] * 4 + [vmem] * 2,
        out_shape=[
            jax.ShapeDtypeStruct((rows, width), BF),
            jax.ShapeDtypeStruct((ext, 2 * width), BF),
            jax.ShapeDtypeStruct((ext, width), BF),
            jax.ShapeDtypeStruct((4, 2, 2, 2, *wide.shape), BF),
            jax.ShapeDtypeStruct((VEC_ROWS, width), F32),
            jax.ShapeDtypeStruct((1, 32 * 128), F32),
        ],
        scratch_shapes=[
            pltpu.VMEM((ext, width), BF),
            pltpu.VMEM((ext, width), BF),
            pltpu.VMEM((4, 2, 2, 2, *wide.shape), BF),
            pltpu.VMEM((4, 2, 2, 2, *vec.shape), BF),
            pltpu.VMEM((rows, width), BF),
            pltpu.VMEM((ext, 2 * width), BF),
            pltpu.SemaphoreType.DMA((4, GATHER_SEMS)),
            pltpu.SemaphoreType.DMA((4, GATHER_SEMS)),
            pltpu.SemaphoreType.DMA((4,)),
            pltpu.SemaphoreType.DMA((2,)),
            pltpu.SemaphoreType.DMA((2,)),
            pltpu.SemaphoreType.DMA,
            pltpu.SemaphoreType.DMA((5,)),
        ],
        compiler_params=pltpu.CompilerParams(
            collective_id=0, has_side_effects=True, vmem_limit_bytes=56 * 2**20
        ),
        name="first",
    )(tokens, wide, vec)
    return queries, key_value, normed, w_qkv.reshape(width, wide.shape[1]), vecs, bias


ITEMS = 10
BACK_GROUP = 5
GROUP = 5


class Images:
    def __init__(self, n0, rows, ext):
        self.n0, self.n1, self.rows, self.ext = n0, n0 + IMG, rows, ext
        me, peers = lax.axis_index(AXIS), lax.axis_size(AXIS)
        limit = jnp.where(me == peers - 1, RIM + rows, 2 * RIM + rows)
        start0 = jnp.where(me == 0, RIM, n0 - 1)
        start1 = RIM + n0
        start2 = start1 + IMG
        self.spans = (
            (start0, start1),
            (start1, jnp.minimum(start1 + IMG, limit)),
            (start2, jnp.minimum(start2 + IMG, limit)),
        )
        one = lambda flag: jnp.where(flag, 1, 0)
        self.b0, self.b1 = lax.div(n0, QB), lax.div(self.n1, QB)
        self.d0 = one(self.b0 * QB != n0)
        self.d1 = one((self.n1 < rows) & (self.b1 * QB != self.n1))
        self.third = self.n1 < rows
        self.end0 = lax.div(n0 - 1, QB)
        self.end1 = lax.div(self.n1 - 1, QB) + self.d0
        self.one = one

    def base(self, start):
        return jnp.minimum(lax.div(start, 16), (self.ext - WIN) // 16)

    def segment(self, item):
        return self.one(item > self.end0) + self.one(item > self.end1)

    def item(self, item):
        blk = (
            item
            - self.d0 * self.one(item > self.b0)
            - self.d1 * self.one(item > self.b1 + self.d0)
        )
        used = blk < self.rows // QB
        blk = jnp.minimum(blk, self.rows // QB - 1)
        seg = self.segment(item)
        choose = lambda i: jnp.where(
            seg == 0, self.spans[0][i], jnp.where(seg == 1, self.spans[1][i], self.spans[2][i])
        )
        start, stop = choose(0), choose(1)
        base = self.base(start) * 16
        row0 = blk * QB
        low = jnp.maximum(start - RIM - row0, 0)
        high = jnp.where(used, jnp.minimum(stop - RIM - row0, QB), 0)
        return blk, row0, base, start - base, stop - base, low, high

    def of_block(self, blk):
        at0 = self.d0 * self.one(blk == self.b0)
        at1 = self.d1 * self.one(blk == self.b1)
        first = blk + self.d0 * self.one(blk > self.b0) + self.d1 * self.one(blk > self.b1)
        split = jnp.where(at0 == 1, self.n0, jnp.where(at1 == 1, self.n1, self.rows)) - blk * QB
        return first, first + at0 + at1, split


def attend_body(n0_ref, q_ref, k_ref, v_ref, out_ref, lse_ref, parts, parts_lse):
    rows = q_ref.shape[0]
    images = Images(n0_ref[0], rows, k_ref.shape[0])

    def scores_of(item):
        _, row0, base, low, high, _, _ = images.item(item)
        queries = stacked(q_ref[pl.ds(row0, QB), :]) * jnp.asarray(0.125, BF)
        scores = dot(k_ref[pl.ds(base, WIN), :], queries, NT)
        return scores + key_mask(low, high), base

    def softmax_of(scores):
        top = jnp.max(scores, axis=0, keepdims=True)
        terms = jnp.exp(scores - top)
        total = jnp.sum(terms, axis=0, keepdims=True)
        return terms.astype(BF), top, total

    @pl.loop(0, ITEMS // GROUP)
    def _(step):
        items = [step * GROUP + g for g in range(GROUP)]
        scored = [scores_of(item) for item in items]
        soft = [softmax_of(scores) for scores, _ in scored]
        mixed = [
            dot(v_ref[pl.ds(base, WIN), :], terms, TN) / total
            for (_, base), (terms, _, total) in zip(scored, soft)
        ]
        for item, value, (_, top, total) in zip(items, mixed, soft):
            parts[item] = unstacked(value)
            parts_lse[item] = jnp.broadcast_to(top + jnp.log(total), parts_lse.shape[1:])

    for blk in range(rows // QB):
        first, last, split = images.of_block(blk)
        row = lax.broadcasted_iota(jnp.int32, (QB, 2 * HDIM), 0)
        out_ref[pl.ds(blk * QB, QB), :] = jnp.where(
            row < split, parts[first], parts[last]
        ).astype(BF)
        lane = lax.broadcasted_iota(jnp.int32, parts_lse.shape[1:], 1) % QB
        lse_ref[0, pl.ds(blk, 1), :] = jnp.where(
            lane < split, parts_lse[first], parts_lse[last]
        )[:1]


def attend_kernel(n0_ref, q_ref, k_ref, v_ref, out_ref, lse_ref, parts, parts_lse):
    attend_body(n0_ref, q_ref, k_ref, v_ref, out_ref, lse_ref, parts, parts_lse)


def attend_gather_kernel(
    n0_ref, q_ref, k_ref, v_ref, w_out, w_up, out_ref, lse_ref, full_out, full_up,
    parts, parts_lse, send, recv, own,
):
    tick = pl.program_id(0)
    place = Place()
    pl.when(tick == 0)(lambda: greet(place.partners))
    pieces = []
    for shard, full in ((w_out, full_out), (w_up, full_up)):
        for k in range(shard.shape[1] // UNIT):
            i = len(pieces)
            pieces.append(
                Gather(
                    place, shard, full, pl.ds(k * UNIT, UNIT), send.at[i], recv.at[i], own.at[i]
                )
            )
    run_stages(pieces, tick, range(8))
    attend_body(n0_ref, q_ref, k_ref, v_ref, out_ref, lse_ref, parts, parts_lse)

    @pl.when(tick == 7)
    def _():
        pieces[-1].stage(4)


def attend(n0, queries, key_value, shards=None):
    rows, width = queries.shape
    pairs = width // (2 * HDIM)
    ext = key_value.shape[0]
    hbm = pl.BlockSpec(memory_space=pl.ANY)
    in_specs = [
        pl.BlockSpec(memory_space=pltpu.SMEM),
        pl.BlockSpec((rows, 2 * HDIM), lambda p: (0, p)),
        pl.BlockSpec((ext, 2 * HDIM), lambda p: (0, p)),
        pl.BlockSpec((ext, 2 * HDIM), lambda p: (0, pairs + p)),
    ]
    out_specs = [
        pl.BlockSpec((rows, 2 * HDIM), lambda p: (0, p)),
        pl.BlockSpec((1, rows // QB, 2 * QB), lambda p: (p, 0, 0)),
    ]
    out_shape = [
        jax.ShapeDtypeStruct((rows, width), BF),
        jax.ShapeDtypeStruct((pairs, rows // QB, 2 * QB), F32),
    ]
    scratch = [
        pltpu.VMEM((ITEMS, QB, 2 * HDIM), F32),
        pltpu.VMEM((ITEMS, 8, 2 * QB), F32),
    ]
    params = dict(vmem_limit_bytes=48 * 2**20)
    args = [n0, queries, key_value, key_value]
    kernel = attend_kernel
    if shards is not None:
        kernel = attend_gather_kernel
        in_specs += [hbm] * 2
        out_specs += [hbm] * 2
        out_shape += [jax.ShapeDtypeStruct((4, 2, 2, 2, *v.shape), BF) for v in shards]
        count = sum(v.shape[1] // UNIT for v in shards)
        scratch += [
            pltpu.SemaphoreType.DMA((count, GATHER_SEMS)),
            pltpu.SemaphoreType.DMA((count, GATHER_SEMS)),
            pltpu.SemaphoreType.DMA((count,)),
        ]
        params |= dict(collective_id=1, has_side_effects=True)
        args += shards
    return pl.pallas_call(
        kernel,
        grid=(pairs,),
        in_specs=in_specs,
        out_specs=out_specs,
        out_shape=out_shape,
        scratch_shapes=scratch,
        compiler_params=pltpu.CompilerParams(**params),
        name="attend",
    )(*args)


def attend_back_body(
    pair, n0_ref, q_ref, k_ref, v_ref, up_ref, lse_ref, wk_ref, wv_ref, dq_ref, dk_ref, dv_ref,
    dn_ref, slots, parts, total,
):
    rows = q_ref.shape[0]
    images = Images(n0_ref[0], rows, k_ref.shape[0])

    @pl.when(pair == 0)
    def _():
        slots[0] = jnp.zeros(slots.shape[1:], F32)
        total[...] = jnp.zeros(total.shape, F32)

    lane = lax.broadcasted_iota(jnp.int32, (1, 2 * QB), 1) % QB

    def begin(item):
        blk, row0, base, low, high, first, stop = images.item(item)
        queries = stacked(q_ref[pl.ds(row0, QB), :]) * jnp.asarray(0.125, BF)
        upstream = stacked(up_ref[pl.ds(row0, QB), :])
        here = (lane >= first) & (lane < stop)
        lse = jnp.where(here, lse_ref[0, pl.ds(blk, 1), :], -NEG)
        scores = dot(k_ref[pl.ds(base, WIN), :], queries, NT)
        dprobs = dot(v_ref[pl.ds(base, WIN), :], upstream, NT)
        return base, queries, upstream, scores + key_mask(low, high), lse, dprobs

    def middle(scores, lse, dprobs):
        probs = jnp.exp(scores - lse)
        row_dot = jnp.sum(probs * dprobs, axis=0, keepdims=True)
        return probs.astype(BF), (probs * (dprobs - row_dot)).astype(BF)

    def finish(item, base, queries, upstream, probs, dscores):
        keep = (item > 0) & (images.segment(item) == images.segment(item - 1))
        old = jnp.where(keep, slots[item], jnp.zeros(slots.shape[1:], F32))
        slots[item + 1, :, : 2 * HDIM] = old[:, : 2 * HDIM] + dot(dscores, queries)
        slots[item + 1, :, 2 * HDIM :] = old[:, 2 * HDIM :] + dot(probs, upstream)
        parts[item] = unstacked(dot(k_ref[pl.ds(base, WIN), :], dscores, TN)) * 0.125

    @pl.loop(0, ITEMS // BACK_GROUP)
    def _(step):
        items = [step * BACK_GROUP + g for g in range(BACK_GROUP)]
        begun = [begin(items[0])]
        done = []
        for g in range(BACK_GROUP + 1):
            if g + 1 < BACK_GROUP:
                begun.append(begin(items[g + 1]))
            if g < BACK_GROUP:
                done.append(middle(*begun[g][3:]))
            if g > 0:
                finish(items[g - 1], *begun[g - 1][:3], *done[g - 1])

    for blk in range(rows // QB):
        first, last, split = images.of_block(blk)
        row = lax.broadcasted_iota(jnp.int32, (QB, 2 * HDIM), 0)
        dq_ref[pl.ds(blk * QB, QB), :] = jnp.where(
            row < split, parts[first], parts[last]
        ).astype(BF)
    ends = (
        images.end0 + 1,
        jnp.minimum(images.end1, (rows - 1) // QB + images.d0) + 1,
        jnp.where(images.third, ITEMS, 0),
    )
    weights = jnp.concatenate([wk_ref[...], wv_ref[...]], axis=1)
    for seg, end in enumerate(ends):
        both = slots[end].astype(BF)
        dk_ref[seg] = both[:, : 2 * HDIM]
        dv_ref[seg] = both[:, 2 * HDIM :]
        total[seg] += dot(both, weights, NT)

    @pl.when(pair == pl.num_programs(0) - 1)
    def _():
        dn_ref[...] = total[...].astype(BF)


def attend_back_kernel(*refs):
    attend_back_body(pl.program_id(0), *refs)


def attend_back_scatter_kernel(*refs):
    base, (g_out, g_up), rest = refs[:8], refs[8:10], refs[10:]
    outs, (r_out, r_up), scratch = rest[:4], rest[4:6], rest[6:]
    mine, comm = scratch[:3], scratch[3:]
    pair = pl.program_id(0)
    place = Place()
    pl.when(pair == 0)(lambda: greet(place.partners))
    pieces = []
    for grad, out in ((g_out, r_out), (g_up, r_up)):
        for k in range(grad.shape[5] // UNIT):
            cols = pl.ds(k * UNIT, UNIT)
            bufs = comm[len(pieces) * 8 : len(pieces) * 8 + 8]
            pieces.append(
                Scatter(
                    place, grad.at[:, :, :, :, :, cols], *bufs[:5], out.at[:, cols], bufs[5:]
                )
            )
    run_stages(pieces, pair, range(8))
    attend_back_body(pair, *base, *outs, *mine)

    @pl.when(pair == pl.num_programs(0) - 1)
    def _():
        pieces[-1].stage(4)


def attend_back(n0, queries, key_value, upstream, lse, w_qkv, grads=None):
    rows, width = queries.shape
    pairs = width // (2 * HDIM)
    ext = key_value.shape[0]
    hbm, vmem = pl.BlockSpec(memory_space=pl.ANY), pl.BlockSpec(memory_space=pltpu.VMEM)
    own = pl.BlockSpec((rows, 2 * HDIM), lambda p: (0, p))
    windows = pl.BlockSpec((3, WIN, 2 * HDIM), lambda p: (0, 0, p))
    in_specs = [
        pl.BlockSpec(memory_space=pltpu.SMEM),
        own,
        pl.BlockSpec((ext, 2 * HDIM), lambda p: (0, p)),
        pl.BlockSpec((ext, 2 * HDIM), lambda p: (0, pairs + p)),
        own,
        pl.BlockSpec((1, rows // QB, 2 * QB), lambda p: (p, 0, 0)),
        pl.BlockSpec((width, 2 * HDIM), lambda p: (0, pairs + p)),
        pl.BlockSpec((width, 2 * HDIM), lambda p: (0, 2 * pairs + p)),
    ]
    out_specs = [own, windows, windows, pl.BlockSpec((3, WIN, width), lambda p: (0, 0, 0))]
    out_shape = [jax.ShapeDtypeStruct((rows, width), BF)]
    out_shape += [jax.ShapeDtypeStruct((3, WIN, width), BF)] * 3
    scratch = [
        pltpu.VMEM((ITEMS + 1, WIN, 4 * HDIM), F32),
        pltpu.VMEM((ITEMS, QB, 2 * HDIM), F32),
        pltpu.VMEM((3, WIN, width), F32),
    ]
    args = [n0, queries, key_value, key_value, upstream, lse, w_qkv, w_qkv]
    kernel, params = attend_back_kernel, dict(vmem_limit_bytes=58 * 2**20)
    if grads is not None:
        kernel = attend_back_scatter_kernel
        params |= dict(collective_id=2, has_side_effects=True)
        args += map(blocks, grads)
        in_specs += [hbm] * 2
        out_specs += [vmem] * 2
        out_shape += [jax.ShapeDtypeStruct((v.shape[0] // 32, v.shape[1]), F32) for v in grads]
        for v in grads:
            scratch += scatter_scratch(v.shape[0] // 32, UNIT) * (v.shape[1] // UNIT)
    return pl.pallas_call(
        kernel,
        grid=(pairs,),
        in_specs=in_specs,
        out_specs=out_specs,
        out_shape=out_shape,
        scratch_shapes=scratch,
        compiler_params=pltpu.CompilerParams(**params),
        name="attend_back",
    )(*args)


ROW_TILE = 256
FF_TILE = 512
ROOT_HALF = 1.0 / math.sqrt(2.0)
PDF_SCALE = 1.0 / math.sqrt(2.0 * math.pi)


def row_stats(value):
    mean = jnp.mean(value, axis=1, keepdims=True)
    center = value - mean
    inv_std = lax.rsqrt(jnp.mean(center * center, axis=1, keepdims=True) + EPS)
    return center * inv_std, inv_std


def mlp_up_body(
    step, row_steps, mixed, tokens, w_out, vecs, w_up, up_bias, cot, resid, normed, act, slope,
    g_down, held,
):
    @pl.when(step < row_steps)
    def _():
        value = tokens[...].astype(F32) + dot(mixed[...], w_out[...]) + vecs[0:1]
        resid[...] = value
        low = (row_stats(value)[0] * vecs[1:2] + vecs[2:3]).astype(BF)
        normed[...] = low
        held[pl.ds(step * ROW_TILE, ROW_TILE), :] = low

    @pl.when(step >= row_steps)
    def _():
        rows = held.shape[0]

        for row in range(0, rows, ROW_TILE):
            part = pl.ds(row, ROW_TILE)
            upward = dot(held[part, :], w_up[...]) + up_bias[...]
            cdf = 0.5 * (1.0 + lax.erf(upward * ROOT_HALF))
            pdf = jnp.exp(-0.5 * upward * upward) * PDF_SCALE
            act[part, :] = (upward * cdf).astype(BF)
            slope[part, :] = (cdf + upward * pdf).astype(BF)
        g_down[...] = dot(act[...], cot[...], TN).astype(BF)


def mlp_up_kernel(row_steps, *refs):
    mlp_up_body(pl.program_id(0), row_steps, *refs)


def mlp_up_gather_kernel(row_steps, *refs):
    ins, shard, outs, full = refs[:7], refs[7], refs[8:13], refs[13]
    held, send, recv, own = refs[14:]
    step = pl.program_id(0)
    place = Place()
    pl.when(step == 0)(lambda: greet(place.partners))
    cols = shard.shape[1] // 4
    pieces = [
        Gather(place, shard, full, pl.ds(k * cols, cols), send.at[k], recv.at[k], own.at[k])
        for k in range(4)
    ]
    run_stages(pieces, step, (0, 2, 4, 5, 7, 9, 11))
    mlp_up_body(step, row_steps, *ins, *outs, held)

    @pl.when(step == pl.num_programs(0) - 1)
    def _():
        pieces[3].stage(4)


def mlp_up(mixed, tokens, w_out, vecs, w_up, up_bias, cot, shard=None):
    rows, width = tokens.shape
    hidden = w_up.shape[1]
    row_steps, ff_steps = rows // ROW_TILE, hidden // FF_TILE
    at_row = lambda s: (jnp.minimum(s, row_steps - 1), 0)
    at_col = lambda s: (0, jnp.maximum(s - row_steps, 0))
    at_ff = lambda s: (jnp.maximum(s - row_steps, 0), 0)
    const = lambda s: (0, 0)
    hbm = pl.BlockSpec(memory_space=pl.ANY)
    tall = pl.BlockSpec((rows, FF_TILE), at_col)
    in_specs = [
        pl.BlockSpec((ROW_TILE, width), at_row),
        pl.BlockSpec((ROW_TILE, width), at_row),
        pl.BlockSpec((width, width), const),
        pl.BlockSpec((8, width), const),
        pl.BlockSpec((width, FF_TILE), at_col),
        pl.BlockSpec((1, FF_TILE), at_col),
        pl.BlockSpec((rows, width), const),
    ]
    out_specs = [
        pl.BlockSpec((ROW_TILE, width), at_row),
        pl.BlockSpec((ROW_TILE, width), at_row),
        tall,
        tall,
        pl.BlockSpec((FF_TILE, width), at_ff),
    ]
    out_shape = [
        jax.ShapeDtypeStruct((rows, width), F32),
        jax.ShapeDtypeStruct((rows, width), BF),
        jax.ShapeDtypeStruct((rows, hidden), BF),
        jax.ShapeDtypeStruct((rows, hidden), BF),
        jax.ShapeDtypeStruct((hidden, width), BF),
    ]
    scratch = [pltpu.VMEM((rows, width), BF)]
    params = dict(vmem_limit_bytes=58 * 2**20)
    args = [mixed, tokens, w_out, vecs, w_up, up_bias, cot]
    kernel = mlp_up_kernel
    if shard is not None:
        kernel = mlp_up_gather_kernel
        in_specs += [hbm]
        out_specs += [hbm]
        out_shape += [jax.ShapeDtypeStruct((4, 2, 2, 2, *shard.shape), BF)]
        scratch += [
            pltpu.SemaphoreType.DMA((4, GATHER_SEMS)),
            pltpu.SemaphoreType.DMA((4, GATHER_SEMS)),
            pltpu.SemaphoreType.DMA((4,)),
        ]
        params |= dict(collective_id=5, has_side_effects=True)
        args += [shard]
    return pl.pallas_call(
        functools.partial(kernel, row_steps),
        grid=(row_steps + ff_steps,),
        in_specs=in_specs,
        out_specs=out_specs,
        out_shape=out_shape,
        scratch_shapes=scratch,
        compiler_params=pltpu.CompilerParams(**params),
        name="mlp_up",
    )(*args)


def mlp_back_body(
    step, ff_steps, act, slope, w_up, w_down, cot, normed, resid, mixed, w_out, vecs,
    g_up, up_sums, layer_out, dresid, dmixed, g_out, sums, total, dnormed, branches, dup,
):
    rows, width = cot.shape

    @pl.when(step == 0)
    def _():
        total[...] = jnp.zeros(total.shape, F32)
        dnormed[...] = jnp.zeros(dnormed.shape, F32)
        sums[...] = jnp.zeros(sums.shape, F32)

    @pl.when(step < ff_steps)
    def _():
        count = jnp.zeros(up_sums.shape, F32)
        for row in range(0, rows, ROW_TILE):
            part = pl.ds(row, ROW_TILE)
            total[part, :] += dot(act[part, :], w_down[...])
            dact = dot(cot[part, :], w_down[...], NT)
            low = (dact * slope[part, :].astype(F32)).astype(BF)
            dup[part, :] = low
            count += jnp.sum(low.astype(F32), axis=0, keepdims=True)
            dnormed[part, :] += dot(low, w_up[...], NT)
        up_sums[...] = count
        g_up[...] = dot(normed[...], dup[...], TN).astype(BF)

    @pl.when(step >= ff_steps)
    def _():
        part = pl.ds((step - ff_steps) * ROW_TILE, ROW_TILE)
        value = resid[...]
        scaled, inv_std = row_stats(value)
        upstream = dnormed[part, :]
        above = cot[part, :].astype(F32)
        through = upstream * vecs[1:2]
        inner = (
            through
            - jnp.mean(through, axis=1, keepdims=True)
            - scaled * jnp.mean(through * scaled, axis=1, keepdims=True)
        )
        grad = above + inv_std * inner
        dresid[...] = grad
        low = grad.astype(BF)
        branches[part, :] = low
        dmixed[...] = dot(low, w_out[...], NT).astype(BF)
        layer_out[...] = (value + total[part, :] + vecs[3:4]).astype(BF)
        sums[0:1] += jnp.sum(low.astype(F32), axis=0, keepdims=True)
        sums[1:2] += jnp.sum(upstream * scaled, axis=0, keepdims=True)
        sums[2:3] += jnp.sum(upstream, axis=0, keepdims=True)
        sums[3:4] += jnp.sum(above, axis=0, keepdims=True)

    @pl.when(step == pl.num_programs(0) - 1)
    def _():
        g_out[...] = dot(mixed[...], branches[...], TN).astype(BF)


def mlp_back_kernel(ff_steps, *refs):
    mlp_back_body(pl.program_id(0), ff_steps, *refs)


def mlp_back_scatter_kernel(ff_steps, *refs):
    ins, grad, outs, reduced, scratch, comm = (
        refs[:10], refs[10], refs[11:18], refs[18], refs[19:23], refs[23:],
    )
    step = pl.program_id(0)
    place = Place()
    pl.when(step == 0)(lambda: greet(place.partners))
    cols = reduced.shape[1] // 4
    pieces = []
    for k in range(4):
        here = pl.ds(k * cols, cols)
        bufs = comm[k * 8 : k * 8 + 8]
        pieces.append(
            Scatter(
                place, grad.at[:, :, :, :, :, here], *bufs[:5], reduced.at[:, here], bufs[5:]
            )
        )
    run_stages(pieces, step, (0, 1, 2, 4, 5, 7, 9))
    mlp_back_body(step, ff_steps, *ins, *outs, *scratch)

    @pl.when(step == pl.num_programs(0) - 1)
    def _():
        pieces[3].stage(4)


def mlp_back(act, slope, w_up, w_down, cot, normed, resid, mixed, w_out, vecs, grad=None):
    rows, width = cot.shape
    hidden = w_up.shape[1]
    row_steps, ff_steps = rows // ROW_TILE, hidden // FF_TILE
    at_row = lambda s: (jnp.maximum(s - ff_steps, 0), 0)
    at_col = lambda s: (0, jnp.minimum(s, ff_steps - 1))
    at_ff = lambda s: (jnp.minimum(s, ff_steps - 1), 0)
    const = lambda s: (0, 0)
    hbm, vmem = pl.BlockSpec(memory_space=pl.ANY), pl.BlockSpec(memory_space=pltpu.VMEM)
    once = lambda *shape: pl.BlockSpec(shape, const, pipeline_mode=pl.Buffered(1))
    tall = pl.BlockSpec((rows, FF_TILE), at_col)
    tile = pl.BlockSpec((ROW_TILE, width), at_row)
    in_specs = [
        tall, tall, pl.BlockSpec((width, FF_TILE), at_col), pl.BlockSpec((FF_TILE, width), at_ff),
        once(rows, width), once(rows, width), tile, once(rows, width), once(width, width),
        once(8, width),
    ]
    out_specs = [
        pl.BlockSpec((width, FF_TILE), at_col), pl.BlockSpec((1, FF_TILE), at_col), tile, tile,
        tile, once(width, width), once(8, width),
    ]
    out_shape = [
        jax.ShapeDtypeStruct((width, hidden), BF),
        jax.ShapeDtypeStruct((1, hidden), F32),
        jax.ShapeDtypeStruct((rows, width), BF),
        jax.ShapeDtypeStruct((rows, width), F32),
        jax.ShapeDtypeStruct((rows, width), BF),
        jax.ShapeDtypeStruct((width, width), BF),
        jax.ShapeDtypeStruct((8, width), F32),
    ]
    scratch = [
        pltpu.VMEM((rows, width), F32),
        pltpu.VMEM((rows, width), F32),
        pltpu.VMEM((rows, width), BF),
        pltpu.VMEM((rows, FF_TILE), BF),
    ]
    params = dict(vmem_limit_bytes=60 * 2**20)
    args = [act, slope, w_up, w_down, cot, normed, resid, mixed, w_out, vecs]
    kernel = mlp_back_kernel
    if grad is not None:
        kernel = mlp_back_scatter_kernel
        part = grad.shape[0] // 32
        in_specs += [hbm]
        out_specs += [vmem]
        out_shape += [jax.ShapeDtypeStruct((part, width), F32)]
        scratch += scatter_scratch(part, width // 4) * 4
        params |= dict(collective_id=6, has_side_effects=True)
        args += [blocks(grad)]
    return pl.pallas_call(
        functools.partial(kernel, ff_steps),
        grid=(row_steps + ff_steps,),
        in_specs=in_specs,
        out_specs=out_specs,
        out_shape=out_shape,
        scratch_shapes=scratch,
        compiler_params=pltpu.CompilerParams(**params),
        name="mlp_back",
    )(*args)


TILE = 64


class Total:
    def __init__(self, place, value, arrived, send, recv):
        p = place
        self.rounds = [p.zp, [p.xp, p.yp, p.far], [p.sib]]
        self.value, self.arrived, self.send, self.recv = value, arrived, send, recv

    def run(self):
        slot = 0
        for i, targets in enumerate(self.rounds):
            copies = [
                mesh_copy(
                    self.value.at[i], self.arrived.at[slot + k], self.send.at[slot + k],
                    self.recv.at[slot + k], to,
                )
                for k, to in enumerate(targets)
            ]
            for copy in copies:
                copy.start()
            total = self.value[i]
            for k, copy in enumerate(copies):
                copy.wait()
                total = total + self.arrived[slot + k]
            self.value[i + 1] = total
            slot += len(targets)


def last_body(
    step, n0_ref, normed, dq, dk, dv, dn, w_q, tokens, dresid, vecs, sums, up_sums, out, grads,
    padded, outgoing, incoming, send, recv, vector_out,
):
    rows = dq.shape[0]
    ext, width = normed.shape
    images = Images(n0_ref[0], rows, ext)
    bases = [images.base(span[0]) for span in images.spans]
    me, peers = lax.axis_index(AXIS), lax.axis_size(AXIS)
    wide = slice(TILE, TILE + WIN)

    def halo(way):
        return mesh_copy(
            outgoing if way else dn.at[0], incoming.at[way], send.at[way], recv.at[way],
            me + 1 if way else me - 1,
        )

    def column_sums(value):
        return jnp.sum(value.astype(F32), axis=0, keepdims=True)

    @pl.when(step == 0)
    def _():
        outgoing[...] = jnp.where(images.third, dn[2], dn[1])
        pl.when(me > 0)(lambda: halo(0).start())
        pl.when(me < peers - 1)(lambda: halo(1).start())
        vector_out[...] = jnp.zeros(vector_out.shape, F32)
        vector_out[4:8] = sums[0:4]
        for k in range(up_sums.shape[1] // width):
            vector_out[8 + k : 9 + k] = up_sums[:, k * width : (k + 1) * width]
        vector_out[2:3] = column_sums(dq[...])
        padded[...] = jnp.zeros(padded.shape, F32)

        @pl.when(me == 0)
        def _():
            incoming[1] = jnp.zeros(incoming.shape[1:], BF)

        @pl.when(me == peers - 1)
        def _():
            incoming[0] = jnp.zeros(incoming.shape[1:], BF)

        for col in range(0, width, ROW_TILE):
            cols = pl.ds(col, ROW_TILE)
            grads[0, cols, :] = dot(normed[pl.ds(RIM, rows), cols], dq[...], TN).astype(BF)

    for which, part in ((1, dk), (2, dv)):
        @pl.when(step == which)
        def _():
            for col in range(0, width, ROW_TILE):
                cols = pl.ds(col, ROW_TILE)
                total = None
                for seg, base in enumerate(bases):
                    term = dot(normed[pl.ds(base * 16, WIN), cols], part[seg], TN)
                    total = term if total is None else total + term
                grads[which, cols, :] = total.astype(BF)
            if which == 2:
                vector_out[3:4] = (
                    column_sums(dv[0]) + column_sums(dv[1]) + column_sums(dv[2])
                )

    @pl.when(step == 5)
    def _():
        @pl.when(me > 0)
        def _():
            halo(0).wait_send()
            halo(1).wait_recv()

        @pl.when(me < peers - 1)
        def _():
            halo(1).wait_send()
            halo(0).wait_recv()

        none = jnp.zeros((WIN, width), F32)
        stop = jnp.where(images.third, images.spans[2][1], images.spans[1][1])
        cut = (stop > RIM + rows) & (me < peers - 1)
        after = jnp.where(cut, incoming[0].astype(F32), none)
        before = jnp.where(images.spans[0][0] < RIM, incoming[1].astype(F32), none)
        padded[0, wide] = dn[0].astype(F32) + before
        padded[1, wide] = dn[1].astype(F32) + jnp.where(images.third, none, after)
        padded[2, wide] = dn[2].astype(F32) + jnp.where(images.third, after, none)

    @pl.when(step >= 5)
    def _():
        first = (step - 5) * ROW_TILE
        upstream = dot(dq[pl.ds(first, ROW_TILE), :], w_q[...], NT)
        places = []
        for k in range(ROW_TILE // TILE):
            total = upstream[k * TILE : (k + 1) * TILE]
            for seg, base in enumerate(bases):
                off = jnp.maximum(
                    (RIM + TILE) // 16 + (step - 5) * (ROW_TILE // 16) + k * (TILE // 16) - base, 0
                )
                off = jnp.minimum(off, (WIN + TILE) // 16) * 16
                total = total + padded[seg, pl.ds(off, TILE), :]
            places.append(total)
        upstream = jnp.concatenate(places, axis=0)
        scaled, inv_std = row_stats(tokens[...].astype(F32))
        through = upstream * vecs[0:1]
        inner = (
            through
            - jnp.mean(through, axis=1, keepdims=True)
            - scaled * jnp.mean(through * scaled, axis=1, keepdims=True)
        )
        out[...] = dresid[...] + inv_std * inner
        vector_out[0:1] += jnp.sum(upstream * scaled, axis=0, keepdims=True)
        vector_out[1:2] += jnp.sum(upstream, axis=0, keepdims=True)


LAST_STEPS = 9


def last_kernel(*refs):
    step = pl.program_id(0)
    me, peers = lax.axis_index(AXIS), lax.axis_size(AXIS)
    ins, (out, vector_out, grads_out), scratch = refs[:12], refs[12:15], refs[15:]
    grads, padded, outgoing, incoming, send, recv = scratch
    pl.when(step == 0)(lambda: greet([], me > 0, me < peers - 1))
    last_body(step, *ins, out, grads, padded, outgoing, incoming, send, recv, vector_out)

    @pl.when(step == LAST_STEPS - 1)
    def _():
        grads_out[...] = grads[...]


def last_scatter_kernel(*refs):
    step = pl.program_id(0)
    me, peers = lax.axis_index(AXIS), lax.axis_size(AXIS)
    ins, (out, vector_out, reduced), scratch = refs[:12], refs[12:15], refs[15:]
    grads, padded, outgoing, incoming, send, recv = scratch[:6]
    vectors, arrived, vec_send, vec_recv = scratch[6:10]
    comm = scratch[10:]
    place = Place()
    pl.when(step == 0)(
        lambda: greet([*place.partners, place.far], me > 0, me < peers - 1)
    )
    pieces = [
        Scatter(
            place, grads.at[k], *comm[k * 8 : k * 8 + 5], reduced.at[:, pl.ds(k * UNIT, UNIT)],
            comm[k * 8 + 5 : k * 8 + 8], True,
        )
        for k in range(3)
    ]
    run_stages(pieces, step, (1, 2, 3, 4, 5, 6))
    last_body(
        step, *ins, out, Flat(grads), padded, outgoing, incoming, send, recv, vectors.at[0]
    )

    @pl.when(step == LAST_STEPS - 1)
    def _():
        Total(place, vectors, arrived, vec_send, vec_recv).run()
        vector_out[...] = vectors[3]
        pieces[2].stage(4)


class Flat:
    def __init__(self, ref):
        self.ref = ref

    def __setitem__(self, index, value):
        k, rows, _ = index
        part = self.ref.shape[5]
        count = rows.size // part
        first = rows.start // part
        for i in range(0, count, 8):
            block = value[i * part : (i + 8) * part].reshape(2, 2, 2, part, value.shape[1])
            self.ref[k, (first + i) // 8] = block


def last(n0, normed, dq, dk, dv, dn, w_qkv, tokens, dresid, vecs, sums, up_sums, plan):
    rows, width = dq.shape
    ext = normed.shape[0]
    peers = lax.axis_size(AXIS)
    const = lambda s: (0, 0)
    once = lambda *shape: pl.BlockSpec(
        shape, lambda s: (0,) * len(shape), pipeline_mode=pl.Buffered(1)
    )
    tile = pl.BlockSpec((ROW_TILE, width), lambda s: (jnp.maximum(s - 5, 0), 0))
    vmem = pl.BlockSpec(memory_space=pltpu.VMEM)
    in_specs = [
        pl.BlockSpec(memory_space=pltpu.SMEM),
        once(ext, width), once(rows, width), once(3, WIN, width), once(3, WIN, width),
        once(3, WIN, width), once(width, width), tile, tile, once(8, width), once(8, width),
        once(*up_sums.shape),
    ]
    vector_rows = 16
    shared = [
        pltpu.VMEM((3, WIN + 2 * TILE, width), F32),
        pltpu.VMEM((WIN, width), BF),
        pltpu.VMEM((2, WIN, width), BF),
        pltpu.SemaphoreType.DMA((2,)),
        pltpu.SemaphoreType.DMA((2,)),
    ]
    if plan:
        part = width // peers
        kernel, collective = last_scatter_kernel, 3
        scratch = [pltpu.VMEM((3, 4, 2, 2, 2, part, width), BF)] + shared + [
            pltpu.VMEM((4, vector_rows, width), F32),
            pltpu.VMEM((7, vector_rows, width), F32),
            pltpu.SemaphoreType.DMA((7,)),
            pltpu.SemaphoreType.DMA((7,)),
        ] + scatter_scratch(part, UNIT, tilt=True) * 3
        third_out = jax.ShapeDtypeStruct((part, 3 * width), F32)
    else:
        kernel, collective = last_kernel, 4
        scratch = [pltpu.VMEM((3, width, width), BF)] + shared
        third_out = jax.ShapeDtypeStruct((3, width, width), BF)
    return pl.pallas_call(
        kernel,
        grid=(LAST_STEPS,),
        in_specs=in_specs,
        out_specs=[tile, once(vector_rows, width), once(*third_out.shape)],
        out_shape=[
            jax.ShapeDtypeStruct((rows, width), F32),
            jax.ShapeDtypeStruct((vector_rows, width), F32),
            third_out,
        ],
        scratch_shapes=scratch,
        compiler_params=pltpu.CompilerParams(
            vmem_limit_bytes=61 * 2**20, collective_id=collective, has_side_effects=True
        ),
        name="last",
    )(n0, normed, dq, dk, dv, dn, w_qkv, tokens, dresid, vecs, sums, up_sums)


def shifted(value, by):
    peers = lax.axis_size(AXIS)
    pairs = [(i, i + by) for i in range(peers) if 0 <= i + by < peers]
    return lax.ppermute(value, AXIS, pairs)


def gathered(value):
    return lax.all_gather(value, AXIS, axis=0, tiled=True)


def scattered(value):
    return lax.psum_scatter(value, AXIS, scatter_dimension=0, tiled=True)


def local(
    tokens,
    image_ids,
    cotangent,
    norm1_gain,
    norm1_shift,
    qkv_weight,
    query_bias,
    value_bias,
    out_weight,
    out_bias,
    norm2_gain,
    norm2_shift,
    up_weight,
    up_bias,
    down_weight,
    down_bias,
):
    rows, width = tokens.shape
    me = lax.axis_index(AXIS)
    peers = lax.axis_size(AXIS)
    n0 = jnp.sum((image_ids == image_ids[0]).astype(jnp.int32)).reshape(1)
    ext = -(-(rows + 2 * RIM + 64) // 128) * 128
    vectors = [
        norm1_gain, norm1_shift, query_bias, value_bias, out_bias, norm2_gain, norm2_shift,
        down_bias,
    ]
    part = norm1_gain.shape[0]
    block_plan = peers == 32
    if block_plan:
        lane = lax.broadcasted_iota(jnp.int32, (1, 128), 1) // part
        spread = jnp.tile(jnp.stack(vectors), (1, 128 // part))
        spread = jnp.where(lane == me % (128 // part), spread, jnp.zeros_like(spread))
        vec = jnp.concatenate(
            [spread, up_bias[None], jnp.zeros((VEC_ROWS - 9, 128), BF)], axis=0
        )
        queries, key_value, normed_ext, w_qkv, vectors, u_bias = first(
            tokens, qkv_weight, vec, ext
        )
        u_bias = u_bias[0]
        gain1 = vectors[0]
        vecs = vectors[4:8]
    else:
        gathered_vec = gathered(jnp.concatenate([*vectors, up_bias])[None]).astype(F32)
        gain1, shift1, q_bias, v_bias, o_bias, gain2, shift2, d_bias = (
            gathered_vec[:, i * part : (i + 1) * part].reshape(-1) for i in range(8)
        )
        u_bias = gathered_vec[:, 8 * part :].reshape(-1)
        vecs = jnp.stack([o_bias, gain2, shift2, d_bias])
        w_qkv, w_out, w_up, w_down = map(
            gathered, (qkv_weight, out_weight, up_weight, down_weight)
        )
        low_rim = shifted(tokens[rows - RIM :], 1)
        high_rim = shifted(tokens[:RIM], -1)
        pad = jnp.zeros((ext - rows - 2 * RIM, width), BF)
        tokens_ext = jnp.concatenate([low_rim, tokens, high_rim, pad], axis=0).astype(F32)
        normed_ext = (row_stats(tokens_ext)[0] * gain1 + shift1).astype(BF)
        normed_low = normed_ext[RIM : RIM + rows]
        queries = (dot(normed_low, w_qkv[:, :width]) + q_bias).astype(BF)
        key_value = (
            dot(normed_ext, w_qkv[:, width:])
            + jnp.concatenate([jnp.zeros_like(v_bias), v_bias])
        ).astype(BF)
    vecs = jnp.concatenate([vecs, jnp.zeros((4, width), F32)])
    if block_plan:
        mixed_low, lse, w_out, w_up = attend(
            n0, queries, key_value, (out_weight, up_weight)
        )
        w_out, w_up = w_out.reshape(width, -1), w_up.reshape(width, -1)
    else:
        mixed_low, lse = attend(n0, queries, key_value)

    args = (mixed_low, tokens, w_out, vecs, w_up, u_bias[None], cotangent)
    if block_plan:
        resid, normed_two, act, slope, grad_down, w_down = mlp_up(*args, down_weight)
        w_down = w_down.reshape(-1, width)
    else:
        resid, normed_two, act, slope, grad_down = mlp_up(*args)
    args = (act, slope, w_up, w_down, cotangent, normed_two, resid, mixed_low, w_out, vecs)
    if block_plan:
        grad_up, up_sums, layer_out, dresid, dmixed_low, grad_out, sums, r_down = mlp_back(
            *args, grad_down
        )
    else:
        grad_up, up_sums, layer_out, dresid, dmixed_low, grad_out, sums = mlp_back(*args)
        r_down = scattered(grad_down).astype(F32)
    if block_plan:
        dquery, dkey, dvalue, dnormed, r_out, r_up = attend_back(
            n0, queries, key_value, dmixed_low, lse, w_qkv, (grad_out, grad_up)
        )
    else:
        dquery, dkey, dvalue, dnormed = attend_back(
            n0, queries, key_value, dmixed_low, lse, w_qkv
        )
        r_out, r_up = (scattered(v).astype(F32) for v in (grad_out, grad_up))
    vecs = jnp.concatenate([gain1[None], jnp.zeros((7, width), F32)])
    grad_tokens, totals, r_qkv = last(
        n0, normed_ext, dquery, dkey, dvalue, dnormed, w_qkv, tokens, dresid, vecs, sums,
        up_sums, block_plan,
    )
    if not block_plan:
        totals = lax.psum(totals, AXIS)
        r_qkv = jnp.concatenate([scattered(v) for v in r_qkv], axis=1).astype(F32)
    owned = lax.dynamic_slice_in_dim(totals[:8], me * part, part, 1)
    size = u_bias.shape[0] // peers
    up_own = lax.dynamic_slice_in_dim(totals[8 : 8 + u_bias.shape[0] // width].reshape(-1), me * size, size)
    g = [owned[i] for i in range(8)] + [up_own]
    return (
        layer_out, grad_tokens, g[0], g[1], r_qkv, g[2], g[3], r_out, g[4], g[5], g[6], r_up,
        g[8], r_down, g[7],
    )


def solution(mesh):
    row, vec = P(AXIS, None), P(AXIS)
    return jax.shard_map(
        local,
        mesh=mesh,
        in_specs=(
            row, vec, row, vec, vec, row, vec, vec, row, vec, vec, vec, row, vec, row, vec,
        ),
        out_specs=(
            row, row, vec, vec, row, vec, vec, row, vec, vec, vec, row, vec, row, vec,
        ),
        check_vma=False,
    )
```

```python
import functools
import math

import jax
import jax.numpy as jnp
from jax import lax
from jax.experimental import pallas as pl
from jax.experimental.pallas import tpu as pltpu
from jax.sharding import PartitionSpec as P

HDIM = 64
IMG = 577
RIM = IMG - 1
WIN = 592
QB = 128
EPS = 1e-06
NEG = -1e30
AXIS = "fsdp"
BF = jnp.bfloat16
F32 = jnp.float32
NT = (((1,), (1,)), ((), ()))
TN = (((0,), (0,)), ((), ()))
NN = (((1,), (0,)), ((), ()))


def dot(a, b, dims=NN):
    return lax.dot_general(a, b, dims, preferred_element_type=F32)


def stacked(block):
    lane = lax.broadcasted_iota(jnp.int32, block.shape, 1)
    zero = jnp.zeros_like(block)
    return jnp.concatenate(
        [jnp.where(lane < HDIM, block, zero), jnp.where(lane >= HDIM, block, zero)], axis=0
    )


def unstacked(wide):
    return jnp.concatenate([wide[:HDIM, :QB], wide[HDIM:, QB:]], axis=0).T


def key_mask(low, high):
    row = lax.broadcasted_iota(jnp.int32, (WIN, QB), 0)
    bias = jnp.where((row >= low) & (row < high), 0.0, NEG)
    return jnp.concatenate([bias, bias], axis=1)


def mesh_copy(src, dst, send_sem, recv_sem, to):
    return pltpu.make_async_remote_copy(
        src_ref=src,
        dst_ref=dst,
        send_sem=send_sem,
        recv_sem=recv_sem,
        device_id=(to,),
        device_id_type=pl.DeviceIdType.MESH,
    )


class Place:
    def __init__(self):
        me = lax.axis_index(AXIS)
        self.c, self.x, self.y, self.z = me % 2, me // 2 % 2, me // 4 % 2, me // 8
        self.sib = self.at(self.z, self.y, self.x, 1 - self.c)
        self.xp = self.at(self.z, self.y, 1 - self.x, self.c)
        self.yp = self.at(self.z, 1 - self.y, self.x, self.c)
        self.zp = [self.at((self.z + k) % 4, self.y, self.x, self.c) for k in (1, 2, 3)]
        self.far = self.at(self.z, 1 - self.y, 1 - self.x, self.c)
        self.partners = [self.sib, self.xp, self.yp, *self.zp]

    @staticmethod
    def at(z, y, x, c):
        return ((z * 2 + y) * 2 + x) * 2 + c


def greet(partners, before=None, after=None):
    barrier = pltpu.get_barrier_semaphore()

    def hello(to):
        pl.semaphore_signal(
            barrier, inc=1, device_id=(to,), device_id_type=pl.DeviceIdType.MESH
        )

    for to in partners:
        hello(to)
    if before is None:
        pl.semaphore_wait(barrier, len(partners))
        return
    me = lax.axis_index(AXIS)
    pl.when(before)(lambda: hello(me - 1))
    pl.when(after)(lambda: hello(me + 1))
    pl.semaphore_wait(
        barrier, len(partners) + before.astype(jnp.int32) + after.astype(jnp.int32)
    )


class Gather:
    def __init__(self, place, shard, full, cols, send, recv, own, tilt=False):
        self.shard, self.own = shard.at[:, cols], own
        p, rows = place, shard.shape[0]
        half = rows // 2

        def block(y, x, part=slice(None)):
            return full.at[:, y, x, p.c, part, cols]

        mine = full.at[p.z, p.y, p.x, p.c, :, cols]
        self.local = lambda: pltpu.make_async_copy(self.shard, mine, own)

        def copy(i, src, dst, to):
            return lambda: mesh_copy(src, dst, send.at[i], recv.at[i], to)

        same = lambda i, ref, to: copy(i, ref, ref, to)
        first, second = pl.ds(0, half), pl.ds(half, half)
        self.z = [copy(i, self.shard, mine, to) for i, to in enumerate(p.zp)]
        self.xy = [same(3, block(p.y, p.x), p.xp), same(4, block(p.y, p.x), p.yp)]
        self.far = [
            same(5, block(p.y, 1 - p.x, first), p.yp),
            same(6, block(1 - p.y, p.x, second), p.xp),
        ]
        if tilt:
            self.far = [same(5, block(p.y, 1 - p.x), p.yp)]
        self.pair = [
            same(7, block(p.y, p.x), p.sib),
            same(8, block(p.y, 1 - p.x), p.sib),
            same(9, block(1 - p.y, p.x), p.sib),
            same(10, block(1 - p.y, 1 - p.x), p.sib),
        ]

    def stage(self, number):
        if number == 0:
            self.local().start()
            for c in self.z:
                c().start()
        elif number == 1:
            self.local().wait()
            for c in self.z:
                c().wait()
            for c in (*self.xy, self.pair[0]):
                c().start()
        elif number == 2:
            for c in self.xy:
                c().wait()
            for c in (*self.far, self.pair[1], self.pair[2]):
                c().start()
        elif number == 3:
            for c in self.far:
                c().wait()
            self.pair[3]().start()
        else:
            for c in self.pair:
                c().wait()


GATHER_SEMS = 11


def run_stages(pieces, step, steps):
    for at in sorted(set(steps)):
        todo = [
            (q, piece)
            for tick, when in enumerate(steps)
            if when == at
            for k, piece in enumerate(pieces)
            for q in (4, 3, 2, 1, 0)
            if k + q == tick
        ][::-1]

        @pl.when(step == at)
        def _():
            for q, piece in todo:
                piece.stage(q)


def run_rest(pieces, ticks):
    for tick in range(ticks, len(pieces) + 4):
        for q in range(5):
            if 0 <= tick - q < len(pieces):
                pieces[tick - q].stage(q)


class Scatter:
    def __init__(self, place, grad, held, from_pair, far, side, line, out, sems, tilt=False):
        self.tilt = tilt
        self.p, self.out = place, out
        self.held, self.from_pair, self.far, self.side, self.line = held, from_pair, far, side, line
        p, rows = place, held.shape[3]
        self.half = rows // 2
        own, send, recv = sems
        first, second = pl.ds(0, self.half), pl.ds(self.half, self.half)

        def copy(i, src, dst, to):
            return lambda: mesh_copy(src, dst, send.at[i], recv.at[i], to)

        self.load = lambda: pltpu.make_async_copy(grad.at[:, :, :, p.c], held, own)
        self.to_pair = copy(0, grad.at[:, :, :, 1 - p.c], from_pair, p.sib)
        self.to_far = [
            copy(1, held.at[:, 1 - p.y, 1 - p.x, first], far.at[0], p.xp),
            copy(2, held.at[:, 1 - p.y, 1 - p.x, second], far.at[1], p.yp),
        ]
        if tilt:
            self.to_far = [copy(1, held.at[:, 1 - p.y, 1 - p.x], far, p.yp)]
        self.to_side = [
            copy(3, held.at[:, p.y, 1 - p.x], side.at[0], p.xp),
            copy(4, held.at[:, 1 - p.y, p.x], side.at[1], p.yp),
        ]
        self.to_line = [
            copy(5 + k, held.at[(p.z + k + 1) % 4, p.y, p.x], line.at[k], to)
            for k, to in enumerate(p.zp)
        ]

    def stage(self, number):
        p, half = self.p, self.half
        held, far, side, line = self.held, self.far, self.side, self.line
        if number == 0:
            self.load().start()
            self.to_pair().start()
        elif number == 1:
            self.load().wait()
            self.to_pair().wait()

            @pl.loop(0, 4)
            def _(z):
                for y in range(2):
                    for x in range(2):
                        held[z, y, x] = (
                            held[z, y, x].astype(F32) + self.from_pair[z, y, x].astype(F32)
                        ).astype(held.dtype)

            for c in self.to_far:
                c().start()
        elif number == 2:
            for c in self.to_far:
                c().wait()

            @pl.loop(0, 4)
            def _(z):
                if self.tilt:
                    held[z, p.y, 1 - p.x] = (
                        held[z, p.y, 1 - p.x].astype(F32) + far[z].astype(F32)
                    ).astype(held.dtype)
                    return
                held[z, 1 - p.y, p.x, :half] = (
                    held[z, 1 - p.y, p.x, :half].astype(F32) + far[0, z].astype(F32)
                ).astype(held.dtype)
                held[z, p.y, 1 - p.x, half:] = (
                    held[z, p.y, 1 - p.x, half:].astype(F32) + far[1, z].astype(F32)
                ).astype(held.dtype)

            for c in self.to_side:
                c().start()
        elif number == 3:
            for c in self.to_side:
                c().wait()

            @pl.loop(0, 4)
            def _(z):
                held[z, p.y, p.x] = (
                    held[z, p.y, p.x].astype(F32)
                    + side[0, z].astype(F32)
                    + side[1, z].astype(F32)
                ).astype(held.dtype)

            for c in self.to_line:
                c().start()
        else:
            for c in self.to_line:
                c().wait()
            self.out[...] = (
                held[p.z, p.y, p.x].astype(F32)
                + line[0].astype(F32)
                + line[1].astype(F32)
                + line[2].astype(F32)
            )


SCATTER_SEMS = 8
UNIT = 1024


def scatter_scratch(rows, cols, dtype=BF, tilt=False):
    return [
        pltpu.VMEM((4, 2, 2, rows, cols), dtype),
        pltpu.VMEM((4, 2, 2, rows, cols), dtype),
        pltpu.VMEM((4, rows, cols) if tilt else (2, 4, rows // 2, cols), dtype),
        pltpu.VMEM((2, 4, rows, cols), dtype),
        pltpu.VMEM((3, rows, cols), dtype),
        pltpu.SemaphoreType.DMA,
        pltpu.SemaphoreType.DMA((SCATTER_SEMS,)),
        pltpu.SemaphoreType.DMA((SCATTER_SEMS,)),
    ]


def blocks(value):
    return value.reshape(4, 2, 2, 2, value.shape[0] // 32, value.shape[1])


VEC_ROWS = 16


def first_body(
    rows, tokens, wide, vec, ids, q_out, kv_out, normed_out, scaled_out, w_out, vecs_out,
    bias_out, n0_out, near, normed, scaled, weights, gathered_vec, queries, pairs, send, recv,
    own, halo_send, halo_recv, load, store,
):
    place = Place()
    me, peers = lax.axis_index(AXIS), lax.axis_size(AXIS)
    greet(place.partners, me > 0, me < peers - 1)
    width = near.shape[1]
    mine = pl.ds(RIM, rows)

    def halo(way):
        if way == 0:
            src, dst, to = tokens.at[pl.ds(0, RIM)], near.at[pl.ds(RIM + rows, RIM)], me - 1
        else:
            src, dst, to = tokens.at[pl.ds(rows - RIM, RIM)], near.at[pl.ds(0, RIM)], me + 1
        return mesh_copy(src, dst, halo_send.at[way], halo_recv.at[way], to)

    pieces = [
        Gather(
            place, vec, gathered_vec, pl.ds(0, vec.shape[1]), send.at[0], recv.at[0], own.at[0],
            True,
        )
    ]
    for i, k in enumerate((1, 2, 0)):
        pieces.append(
            Gather(
                place, wide, weights, pl.ds(k * UNIT, UNIT), send.at[i + 1], recv.at[i + 1],
                own.at[i + 1], i == 2,
            )
        )
    g_vec, g_k, g_v, g_q = pieces
    own_copy = pltpu.make_async_copy(tokens, near.at[mine], load)
    own_copy.start()
    g_vec.stage(0)
    g_k.stage(0)
    pl.when(me > 0)(lambda: halo(0).start())
    pl.when(me < peers - 1)(lambda: halo(1).start())
    n0_out[0] = jnp.sum((ids[...] == ids[0:1, 0:1]).astype(jnp.int32))
    near[pl.ds(2 * RIM + rows, near.shape[0] - rows - 2 * RIM), :] = jnp.zeros(
        (near.shape[0] - rows - 2 * RIM, width), BF
    )

    @pl.when(me == 0)
    def _():
        near[pl.ds(0, RIM), :] = jnp.zeros((RIM, width), BF)

    @pl.when(me == peers - 1)
    def _():
        near[pl.ds(RIM + rows, RIM), :] = jnp.zeros((RIM, width), BF)

    g_vec.stage(1)
    g_k.stage(1)
    g_v.stage(0)
    g_vec.stage(2)
    g_vec.stage(3)
    g_vec.stage(4)
    table = []
    for z in range(4):
        for y in range(2):
            group = [gathered_vec[z, y, x, c].astype(F32) for x in range(2) for c in range(2)]
            table.append(group[0] + group[1] + group[2] + group[3])
            for x in range(2):
                for c in range(2):
                    at = ((z * 2 + y) * 2 + x) * 2 + c
                    bias_out[:, at * 128 : (at + 1) * 128] = group[x * 2 + c][8:9]
    vecs = jnp.concatenate(table, axis=1)
    vecs_out[...] = vecs
    gain, shift = vecs[0:1], vecs[1:2]
    q_bias, v_bias = vecs[2:3], vecs[3:4]

    def norm(first, count):
        part = pl.ds(first, count)
        value = row_stats(near[part, :].astype(F32))[0]
        scaled[part, :] = value.astype(BF)
        normed[part, :] = (value * gain + shift).astype(BF)

    own_copy.wait()
    for row in range(RIM, RIM + rows, 256):
        norm(row, 256)
    g_k.stage(2)
    g_v.stage(1)
    g_q.stage(0)
    g_k.stage(3)
    g_v.stage(2)
    g_q.stage(1)
    g_k.stage(4)

    def full(k):
        return weights[:, :, :, :, :, pl.ds(k * UNIT, UNIT)].reshape(width, UNIT)

    def project(target, k, first, stop, bias, at):
        matrix = full(k)
        for row in range(first, stop, 256):
            size = min(256, stop - row)
            value = dot(normed[pl.ds(row, size), :], matrix)
            value = value if bias is None else value + bias
            target[pl.ds(row - at[0], size), pl.ds(at[1], UNIT)] = value.astype(BF)

    last_row = near.shape[0]
    project(pairs, 1, RIM, RIM + rows, None, (0, 0))
    g_v.stage(3)
    g_q.stage(2)

    @pl.when(me > 0)
    def _():
        halo(0).wait_send()
        halo(1).wait_recv()

    @pl.when(me < peers - 1)
    def _():
        halo(1).wait_send()
        halo(0).wait_recv()

    for row in range(0, RIM, 192):
        norm(row, 192)
    for row in range(RIM + rows, last_row, 176):
        norm(row, 176)
    normed_copy = pltpu.make_async_copy(normed, normed_out, store.at[0])
    normed_copy.start()
    scaled_copy = pltpu.make_async_copy(scaled, scaled_out, store.at[5])
    scaled_copy.start()
    project(pairs, 1, 0, RIM, None, (0, 0))
    project(pairs, 1, RIM + rows, last_row, None, (0, 0))
    k_copy = pltpu.make_async_copy(
        pairs.at[:, pl.ds(0, UNIT)], kv_out.at[:, pl.ds(0, UNIT)], store.at[1]
    )
    k_copy.start()
    g_v.stage(4)
    g_q.stage(3)
    project(pairs, 2, 0, last_row, v_bias, (0, UNIT))
    v_copy = pltpu.make_async_copy(
        pairs.at[:, pl.ds(UNIT, UNIT)], kv_out.at[:, pl.ds(UNIT, UNIT)], store.at[2]
    )
    v_copy.start()
    g_q.stage(4)
    w_copy = pltpu.make_async_copy(weights, w_out, store.at[3])
    w_copy.start()
    project(queries, 0, RIM, RIM + rows, q_bias, (RIM, 0))
    q_copy = pltpu.make_async_copy(queries, q_out, store.at[4])
    q_copy.start()
    for copy in (normed_copy, scaled_copy, k_copy, v_copy, w_copy, q_copy):
        copy.wait()


def first(tokens, wide, vec, ids, ext):
    rows, width = tokens.shape
    part = wide.shape[0]
    hbm, vmem = pl.BlockSpec(memory_space=pl.ANY), pl.BlockSpec(memory_space=pltpu.VMEM)
    queries, key_value, normed, scaled, w_qkv, vecs, bias, n0 = pl.pallas_call(
        functools.partial(first_body, rows),
        in_specs=[hbm] * 3 + [vmem],
        out_specs=[hbm] * 5 + [vmem] * 2 + [pl.BlockSpec(memory_space=pltpu.SMEM)],
        out_shape=[
            jax.ShapeDtypeStruct((rows, width), BF),
            jax.ShapeDtypeStruct((ext, 2 * width), BF),
            jax.ShapeDtypeStruct((ext, width), BF),
            jax.ShapeDtypeStruct((ext, width), BF),
            jax.ShapeDtypeStruct((4, 2, 2, 2, *wide.shape), BF),
            jax.ShapeDtypeStruct((VEC_ROWS, width), F32),
            jax.ShapeDtypeStruct((1, 32 * 128), F32),
            jax.ShapeDtypeStruct((1,), jnp.int32),
        ],
        scratch_shapes=[
            pltpu.VMEM((ext, width), BF),
            pltpu.VMEM((ext, width), BF),
            pltpu.VMEM((ext, width), BF),
            pltpu.VMEM((4, 2, 2, 2, *wide.shape), BF),
            pltpu.VMEM((4, 2, 2, 2, *vec.shape), BF),
            pltpu.VMEM((rows, width), BF),
            pltpu.VMEM((ext, 2 * width), BF),
            pltpu.SemaphoreType.DMA((4, GATHER_SEMS)),
            pltpu.SemaphoreType.DMA((4, GATHER_SEMS)),
            pltpu.SemaphoreType.DMA((4,)),
            pltpu.SemaphoreType.DMA((2,)),
            pltpu.SemaphoreType.DMA((2,)),
            pltpu.SemaphoreType.DMA,
            pltpu.SemaphoreType.DMA((6,)),
        ],
        compiler_params=pltpu.CompilerParams(
            collective_id=0, has_side_effects=True, vmem_limit_bytes=56 * 2**20
        ),
        name="first",
    )(tokens, wide, vec, ids)
    w_qkv = w_qkv.reshape(width, wide.shape[1])
    return queries, key_value, normed, scaled, w_qkv, vecs, bias, n0


ITEMS = 10
BACK_GROUP = 5
GROUP = 5


class Images:
    def __init__(self, n0, rows, ext):
        self.n0, self.n1, self.rows, self.ext = n0, n0 + IMG, rows, ext
        me, peers = lax.axis_index(AXIS), lax.axis_size(AXIS)
        limit = jnp.where(me == peers - 1, RIM + rows, 2 * RIM + rows)
        start0 = jnp.where(me == 0, RIM, n0 - 1)
        start1 = RIM + n0
        start2 = start1 + IMG
        self.spans = (
            (start0, start1),
            (start1, jnp.minimum(start1 + IMG, limit)),
            (start2, jnp.minimum(start2 + IMG, limit)),
        )
        one = lambda flag: jnp.where(flag, 1, 0)
        self.b0, self.b1 = lax.div(n0, QB), lax.div(self.n1, QB)
        self.d0 = one(self.b0 * QB != n0)
        self.d1 = one((self.n1 < rows) & (self.b1 * QB != self.n1))
        self.third = self.n1 < rows
        self.end0 = lax.div(n0 - 1, QB)
        self.end1 = lax.div(self.n1 - 1, QB) + self.d0
        self.one = one

    def base(self, start):
        return jnp.minimum(lax.div(start, 16), (self.ext - WIN) // 16)

    def segment(self, item):
        return self.one(item > self.end0) + self.one(item > self.end1)

    def item(self, item):
        blk = (
            item
            - self.d0 * self.one(item > self.b0)
            - self.d1 * self.one(item > self.b1 + self.d0)
        )
        used = blk < self.rows // QB
        blk = jnp.minimum(blk, self.rows // QB - 1)
        seg = self.segment(item)
        choose = lambda i: jnp.where(
            seg == 0, self.spans[0][i], jnp.where(seg == 1, self.spans[1][i], self.spans[2][i])
        )
        start, stop = choose(0), choose(1)
        base = self.base(start) * 16
        row0 = blk * QB
        low = jnp.maximum(start - RIM - row0, 0)
        high = jnp.where(used, jnp.minimum(stop - RIM - row0, QB), 0)
        return blk, row0, base, start - base, stop - base, low, high

    def of_block(self, blk):
        at0 = self.d0 * self.one(blk == self.b0)
        at1 = self.d1 * self.one(blk == self.b1)
        first = blk + self.d0 * self.one(blk > self.b0) + self.d1 * self.one(blk > self.b1)
        split = jnp.where(at0 == 1, self.n0, jnp.where(at1 == 1, self.n1, self.rows)) - blk * QB
        return first, first + at0 + at1, split


def attend_body(n0_ref, q_ref, k_ref, v_ref, out_ref, lse_ref, parts, parts_lse):
    rows = q_ref.shape[0]
    images = Images(n0_ref[0], rows, k_ref.shape[0])

    def scores_of(item):
        _, row0, base, low, high, _, _ = images.item(item)
        queries = stacked(q_ref[pl.ds(row0, QB), :]) * jnp.asarray(0.125, BF)
        scores = dot(k_ref[pl.ds(base, WIN), :], queries, NT)
        return scores + key_mask(low, high), base

    def softmax_of(scores):
        top = jnp.max(scores, axis=0, keepdims=True)
        terms = jnp.exp(scores - top)
        total = jnp.sum(terms, axis=0, keepdims=True)
        return terms.astype(BF), top, total

    @pl.loop(0, ITEMS // GROUP)
    def _(step):
        items = [step * GROUP + g for g in range(GROUP)]
        scored = [scores_of(item) for item in items]
        soft = [softmax_of(scores) for scores, _ in scored]
        mixed = [
            dot(v_ref[pl.ds(base, WIN), :], terms, TN) / total
            for (_, base), (terms, _, total) in zip(scored, soft)
        ]
        for item, value, (_, top, total) in zip(items, mixed, soft):
            parts[item] = unstacked(value)
            parts_lse[item] = jnp.broadcast_to(top + jnp.log(total), parts_lse.shape[1:])

    for blk in range(rows // QB):
        first, last, split = images.of_block(blk)
        row = lax.broadcasted_iota(jnp.int32, (QB, 2 * HDIM), 0)
        out_ref[pl.ds(blk * QB, QB), :] = jnp.where(
            row < split, parts[first], parts[last]
        ).astype(BF)
        lane = lax.broadcasted_iota(jnp.int32, parts_lse.shape[1:], 1) % QB
        lse_ref[0, pl.ds(blk, 1), :] = jnp.where(
            lane < split, parts_lse[first], parts_lse[last]
        )[:1]


def attend_kernel(n0_ref, q_ref, k_ref, v_ref, out_ref, lse_ref, parts, parts_lse):
    attend_body(n0_ref, q_ref, k_ref, v_ref, out_ref, lse_ref, parts, parts_lse)


def attend_gather_kernel(
    n0_ref, q_ref, k_ref, v_ref, w_out, w_up, out_ref, lse_ref, full_out, full_up,
    parts, parts_lse, send, recv, own,
):
    tick = pl.program_id(0)
    place = Place()
    pl.when(tick == 0)(lambda: greet(place.partners))
    pieces = []
    for shard, full in ((w_out, full_out), (w_up, full_up)):
        for k in range(shard.shape[1] // UNIT):
            i = len(pieces)
            pieces.append(
                Gather(
                    place, shard, full, pl.ds(k * UNIT, UNIT), send.at[i], recv.at[i], own.at[i]
                )
            )
    run_stages(pieces, tick, range(8))
    attend_body(n0_ref, q_ref, k_ref, v_ref, out_ref, lse_ref, parts, parts_lse)

    @pl.when(tick == 7)
    def _():
        pieces[-1].stage(4)


def attend(n0, queries, key_value, shards=None):
    rows, width = queries.shape
    pairs = width // (2 * HDIM)
    ext = key_value.shape[0]
    hbm = pl.BlockSpec(memory_space=pl.ANY)
    in_specs = [
        pl.BlockSpec(memory_space=pltpu.SMEM),
        pl.BlockSpec((rows, 2 * HDIM), lambda p: (0, p)),
        pl.BlockSpec((ext, 2 * HDIM), lambda p: (0, p)),
        pl.BlockSpec((ext, 2 * HDIM), lambda p: (0, pairs + p)),
    ]
    out_specs = [
        pl.BlockSpec((rows, 2 * HDIM), lambda p: (0, p)),
        pl.BlockSpec((1, rows // QB, 2 * QB), lambda p: (p, 0, 0)),
    ]
    out_shape = [
        jax.ShapeDtypeStruct((rows, width), BF),
        jax.ShapeDtypeStruct((pairs, rows // QB, 2 * QB), F32),
    ]
    scratch = [
        pltpu.VMEM((ITEMS, QB, 2 * HDIM), F32),
        pltpu.VMEM((ITEMS, 8, 2 * QB), F32),
    ]
    params = dict(vmem_limit_bytes=48 * 2**20)
    args = [n0, queries, key_value, key_value]
    kernel = attend_kernel
    if shards is not None:
        kernel = attend_gather_kernel
        in_specs += [hbm] * 2
        out_specs += [hbm] * 2
        out_shape += [jax.ShapeDtypeStruct((4, 2, 2, 2, *v.shape), BF) for v in shards]
        count = sum(v.shape[1] // UNIT for v in shards)
        scratch += [
            pltpu.SemaphoreType.DMA((count, GATHER_SEMS)),
            pltpu.SemaphoreType.DMA((count, GATHER_SEMS)),
            pltpu.SemaphoreType.DMA((count,)),
        ]
        params |= dict(collective_id=1, has_side_effects=True)
        args += shards
    return pl.pallas_call(
        kernel,
        grid=(pairs,),
        in_specs=in_specs,
        out_specs=out_specs,
        out_shape=out_shape,
        scratch_shapes=scratch,
        compiler_params=pltpu.CompilerParams(**params),
        name="attend",
    )(*args)


def attend_back_body(
    pair, n0_ref, q_ref, k_ref, v_ref, up_ref, lse_ref, wk_ref, wv_ref, scaled_ref, dq_ref, dk_ref, dv_ref,
    dn_ref, sums_ref, slots, parts, total,
):
    rows = q_ref.shape[0]
    images = Images(n0_ref[0], rows, k_ref.shape[0])

    @pl.when(pair == 0)
    def _():
        slots[0] = jnp.zeros(slots.shape[1:], F32)
        total[...] = jnp.zeros(total.shape, F32)

    lane = lax.broadcasted_iota(jnp.int32, (1, 2 * QB), 1) % QB

    def begin(item):
        blk, row0, base, low, high, first, stop = images.item(item)
        queries = stacked(q_ref[pl.ds(row0, QB), :]) * jnp.asarray(0.125, BF)
        upstream = stacked(up_ref[pl.ds(row0, QB), :])
        here = (lane >= first) & (lane < stop)
        lse = jnp.where(here, lse_ref[0, pl.ds(blk, 1), :], -NEG)
        scores = dot(k_ref[pl.ds(base, WIN), :], queries, NT)
        dprobs = dot(v_ref[pl.ds(base, WIN), :], upstream, NT)
        return base, queries, upstream, scores + key_mask(low, high), lse, dprobs

    def middle(scores, lse, dprobs):
        probs = jnp.exp(scores - lse)
        row_dot = jnp.sum(probs * dprobs, axis=0, keepdims=True)
        return probs.astype(BF), (probs * (dprobs - row_dot)).astype(BF)

    def finish(item, base, queries, upstream, probs, dscores):
        keep = (item > 0) & (images.segment(item) == images.segment(item - 1))
        old = jnp.where(keep, slots[item], jnp.zeros(slots.shape[1:], F32))
        slots[item + 1, :, : 2 * HDIM] = old[:, : 2 * HDIM] + dot(dscores, queries)
        slots[item + 1, :, 2 * HDIM :] = old[:, 2 * HDIM :] + dot(probs, upstream)
        parts[item] = unstacked(dot(k_ref[pl.ds(base, WIN), :], dscores, TN)) * 0.125

    @pl.loop(0, ITEMS // BACK_GROUP)
    def _(step):
        items = [step * BACK_GROUP + g for g in range(BACK_GROUP)]
        begun = [begin(items[0])]
        done = []
        for g in range(BACK_GROUP + 1):
            if g + 1 < BACK_GROUP:
                begun.append(begin(items[g + 1]))
            if g < BACK_GROUP:
                done.append(middle(*begun[g][3:]))
            if g > 0:
                finish(items[g - 1], *begun[g - 1][:3], *done[g - 1])

    for blk in range(rows // QB):
        first, last, split = images.of_block(blk)
        row = lax.broadcasted_iota(jnp.int32, (QB, 2 * HDIM), 0)
        dq_ref[pl.ds(blk * QB, QB), :] = jnp.where(
            row < split, parts[first], parts[last]
        ).astype(BF)
    ends = (
        images.end0 + 1,
        jnp.minimum(images.end1, (rows - 1) // QB + images.d0) + 1,
        jnp.where(images.third, ITEMS, 0),
    )
    weights = jnp.concatenate([wk_ref[...], wv_ref[...]], axis=1)
    for seg, end in enumerate(ends):
        both = slots[end].astype(BF)
        dk_ref[seg] = both[:, : 2 * HDIM]
        dv_ref[seg] = both[:, 2 * HDIM :]
        total[seg] += dot(both, weights, NT)

    @pl.when(pair == pl.num_programs(0) - 1)
    def _():
        dn_ref[...] = total[...].astype(BF)
        sums_ref[...] = jnp.zeros(sums_ref.shape, F32)
        for seg, span in enumerate(images.spans):
            window = scaled_ref[pl.ds(images.base(span[0]) * 16, WIN), :].astype(F32)
            sums_ref[0:1] += jnp.sum(total[seg] * window, axis=0, keepdims=True)
            sums_ref[1:2] += jnp.sum(total[seg], axis=0, keepdims=True)


def attend_back_kernel(*refs):
    attend_back_body(pl.program_id(0), *refs)


def attend_back_scatter_kernel(*refs):
    base, (g_out, g_up), rest = refs[:9], refs[9:11], refs[11:]
    outs, (r_out, r_up), scratch = rest[:5], rest[5:7], rest[7:]
    mine, comm = scratch[:3], scratch[3:]
    pair = pl.program_id(0)
    place = Place()
    pl.when(pair == 0)(lambda: greet(place.partners))
    pieces = []
    for grad, out in ((g_out, r_out), (g_up, r_up)):
        for k in range(grad.shape[5] // UNIT):
            cols = pl.ds(k * UNIT, UNIT)
            bufs = comm[len(pieces) * 8 : len(pieces) * 8 + 8]
            pieces.append(
                Scatter(
                    place, grad.at[:, :, :, :, :, cols], *bufs[:5], out.at[:, cols], bufs[5:]
                )
            )
    run_stages(pieces, pair, range(8))
    attend_back_body(pair, *base, *outs, *mine)

    @pl.when(pair == pl.num_programs(0) - 1)
    def _():
        pieces[-1].stage(4)


def attend_back(n0, queries, key_value, upstream, lse, w_qkv, scaled, grads=None):
    rows, width = queries.shape
    pairs = width // (2 * HDIM)
    ext = key_value.shape[0]
    hbm, vmem = pl.BlockSpec(memory_space=pl.ANY), pl.BlockSpec(memory_space=pltpu.VMEM)
    own = pl.BlockSpec((rows, 2 * HDIM), lambda p: (0, p))
    windows = pl.BlockSpec((3, WIN, 2 * HDIM), lambda p: (0, 0, p))
    in_specs = [
        pl.BlockSpec(memory_space=pltpu.SMEM),
        own,
        pl.BlockSpec((ext, 2 * HDIM), lambda p: (0, p)),
        pl.BlockSpec((ext, 2 * HDIM), lambda p: (0, pairs + p)),
        own,
        pl.BlockSpec((1, rows // QB, 2 * QB), lambda p: (p, 0, 0)),
        pl.BlockSpec((width, 2 * HDIM), lambda p: (0, pairs + p)),
        pl.BlockSpec((width, 2 * HDIM), lambda p: (0, 2 * pairs + p)),
        pl.BlockSpec((ext, width), lambda p: (0, 0), pipeline_mode=pl.Buffered(1)),
    ]
    out_specs = [
        own, windows, windows,
        pl.BlockSpec((3, WIN, width), lambda p: (0, 0, 0), pipeline_mode=pl.Buffered(1)),
        pl.BlockSpec((8, width), lambda p: (0, 0)),
    ]
    out_shape = [jax.ShapeDtypeStruct((rows, width), BF)]
    out_shape += [jax.ShapeDtypeStruct((3, WIN, width), BF)] * 3
    out_shape += [jax.ShapeDtypeStruct((8, width), F32)]
    scratch = [
        pltpu.VMEM((ITEMS + 1, WIN, 4 * HDIM), F32),
        pltpu.VMEM((ITEMS, QB, 2 * HDIM), F32),
        pltpu.VMEM((3, WIN, width), F32),
    ]
    args = [n0, queries, key_value, key_value, upstream, lse, w_qkv, w_qkv, scaled]
    kernel, params = attend_back_kernel, dict(vmem_limit_bytes=58 * 2**20)
    if grads is not None:
        kernel = attend_back_scatter_kernel
        params |= dict(collective_id=2, has_side_effects=True)
        args += map(blocks, grads)
        in_specs += [hbm] * 2
        out_specs += [vmem] * 2
        out_shape += [jax.ShapeDtypeStruct((v.shape[0] // 32, v.shape[1]), F32) for v in grads]
        for v in grads:
            scratch += scatter_scratch(v.shape[0] // 32, UNIT) * (v.shape[1] // UNIT)
    return pl.pallas_call(
        kernel,
        grid=(pairs,),
        in_specs=in_specs,
        out_specs=out_specs,
        out_shape=out_shape,
        scratch_shapes=scratch,
        compiler_params=pltpu.CompilerParams(**params),
        name="attend_back",
    )(*args)


ROW_TILE = 256
FF_TILE = 512
ROOT_HALF = 1.0 / math.sqrt(2.0)
PDF_SCALE = 1.0 / math.sqrt(2.0 * math.pi)


def row_stats(value):
    mean = jnp.mean(value, axis=1, keepdims=True)
    center = value - mean
    inv_std = lax.rsqrt(jnp.mean(center * center, axis=1, keepdims=True) + EPS)
    return center * inv_std, inv_std


def mlp_up_body(
    step, row_steps, mixed, tokens, w_out, vecs, w_up, up_bias, cot, resid, normed, act, slope,
    g_down, held,
):
    @pl.when(step < row_steps)
    def _():
        value = tokens[...].astype(F32) + dot(mixed[...], w_out[...]) + vecs[0:1]
        resid[...] = value
        low = (row_stats(value)[0] * vecs[1:2] + vecs[2:3]).astype(BF)
        normed[...] = low
        held[pl.ds(step * ROW_TILE, ROW_TILE), :] = low

    @pl.when(step >= row_steps)
    def _():
        rows = held.shape[0]

        for row in range(0, rows, ROW_TILE):
            part = pl.ds(row, ROW_TILE)
            upward = dot(held[part, :], w_up[...]) + up_bias[...]
            cdf = 0.5 * (1.0 + lax.erf(upward * ROOT_HALF))
            pdf = jnp.exp(-0.5 * upward * upward) * PDF_SCALE
            act[part, :] = (upward * cdf).astype(BF)
            slope[part, :] = (cdf + upward * pdf).astype(BF)
        g_down[...] = dot(act[...], cot[...], TN).astype(BF)


def mlp_up_kernel(row_steps, *refs):
    mlp_up_body(pl.program_id(0), row_steps, *refs)


def mlp_up_gather_kernel(row_steps, *refs):
    ins, shard, outs, full = refs[:7], refs[7], refs[8:13], refs[13]
    held, send, recv, own = refs[14:]
    step = pl.program_id(0)
    place = Place()
    pl.when(step == 0)(lambda: greet(place.partners))
    cols = shard.shape[1] // 4
    pieces = [
        Gather(place, shard, full, pl.ds(k * cols, cols), send.at[k], recv.at[k], own.at[k])
        for k in range(4)
    ]
    run_stages(pieces, step, (0, 4, 7, 9, 11))
    mlp_up_body(step, row_steps, *ins, *outs, held)
    pl.when(step == pl.num_programs(0) - 1)(lambda: run_rest(pieces, 5))


def mlp_up(mixed, tokens, w_out, vecs, w_up, up_bias, cot, shard=None):
    rows, width = tokens.shape
    hidden = w_up.shape[1]
    row_steps, ff_steps = rows // ROW_TILE, hidden // FF_TILE
    at_row = lambda s: (jnp.minimum(s, row_steps - 1), 0)
    at_col = lambda s: (0, jnp.maximum(s - row_steps, 0))
    at_ff = lambda s: (jnp.maximum(s - row_steps, 0), 0)
    const = lambda s: (0, 0)
    hbm = pl.BlockSpec(memory_space=pl.ANY)
    tall = pl.BlockSpec((rows, FF_TILE), at_col)
    in_specs = [
        pl.BlockSpec((ROW_TILE, width), at_row),
        pl.BlockSpec((ROW_TILE, width), at_row),
        pl.BlockSpec((width, width), const),
        pl.BlockSpec((8, width), const),
        pl.BlockSpec((width, FF_TILE), at_col),
        pl.BlockSpec((1, FF_TILE), at_col),
        pl.BlockSpec((rows, width), const),
    ]
    out_specs = [
        pl.BlockSpec((ROW_TILE, width), at_row),
        pl.BlockSpec((ROW_TILE, width), at_row),
        tall,
        tall,
        pl.BlockSpec((FF_TILE, width), at_ff),
    ]
    out_shape = [
        jax.ShapeDtypeStruct((rows, width), F32),
        jax.ShapeDtypeStruct((rows, width), BF),
        jax.ShapeDtypeStruct((rows, hidden), BF),
        jax.ShapeDtypeStruct((rows, hidden), BF),
        jax.ShapeDtypeStruct((hidden, width), BF),
    ]
    scratch = [pltpu.VMEM((rows, width), BF)]
    params = dict(vmem_limit_bytes=58 * 2**20)
    args = [mixed, tokens, w_out, vecs, w_up, up_bias, cot]
    kernel = mlp_up_kernel
    if shard is not None:
        kernel = mlp_up_gather_kernel
        in_specs += [hbm]
        out_specs += [hbm]
        out_shape += [jax.ShapeDtypeStruct((4, 2, 2, 2, *shard.shape), BF)]
        scratch += [
            pltpu.SemaphoreType.DMA((4, GATHER_SEMS)),
            pltpu.SemaphoreType.DMA((4, GATHER_SEMS)),
            pltpu.SemaphoreType.DMA((4,)),
        ]
        params |= dict(collective_id=5, has_side_effects=True)
        args += [shard]
    return pl.pallas_call(
        functools.partial(kernel, row_steps),
        grid=(row_steps + ff_steps,),
        in_specs=in_specs,
        out_specs=out_specs,
        out_shape=out_shape,
        scratch_shapes=scratch,
        compiler_params=pltpu.CompilerParams(**params),
        name="mlp_up",
    )(*args)


def mlp_back_body(
    step, ff_steps, act, slope, w_up, w_down, cot, normed, resid, mixed, w_out, vecs,
    g_up, up_sums, layer_out, dresid, dmixed, g_out, sums, total, dnormed, branches, dup,
):
    rows, width = cot.shape

    @pl.when(step == 0)
    def _():
        total[...] = jnp.zeros(total.shape, F32)
        dnormed[...] = jnp.zeros(dnormed.shape, F32)
        sums[...] = jnp.zeros(sums.shape, F32)

    @pl.when(step < ff_steps)
    def _():
        count = jnp.zeros(up_sums.shape, F32)
        for row in range(0, rows, ROW_TILE):
            part = pl.ds(row, ROW_TILE)
            total[part, :] += dot(act[part, :], w_down[...])
            dact = dot(cot[part, :], w_down[...], NT)
            low = (dact * slope[part, :].astype(F32)).astype(BF)
            dup[part, :] = low
            count += jnp.sum(low.astype(F32), axis=0, keepdims=True)
            dnormed[part, :] += dot(low, w_up[...], NT)
        up_sums[...] = count
        g_up[...] = dot(normed[...], dup[...], TN).astype(BF)

    @pl.when(step >= ff_steps)
    def _():
        part = pl.ds((step - ff_steps) * ROW_TILE, ROW_TILE)
        value = resid[...]
        scaled, inv_std = row_stats(value)
        upstream = dnormed[part, :]
        above = cot[part, :].astype(F32)
        through = upstream * vecs[1:2]
        inner = (
            through
            - jnp.mean(through, axis=1, keepdims=True)
            - scaled * jnp.mean(through * scaled, axis=1, keepdims=True)
        )
        grad = above + inv_std * inner
        dresid[...] = grad
        low = grad.astype(BF)
        branches[part, :] = low
        dmixed[...] = dot(low, w_out[...], NT).astype(BF)
        layer_out[...] = (value + total[part, :] + vecs[3:4]).astype(BF)
        sums[0:1] += jnp.sum(low.astype(F32), axis=0, keepdims=True)
        sums[1:2] += jnp.sum(upstream * scaled, axis=0, keepdims=True)
        sums[2:3] += jnp.sum(upstream, axis=0, keepdims=True)
        sums[3:4] += jnp.sum(above, axis=0, keepdims=True)

    @pl.when(step == pl.num_programs(0) - 1)
    def _():
        g_out[...] = dot(mixed[...], branches[...], TN).astype(BF)


def mlp_back_kernel(ff_steps, *refs):
    mlp_back_body(pl.program_id(0), ff_steps, *refs)


def mlp_back_scatter_kernel(ff_steps, *refs):
    ins, grad, outs, reduced, scratch, comm = (
        refs[:10], refs[10], refs[11:18], refs[18], refs[19:23], refs[23:],
    )
    step = pl.program_id(0)
    place = Place()
    pl.when(step == 0)(lambda: greet(place.partners))
    cols = reduced.shape[1] // 4
    pieces = []
    for k in range(4):
        here = pl.ds(k * cols, cols)
        bufs = comm[k * 8 : k * 8 + 8]
        pieces.append(
            Scatter(
                place, grad.at[:, :, :, :, :, here], *bufs[:5], reduced.at[:, here], bufs[5:]
            )
        )
    run_stages(pieces, step, (0, 1, 2, 4, 5, 7, 9))
    mlp_back_body(step, ff_steps, *ins, *outs, *scratch)

    @pl.when(step == pl.num_programs(0) - 1)
    def _():
        pieces[3].stage(4)


def mlp_back(act, slope, w_up, w_down, cot, normed, resid, mixed, w_out, vecs, grad=None):
    rows, width = cot.shape
    hidden = w_up.shape[1]
    row_steps, ff_steps = rows // ROW_TILE, hidden // FF_TILE
    at_row = lambda s: (jnp.maximum(s - ff_steps, 0), 0)
    at_col = lambda s: (0, jnp.minimum(s, ff_steps - 1))
    at_ff = lambda s: (jnp.minimum(s, ff_steps - 1), 0)
    const = lambda s: (0, 0)
    hbm, vmem = pl.BlockSpec(memory_space=pl.ANY), pl.BlockSpec(memory_space=pltpu.VMEM)
    once = lambda *shape: pl.BlockSpec(shape, const, pipeline_mode=pl.Buffered(1))
    tall = pl.BlockSpec((rows, FF_TILE), at_col)
    tile = pl.BlockSpec((ROW_TILE, width), at_row)
    in_specs = [
        tall, tall, pl.BlockSpec((width, FF_TILE), at_col), pl.BlockSpec((FF_TILE, width), at_ff),
        once(rows, width), once(rows, width), tile, once(rows, width), once(width, width),
        once(8, width),
    ]
    out_specs = [
        pl.BlockSpec((width, FF_TILE), at_col), pl.BlockSpec((1, FF_TILE), at_col), tile, tile,
        tile, once(width, width), once(8, width),
    ]
    out_shape = [
        jax.ShapeDtypeStruct((width, hidden), BF),
        jax.ShapeDtypeStruct((1, hidden), F32),
        jax.ShapeDtypeStruct((rows, width), BF),
        jax.ShapeDtypeStruct((rows, width), F32),
        jax.ShapeDtypeStruct((rows, width), BF),
        jax.ShapeDtypeStruct((width, width), BF),
        jax.ShapeDtypeStruct((8, width), F32),
    ]
    scratch = [
        pltpu.VMEM((rows, width), F32),
        pltpu.VMEM((rows, width), F32),
        pltpu.VMEM((rows, width), BF),
        pltpu.VMEM((rows, FF_TILE), BF),
    ]
    params = dict(vmem_limit_bytes=60 * 2**20)
    args = [act, slope, w_up, w_down, cot, normed, resid, mixed, w_out, vecs]
    kernel = mlp_back_kernel
    if grad is not None:
        kernel = mlp_back_scatter_kernel
        part = grad.shape[0] // 32
        in_specs += [hbm]
        out_specs += [vmem]
        out_shape += [jax.ShapeDtypeStruct((part, width), F32)]
        scratch += scatter_scratch(part, width // 4) * 4
        params |= dict(collective_id=6, has_side_effects=True)
        args += [blocks(grad)]
    return pl.pallas_call(
        functools.partial(kernel, ff_steps),
        grid=(row_steps + ff_steps,),
        in_specs=in_specs,
        out_specs=out_specs,
        out_shape=out_shape,
        scratch_shapes=scratch,
        compiler_params=pltpu.CompilerParams(**params),
        name="mlp_back",
    )(*args)


TILE = 64


class Total:
    def __init__(self, place, value, arrived, send, recv):
        p = place
        self.rounds = [p.zp, [p.xp, p.yp, p.far], [p.sib]]
        self.value, self.arrived, self.send, self.recv = value, arrived, send, recv

    def copies(self, i):
        slot = sum(len(targets) for targets in self.rounds[:i])
        return slot, [
            mesh_copy(
                self.value.at[i], self.arrived.at[slot + k], self.send.at[slot + k],
                self.recv.at[slot + k], to,
            )
            for k, to in enumerate(self.rounds[i])
        ]

    def stage(self, number):
        if number > 0:
            slot, copies = self.copies(number - 1)
            total = self.value[number - 1]
            for k, copy in enumerate(copies):
                copy.wait()
                total = total + self.arrived[slot + k]
            self.value[number] = total
        if number < len(self.rounds):
            for copy in self.copies(number)[1]:
                copy.start()


def last_body(
    step, n0_ref, normed, dq, dk, dv, dn, w_q, tokens, dresid, vecs, sums, up_sums, kv_sums,
    out, grads, padded, outgoing, incoming, send, recv, dqw, vector_out,
):
    rows = dq.shape[0]
    ext, width = normed.shape
    images = Images(n0_ref[0], rows, ext)
    bases = [images.base(span[0]) for span in images.spans]
    me, peers = lax.axis_index(AXIS), lax.axis_size(AXIS)
    wide = slice(TILE, TILE + WIN)

    def halo(way):
        return mesh_copy(
            outgoing if way else dn.at[0], incoming.at[way], send.at[way], recv.at[way],
            me + 1 if way else me - 1,
        )

    def column_sums(value):
        return jnp.sum(value.astype(F32), axis=0, keepdims=True)

    @pl.when(step == 0)
    def _():
        outgoing[...] = jnp.where(images.third, dn[2], dn[1])
        pl.when(me > 0)(lambda: halo(0).start())
        pl.when(me < peers - 1)(lambda: halo(1).start())
        vector_out[...] = jnp.zeros(vector_out.shape, F32)
        vector_out[0:2] = kv_sums[0:2]
        vector_out[4:8] = sums[0:4]
        for k in range(up_sums.shape[1] // width):
            vector_out[8 + k : 9 + k] = up_sums[:, k * width : (k + 1) * width]
        vector_out[2:3] = column_sums(dq[...])
        padded[...] = jnp.zeros(padded.shape, BF)

        @pl.when(me == 0)
        def _():
            incoming[1] = jnp.zeros(incoming.shape[1:], BF)

        @pl.when(me == peers - 1)
        def _():
            incoming[0] = jnp.zeros(incoming.shape[1:], BF)

        for col in range(0, width, ROW_TILE):
            cols = pl.ds(col, ROW_TILE)
            grads[0, cols, :] = dot(normed[pl.ds(RIM, rows), cols], dq[...], TN).astype(BF)

    for which, part in ((1, dk), (2, dv)):
        @pl.when(step == which)
        def _():
            for col in range(0, width, ROW_TILE):
                cols = pl.ds(col, ROW_TILE)
                total = None
                for seg, base in enumerate(bases):
                    term = dot(normed[pl.ds(base * 16, WIN), cols], part[seg], TN)
                    total = term if total is None else total + term
                grads[which, cols, :] = total.astype(BF)
            if which == 2:
                vector_out[3:4] = (
                    column_sums(dv[0]) + column_sums(dv[1]) + column_sums(dv[2])
                )

    @pl.when((step >= 3) & (step < 7))
    def _():
        part = pl.ds((step - 3) * ROW_TILE, ROW_TILE)
        upstream = dot(dq[part, :], w_q[...], NT)
        dqw[part, :] = upstream
        scaled = row_stats(tokens[...].astype(F32))[0]
        vector_out[0:1] += jnp.sum(upstream * scaled, axis=0, keepdims=True)
        vector_out[1:2] += jnp.sum(upstream, axis=0, keepdims=True)

    @pl.when(step == 7)
    def _():
        @pl.when(me > 0)
        def _():
            halo(0).wait_send()
            halo(1).wait_recv()

        @pl.when(me < peers - 1)
        def _():
            halo(1).wait_send()
            halo(0).wait_recv()

        none = jnp.zeros((WIN, width), F32)
        stop = jnp.where(images.third, images.spans[2][1], images.spans[1][1])
        cut = (stop > RIM + rows) & (me < peers - 1)
        after = jnp.where(cut, incoming[0].astype(F32), none)
        before = jnp.where(images.spans[0][0] < RIM, incoming[1].astype(F32), none)
        padded[0, wide] = (dn[0].astype(F32) + before).astype(BF)
        padded[1, wide] = (dn[1].astype(F32) + jnp.where(images.third, none, after)).astype(BF)
        padded[2, wide] = (dn[2].astype(F32) + jnp.where(images.third, after, none)).astype(BF)

    @pl.when(step >= 7)
    def _():
        upstream = dqw[pl.ds((step - 7) * ROW_TILE, ROW_TILE), :]
        places = []
        for k in range(ROW_TILE // TILE):
            total = upstream[k * TILE : (k + 1) * TILE]
            for seg, base in enumerate(bases):
                off = jnp.maximum(
                    (RIM + TILE) // 16 + (step - 7) * (ROW_TILE // 16) + k * (TILE // 16) - base, 0
                )
                off = jnp.minimum(off, (WIN + TILE) // 16) * 16
                total = total + padded[seg, pl.ds(off, TILE), :].astype(F32)
            places.append(total)
        upstream = jnp.concatenate(places, axis=0)
        scaled, inv_std = row_stats(tokens[...].astype(F32))
        through = upstream * vecs[0:1]
        inner = (
            through
            - jnp.mean(through, axis=1, keepdims=True)
            - scaled * jnp.mean(through * scaled, axis=1, keepdims=True)
        )
        out[...] = dresid[...] + inv_std * inner


LAST_STEPS = 11


def last_kernel(*refs):
    step = pl.program_id(0)
    me, peers = lax.axis_index(AXIS), lax.axis_size(AXIS)
    ins, (out, vector_out, grads_out), scratch = refs[:13], refs[13:16], refs[16:]
    grads, padded, outgoing, incoming, send, recv, dqw = scratch
    pl.when(step == 0)(lambda: greet([], me > 0, me < peers - 1))
    last_body(step, *ins, out, grads, padded, outgoing, incoming, send, recv, dqw, vector_out)

    @pl.when(step == LAST_STEPS - 1)
    def _():
        grads_out[...] = grads[...]


def last_scatter_kernel(*refs):
    step = pl.program_id(0)
    me, peers = lax.axis_index(AXIS), lax.axis_size(AXIS)
    ins, (out, vector_out, reduced), scratch = refs[:13], refs[13:16], refs[16:]
    grads, padded, outgoing, incoming, send, recv, dqw = scratch[:7]
    vectors, arrived, vec_send, vec_recv = scratch[7:11]
    comm = scratch[11:]
    place = Place()
    pl.when(step == 0)(
        lambda: greet([*place.partners, place.far], me > 0, me < peers - 1)
    )
    pieces = [
        Scatter(
            place, grads.at[k], *comm[k * 8 : k * 8 + 5], reduced.at[:, pl.ds(k * UNIT, UNIT)],
            comm[k * 8 + 5 : k * 8 + 8], True,
        )
        for k in range(3)
    ]
    total = Total(place, vectors, arrived, vec_send, vec_recv)
    for i in range(4):
        pl.when(step == 7 + i)(functools.partial(total.stage, i))
    run_stages(pieces, step, (1, 2, 3, 7, 8, 9))
    last_body(
        step, *ins, out, Flat(grads), padded, outgoing, incoming, send, recv, dqw, vectors.at[0]
    )

    @pl.when(step == LAST_STEPS - 1)
    def _():
        vector_out[...] = vectors[3]
        pieces[2].stage(4)


class Flat:
    def __init__(self, ref):
        self.ref = ref

    def __setitem__(self, index, value):
        k, rows, _ = index
        part = self.ref.shape[5]
        count = rows.size // part
        first = rows.start // part
        for i in range(0, count, 8):
            block = value[i * part : (i + 8) * part].reshape(2, 2, 2, part, value.shape[1])
            self.ref[k, (first + i) // 8] = block


def last(
    n0, normed, dq, dk, dv, dn, w_qkv, tokens, dresid, vecs, sums, up_sums, kv_sums, plan
):
    rows, width = dq.shape
    ext = normed.shape[0]
    peers = lax.axis_size(AXIS)
    const = lambda s: (0, 0)
    once = lambda *shape: pl.BlockSpec(
        shape, lambda s: (0,) * len(shape), pipeline_mode=pl.Buffered(1)
    )
    tile = pl.BlockSpec((ROW_TILE, width), lambda s: (jnp.maximum(s - 7, 0), 0))
    twice = pl.BlockSpec(
        (ROW_TILE, width), lambda s: (jnp.where(s < 7, jnp.maximum(s - 3, 0), s - 7), 0)
    )
    vmem = pl.BlockSpec(memory_space=pltpu.VMEM)
    in_specs = [
        pl.BlockSpec(memory_space=pltpu.SMEM),
        once(ext, width), once(rows, width), once(3, WIN, width), once(3, WIN, width),
        once(3, WIN, width), once(width, width), twice, tile, once(8, width), once(8, width),
        once(*up_sums.shape), once(8, width),
    ]
    vector_rows = 16
    shared = [
        pltpu.VMEM((3, WIN + 2 * TILE, width), BF),
        pltpu.VMEM((WIN, width), BF),
        pltpu.VMEM((2, WIN, width), BF),
        pltpu.SemaphoreType.DMA((2,)),
        pltpu.SemaphoreType.DMA((2,)),
        pltpu.VMEM((rows, width), F32),
    ]
    if plan:
        part = width // peers
        kernel, collective = last_scatter_kernel, 3
        scratch = [pltpu.VMEM((3, 4, 2, 2, 2, part, width), BF)] + shared + [
            pltpu.VMEM((4, vector_rows, width), F32),
            pltpu.VMEM((7, vector_rows, width), F32),
            pltpu.SemaphoreType.DMA((7,)),
            pltpu.SemaphoreType.DMA((7,)),
        ] + scatter_scratch(part, UNIT, tilt=True) * 3
        third_out = jax.ShapeDtypeStruct((part, 3 * width), F32)
    else:
        kernel, collective = last_kernel, 4
        scratch = [pltpu.VMEM((3, width, width), BF)] + shared
        third_out = jax.ShapeDtypeStruct((3, width, width), BF)
    return pl.pallas_call(
        kernel,
        grid=(LAST_STEPS,),
        in_specs=in_specs,
        out_specs=[tile, once(vector_rows, width), once(*third_out.shape)],
        out_shape=[
            jax.ShapeDtypeStruct((rows, width), F32),
            jax.ShapeDtypeStruct((vector_rows, width), F32),
            third_out,
        ],
        scratch_shapes=scratch,
        compiler_params=pltpu.CompilerParams(
            vmem_limit_bytes=61 * 2**20, collective_id=collective, has_side_effects=True
        ),
        name="last",
    )(n0, normed, dq, dk, dv, dn, w_qkv, tokens, dresid, vecs, sums, up_sums, kv_sums)


def shifted(value, by):
    peers = lax.axis_size(AXIS)
    pairs = [(i, i + by) for i in range(peers) if 0 <= i + by < peers]
    return lax.ppermute(value, AXIS, pairs)


def gathered(value):
    return lax.all_gather(value, AXIS, axis=0, tiled=True)


def scattered(value):
    return lax.psum_scatter(value, AXIS, scatter_dimension=0, tiled=True)


def local(
    tokens,
    image_ids,
    cotangent,
    norm1_gain,
    norm1_shift,
    qkv_weight,
    query_bias,
    value_bias,
    out_weight,
    out_bias,
    norm2_gain,
    norm2_shift,
    up_weight,
    up_bias,
    down_weight,
    down_bias,
):
    rows, width = tokens.shape
    me = lax.axis_index(AXIS)
    peers = lax.axis_size(AXIS)
    ext = -(-(rows + 2 * RIM + 64) // 128) * 128
    vectors = [
        norm1_gain, norm1_shift, query_bias, value_bias, out_bias, norm2_gain, norm2_shift,
        down_bias,
    ]
    part = norm1_gain.shape[0]
    block_plan = peers == 32
    if block_plan:
        lane = lax.broadcasted_iota(jnp.int32, (1, 128), 1) // part
        spread = jnp.tile(jnp.stack(vectors), (1, 128 // part))
        spread = jnp.where(lane == me % (128 // part), spread, jnp.zeros_like(spread))
        vec = jnp.concatenate(
            [spread, up_bias[None], jnp.zeros((VEC_ROWS - 9, 128), BF)], axis=0
        )
        queries, key_value, normed_ext, scaled_ext, w_qkv, vectors, u_bias, n0 = first(
            tokens, qkv_weight, vec, image_ids.reshape(-1, 128), ext
        )
        u_bias = u_bias[0]
        gain1 = vectors[0]
        vecs = vectors[4:8]
    else:
        n0 = jnp.sum((image_ids == image_ids[0]).astype(jnp.int32)).reshape(1)
        gathered_vec = gathered(jnp.concatenate([*vectors, up_bias])[None]).astype(F32)
        gain1, shift1, q_bias, v_bias, o_bias, gain2, shift2, d_bias = (
            gathered_vec[:, i * part : (i + 1) * part].reshape(-1) for i in range(8)
        )
        u_bias = gathered_vec[:, 8 * part :].reshape(-1)
        vecs = jnp.stack([o_bias, gain2, shift2, d_bias])
        w_qkv, w_out, w_up, w_down = map(
            gathered, (qkv_weight, out_weight, up_weight, down_weight)
        )
        low_rim = shifted(tokens[rows - RIM :], 1)
        high_rim = shifted(tokens[:RIM], -1)
        pad = jnp.zeros((ext - rows - 2 * RIM, width), BF)
        tokens_ext = jnp.concatenate([low_rim, tokens, high_rim, pad], axis=0).astype(F32)
        scaled_ext = row_stats(tokens_ext)[0]
        normed_ext = (scaled_ext * gain1 + shift1).astype(BF)
        scaled_ext = scaled_ext.astype(BF)
        normed_low = normed_ext[RIM : RIM + rows]
        queries = (dot(normed_low, w_qkv[:, :width]) + q_bias).astype(BF)
        key_value = (
            dot(normed_ext, w_qkv[:, width:])
            + jnp.concatenate([jnp.zeros_like(v_bias), v_bias])
        ).astype(BF)
    vecs = jnp.concatenate([vecs, jnp.zeros((4, width), F32)])
    if block_plan:
        mixed_low, lse, w_out, w_up = attend(
            n0, queries, key_value, (out_weight, up_weight)
        )
        w_out, w_up = w_out.reshape(width, -1), w_up.reshape(width, -1)
    else:
        mixed_low, lse = attend(n0, queries, key_value)

    args = (mixed_low, tokens, w_out, vecs, w_up, u_bias[None], cotangent)
    if block_plan:
        resid, normed_two, act, slope, grad_down, w_down = mlp_up(*args, down_weight)
        w_down = w_down.reshape(-1, width)
    else:
        resid, normed_two, act, slope, grad_down = mlp_up(*args)
    args = (act, slope, w_up, w_down, cotangent, normed_two, resid, mixed_low, w_out, vecs)
    if block_plan:
        grad_up, up_sums, layer_out, dresid, dmixed_low, grad_out, sums, r_down = mlp_back(
            *args, grad_down
        )
    else:
        grad_up, up_sums, layer_out, dresid, dmixed_low, grad_out, sums = mlp_back(*args)
        r_down = scattered(grad_down).astype(F32)
    if block_plan:
        dquery, dkey, dvalue, dnormed, kv_sums, r_out, r_up = attend_back(
            n0, queries, key_value, dmixed_low, lse, w_qkv, scaled_ext, (grad_out, grad_up)
        )
    else:
        dquery, dkey, dvalue, dnormed, kv_sums = attend_back(
            n0, queries, key_value, dmixed_low, lse, w_qkv, scaled_ext
        )
        r_out, r_up = (scattered(v).astype(F32) for v in (grad_out, grad_up))
    vecs = jnp.concatenate([gain1[None], jnp.zeros((7, width), F32)])
    grad_tokens, totals, r_qkv = last(
        n0, normed_ext, dquery, dkey, dvalue, dnormed, w_qkv, tokens, dresid, vecs, sums,
        up_sums, kv_sums, block_plan,
    )
    if not block_plan:
        totals = lax.psum(totals, AXIS)
        r_qkv = jnp.concatenate([scattered(v) for v in r_qkv], axis=1).astype(F32)
    owned = lax.dynamic_slice_in_dim(totals[:8], me * part, part, 1)
    size = u_bias.shape[0] // peers
    up_own = lax.dynamic_slice_in_dim(totals[8 : 8 + u_bias.shape[0] // width].reshape(-1), me * size, size)
    g = [owned[i] for i in range(8)] + [up_own]
    return (
        layer_out, grad_tokens, g[0], g[1], r_qkv, g[2], g[3], r_out, g[4], g[5], g[6], r_up,
        g[8], r_down, g[7],
    )


def solution(mesh):
    row, vec = P(AXIS, None), P(AXIS)
    return jax.shard_map(
        local,
        mesh=mesh,
        in_specs=(
            row, vec, row, vec, vec, row, vec, vec, row, vec, vec, vec, row, vec, row, vec,
        ),
        out_specs=(
            row, row, vec, vec, row, vec, vec, row, vec, vec, vec, row, vec, row, vec,
        ),
        check_vma=False,
    )
```

```python
import functools
import math

import jax
import jax.numpy as jnp
from jax import lax
from jax.experimental import pallas as pl
from jax.experimental.pallas import tpu as pltpu
from jax.sharding import PartitionSpec as P

HDIM = 64
IMG = 577
RIM = IMG - 1
WIN = 592
QB = 128
EPS = 1e-06
NEG = -1e30
AXIS = "fsdp"
BF = jnp.bfloat16
F32 = jnp.float32
NT = (((1,), (1,)), ((), ()))
TN = (((0,), (0,)), ((), ()))
NN = (((1,), (0,)), ((), ()))


def dot(a, b, dims=NN):
    return lax.dot_general(a, b, dims, preferred_element_type=F32)


def stacked(block):
    lane = lax.broadcasted_iota(jnp.int32, block.shape, 1)
    zero = jnp.zeros_like(block)
    return jnp.concatenate(
        [jnp.where(lane < HDIM, block, zero), jnp.where(lane >= HDIM, block, zero)], axis=0
    )


def unstacked(wide):
    return jnp.concatenate([wide[:HDIM, :QB], wide[HDIM:, QB:]], axis=0).T


def key_mask(low, high):
    row = lax.broadcasted_iota(jnp.int32, (WIN, QB), 0)
    bias = jnp.where((row >= low) & (row < high), 0.0, NEG)
    return jnp.concatenate([bias, bias], axis=1)


def mesh_copy(src, dst, send_sem, recv_sem, to):
    return pltpu.make_async_remote_copy(
        src_ref=src,
        dst_ref=dst,
        send_sem=send_sem,
        recv_sem=recv_sem,
        device_id=(to,),
        device_id_type=pl.DeviceIdType.MESH,
    )


class Place:
    def __init__(self):
        me = lax.axis_index(AXIS)
        self.c, self.x, self.y, self.z = me % 2, me // 2 % 2, me // 4 % 2, me // 8
        self.sib = self.at(self.z, self.y, self.x, 1 - self.c)
        self.xp = self.at(self.z, self.y, 1 - self.x, self.c)
        self.yp = self.at(self.z, 1 - self.y, self.x, self.c)
        self.zp = [self.at((self.z + k) % 4, self.y, self.x, self.c) for k in (1, 2, 3)]
        self.far = self.at(self.z, 1 - self.y, 1 - self.x, self.c)
        self.partners = [self.sib, self.xp, self.yp, *self.zp]

    @staticmethod
    def at(z, y, x, c):
        return ((z * 2 + y) * 2 + x) * 2 + c


def greet(partners, before=None, after=None):
    barrier = pltpu.get_barrier_semaphore()

    def hello(to):
        pl.semaphore_signal(
            barrier, inc=1, device_id=(to,), device_id_type=pl.DeviceIdType.MESH
        )

    for to in partners:
        hello(to)
    if before is None:
        pl.semaphore_wait(barrier, len(partners))
        return
    me = lax.axis_index(AXIS)
    pl.when(before)(lambda: hello(me - 1))
    pl.when(after)(lambda: hello(me + 1))
    pl.semaphore_wait(
        barrier, len(partners) + before.astype(jnp.int32) + after.astype(jnp.int32)
    )


class Gather:
    def __init__(self, place, shard, full, cols, send, recv, own, tilt=False):
        self.shard, self.own = shard.at[:, cols], own
        p, rows = place, shard.shape[0]
        half = rows // 2

        def block(y, x, part=slice(None)):
            return full.at[:, y, x, p.c, part, cols]

        mine = full.at[p.z, p.y, p.x, p.c, :, cols]
        self.local = lambda: pltpu.make_async_copy(self.shard, mine, own)

        def copy(i, src, dst, to):
            return lambda: mesh_copy(src, dst, send.at[i], recv.at[i], to)

        same = lambda i, ref, to: copy(i, ref, ref, to)
        first, second = pl.ds(0, half), pl.ds(half, half)
        self.z = [copy(i, self.shard, mine, to) for i, to in enumerate(p.zp)]
        self.xy = [same(3, block(p.y, p.x), p.xp), same(4, block(p.y, p.x), p.yp)]
        self.far = [
            same(5, block(p.y, 1 - p.x, first), p.yp),
            same(6, block(1 - p.y, p.x, second), p.xp),
        ]
        if tilt:
            self.far = [same(5, block(p.y, 1 - p.x), p.yp)]
        self.pair = [
            same(7, block(p.y, p.x), p.sib),
            same(8, block(p.y, 1 - p.x), p.sib),
            same(9, block(1 - p.y, p.x), p.sib),
            same(10, block(1 - p.y, 1 - p.x), p.sib),
        ]

    def stage(self, number):
        if number == 0:
            self.local().start()
            for c in self.z:
                c().start()
        elif number == 1:
            self.local().wait()
            for c in self.z:
                c().wait()
            for c in (*self.xy, self.pair[0]):
                c().start()
        elif number == 2:
            for c in self.xy:
                c().wait()
            for c in (*self.far, self.pair[1], self.pair[2]):
                c().start()
        elif number == 3:
            for c in self.far:
                c().wait()
            self.pair[3]().start()
        else:
            for c in self.pair:
                c().wait()


GATHER_SEMS = 11


def run_stages(pieces, step, steps):
    for at in sorted(set(steps)):
        todo = [
            (q, pieces[tick - q])
            for tick, when in enumerate(steps)
            if when == at
            for q in range(5)
            if 0 <= tick - q < len(pieces)
        ]

        @pl.when(step == at)
        def _():
            for q, piece in todo:
                piece.stage(q)


def run_rest(pieces, ticks):
    for tick in range(ticks, len(pieces) + 4):
        for q in range(5):
            if 0 <= tick - q < len(pieces):
                pieces[tick - q].stage(q)


class Scatter:
    def __init__(self, place, grad, held, from_pair, far, side, line, out, sems, tilt=False):
        self.tilt = tilt
        self.p, self.out = place, out
        self.held, self.from_pair, self.far, self.side, self.line = held, from_pair, far, side, line
        p, rows = place, held.shape[3]
        self.half = rows // 2
        own, send, recv = sems
        first, second = pl.ds(0, self.half), pl.ds(self.half, self.half)

        def copy(i, src, dst, to):
            return lambda: mesh_copy(src, dst, send.at[i], recv.at[i], to)

        self.load = lambda: pltpu.make_async_copy(grad.at[:, :, :, p.c], held, own)
        self.to_pair = copy(0, grad.at[:, :, :, 1 - p.c], from_pair, p.sib)
        self.to_far = [
            copy(1, held.at[:, 1 - p.y, 1 - p.x, first], far.at[0], p.xp),
            copy(2, held.at[:, 1 - p.y, 1 - p.x, second], far.at[1], p.yp),
        ]
        if tilt:
            self.to_far = [copy(1, held.at[:, 1 - p.y, 1 - p.x], far, p.yp)]
        self.to_side = [
            copy(3, held.at[:, p.y, 1 - p.x], side.at[0], p.xp),
            copy(4, held.at[:, 1 - p.y, p.x], side.at[1], p.yp),
        ]
        self.to_line = [
            copy(5 + k, held.at[(p.z + k + 1) % 4, p.y, p.x], line.at[k], to)
            for k, to in enumerate(p.zp)
        ]

    def stage(self, number):
        p, half = self.p, self.half
        held, far, side, line = self.held, self.far, self.side, self.line
        if number == 0:
            self.load().start()
            self.to_pair().start()
        elif number == 1:
            self.load().wait()
            self.to_pair().wait()

            @pl.loop(0, 4)
            def _(z):
                for y in range(2):
                    for x in range(2):
                        held[z, y, x] = (
                            held[z, y, x].astype(F32) + self.from_pair[z, y, x].astype(F32)
                        ).astype(held.dtype)

            for c in self.to_far:
                c().start()
        elif number == 2:
            for c in self.to_far:
                c().wait()

            @pl.loop(0, 4)
            def _(z):
                if self.tilt:
                    held[z, p.y, 1 - p.x] = (
                        held[z, p.y, 1 - p.x].astype(F32) + far[z].astype(F32)
                    ).astype(held.dtype)
                    return
                held[z, 1 - p.y, p.x, :half] = (
                    held[z, 1 - p.y, p.x, :half].astype(F32) + far[0, z].astype(F32)
                ).astype(held.dtype)
                held[z, p.y, 1 - p.x, half:] = (
                    held[z, p.y, 1 - p.x, half:].astype(F32) + far[1, z].astype(F32)
                ).astype(held.dtype)

            for c in self.to_side:
                c().start()
        elif number == 3:
            for c in self.to_side:
                c().wait()

            @pl.loop(0, 4)
            def _(z):
                held[z, p.y, p.x] = (
                    held[z, p.y, p.x].astype(F32)
                    + side[0, z].astype(F32)
                    + side[1, z].astype(F32)
                ).astype(held.dtype)

            for c in self.to_line:
                c().start()
        else:
            for c in self.to_line:
                c().wait()
            self.out[...] = (
                held[p.z, p.y, p.x].astype(F32)
                + line[0].astype(F32)
                + line[1].astype(F32)
                + line[2].astype(F32)
            )


SCATTER_SEMS = 8
UNIT = 1024


def scatter_scratch(rows, cols, dtype=BF, tilt=False):
    return [
        pltpu.VMEM((4, 2, 2, rows, cols), dtype),
        pltpu.VMEM((4, 2, 2, rows, cols), dtype),
        pltpu.VMEM((4, rows, cols) if tilt else (2, 4, rows // 2, cols), dtype),
        pltpu.VMEM((2, 4, rows, cols), dtype),
        pltpu.VMEM((3, rows, cols), dtype),
        pltpu.SemaphoreType.DMA,
        pltpu.SemaphoreType.DMA((SCATTER_SEMS,)),
        pltpu.SemaphoreType.DMA((SCATTER_SEMS,)),
    ]


def blocks(value):
    return value.reshape(4, 2, 2, 2, value.shape[0] // 32, value.shape[1])


VEC_ROWS = 16


def first_body(
    rows, tokens, wide, vec, ids, q_out, kv_out, normed_out, scaled_out, w_out, vecs_out,
    bias_out, n0_out, near, normed, scaled, weights, gathered_vec, queries, pairs, send, recv,
    own, halo_send, halo_recv, load, store,
):
    place = Place()
    me, peers = lax.axis_index(AXIS), lax.axis_size(AXIS)
    greet(place.partners, me > 0, me < peers - 1)
    width = near.shape[1]
    mine = pl.ds(RIM, rows)

    def halo(way):
        if way == 0:
            src, dst, to = tokens.at[pl.ds(0, RIM)], near.at[pl.ds(RIM + rows, RIM)], me - 1
        else:
            src, dst, to = tokens.at[pl.ds(rows - RIM, RIM)], near.at[pl.ds(0, RIM)], me + 1
        return mesh_copy(src, dst, halo_send.at[way], halo_recv.at[way], to)

    pieces = [
        Gather(
            place, vec, gathered_vec, pl.ds(0, vec.shape[1]), send.at[0], recv.at[0], own.at[0],
            True,
        )
    ]
    for i, k in enumerate((1, 2, 0)):
        pieces.append(
            Gather(
                place, wide, weights, pl.ds(k * UNIT, UNIT), send.at[i + 1], recv.at[i + 1],
                own.at[i + 1],
            )
        )
    g_vec, g_k, g_v, g_q = pieces
    own_copy = pltpu.make_async_copy(tokens, near.at[mine], load)
    own_copy.start()
    g_vec.stage(0)
    g_k.stage(0)
    pl.when(me > 0)(lambda: halo(0).start())
    pl.when(me < peers - 1)(lambda: halo(1).start())
    n0_out[0] = jnp.sum((ids[...] == ids[0:1, 0:1]).astype(jnp.int32))
    near[pl.ds(2 * RIM + rows, near.shape[0] - rows - 2 * RIM), :] = jnp.zeros(
        (near.shape[0] - rows - 2 * RIM, width), BF
    )

    @pl.when(me == 0)
    def _():
        near[pl.ds(0, RIM), :] = jnp.zeros((RIM, width), BF)

    @pl.when(me == peers - 1)
    def _():
        near[pl.ds(RIM + rows, RIM), :] = jnp.zeros((RIM, width), BF)

    g_vec.stage(1)
    g_k.stage(1)
    g_v.stage(0)
    g_vec.stage(2)
    g_vec.stage(3)
    g_vec.stage(4)
    table = []
    for z in range(4):
        for y in range(2):
            group = [gathered_vec[z, y, x, c].astype(F32) for x in range(2) for c in range(2)]
            table.append(group[0] + group[1] + group[2] + group[3])
            for x in range(2):
                for c in range(2):
                    at = ((z * 2 + y) * 2 + x) * 2 + c
                    bias_out[:, at * 128 : (at + 1) * 128] = group[x * 2 + c][8:9]
    vecs = jnp.concatenate(table, axis=1)
    vecs_out[...] = vecs
    gain, shift = vecs[0:1], vecs[1:2]
    q_bias, v_bias = vecs[2:3], vecs[3:4]

    def norm(first, count):
        part = pl.ds(first, count)
        value = row_stats(near[part, :].astype(F32))[0]
        scaled[part, :] = value.astype(BF)
        normed[part, :] = (value * gain + shift).astype(BF)

    own_copy.wait()
    for row in range(RIM, RIM + rows, 256):
        norm(row, 256)
    g_k.stage(2)
    g_v.stage(1)
    g_q.stage(0)
    g_k.stage(3)
    g_v.stage(2)
    g_q.stage(1)
    g_k.stage(4)

    def full(k):
        return weights[:, :, :, :, :, pl.ds(k * UNIT, UNIT)].reshape(width, UNIT)

    def project(target, k, first, stop, bias, at):
        matrix = full(k)
        for row in range(first, stop, 256):
            size = min(256, stop - row)
            value = dot(normed[pl.ds(row, size), :], matrix)
            value = value if bias is None else value + bias
            target[pl.ds(row - at[0], size), pl.ds(at[1], UNIT)] = value.astype(BF)

    last_row = near.shape[0]
    project(pairs, 1, RIM, RIM + rows, None, (0, 0))
    g_v.stage(3)
    g_q.stage(2)

    @pl.when(me > 0)
    def _():
        halo(0).wait_send()
        halo(1).wait_recv()

    @pl.when(me < peers - 1)
    def _():
        halo(1).wait_send()
        halo(0).wait_recv()

    for row in range(0, RIM, 192):
        norm(row, 192)
    for row in range(RIM + rows, last_row, 176):
        norm(row, 176)
    normed_copy = pltpu.make_async_copy(normed, normed_out, store.at[0])
    normed_copy.start()
    scaled_copy = pltpu.make_async_copy(scaled, scaled_out, store.at[5])
    scaled_copy.start()
    project(pairs, 1, 0, RIM, None, (0, 0))
    project(pairs, 1, RIM + rows, last_row, None, (0, 0))
    k_copy = pltpu.make_async_copy(
        pairs.at[:, pl.ds(0, UNIT)], kv_out.at[:, pl.ds(0, UNIT)], store.at[1]
    )
    k_copy.start()
    g_v.stage(4)
    g_q.stage(3)
    project(pairs, 2, 0, last_row, v_bias, (0, UNIT))
    v_copy = pltpu.make_async_copy(
        pairs.at[:, pl.ds(UNIT, UNIT)], kv_out.at[:, pl.ds(UNIT, UNIT)], store.at[2]
    )
    v_copy.start()
    g_q.stage(4)
    w_copy = pltpu.make_async_copy(weights, w_out, store.at[3])
    w_copy.start()
    project(queries, 0, RIM, RIM + rows, q_bias, (RIM, 0))
    q_copy = pltpu.make_async_copy(queries, q_out, store.at[4])
    q_copy.start()
    for copy in (normed_copy, scaled_copy, k_copy, v_copy, w_copy, q_copy):
        copy.wait()


def first(tokens, wide, vec, ids, ext):
    rows, width = tokens.shape
    part = wide.shape[0]
    hbm, vmem = pl.BlockSpec(memory_space=pl.ANY), pl.BlockSpec(memory_space=pltpu.VMEM)
    queries, key_value, normed, scaled, w_qkv, vecs, bias, n0 = pl.pallas_call(
        functools.partial(first_body, rows),
        in_specs=[hbm] * 3 + [vmem],
        out_specs=[hbm] * 5 + [vmem] * 2 + [pl.BlockSpec(memory_space=pltpu.SMEM)],
        out_shape=[
            jax.ShapeDtypeStruct((rows, width), BF),
            jax.ShapeDtypeStruct((ext, 2 * width), BF),
            jax.ShapeDtypeStruct((ext, width), BF),
            jax.ShapeDtypeStruct((ext, width), BF),
            jax.ShapeDtypeStruct((4, 2, 2, 2, *wide.shape), BF),
            jax.ShapeDtypeStruct((VEC_ROWS, width), F32),
            jax.ShapeDtypeStruct((1, 32 * 128), F32),
            jax.ShapeDtypeStruct((1,), jnp.int32),
        ],
        scratch_shapes=[
            pltpu.VMEM((ext, width), BF),
            pltpu.VMEM((ext, width), BF),
            pltpu.VMEM((ext, width), BF),
            pltpu.VMEM((4, 2, 2, 2, *wide.shape), BF),
            pltpu.VMEM((4, 2, 2, 2, *vec.shape), BF),
            pltpu.VMEM((rows, width), BF),
            pltpu.VMEM((ext, 2 * width), BF),
            pltpu.SemaphoreType.DMA((4, GATHER_SEMS)),
            pltpu.SemaphoreType.DMA((4, GATHER_SEMS)),
            pltpu.SemaphoreType.DMA((4,)),
            pltpu.SemaphoreType.DMA((2,)),
            pltpu.SemaphoreType.DMA((2,)),
            pltpu.SemaphoreType.DMA,
            pltpu.SemaphoreType.DMA((6,)),
        ],
        compiler_params=pltpu.CompilerParams(
            collective_id=0, has_side_effects=True, vmem_limit_bytes=62 * 2**20
        ),
        name="first",
    )(tokens, wide, vec, ids)
    w_qkv = w_qkv.reshape(width, wide.shape[1])
    return queries, key_value, normed, scaled, w_qkv, vecs, bias, n0


ITEMS = 10
BACK_GROUP = 5
GROUP = 5


class Images:
    def __init__(self, n0, rows, ext):
        self.n0, self.n1, self.rows, self.ext = n0, n0 + IMG, rows, ext
        me, peers = lax.axis_index(AXIS), lax.axis_size(AXIS)
        limit = jnp.where(me == peers - 1, RIM + rows, 2 * RIM + rows)
        start0 = jnp.where(me == 0, RIM, n0 - 1)
        start1 = RIM + n0
        start2 = start1 + IMG
        self.spans = (
            (start0, start1),
            (start1, jnp.minimum(start1 + IMG, limit)),
            (start2, jnp.minimum(start2 + IMG, limit)),
        )
        one = lambda flag: jnp.where(flag, 1, 0)
        self.b0, self.b1 = lax.div(n0, QB), lax.div(self.n1, QB)
        self.d0 = one(self.b0 * QB != n0)
        self.d1 = one((self.n1 < rows) & (self.b1 * QB != self.n1))
        self.third = self.n1 < rows
        self.end0 = lax.div(n0 - 1, QB)
        self.end1 = lax.div(self.n1 - 1, QB) + self.d0
        self.one = one

    def base(self, start):
        return jnp.minimum(lax.div(start, 16), (self.ext - WIN) // 16)

    def segment(self, item):
        return self.one(item > self.end0) + self.one(item > self.end1)

    def item(self, item):
        blk = (
            item
            - self.d0 * self.one(item > self.b0)
            - self.d1 * self.one(item > self.b1 + self.d0)
        )
        used = blk < self.rows // QB
        blk = jnp.minimum(blk, self.rows // QB - 1)
        seg = self.segment(item)
        choose = lambda i: jnp.where(
            seg == 0, self.spans[0][i], jnp.where(seg == 1, self.spans[1][i], self.spans[2][i])
        )
        start, stop = choose(0), choose(1)
        base = self.base(start) * 16
        row0 = blk * QB
        low = jnp.maximum(start - RIM - row0, 0)
        high = jnp.where(used, jnp.minimum(stop - RIM - row0, QB), 0)
        return blk, row0, base, start - base, stop - base, low, high

    def of_block(self, blk):
        at0 = self.d0 * self.one(blk == self.b0)
        at1 = self.d1 * self.one(blk == self.b1)
        first = blk + self.d0 * self.one(blk > self.b0) + self.d1 * self.one(blk > self.b1)
        split = jnp.where(at0 == 1, self.n0, jnp.where(at1 == 1, self.n1, self.rows)) - blk * QB
        return first, first + at0 + at1, split


def attend_body(n0_ref, q_ref, k_ref, v_ref, out_ref, lse_ref, parts, parts_lse):
    rows = q_ref.shape[0]
    images = Images(n0_ref[0], rows, k_ref.shape[0])

    def scores_of(item):
        _, row0, base, low, high, _, _ = images.item(item)
        queries = stacked(q_ref[pl.ds(row0, QB), :]) * jnp.asarray(0.125, BF)
        scores = dot(k_ref[pl.ds(base, WIN), :], queries, NT)
        return scores + key_mask(low, high), base

    def softmax_of(scores):
        top = jnp.max(scores, axis=0, keepdims=True)
        terms = jnp.exp(scores - top)
        total = jnp.sum(terms, axis=0, keepdims=True)
        return terms.astype(BF), top, total

    @pl.loop(0, ITEMS // GROUP)
    def _(step):
        items = [step * GROUP + g for g in range(GROUP)]
        scored = [scores_of(item) for item in items]
        soft = [softmax_of(scores) for scores, _ in scored]
        mixed = [
            dot(v_ref[pl.ds(base, WIN), :], terms, TN) / total
            for (_, base), (terms, _, total) in zip(scored, soft)
        ]
        for item, value, (_, top, total) in zip(items, mixed, soft):
            parts[item] = unstacked(value)
            parts_lse[item] = jnp.broadcast_to(top + jnp.log(total), parts_lse.shape[1:])

    for blk in range(rows // QB):
        first, last, split = images.of_block(blk)
        row = lax.broadcasted_iota(jnp.int32, (QB, 2 * HDIM), 0)
        out_ref[pl.ds(blk * QB, QB), :] = jnp.where(
            row < split, parts[first], parts[last]
        ).astype(BF)
        lane = lax.broadcasted_iota(jnp.int32, parts_lse.shape[1:], 1) % QB
        lse_ref[0, pl.ds(blk, 1), :] = jnp.where(
            lane < split, parts_lse[first], parts_lse[last]
        )[:1]


def attend_kernel(n0_ref, q_ref, k_ref, v_ref, out_ref, lse_ref, parts, parts_lse):
    attend_body(n0_ref, q_ref, k_ref, v_ref, out_ref, lse_ref, parts, parts_lse)


def attend_gather_kernel(
    n0_ref, q_ref, k_ref, v_ref, w_out, w_up, out_ref, lse_ref, full_out, full_up,
    parts, parts_lse, send, recv, own,
):
    tick = pl.program_id(0)
    place = Place()
    pl.when(tick == 0)(lambda: greet(place.partners))
    pieces = []
    for shard, full in ((w_out, full_out), (w_up, full_up)):
        for k in range(shard.shape[1] // UNIT):
            i = len(pieces)
            pieces.append(
                Gather(
                    place, shard, full, pl.ds(k * UNIT, UNIT), send.at[i], recv.at[i], own.at[i]
                )
            )
    run_stages(pieces, tick, range(8))
    attend_body(n0_ref, q_ref, k_ref, v_ref, out_ref, lse_ref, parts, parts_lse)

    @pl.when(tick == 7)
    def _():
        pieces[-1].stage(4)


def attend(n0, queries, key_value, shards=None):
    rows, width = queries.shape
    pairs = width // (2 * HDIM)
    ext = key_value.shape[0]
    hbm = pl.BlockSpec(memory_space=pl.ANY)
    in_specs = [
        pl.BlockSpec(memory_space=pltpu.SMEM),
        pl.BlockSpec((rows, 2 * HDIM), lambda p: (0, p)),
        pl.BlockSpec((ext, 2 * HDIM), lambda p: (0, p)),
        pl.BlockSpec((ext, 2 * HDIM), lambda p: (0, pairs + p)),
    ]
    out_specs = [
        pl.BlockSpec((rows, 2 * HDIM), lambda p: (0, p)),
        pl.BlockSpec((1, rows // QB, 2 * QB), lambda p: (p, 0, 0)),
    ]
    out_shape = [
        jax.ShapeDtypeStruct((rows, width), BF),
        jax.ShapeDtypeStruct((pairs, rows // QB, 2 * QB), F32),
    ]
    scratch = [
        pltpu.VMEM((ITEMS, QB, 2 * HDIM), F32),
        pltpu.VMEM((ITEMS, 8, 2 * QB), F32),
    ]
    params = dict(vmem_limit_bytes=62 * 2**20)
    args = [n0, queries, key_value, key_value]
    kernel = attend_kernel
    if shards is not None:
        kernel = attend_gather_kernel
        in_specs += [hbm] * 2
        out_specs += [hbm] * 2
        out_shape += [jax.ShapeDtypeStruct((4, 2, 2, 2, *v.shape), BF) for v in shards]
        count = sum(v.shape[1] // UNIT for v in shards)
        scratch += [
            pltpu.SemaphoreType.DMA((count, GATHER_SEMS)),
            pltpu.SemaphoreType.DMA((count, GATHER_SEMS)),
            pltpu.SemaphoreType.DMA((count,)),
        ]
        params |= dict(collective_id=1, has_side_effects=True)
        args += shards
    return pl.pallas_call(
        kernel,
        grid=(pairs,),
        in_specs=in_specs,
        out_specs=out_specs,
        out_shape=out_shape,
        scratch_shapes=scratch,
        compiler_params=pltpu.CompilerParams(**params),
        name="attend",
    )(*args)


def attend_back_body(
    pair, n0_ref, q_ref, k_ref, v_ref, up_ref, lse_ref, wk_ref, wv_ref, scaled_ref, dq_ref, dk_ref, dv_ref,
    dn_ref, sums_ref, slots, parts, total,
):
    rows = q_ref.shape[0]
    images = Images(n0_ref[0], rows, k_ref.shape[0])

    @pl.when(pair == 0)
    def _():
        slots[0] = jnp.zeros(slots.shape[1:], F32)
        total[...] = jnp.zeros(total.shape, F32)

    lane = lax.broadcasted_iota(jnp.int32, (1, 2 * QB), 1) % QB

    def begin(item):
        blk, row0, base, low, high, first, stop = images.item(item)
        queries = stacked(q_ref[pl.ds(row0, QB), :]) * jnp.asarray(0.125, BF)
        upstream = stacked(up_ref[pl.ds(row0, QB), :])
        here = (lane >= first) & (lane < stop)
        lse = jnp.where(here, lse_ref[0, pl.ds(blk, 1), :], -NEG)
        scores = dot(k_ref[pl.ds(base, WIN), :], queries, NT)
        dprobs = dot(v_ref[pl.ds(base, WIN), :], upstream, NT)
        return base, queries, upstream, scores + key_mask(low, high), lse, dprobs

    def middle(scores, lse, dprobs):
        probs = jnp.exp(scores - lse)
        row_dot = jnp.sum(probs * dprobs, axis=0, keepdims=True)
        return probs.astype(BF), (probs * (dprobs - row_dot)).astype(BF)

    def finish(item, base, queries, upstream, probs, dscores):
        keep = (item > 0) & (images.segment(item) == images.segment(item - 1))
        old = jnp.where(keep, slots[item], jnp.zeros(slots.shape[1:], F32))
        slots[item + 1, :, : 2 * HDIM] = old[:, : 2 * HDIM] + dot(dscores, queries)
        slots[item + 1, :, 2 * HDIM :] = old[:, 2 * HDIM :] + dot(probs, upstream)
        parts[item] = unstacked(dot(k_ref[pl.ds(base, WIN), :], dscores, TN)) * 0.125

    @pl.loop(0, ITEMS // BACK_GROUP)
    def _(step):
        items = [step * BACK_GROUP + g for g in range(BACK_GROUP)]
        begun = [begin(items[0])]
        done = []
        for g in range(BACK_GROUP + 1):
            if g + 1 < BACK_GROUP:
                begun.append(begin(items[g + 1]))
            if g < BACK_GROUP:
                done.append(middle(*begun[g][3:]))
            if g > 0:
                finish(items[g - 1], *begun[g - 1][:3], *done[g - 1])

    for blk in range(rows // QB):
        first, last, split = images.of_block(blk)
        row = lax.broadcasted_iota(jnp.int32, (QB, 2 * HDIM), 0)
        dq_ref[pl.ds(blk * QB, QB), :] = jnp.where(
            row < split, parts[first], parts[last]
        ).astype(BF)
    ends = (
        images.end0 + 1,
        jnp.minimum(images.end1, (rows - 1) // QB + images.d0) + 1,
        jnp.where(images.third, ITEMS, 0),
    )
    weights = jnp.concatenate([wk_ref[...], wv_ref[...]], axis=1)
    for seg, end in enumerate(ends):
        both = slots[end].astype(BF)
        dk_ref[seg] = both[:, : 2 * HDIM]
        dv_ref[seg] = both[:, 2 * HDIM :]
        total[seg] += dot(both, weights, NT)

    @pl.when(pair == pl.num_programs(0) - 1)
    def _():
        dn_ref[...] = total[...].astype(BF)
        sums_ref[...] = jnp.zeros(sums_ref.shape, F32)
        for seg, span in enumerate(images.spans):
            window = scaled_ref[pl.ds(images.base(span[0]) * 16, WIN), :].astype(F32)
            sums_ref[0:1] += jnp.sum(total[seg] * window, axis=0, keepdims=True)
            sums_ref[1:2] += jnp.sum(total[seg], axis=0, keepdims=True)


def attend_back_kernel(*refs):
    attend_back_body(pl.program_id(0), *refs)


def attend_back_scatter_kernel(*refs):
    base, (g_out, g_up), rest = refs[:9], refs[9:11], refs[11:]
    outs, (r_out, r_up), scratch = rest[:5], rest[5:7], rest[7:]
    mine, comm = scratch[:3], scratch[3:]
    pair = pl.program_id(0)
    place = Place()
    pl.when(pair == 0)(lambda: greet(place.partners))
    pieces = []
    for grad, out in ((g_out, r_out), (g_up, r_up)):
        for k in range(grad.shape[5] // UNIT):
            cols = pl.ds(k * UNIT, UNIT)
            bufs = comm[len(pieces) * 8 : len(pieces) * 8 + 8]
            pieces.append(
                Scatter(
                    place, grad.at[:, :, :, :, :, cols], *bufs[:5], out.at[:, cols], bufs[5:]
                )
            )
    run_stages(pieces, pair, range(8))
    attend_back_body(pair, *base, *outs, *mine)

    @pl.when(pair == pl.num_programs(0) - 1)
    def _():
        pieces[-1].stage(4)


def attend_back(n0, queries, key_value, upstream, lse, w_qkv, scaled, grads=None):
    rows, width = queries.shape
    pairs = width // (2 * HDIM)
    ext = key_value.shape[0]
    hbm, vmem = pl.BlockSpec(memory_space=pl.ANY), pl.BlockSpec(memory_space=pltpu.VMEM)
    own = pl.BlockSpec((rows, 2 * HDIM), lambda p: (0, p))
    windows = pl.BlockSpec((3, WIN, 2 * HDIM), lambda p: (0, 0, p))
    in_specs = [
        pl.BlockSpec(memory_space=pltpu.SMEM),
        own,
        pl.BlockSpec((ext, 2 * HDIM), lambda p: (0, p)),
        pl.BlockSpec((ext, 2 * HDIM), lambda p: (0, pairs + p)),
        own,
        pl.BlockSpec((1, rows // QB, 2 * QB), lambda p: (p, 0, 0)),
        pl.BlockSpec((width, 2 * HDIM), lambda p: (0, pairs + p)),
        pl.BlockSpec((width, 2 * HDIM), lambda p: (0, 2 * pairs + p)),
        pl.BlockSpec((ext, width), lambda p: (0, 0), pipeline_mode=pl.Buffered(1)),
    ]
    out_specs = [
        own, windows, windows,
        pl.BlockSpec((3, WIN, width), lambda p: (0, 0, 0), pipeline_mode=pl.Buffered(1)),
        pl.BlockSpec((8, width), lambda p: (0, 0)),
    ]
    out_shape = [jax.ShapeDtypeStruct((rows, width), BF)]
    out_shape += [jax.ShapeDtypeStruct((3, WIN, width), BF)] * 3
    out_shape += [jax.ShapeDtypeStruct((8, width), F32)]
    scratch = [
        pltpu.VMEM((ITEMS + 1, WIN, 4 * HDIM), F32),
        pltpu.VMEM((ITEMS, QB, 2 * HDIM), F32),
        pltpu.VMEM((3, WIN, width), F32),
    ]
    args = [n0, queries, key_value, key_value, upstream, lse, w_qkv, w_qkv, scaled]
    kernel, params = attend_back_kernel, dict(vmem_limit_bytes=62 * 2**20)
    if grads is not None:
        kernel = attend_back_scatter_kernel
        params |= dict(collective_id=2, has_side_effects=True)
        args += map(blocks, grads)
        in_specs += [hbm] * 2
        out_specs += [vmem] * 2
        out_shape += [jax.ShapeDtypeStruct((v.shape[0] // 32, v.shape[1]), F32) for v in grads]
        for v in grads:
            scratch += scatter_scratch(v.shape[0] // 32, UNIT) * (v.shape[1] // UNIT)
    return pl.pallas_call(
        kernel,
        grid=(pairs,),
        in_specs=in_specs,
        out_specs=out_specs,
        out_shape=out_shape,
        scratch_shapes=scratch,
        compiler_params=pltpu.CompilerParams(**params),
        name="attend_back",
    )(*args)


ROW_TILE = 256
FF_TILE = 512
ROOT_HALF = 1.0 / math.sqrt(2.0)
PDF_SCALE = 1.0 / math.sqrt(2.0 * math.pi)


def row_stats(value):
    mean = jnp.mean(value, axis=1, keepdims=True)
    center = value - mean
    inv_std = lax.rsqrt(jnp.mean(center * center, axis=1, keepdims=True) + EPS)
    return center * inv_std, inv_std


def mlp_up_body(
    step, row_steps, mixed, tokens, w_out, vecs, w_up, up_bias, cot, resid, normed, act, slope,
    g_down, held,
):
    @pl.when(step < row_steps)
    def _():
        value = tokens[...].astype(F32) + dot(mixed[...], w_out[...]) + vecs[0:1]
        resid[...] = value
        low = (row_stats(value)[0] * vecs[1:2] + vecs[2:3]).astype(BF)
        normed[...] = low
        held[pl.ds(step * ROW_TILE, ROW_TILE), :] = low

    @pl.when(step >= row_steps)
    def _():
        rows = held.shape[0]

        for row in range(0, rows, ROW_TILE):
            part = pl.ds(row, ROW_TILE)
            upward = dot(held[part, :], w_up[...]) + up_bias[...]
            cdf = 0.5 * (1.0 + lax.erf(upward * ROOT_HALF))
            pdf = jnp.exp(-0.5 * upward * upward) * PDF_SCALE
            act[part, :] = (upward * cdf).astype(BF)
            slope[part, :] = (cdf + upward * pdf).astype(BF)
        g_down[...] = dot(act[...], cot[...], TN).astype(BF)


def mlp_up_kernel(row_steps, *refs):
    mlp_up_body(pl.program_id(0), row_steps, *refs)


def mlp_up_gather_kernel(row_steps, *refs):
    ins, shard, outs, full = refs[:7], refs[7], refs[8:13], refs[13]
    held, send, recv, own = refs[14:]
    step = pl.program_id(0)
    place = Place()
    pl.when(step == 0)(lambda: greet(place.partners))
    cols = shard.shape[1] // 4
    pieces = [
        Gather(place, shard, full, pl.ds(k * cols, cols), send.at[k], recv.at[k], own.at[k])
        for k in range(4)
    ]
    run_stages(pieces, step, (0, 4, 7, 9, 11))
    mlp_up_body(step, row_steps, *ins, *outs, held)
    pl.when(step == pl.num_programs(0) - 1)(lambda: run_rest(pieces, 5))


def mlp_up(mixed, tokens, w_out, vecs, w_up, up_bias, cot, shard=None):
    rows, width = tokens.shape
    hidden = w_up.shape[1]
    row_steps, ff_steps = rows // ROW_TILE, hidden // FF_TILE
    at_row = lambda s: (jnp.minimum(s, row_steps - 1), 0)
    at_col = lambda s: (0, jnp.maximum(s - row_steps, 0))
    at_ff = lambda s: (jnp.maximum(s - row_steps, 0), 0)
    const = lambda s: (0, 0)
    hbm = pl.BlockSpec(memory_space=pl.ANY)
    tall = pl.BlockSpec((rows, FF_TILE), at_col)
    in_specs = [
        pl.BlockSpec((ROW_TILE, width), at_row),
        pl.BlockSpec((ROW_TILE, width), at_row),
        pl.BlockSpec((width, width), const),
        pl.BlockSpec((8, width), const),
        pl.BlockSpec((width, FF_TILE), at_col),
        pl.BlockSpec((1, FF_TILE), at_col),
        pl.BlockSpec((rows, width), const),
    ]
    out_specs = [
        pl.BlockSpec((ROW_TILE, width), at_row),
        pl.BlockSpec((ROW_TILE, width), at_row),
        tall,
        tall,
        pl.BlockSpec((FF_TILE, width), at_ff),
    ]
    out_shape = [
        jax.ShapeDtypeStruct((rows, width), F32),
        jax.ShapeDtypeStruct((rows, width), BF),
        jax.ShapeDtypeStruct((rows, hidden), BF),
        jax.ShapeDtypeStruct((rows, hidden), BF),
        jax.ShapeDtypeStruct((hidden, width), BF),
    ]
    scratch = [pltpu.VMEM((rows, width), BF)]
    params = dict(vmem_limit_bytes=62 * 2**20)
    args = [mixed, tokens, w_out, vecs, w_up, up_bias, cot]
    kernel = mlp_up_kernel
    if shard is not None:
        kernel = mlp_up_gather_kernel
        in_specs += [hbm]
        out_specs += [hbm]
        out_shape += [jax.ShapeDtypeStruct((4, 2, 2, 2, *shard.shape), BF)]
        scratch += [
            pltpu.SemaphoreType.DMA((4, GATHER_SEMS)),
            pltpu.SemaphoreType.DMA((4, GATHER_SEMS)),
            pltpu.SemaphoreType.DMA((4,)),
        ]
        params |= dict(collective_id=5, has_side_effects=True)
        args += [shard]
    return pl.pallas_call(
        functools.partial(kernel, row_steps),
        grid=(row_steps + ff_steps,),
        in_specs=in_specs,
        out_specs=out_specs,
        out_shape=out_shape,
        scratch_shapes=scratch,
        compiler_params=pltpu.CompilerParams(**params),
        name="mlp_up",
    )(*args)


def mlp_back_body(
    step, ff_steps, act, slope, w_up, w_down, cot, normed, resid, mixed, w_out, vecs,
    g_up, up_sums, layer_out, dresid, dmixed, g_out, sums, total, dnormed, branches, dup,
):
    rows, width = cot.shape

    @pl.when(step == 0)
    def _():
        total[...] = jnp.zeros(total.shape, F32)
        dnormed[...] = jnp.zeros(dnormed.shape, F32)
        sums[...] = jnp.zeros(sums.shape, F32)

    @pl.when(step < ff_steps)
    def _():
        count = jnp.zeros(up_sums.shape, F32)
        for row in range(0, rows, ROW_TILE):
            part = pl.ds(row, ROW_TILE)
            total[part, :] += dot(act[part, :], w_down[...])
            dact = dot(cot[part, :], w_down[...], NT)
            low = (dact * slope[part, :].astype(F32)).astype(BF)
            dup[part, :] = low
            count += jnp.sum(low.astype(F32), axis=0, keepdims=True)
            dnormed[part, :] += dot(low, w_up[...], NT)
        up_sums[...] = count
        g_up[...] = dot(normed[...], dup[...], TN).astype(BF)

    @pl.when(step >= ff_steps)
    def _():
        part = pl.ds((step - ff_steps) * ROW_TILE, ROW_TILE)
        value = resid[...]
        scaled, inv_std = row_stats(value)
        upstream = dnormed[part, :]
        above = cot[part, :].astype(F32)
        through = upstream * vecs[1:2]
        inner = (
            through
            - jnp.mean(through, axis=1, keepdims=True)
            - scaled * jnp.mean(through * scaled, axis=1, keepdims=True)
        )
        grad = above + inv_std * inner
        dresid[...] = grad
        low = grad.astype(BF)
        branches[part, :] = low
        dmixed[...] = dot(low, w_out[...], NT).astype(BF)
        layer_out[...] = (value + total[part, :] + vecs[3:4]).astype(BF)
        sums[0:1] += jnp.sum(low.astype(F32), axis=0, keepdims=True)
        sums[1:2] += jnp.sum(upstream * scaled, axis=0, keepdims=True)
        sums[2:3] += jnp.sum(upstream, axis=0, keepdims=True)
        sums[3:4] += jnp.sum(above, axis=0, keepdims=True)

    @pl.when(step == pl.num_programs(0) - 1)
    def _():
        g_out[...] = dot(mixed[...], branches[...], TN).astype(BF)


def mlp_back_kernel(ff_steps, *refs):
    mlp_back_body(pl.program_id(0), ff_steps, *refs)


def mlp_back_scatter_kernel(ff_steps, *refs):
    ins, grad, outs, reduced, scratch, comm = (
        refs[:10], refs[10], refs[11:18], refs[18], refs[19:23], refs[23:],
    )
    step = pl.program_id(0)
    place = Place()
    pl.when(step == 0)(lambda: greet(place.partners))
    cols = reduced.shape[1] // 4
    pieces = []
    for k in range(4):
        here = pl.ds(k * cols, cols)
        bufs = comm[k * 8 : k * 8 + 8]
        pieces.append(
            Scatter(
                place, grad.at[:, :, :, :, :, here], *bufs[:5], reduced.at[:, here], bufs[5:]
            )
        )
    run_stages(pieces, step, (0, 1, 2, 4, 5, 7, 9))
    mlp_back_body(step, ff_steps, *ins, *outs, *scratch)

    @pl.when(step == pl.num_programs(0) - 1)
    def _():
        pieces[3].stage(4)


def mlp_back(act, slope, w_up, w_down, cot, normed, resid, mixed, w_out, vecs, grad=None):
    rows, width = cot.shape
    hidden = w_up.shape[1]
    row_steps, ff_steps = rows // ROW_TILE, hidden // FF_TILE
    at_row = lambda s: (jnp.maximum(s - ff_steps, 0), 0)
    at_col = lambda s: (0, jnp.minimum(s, ff_steps - 1))
    at_ff = lambda s: (jnp.minimum(s, ff_steps - 1), 0)
    const = lambda s: (0, 0)
    hbm, vmem = pl.BlockSpec(memory_space=pl.ANY), pl.BlockSpec(memory_space=pltpu.VMEM)
    once = lambda *shape: pl.BlockSpec(shape, const, pipeline_mode=pl.Buffered(1))
    tall = pl.BlockSpec((rows, FF_TILE), at_col)
    tile = pl.BlockSpec((ROW_TILE, width), at_row)
    in_specs = [
        tall, tall, pl.BlockSpec((width, FF_TILE), at_col), pl.BlockSpec((FF_TILE, width), at_ff),
        once(rows, width), once(rows, width), tile, once(rows, width), once(width, width),
        once(8, width),
    ]
    out_specs = [
        pl.BlockSpec((width, FF_TILE), at_col), pl.BlockSpec((1, FF_TILE), at_col), tile, tile,
        tile, once(width, width), once(8, width),
    ]
    out_shape = [
        jax.ShapeDtypeStruct((width, hidden), BF),
        jax.ShapeDtypeStruct((1, hidden), F32),
        jax.ShapeDtypeStruct((rows, width), BF),
        jax.ShapeDtypeStruct((rows, width), F32),
        jax.ShapeDtypeStruct((rows, width), BF),
        jax.ShapeDtypeStruct((width, width), BF),
        jax.ShapeDtypeStruct((8, width), F32),
    ]
    scratch = [
        pltpu.VMEM((rows, width), F32),
        pltpu.VMEM((rows, width), F32),
        pltpu.VMEM((rows, width), BF),
        pltpu.VMEM((rows, FF_TILE), BF),
    ]
    params = dict(vmem_limit_bytes=62 * 2**20)
    args = [act, slope, w_up, w_down, cot, normed, resid, mixed, w_out, vecs]
    kernel = mlp_back_kernel
    if grad is not None:
        kernel = mlp_back_scatter_kernel
        part = grad.shape[0] // 32
        in_specs += [hbm]
        out_specs += [vmem]
        out_shape += [jax.ShapeDtypeStruct((part, width), F32)]
        scratch += scatter_scratch(part, width // 4) * 4
        params |= dict(collective_id=6, has_side_effects=True)
        args += [blocks(grad)]
    return pl.pallas_call(
        functools.partial(kernel, ff_steps),
        grid=(row_steps + ff_steps,),
        in_specs=in_specs,
        out_specs=out_specs,
        out_shape=out_shape,
        scratch_shapes=scratch,
        compiler_params=pltpu.CompilerParams(**params),
        name="mlp_back",
    )(*args)


TILE = 64


class Total:
    def __init__(self, place, value, arrived, send, recv):
        p = place
        self.rounds = [p.zp, [p.xp, p.yp, p.far], [p.sib]]
        self.value, self.arrived, self.send, self.recv = value, arrived, send, recv

    def copies(self, i):
        slot = sum(len(targets) for targets in self.rounds[:i])
        return slot, [
            mesh_copy(
                self.value.at[i], self.arrived.at[slot + k], self.send.at[slot + k],
                self.recv.at[slot + k], to,
            )
            for k, to in enumerate(self.rounds[i])
        ]

    def stage(self, number):
        if number > 0:
            slot, copies = self.copies(number - 1)
            total = self.value[number - 1]
            for k, copy in enumerate(copies):
                copy.wait()
                total = total + self.arrived[slot + k]
            self.value[number] = total
        if number < len(self.rounds):
            for copy in self.copies(number)[1]:
                copy.start()


def last_body(
    step, n0_ref, normed, dq, dk, dv, dn, w_q, tokens, dresid, vecs, sums, up_sums, kv_sums,
    out, grads, padded, outgoing, incoming, send, recv, dqw, vector_out,
):
    rows = dq.shape[0]
    ext, width = normed.shape
    images = Images(n0_ref[0], rows, ext)
    bases = [images.base(span[0]) for span in images.spans]
    me, peers = lax.axis_index(AXIS), lax.axis_size(AXIS)
    wide = slice(TILE, TILE + WIN)

    def halo(way):
        return mesh_copy(
            outgoing if way else dn.at[0], incoming.at[way], send.at[way], recv.at[way],
            me + 1 if way else me - 1,
        )

    def column_sums(value):
        return jnp.sum(value.astype(F32), axis=0, keepdims=True)

    @pl.when(step == 0)
    def _():
        outgoing[...] = jnp.where(images.third, dn[2], dn[1])
        pl.when(me > 0)(lambda: halo(0).start())
        pl.when(me < peers - 1)(lambda: halo(1).start())
        vector_out[...] = jnp.zeros(vector_out.shape, F32)
        vector_out[0:2] = kv_sums[0:2]
        vector_out[4:8] = sums[0:4]
        for k in range(up_sums.shape[1] // width):
            vector_out[8 + k : 9 + k] = up_sums[:, k * width : (k + 1) * width]
        vector_out[2:3] = column_sums(dq[...])
        padded[...] = jnp.zeros(padded.shape, BF)

        @pl.when(me == 0)
        def _():
            incoming[1] = jnp.zeros(incoming.shape[1:], BF)

        @pl.when(me == peers - 1)
        def _():
            incoming[0] = jnp.zeros(incoming.shape[1:], BF)

        for col in range(0, width, ROW_TILE):
            cols = pl.ds(col, ROW_TILE)
            grads[0, cols, :] = dot(normed[pl.ds(RIM, rows), cols], dq[...], TN).astype(BF)

    for which, part in ((1, dk), (2, dv)):
        @pl.when(step == which)
        def _():
            for col in range(0, width, ROW_TILE):
                cols = pl.ds(col, ROW_TILE)
                total = None
                for seg, base in enumerate(bases):
                    term = dot(normed[pl.ds(base * 16, WIN), cols], part[seg], TN)
                    total = term if total is None else total + term
                grads[which, cols, :] = total.astype(BF)
            if which == 2:
                vector_out[3:4] = (
                    column_sums(dv[0]) + column_sums(dv[1]) + column_sums(dv[2])
                )

    @pl.when((step >= 3) & (step < 7))
    def _():
        part = pl.ds((step - 3) * ROW_TILE, ROW_TILE)
        upstream = dot(dq[part, :], w_q[...], NT)
        dqw[part, :] = upstream
        scaled = row_stats(tokens[...].astype(F32))[0]
        vector_out[0:1] += jnp.sum(upstream * scaled, axis=0, keepdims=True)
        vector_out[1:2] += jnp.sum(upstream, axis=0, keepdims=True)

    @pl.when(step == 7)
    def _():
        @pl.when(me > 0)
        def _():
            halo(0).wait_send()
            halo(1).wait_recv()

        @pl.when(me < peers - 1)
        def _():
            halo(1).wait_send()
            halo(0).wait_recv()

        none = jnp.zeros((WIN, width), F32)
        stop = jnp.where(images.third, images.spans[2][1], images.spans[1][1])
        cut = (stop > RIM + rows) & (me < peers - 1)
        after = jnp.where(cut, incoming[0].astype(F32), none)
        before = jnp.where(images.spans[0][0] < RIM, incoming[1].astype(F32), none)
        padded[0, wide] = (dn[0].astype(F32) + before).astype(BF)
        padded[1, wide] = (dn[1].astype(F32) + jnp.where(images.third, none, after)).astype(BF)
        padded[2, wide] = (dn[2].astype(F32) + jnp.where(images.third, after, none)).astype(BF)

    @pl.when(step >= 7)
    def _():
        upstream = dqw[pl.ds((step - 7) * ROW_TILE, ROW_TILE), :]
        places = []
        for k in range(ROW_TILE // TILE):
            total = upstream[k * TILE : (k + 1) * TILE]
            for seg, base in enumerate(bases):
                off = jnp.maximum(
                    (RIM + TILE) // 16 + (step - 7) * (ROW_TILE // 16) + k * (TILE // 16) - base, 0
                )
                off = jnp.minimum(off, (WIN + TILE) // 16) * 16
                total = total + padded[seg, pl.ds(off, TILE), :].astype(F32)
            places.append(total)
        upstream = jnp.concatenate(places, axis=0)
        scaled, inv_std = row_stats(tokens[...].astype(F32))
        through = upstream * vecs[0:1]
        inner = (
            through
            - jnp.mean(through, axis=1, keepdims=True)
            - scaled * jnp.mean(through * scaled, axis=1, keepdims=True)
        )
        out[...] = dresid[...] + inv_std * inner


LAST_STEPS = 11


def last_kernel(*refs):
    step = pl.program_id(0)
    me, peers = lax.axis_index(AXIS), lax.axis_size(AXIS)
    ins, (out, vector_out, grads_out), scratch = refs[:13], refs[13:16], refs[16:]
    grads, padded, outgoing, incoming, send, recv, dqw = scratch
    pl.when(step == 0)(lambda: greet([], me > 0, me < peers - 1))
    last_body(step, *ins, out, grads, padded, outgoing, incoming, send, recv, dqw, vector_out)

    @pl.when(step == LAST_STEPS - 1)
    def _():
        grads_out[...] = grads[...]


def last_scatter_kernel(*refs):
    step = pl.program_id(0)
    me, peers = lax.axis_index(AXIS), lax.axis_size(AXIS)
    ins, (out, vector_out, reduced), scratch = refs[:13], refs[13:16], refs[16:]
    grads, padded, outgoing, incoming, send, recv, dqw = scratch[:7]
    vectors, arrived, vec_send, vec_recv = scratch[7:11]
    comm = scratch[11:]
    place = Place()
    pl.when(step == 0)(
        lambda: greet([*place.partners, place.far], me > 0, me < peers - 1)
    )
    pieces = [
        Scatter(
            place, grads.at[k], *comm[k * 8 : k * 8 + 5], reduced.at[:, pl.ds(k * UNIT, UNIT)],
            comm[k * 8 + 5 : k * 8 + 8], k == 0,
        )
        for k in range(3)
    ]
    total = Total(place, vectors, arrived, vec_send, vec_recv)
    for i in range(4):
        pl.when(step == 7 + i)(functools.partial(total.stage, i))
    run_stages(pieces, step, (1, 2, 3, 7, 8, 9))
    last_body(
        step, *ins, out, Flat(grads), padded, outgoing, incoming, send, recv, dqw, vectors.at[0]
    )

    @pl.when(step == LAST_STEPS - 1)
    def _():
        vector_out[...] = vectors[3]
        pieces[2].stage(4)


class Flat:
    def __init__(self, ref):
        self.ref = ref

    def __setitem__(self, index, value):
        k, rows, _ = index
        part = self.ref.shape[5]
        count = rows.size // part
        first = rows.start // part
        for i in range(0, count, 8):
            block = value[i * part : (i + 8) * part].reshape(2, 2, 2, part, value.shape[1])
            self.ref[k, (first + i) // 8] = block


def last(
    n0, normed, dq, dk, dv, dn, w_qkv, tokens, dresid, vecs, sums, up_sums, kv_sums, plan
):
    rows, width = dq.shape
    ext = normed.shape[0]
    peers = lax.axis_size(AXIS)
    const = lambda s: (0, 0)
    once = lambda *shape: pl.BlockSpec(
        shape, lambda s: (0,) * len(shape), pipeline_mode=pl.Buffered(1)
    )
    tile = pl.BlockSpec((ROW_TILE, width), lambda s: (jnp.maximum(s - 7, 0), 0))
    twice = pl.BlockSpec(
        (ROW_TILE, width), lambda s: (jnp.where(s < 7, jnp.maximum(s - 3, 0), s - 7), 0)
    )
    vmem = pl.BlockSpec(memory_space=pltpu.VMEM)
    in_specs = [
        pl.BlockSpec(memory_space=pltpu.SMEM),
        once(ext, width), once(rows, width), once(3, WIN, width), once(3, WIN, width),
        once(3, WIN, width), once(width, width), twice, tile, once(8, width), once(8, width),
        once(*up_sums.shape), once(8, width),
    ]
    vector_rows = 16
    shared = [
        pltpu.VMEM((3, WIN + 2 * TILE, width), BF),
        pltpu.VMEM((WIN, width), BF),
        pltpu.VMEM((2, WIN, width), BF),
        pltpu.SemaphoreType.DMA((2,)),
        pltpu.SemaphoreType.DMA((2,)),
        pltpu.VMEM((rows, width), F32),
    ]
    if plan:
        part = width // peers
        kernel, collective = last_scatter_kernel, 3
        scratch = [pltpu.VMEM((3, 4, 2, 2, 2, part, width), BF)] + shared + [
            pltpu.VMEM((4, vector_rows, width), F32),
            pltpu.VMEM((7, vector_rows, width), F32),
            pltpu.SemaphoreType.DMA((7,)),
            pltpu.SemaphoreType.DMA((7,)),
        ] + scatter_scratch(part, UNIT, tilt=True) + scatter_scratch(part, UNIT) * 2
        third_out = jax.ShapeDtypeStruct((part, 3 * width), F32)
    else:
        kernel, collective = last_kernel, 4
        scratch = [pltpu.VMEM((3, width, width), BF)] + shared
        third_out = jax.ShapeDtypeStruct((3, width, width), BF)
    return pl.pallas_call(
        kernel,
        grid=(LAST_STEPS,),
        in_specs=in_specs,
        out_specs=[tile, once(vector_rows, width), once(*third_out.shape)],
        out_shape=[
            jax.ShapeDtypeStruct((rows, width), F32),
            jax.ShapeDtypeStruct((vector_rows, width), F32),
            third_out,
        ],
        scratch_shapes=scratch,
        compiler_params=pltpu.CompilerParams(
            vmem_limit_bytes=62 * 2**20, collective_id=collective, has_side_effects=True
        ),
        name="last",
    )(n0, normed, dq, dk, dv, dn, w_qkv, tokens, dresid, vecs, sums, up_sums, kv_sums)


def shifted(value, by):
    peers = lax.axis_size(AXIS)
    pairs = [(i, i + by) for i in range(peers) if 0 <= i + by < peers]
    return lax.ppermute(value, AXIS, pairs)


def gathered(value):
    return lax.all_gather(value, AXIS, axis=0, tiled=True)


def scattered(value):
    return lax.psum_scatter(value, AXIS, scatter_dimension=0, tiled=True)


def local(
    tokens,
    image_ids,
    cotangent,
    norm1_gain,
    norm1_shift,
    qkv_weight,
    query_bias,
    value_bias,
    out_weight,
    out_bias,
    norm2_gain,
    norm2_shift,
    up_weight,
    up_bias,
    down_weight,
    down_bias,
):
    rows, width = tokens.shape
    me = lax.axis_index(AXIS)
    peers = lax.axis_size(AXIS)
    ext = -(-(rows + 2 * RIM + 64) // 128) * 128
    vectors = [
        norm1_gain, norm1_shift, query_bias, value_bias, out_bias, norm2_gain, norm2_shift,
        down_bias,
    ]
    part = norm1_gain.shape[0]
    block_plan = peers == 32
    if block_plan:
        lane = lax.broadcasted_iota(jnp.int32, (1, 128), 1) // part
        spread = jnp.tile(jnp.stack(vectors), (1, 128 // part))
        spread = jnp.where(lane == me % (128 // part), spread, jnp.zeros_like(spread))
        vec = jnp.concatenate(
            [spread, up_bias[None], jnp.zeros((VEC_ROWS - 9, 128), BF)], axis=0
        )
        queries, key_value, normed_ext, scaled_ext, w_qkv, vectors, u_bias, n0 = first(
            tokens, qkv_weight, vec, image_ids.reshape(-1, 128), ext
        )
        u_bias = u_bias[0]
        gain1 = vectors[0]
        vecs = vectors[4:8]
    else:
        n0 = jnp.sum((image_ids == image_ids[0]).astype(jnp.int32)).reshape(1)
        gathered_vec = gathered(jnp.concatenate([*vectors, up_bias])[None]).astype(F32)
        gain1, shift1, q_bias, v_bias, o_bias, gain2, shift2, d_bias = (
            gathered_vec[:, i * part : (i + 1) * part].reshape(-1) for i in range(8)
        )
        u_bias = gathered_vec[:, 8 * part :].reshape(-1)
        vecs = jnp.stack([o_bias, gain2, shift2, d_bias])
        w_qkv, w_out, w_up, w_down = map(
            gathered, (qkv_weight, out_weight, up_weight, down_weight)
        )
        low_rim = shifted(tokens[rows - RIM :], 1)
        high_rim = shifted(tokens[:RIM], -1)
        pad = jnp.zeros((ext - rows - 2 * RIM, width), BF)
        tokens_ext = jnp.concatenate([low_rim, tokens, high_rim, pad], axis=0).astype(F32)
        scaled_ext = row_stats(tokens_ext)[0]
        normed_ext = (scaled_ext * gain1 + shift1).astype(BF)
        scaled_ext = scaled_ext.astype(BF)
        normed_low = normed_ext[RIM : RIM + rows]
        queries = (dot(normed_low, w_qkv[:, :width]) + q_bias).astype(BF)
        key_value = (
            dot(normed_ext, w_qkv[:, width:])
            + jnp.concatenate([jnp.zeros_like(v_bias), v_bias])
        ).astype(BF)
    vecs = jnp.concatenate([vecs, jnp.zeros((4, width), F32)])
    if block_plan:
        mixed_low, lse, w_out, w_up = attend(
            n0, queries, key_value, (out_weight, up_weight)
        )
        w_out, w_up = w_out.reshape(width, -1), w_up.reshape(width, -1)
    else:
        mixed_low, lse = attend(n0, queries, key_value)

    args = (mixed_low, tokens, w_out, vecs, w_up, u_bias[None], cotangent)
    if block_plan:
        resid, normed_two, act, slope, grad_down, w_down = mlp_up(*args, down_weight)
        w_down = w_down.reshape(-1, width)
    else:
        resid, normed_two, act, slope, grad_down = mlp_up(*args)
    args = (act, slope, w_up, w_down, cotangent, normed_two, resid, mixed_low, w_out, vecs)
    if block_plan:
        grad_up, up_sums, layer_out, dresid, dmixed_low, grad_out, sums, r_down = mlp_back(
            *args, grad_down
        )
    else:
        grad_up, up_sums, layer_out, dresid, dmixed_low, grad_out, sums = mlp_back(*args)
        r_down = scattered(grad_down).astype(F32)
    if block_plan:
        dquery, dkey, dvalue, dnormed, kv_sums, r_out, r_up = attend_back(
            n0, queries, key_value, dmixed_low, lse, w_qkv, scaled_ext, (grad_out, grad_up)
        )
    else:
        dquery, dkey, dvalue, dnormed, kv_sums = attend_back(
            n0, queries, key_value, dmixed_low, lse, w_qkv, scaled_ext
        )
        r_out, r_up = (scattered(v).astype(F32) for v in (grad_out, grad_up))
    vecs = jnp.concatenate([gain1[None], jnp.zeros((7, width), F32)])
    grad_tokens, totals, r_qkv = last(
        n0, normed_ext, dquery, dkey, dvalue, dnormed, w_qkv, tokens, dresid, vecs, sums,
        up_sums, kv_sums, block_plan,
    )
    if not block_plan:
        totals = lax.psum(totals, AXIS)
        r_qkv = jnp.concatenate([scattered(v) for v in r_qkv], axis=1).astype(F32)
    owned = lax.dynamic_slice_in_dim(totals[:8], me * part, part, 1)
    size = u_bias.shape[0] // peers
    up_own = lax.dynamic_slice_in_dim(totals[8 : 8 + u_bias.shape[0] // width].reshape(-1), me * size, size)
    g = [owned[i] for i in range(8)] + [up_own]
    return (
        layer_out, grad_tokens, g[0], g[1], r_qkv, g[2], g[3], r_out, g[4], g[5], g[6], r_up,
        g[8], r_down, g[7],
    )


def solution(mesh):
    row, vec = P(AXIS, None), P(AXIS)
    return jax.shard_map(
        local,
        mesh=mesh,
        in_specs=(
            row, vec, row, vec, vec, row, vec, vec, row, vec, vec, vec, row, vec, row, vec,
        ),
        out_specs=(
            row, row, vec, vec, row, vec, vec, row, vec, vec, vec, row, vec, row, vec,
        ),
        check_vma=False,
    )
```

```python
import functools
import math

import jax
import jax.numpy as jnp
from jax import lax
from jax.experimental import pallas as pl
from jax.experimental.pallas import tpu as pltpu
from jax.sharding import PartitionSpec as P

HDIM = 64
IMG = 577
RIM = IMG - 1
WIN = 592
QB = 128
EPS = 1e-06
NEG = -1e30
AXIS = "fsdp"
BF = jnp.bfloat16
F32 = jnp.float32
NT = (((1,), (1,)), ((), ()))
TN = (((0,), (0,)), ((), ()))
NN = (((1,), (0,)), ((), ()))


def dot(a, b, dims=NN):
    return lax.dot_general(a, b, dims, preferred_element_type=F32)


def stacked(block):
    lane = lax.broadcasted_iota(jnp.int32, block.shape, 1)
    zero = jnp.zeros_like(block)
    return jnp.concatenate(
        [jnp.where(lane < HDIM, block, zero), jnp.where(lane >= HDIM, block, zero)], axis=0
    )


def unstacked(wide):
    return jnp.concatenate([wide[:HDIM, :QB], wide[HDIM:, QB:]], axis=0).T


def key_mask(low, high):
    row = lax.broadcasted_iota(jnp.int32, (WIN, QB), 0)
    bias = jnp.where((row >= low) & (row < high), 0.0, NEG)
    return jnp.concatenate([bias, bias], axis=1)


def mesh_copy(src, dst, send_sem, recv_sem, to):
    return pltpu.make_async_remote_copy(
        src_ref=src,
        dst_ref=dst,
        send_sem=send_sem,
        recv_sem=recv_sem,
        device_id=(to,),
        device_id_type=pl.DeviceIdType.MESH,
    )


class Place:
    def __init__(self):
        me = lax.axis_index(AXIS)
        self.c, self.x, self.y, self.z = me % 2, me // 2 % 2, me // 4 % 2, me // 8
        self.sib = self.at(self.z, self.y, self.x, 1 - self.c)
        self.xp = self.at(self.z, self.y, 1 - self.x, self.c)
        self.yp = self.at(self.z, 1 - self.y, self.x, self.c)
        self.zp = [self.at((self.z + k) % 4, self.y, self.x, self.c) for k in (1, 2, 3)]
        self.far = self.at(self.z, 1 - self.y, 1 - self.x, self.c)
        self.partners = [self.sib, self.xp, self.yp, *self.zp]

    @staticmethod
    def at(z, y, x, c):
        return ((z * 2 + y) * 2 + x) * 2 + c


def greet(partners, before=None, after=None):
    barrier = pltpu.get_barrier_semaphore()

    def hello(to):
        pl.semaphore_signal(
            barrier, inc=1, device_id=(to,), device_id_type=pl.DeviceIdType.MESH
        )

    for to in partners:
        hello(to)
    if before is None:
        pl.semaphore_wait(barrier, len(partners))
        return
    me = lax.axis_index(AXIS)
    pl.when(before)(lambda: hello(me - 1))
    pl.when(after)(lambda: hello(me + 1))
    pl.semaphore_wait(
        barrier, len(partners) + before.astype(jnp.int32) + after.astype(jnp.int32)
    )


class Gather:
    def __init__(self, place, shard, full, cols, send, recv, own, tilt=False):
        self.shard, self.own = shard.at[:, cols], own
        p, rows = place, shard.shape[0]
        half = rows // 2

        def block(y, x, part=slice(None)):
            return full.at[:, y, x, p.c, part, cols]

        mine = full.at[p.z, p.y, p.x, p.c, :, cols]
        self.local = lambda: pltpu.make_async_copy(self.shard, mine, own)

        def copy(i, src, dst, to):
            return lambda: mesh_copy(src, dst, send.at[i], recv.at[i], to)

        same = lambda i, ref, to: copy(i, ref, ref, to)
        first, second = pl.ds(0, half), pl.ds(half, half)
        self.z = [copy(i, self.shard, mine, to) for i, to in enumerate(p.zp)]
        self.xy = [same(3, block(p.y, p.x), p.xp), same(4, block(p.y, p.x), p.yp)]
        self.far = [
            same(5, block(p.y, 1 - p.x, first), p.yp),
            same(6, block(1 - p.y, p.x, second), p.xp),
        ]
        if tilt:
            self.far = [same(5, block(p.y, 1 - p.x), p.yp)]
        self.pair = [
            same(7, block(p.y, p.x), p.sib),
            same(8, block(p.y, 1 - p.x), p.sib),
            same(9, block(1 - p.y, p.x), p.sib),
            same(10, block(1 - p.y, 1 - p.x), p.sib),
        ]

    def stage(self, number):
        if number == 0:
            self.local().start()
            for c in self.z:
                c().start()
        elif number == 1:
            self.local().wait()
            for c in self.z:
                c().wait()
            for c in (*self.xy, self.pair[0]):
                c().start()
        elif number == 2:
            for c in self.xy:
                c().wait()
            for c in (*self.far, self.pair[1], self.pair[2]):
                c().start()
        elif number == 3:
            for c in self.far:
                c().wait()
            self.pair[3]().start()
        else:
            for c in self.pair:
                c().wait()


GATHER_SEMS = 11


def run_stages(pieces, step, steps):
    for at in sorted(set(steps)):
        todo = [
            (q, pieces[tick - q])
            for tick, when in enumerate(steps)
            if when == at
            for q in range(5)
            if 0 <= tick - q < len(pieces)
        ]

        @pl.when(step == at)
        def _():
            for q, piece in todo:
                piece.stage(q)


def run_rest(pieces, ticks):
    for tick in range(ticks, len(pieces) + 4):
        for q in range(5):
            if 0 <= tick - q < len(pieces):
                pieces[tick - q].stage(q)


class Scatter:
    def __init__(self, place, grad, held, from_pair, far, side, line, out, sems, tilt=False):
        self.tilt = tilt
        self.p, self.out = place, out
        self.held, self.from_pair, self.far, self.side, self.line = held, from_pair, far, side, line
        p, rows = place, held.shape[3]
        self.half = rows // 2
        own, send, recv = sems
        first, second = pl.ds(0, self.half), pl.ds(self.half, self.half)

        def copy(i, src, dst, to):
            return lambda: mesh_copy(src, dst, send.at[i], recv.at[i], to)

        self.load = lambda: pltpu.make_async_copy(grad.at[:, :, :, p.c], held, own)
        self.to_pair = copy(0, grad.at[:, :, :, 1 - p.c], from_pair, p.sib)
        self.to_far = [
            copy(1, held.at[:, 1 - p.y, 1 - p.x, first], far.at[0], p.xp),
            copy(2, held.at[:, 1 - p.y, 1 - p.x, second], far.at[1], p.yp),
        ]
        if tilt:
            self.to_far = [copy(1, held.at[:, 1 - p.y, 1 - p.x], far, p.yp)]
        self.to_side = [
            copy(3, held.at[:, p.y, 1 - p.x], side.at[0], p.xp),
            copy(4, held.at[:, 1 - p.y, p.x], side.at[1], p.yp),
        ]
        self.to_line = [
            copy(5 + k, held.at[(p.z + k + 1) % 4, p.y, p.x], line.at[k], to)
            for k, to in enumerate(p.zp)
        ]

    def stage(self, number):
        p, half = self.p, self.half
        held, far, side, line = self.held, self.far, self.side, self.line
        if number == 0:
            self.load().start()
            self.to_pair().start()
        elif number == 1:
            self.load().wait()
            self.to_pair().wait()

            @pl.loop(0, 4)
            def _(z):
                for y in range(2):
                    for x in range(2):
                        held[z, y, x] = held[z, y, x] + self.from_pair[z, y, x]

            for c in self.to_far:
                c().start()
        elif number == 2:
            for c in self.to_far:
                c().wait()

            @pl.loop(0, 4)
            def _(z):
                if self.tilt:
                    held[z, p.y, 1 - p.x] = (
                        held[z, p.y, 1 - p.x].astype(F32) + far[z].astype(F32)
                    ).astype(held.dtype)
                    return
                held[z, 1 - p.y, p.x, :half] = (
                    held[z, 1 - p.y, p.x, :half].astype(F32) + far[0, z].astype(F32)
                ).astype(held.dtype)
                held[z, p.y, 1 - p.x, half:] = (
                    held[z, p.y, 1 - p.x, half:].astype(F32) + far[1, z].astype(F32)
                ).astype(held.dtype)

            for c in self.to_side:
                c().start()
        elif number == 3:
            for c in self.to_side:
                c().wait()

            @pl.loop(0, 4)
            def _(z):
                held[z, p.y, p.x] = (
                    held[z, p.y, p.x].astype(F32)
                    + side[0, z].astype(F32)
                    + side[1, z].astype(F32)
                ).astype(held.dtype)

            for c in self.to_line:
                c().start()
        else:
            for c in self.to_line:
                c().wait()
            self.out[...] = (
                held[p.z, p.y, p.x].astype(F32)
                + line[0].astype(F32)
                + line[1].astype(F32)
                + line[2].astype(F32)
            )


SCATTER_SEMS = 8
UNIT = 1024


def scatter_scratch(rows, cols, dtype=BF, tilt=False):
    return [
        pltpu.VMEM((4, 2, 2, rows, cols), dtype),
        pltpu.VMEM((4, 2, 2, rows, cols), dtype),
        pltpu.VMEM((4, rows, cols) if tilt else (2, 4, rows // 2, cols), dtype),
        pltpu.VMEM((2, 4, rows, cols), dtype),
        pltpu.VMEM((3, rows, cols), dtype),
        pltpu.SemaphoreType.DMA,
        pltpu.SemaphoreType.DMA((SCATTER_SEMS,)),
        pltpu.SemaphoreType.DMA((SCATTER_SEMS,)),
    ]


def blocks(value):
    return value.reshape(4, 2, 2, 2, value.shape[0] // 32, value.shape[1])


VEC_ROWS = 16


def first_body(
    rows, tokens, wide, vec, ids, q_out, kv_out, normed_out, scaled_out, w_out, vecs_out,
    bias_out, mlp_out, n0_out, near, normed, scaled, weights, gathered_vec, queries, pairs, send, recv,
    own, halo_send, halo_recv, load, store,
):
    place = Place()
    me, peers = lax.axis_index(AXIS), lax.axis_size(AXIS)
    greet(place.partners, me > 0, me < peers - 1)
    width = near.shape[1]
    mine = pl.ds(RIM, rows)

    def halo(way):
        if way == 0:
            src, dst, to = tokens.at[pl.ds(0, RIM)], near.at[pl.ds(RIM + rows, RIM)], me - 1
        else:
            src, dst, to = tokens.at[pl.ds(rows - RIM, RIM)], near.at[pl.ds(0, RIM)], me + 1
        return mesh_copy(src, dst, halo_send.at[way], halo_recv.at[way], to)

    pieces = [
        Gather(
            place, vec, gathered_vec, pl.ds(0, vec.shape[1]), send.at[0], recv.at[0], own.at[0],
            True,
        )
    ]
    for i, k in enumerate((1, 2, 0)):
        pieces.append(
            Gather(
                place, wide, weights, pl.ds(k * UNIT, UNIT), send.at[i + 1], recv.at[i + 1],
                own.at[i + 1],
            )
        )
    g_vec, g_k, g_v, g_q = pieces
    own_copy = pltpu.make_async_copy(tokens, near.at[mine], load)
    own_copy.start()
    g_vec.stage(0)
    g_k.stage(0)
    pl.when(me > 0)(lambda: halo(0).start())
    pl.when(me < peers - 1)(lambda: halo(1).start())
    n0_out[0] = jnp.sum((ids[...] == ids[0:1, 0:1]).astype(jnp.int32))
    near[pl.ds(2 * RIM + rows, near.shape[0] - rows - 2 * RIM), :] = jnp.zeros(
        (near.shape[0] - rows - 2 * RIM, width), BF
    )

    @pl.when(me == 0)
    def _():
        near[pl.ds(0, RIM), :] = jnp.zeros((RIM, width), BF)

    @pl.when(me == peers - 1)
    def _():
        near[pl.ds(RIM + rows, RIM), :] = jnp.zeros((RIM, width), BF)

    g_vec.stage(1)
    g_k.stage(1)
    g_v.stage(0)
    g_vec.stage(2)
    g_vec.stage(3)
    g_vec.stage(4)
    table = []
    for z in range(4):
        for y in range(2):
            group = [gathered_vec[z, y, x, c].astype(F32) for x in range(2) for c in range(2)]
            table.append(group[0] + group[1] + group[2] + group[3])
            for x in range(2):
                for c in range(2):
                    at = ((z * 2 + y) * 2 + x) * 2 + c
                    bias_out[:, at * 128 : (at + 1) * 128] = group[x * 2 + c][8:9]
    vecs = jnp.concatenate(table, axis=1)
    vecs_out[...] = vecs
    mlp_out[...] = vecs[4:12]
    gain, shift = vecs[0:1], vecs[1:2]
    q_bias, v_bias = vecs[2:3], vecs[3:4]

    def norm(first, count):
        part = pl.ds(first, count)
        value = row_stats(near[part, :].astype(F32))[0]
        scaled[part, :] = value.astype(BF)
        normed[part, :] = (value * gain + shift).astype(BF)

    own_copy.wait()
    for row in range(RIM, RIM + rows, 256):
        norm(row, 256)
    g_k.stage(2)
    g_v.stage(1)
    g_q.stage(0)
    g_k.stage(3)
    g_v.stage(2)
    g_q.stage(1)
    g_k.stage(4)

    def full(k):
        return weights[:, :, :, :, :, pl.ds(k * UNIT, UNIT)].reshape(width, UNIT)

    def project(target, k, first, stop, bias, at):
        matrix = full(k)
        for row in range(first, stop, 256):
            size = min(256, stop - row)
            value = dot(normed[pl.ds(row, size), :], matrix)
            value = value if bias is None else value + bias
            target[pl.ds(row - at[0], size), pl.ds(at[1], UNIT)] = value.astype(BF)

    last_row = near.shape[0]
    project(pairs, 1, RIM, RIM + rows, None, (0, 0))
    g_v.stage(3)
    g_q.stage(2)

    @pl.when(me > 0)
    def _():
        halo(0).wait_send()
        halo(1).wait_recv()

    @pl.when(me < peers - 1)
    def _():
        halo(1).wait_send()
        halo(0).wait_recv()

    for row in range(0, RIM, 192):
        norm(row, 192)
    for row in range(RIM + rows, last_row, 176):
        norm(row, 176)
    normed_copy = pltpu.make_async_copy(normed, normed_out, store.at[0])
    normed_copy.start()
    scaled_copy = pltpu.make_async_copy(scaled, scaled_out, store.at[5])
    scaled_copy.start()
    project(pairs, 1, 0, RIM, None, (0, 0))
    project(pairs, 1, RIM + rows, last_row, None, (0, 0))
    k_copy = pltpu.make_async_copy(
        pairs.at[:, pl.ds(0, UNIT)], kv_out.at[:, pl.ds(0, UNIT)], store.at[1]
    )
    k_copy.start()
    g_v.stage(4)
    g_q.stage(3)
    project(pairs, 2, 0, last_row, v_bias, (0, UNIT))
    v_copy = pltpu.make_async_copy(
        pairs.at[:, pl.ds(UNIT, UNIT)], kv_out.at[:, pl.ds(UNIT, UNIT)], store.at[2]
    )
    v_copy.start()
    g_q.stage(4)
    w_copy = pltpu.make_async_copy(weights, w_out, store.at[3])
    w_copy.start()
    project(queries, 0, RIM, RIM + rows, q_bias, (RIM, 0))
    q_copy = pltpu.make_async_copy(queries, q_out, store.at[4])
    q_copy.start()
    for copy in (normed_copy, scaled_copy, k_copy, v_copy, w_copy, q_copy):
        copy.wait()


def first(tokens, wide, vec, ids, ext):
    rows, width = tokens.shape
    part = wide.shape[0]
    hbm, vmem = pl.BlockSpec(memory_space=pl.ANY), pl.BlockSpec(memory_space=pltpu.VMEM)
    queries, key_value, normed, scaled, w_qkv, vecs, bias, mlp_vecs, n0 = pl.pallas_call(
        functools.partial(first_body, rows),
        in_specs=[hbm] * 3 + [vmem],
        out_specs=[hbm] * 5 + [vmem] * 3 + [pl.BlockSpec(memory_space=pltpu.SMEM)],
        out_shape=[
            jax.ShapeDtypeStruct((rows, width), BF),
            jax.ShapeDtypeStruct((ext, 2 * width), BF),
            jax.ShapeDtypeStruct((ext, width), BF),
            jax.ShapeDtypeStruct((ext, width), BF),
            jax.ShapeDtypeStruct((4, 2, 2, 2, *wide.shape), BF),
            jax.ShapeDtypeStruct((VEC_ROWS, width), F32),
            jax.ShapeDtypeStruct((1, 32 * 128), F32),
            jax.ShapeDtypeStruct((8, width), F32),
            jax.ShapeDtypeStruct((1,), jnp.int32),
        ],
        scratch_shapes=[
            pltpu.VMEM((ext, width), BF),
            pltpu.VMEM((ext, width), BF),
            pltpu.VMEM((ext, width), BF),
            pltpu.VMEM((4, 2, 2, 2, *wide.shape), BF),
            pltpu.VMEM((4, 2, 2, 2, *vec.shape), BF),
            pltpu.VMEM((rows, width), BF),
            pltpu.VMEM((ext, 2 * width), BF),
            pltpu.SemaphoreType.DMA((4, GATHER_SEMS)),
            pltpu.SemaphoreType.DMA((4, GATHER_SEMS)),
            pltpu.SemaphoreType.DMA((4,)),
            pltpu.SemaphoreType.DMA((2,)),
            pltpu.SemaphoreType.DMA((2,)),
            pltpu.SemaphoreType.DMA,
            pltpu.SemaphoreType.DMA((6,)),
        ],
        compiler_params=pltpu.CompilerParams(
            collective_id=0, has_side_effects=True, vmem_limit_bytes=62 * 2**20
        ),
        name="first",
    )(tokens, wide, vec, ids)
    w_qkv = w_qkv.reshape(width, wide.shape[1])
    return queries, key_value, normed, scaled, w_qkv, vecs, bias, mlp_vecs, n0


ITEMS = 10
BACK_GROUP = 5
GROUP = 5


class Images:
    def __init__(self, n0, rows, ext):
        self.n0, self.n1, self.rows, self.ext = n0, n0 + IMG, rows, ext
        me, peers = lax.axis_index(AXIS), lax.axis_size(AXIS)
        limit = jnp.where(me == peers - 1, RIM + rows, 2 * RIM + rows)
        start0 = jnp.where(me == 0, RIM, n0 - 1)
        start1 = RIM + n0
        start2 = start1 + IMG
        self.spans = (
            (start0, start1),
            (start1, jnp.minimum(start1 + IMG, limit)),
            (start2, jnp.minimum(start2 + IMG, limit)),
        )
        one = lambda flag: jnp.where(flag, 1, 0)
        self.b0, self.b1 = lax.div(n0, QB), lax.div(self.n1, QB)
        self.d0 = one(self.b0 * QB != n0)
        self.d1 = one((self.n1 < rows) & (self.b1 * QB != self.n1))
        self.third = self.n1 < rows
        self.end0 = lax.div(n0 - 1, QB)
        self.end1 = lax.div(self.n1 - 1, QB) + self.d0
        self.one = one

    def base(self, start):
        return jnp.minimum(lax.div(start, 16), (self.ext - WIN) // 16)

    def segment(self, item):
        return self.one(item > self.end0) + self.one(item > self.end1)

    def item(self, item):
        blk = (
            item
            - self.d0 * self.one(item > self.b0)
            - self.d1 * self.one(item > self.b1 + self.d0)
        )
        used = blk < self.rows // QB
        blk = jnp.minimum(blk, self.rows // QB - 1)
        seg = self.segment(item)
        choose = lambda i: jnp.where(
            seg == 0, self.spans[0][i], jnp.where(seg == 1, self.spans[1][i], self.spans[2][i])
        )
        start, stop = choose(0), choose(1)
        base = self.base(start) * 16
        row0 = blk * QB
        low = jnp.maximum(start - RIM - row0, 0)
        high = jnp.where(used, jnp.minimum(stop - RIM - row0, QB), 0)
        return blk, row0, base, start - base, stop - base, low, high

    def of_block(self, blk):
        at0 = self.d0 * self.one(blk == self.b0)
        at1 = self.d1 * self.one(blk == self.b1)
        first = blk + self.d0 * self.one(blk > self.b0) + self.d1 * self.one(blk > self.b1)
        split = jnp.where(at0 == 1, self.n0, jnp.where(at1 == 1, self.n1, self.rows)) - blk * QB
        return first, first + at0 + at1, split


def attend_body(n0_ref, q_ref, k_ref, v_ref, out_ref, lse_ref, parts, parts_lse):
    rows = q_ref.shape[0]
    images = Images(n0_ref[0], rows, k_ref.shape[0])

    def scores_of(item):
        _, row0, base, low, high, _, _ = images.item(item)
        queries = stacked(q_ref[pl.ds(row0, QB), :]) * jnp.asarray(0.125, BF)
        scores = dot(k_ref[pl.ds(base, WIN), :], queries, NT)
        return scores + key_mask(low, high), base

    def softmax_of(scores):
        top = jnp.max(scores, axis=0, keepdims=True)
        terms = jnp.exp(scores - top)
        total = jnp.sum(terms, axis=0, keepdims=True)
        return terms.astype(BF), top, total

    @pl.loop(0, ITEMS // GROUP)
    def _(step):
        items = [step * GROUP + g for g in range(GROUP)]
        scored = [scores_of(item) for item in items]
        soft = [softmax_of(scores) for scores, _ in scored]
        mixed = [
            dot(v_ref[pl.ds(base, WIN), :], terms, TN) / total
            for (_, base), (terms, _, total) in zip(scored, soft)
        ]
        for item, value, (_, top, total) in zip(items, mixed, soft):
            parts[item] = unstacked(value)
            parts_lse[item] = jnp.broadcast_to(top + jnp.log(total), parts_lse.shape[1:])

    for blk in range(rows // QB):
        first, last, split = images.of_block(blk)
        row = lax.broadcasted_iota(jnp.int32, (QB, 2 * HDIM), 0)
        out_ref[pl.ds(blk * QB, QB), :] = jnp.where(
            row < split, parts[first], parts[last]
        ).astype(BF)
        lane = lax.broadcasted_iota(jnp.int32, parts_lse.shape[1:], 1) % QB
        lse_ref[0, pl.ds(blk, 1), :] = jnp.where(
            lane < split, parts_lse[first], parts_lse[last]
        )[:1]


def attend_kernel(n0_ref, q_ref, k_ref, v_ref, out_ref, lse_ref, parts, parts_lse):
    attend_body(n0_ref, q_ref, k_ref, v_ref, out_ref, lse_ref, parts, parts_lse)


def attend_gather_kernel(
    n0_ref, q_ref, k_ref, v_ref, w_out, w_up, out_ref, lse_ref, full_out, full_up,
    parts, parts_lse, send, recv, own,
):
    tick = pl.program_id(0)
    place = Place()
    pl.when(tick == 0)(lambda: greet(place.partners))
    pieces = []
    for shard, full in ((w_out, full_out), (w_up, full_up)):
        for k in range(shard.shape[1] // UNIT):
            i = len(pieces)
            pieces.append(
                Gather(
                    place, shard, full, pl.ds(k * UNIT, UNIT), send.at[i], recv.at[i], own.at[i]
                )
            )
    run_stages(pieces, tick, range(8))
    attend_body(n0_ref, q_ref, k_ref, v_ref, out_ref, lse_ref, parts, parts_lse)

    @pl.when(tick == 7)
    def _():
        pieces[-1].stage(4)


def attend(n0, queries, key_value, shards=None):
    rows, width = queries.shape
    pairs = width // (2 * HDIM)
    ext = key_value.shape[0]
    hbm = pl.BlockSpec(memory_space=pl.ANY)
    in_specs = [
        pl.BlockSpec(memory_space=pltpu.SMEM),
        pl.BlockSpec((rows, 2 * HDIM), lambda p: (0, p)),
        pl.BlockSpec((ext, 2 * HDIM), lambda p: (0, p)),
        pl.BlockSpec((ext, 2 * HDIM), lambda p: (0, pairs + p)),
    ]
    out_specs = [
        pl.BlockSpec((rows, 2 * HDIM), lambda p: (0, p)),
        pl.BlockSpec((1, rows // QB, 2 * QB), lambda p: (p, 0, 0)),
    ]
    out_shape = [
        jax.ShapeDtypeStruct((rows, width), BF),
        jax.ShapeDtypeStruct((pairs, rows // QB, 2 * QB), F32),
    ]
    scratch = [
        pltpu.VMEM((ITEMS, QB, 2 * HDIM), F32),
        pltpu.VMEM((ITEMS, 8, 2 * QB), F32),
    ]
    params = dict(vmem_limit_bytes=62 * 2**20)
    args = [n0, queries, key_value, key_value]
    kernel = attend_kernel
    if shards is not None:
        kernel = attend_gather_kernel
        in_specs += [hbm] * 2
        out_specs += [hbm] * 2
        out_shape += [jax.ShapeDtypeStruct((4, 2, 2, 2, *v.shape), BF) for v in shards]
        count = sum(v.shape[1] // UNIT for v in shards)
        scratch += [
            pltpu.SemaphoreType.DMA((count, GATHER_SEMS)),
            pltpu.SemaphoreType.DMA((count, GATHER_SEMS)),
            pltpu.SemaphoreType.DMA((count,)),
        ]
        params |= dict(collective_id=1, has_side_effects=True)
        args += shards
    return pl.pallas_call(
        kernel,
        grid=(pairs,),
        in_specs=in_specs,
        out_specs=out_specs,
        out_shape=out_shape,
        scratch_shapes=scratch,
        compiler_params=pltpu.CompilerParams(**params),
        name="attend",
    )(*args)


def attend_back_body(
    pair, n0_ref, q_ref, k_ref, v_ref, up_ref, lse_ref, wk_ref, wv_ref, scaled_ref, dq_ref, dk_ref, dv_ref,
    dn_ref, sums_ref, slots, parts, total,
):
    rows = q_ref.shape[0]
    images = Images(n0_ref[0], rows, k_ref.shape[0])

    @pl.when(pair == 0)
    def _():
        slots[0] = jnp.zeros(slots.shape[1:], F32)
        total[...] = jnp.zeros(total.shape, F32)

    lane = lax.broadcasted_iota(jnp.int32, (1, 2 * QB), 1) % QB

    def begin(item):
        blk, row0, base, low, high, first, stop = images.item(item)
        queries = stacked(q_ref[pl.ds(row0, QB), :]) * jnp.asarray(0.125, BF)
        upstream = stacked(up_ref[pl.ds(row0, QB), :])
        here = (lane >= first) & (lane < stop)
        lse = jnp.where(here, lse_ref[0, pl.ds(blk, 1), :], -NEG)
        scores = dot(k_ref[pl.ds(base, WIN), :], queries, NT)
        dprobs = dot(v_ref[pl.ds(base, WIN), :], upstream, NT)
        return base, queries, upstream, scores + key_mask(low, high), lse, dprobs

    def middle(scores, lse, dprobs):
        probs = jnp.exp(scores - lse)
        row_dot = jnp.sum(probs * dprobs, axis=0, keepdims=True)
        return probs.astype(BF), (probs * (dprobs - row_dot)).astype(BF)

    def finish(item, base, queries, upstream, probs, dscores):
        keep = (item > 0) & (images.segment(item) == images.segment(item - 1))
        old = jnp.where(keep, slots[item], jnp.zeros(slots.shape[1:], F32))
        slots[item + 1, :, : 2 * HDIM] = old[:, : 2 * HDIM] + dot(dscores, queries)
        slots[item + 1, :, 2 * HDIM :] = old[:, 2 * HDIM :] + dot(probs, upstream)
        parts[item] = unstacked(dot(k_ref[pl.ds(base, WIN), :], dscores, TN)) * 0.125

    @pl.loop(0, ITEMS // BACK_GROUP)
    def _(step):
        items = [step * BACK_GROUP + g for g in range(BACK_GROUP)]
        begun = [begin(items[0])]
        done = []
        for g in range(BACK_GROUP + 1):
            if g + 1 < BACK_GROUP:
                begun.append(begin(items[g + 1]))
            if g < BACK_GROUP:
                done.append(middle(*begun[g][3:]))
            if g > 0:
                finish(items[g - 1], *begun[g - 1][:3], *done[g - 1])

    for blk in range(rows // QB):
        first, last, split = images.of_block(blk)
        row = lax.broadcasted_iota(jnp.int32, (QB, 2 * HDIM), 0)
        dq_ref[pl.ds(blk * QB, QB), :] = jnp.where(
            row < split, parts[first], parts[last]
        ).astype(BF)
    ends = (
        images.end0 + 1,
        jnp.minimum(images.end1, (rows - 1) // QB + images.d0) + 1,
        jnp.where(images.third, ITEMS, 0),
    )
    weights = jnp.concatenate([wk_ref[...], wv_ref[...]], axis=1)
    for seg, end in enumerate(ends):
        both = slots[end].astype(BF)
        dk_ref[seg] = both[:, : 2 * HDIM]
        dv_ref[seg] = both[:, 2 * HDIM :]
        total[seg] += dot(both, weights, NT)

    @pl.when(pair == pl.num_programs(0) - 1)
    def _():
        dn_ref[...] = total[...].astype(BF)
        sums_ref[...] = jnp.zeros(sums_ref.shape, F32)
        for seg, span in enumerate(images.spans):
            window = scaled_ref[pl.ds(images.base(span[0]) * 16, WIN), :].astype(F32)
            sums_ref[0:1] += jnp.sum(total[seg] * window, axis=0, keepdims=True)
            sums_ref[1:2] += jnp.sum(total[seg], axis=0, keepdims=True)


def attend_back_kernel(*refs):
    attend_back_body(pl.program_id(0), *refs)


def attend_back_scatter_kernel(*refs):
    base, (g_out, g_up), rest = refs[:9], refs[9:11], refs[11:]
    outs, (r_out, r_up), scratch = rest[:5], rest[5:7], rest[7:]
    mine, comm = scratch[:3], scratch[3:]
    pair = pl.program_id(0)
    place = Place()
    pl.when(pair == 0)(lambda: greet(place.partners))
    pieces = []
    for grad, out in ((g_out, r_out), (g_up, r_up)):
        for k in range(grad.shape[5] // UNIT):
            cols = pl.ds(k * UNIT, UNIT)
            bufs = comm[len(pieces) * 8 : len(pieces) * 8 + 8]
            pieces.append(
                Scatter(
                    place, grad.at[:, :, :, :, :, cols], *bufs[:5], out.at[:, cols], bufs[5:]
                )
            )
    run_stages(pieces, pair, range(8))
    attend_back_body(pair, *base, *outs, *mine)

    @pl.when(pair == pl.num_programs(0) - 1)
    def _():
        pieces[-1].stage(4)


def attend_back(n0, queries, key_value, upstream, lse, w_qkv, scaled, grads=None):
    rows, width = queries.shape
    pairs = width // (2 * HDIM)
    ext = key_value.shape[0]
    hbm, vmem = pl.BlockSpec(memory_space=pl.ANY), pl.BlockSpec(memory_space=pltpu.VMEM)
    own = pl.BlockSpec((rows, 2 * HDIM), lambda p: (0, p))
    windows = pl.BlockSpec((3, WIN, 2 * HDIM), lambda p: (0, 0, p))
    in_specs = [
        pl.BlockSpec(memory_space=pltpu.SMEM),
        own,
        pl.BlockSpec((ext, 2 * HDIM), lambda p: (0, p)),
        pl.BlockSpec((ext, 2 * HDIM), lambda p: (0, pairs + p)),
        own,
        pl.BlockSpec((1, rows // QB, 2 * QB), lambda p: (p, 0, 0)),
        pl.BlockSpec((width, 2 * HDIM), lambda p: (0, pairs + p)),
        pl.BlockSpec((width, 2 * HDIM), lambda p: (0, 2 * pairs + p)),
        pl.BlockSpec((ext, width), lambda p: (0, 0), pipeline_mode=pl.Buffered(1)),
    ]
    out_specs = [
        own, windows, windows,
        pl.BlockSpec((3, WIN, width), lambda p: (0, 0, 0), pipeline_mode=pl.Buffered(1)),
        pl.BlockSpec((8, width), lambda p: (0, 0)),
    ]
    out_shape = [jax.ShapeDtypeStruct((rows, width), BF)]
    out_shape += [jax.ShapeDtypeStruct((3, WIN, width), BF)] * 3
    out_shape += [jax.ShapeDtypeStruct((8, width), F32)]
    scratch = [
        pltpu.VMEM((ITEMS + 1, WIN, 4 * HDIM), F32),
        pltpu.VMEM((ITEMS, QB, 2 * HDIM), F32),
        pltpu.VMEM((3, WIN, width), F32),
    ]
    args = [n0, queries, key_value, key_value, upstream, lse, w_qkv, w_qkv, scaled]
    kernel, params = attend_back_kernel, dict(vmem_limit_bytes=62 * 2**20)
    if grads is not None:
        kernel = attend_back_scatter_kernel
        params |= dict(collective_id=2, has_side_effects=True)
        args += map(blocks, grads)
        in_specs += [hbm] * 2
        out_specs += [vmem] * 2
        out_shape += [jax.ShapeDtypeStruct((v.shape[0] // 32, v.shape[1]), F32) for v in grads]
        for v in grads:
            scratch += scatter_scratch(v.shape[0] // 32, UNIT) * (v.shape[1] // UNIT)
    return pl.pallas_call(
        kernel,
        grid=(pairs,),
        in_specs=in_specs,
        out_specs=out_specs,
        out_shape=out_shape,
        scratch_shapes=scratch,
        compiler_params=pltpu.CompilerParams(**params),
        name="attend_back",
    )(*args)


ROW_TILE = 256
FF_TILE = 512
ROOT_HALF = 1.0 / math.sqrt(2.0)
PDF_SCALE = 1.0 / math.sqrt(2.0 * math.pi)


def row_stats(value):
    mean = jnp.mean(value, axis=1, keepdims=True)
    center = value - mean
    inv_std = lax.rsqrt(jnp.mean(center * center, axis=1, keepdims=True) + EPS)
    return center * inv_std, inv_std


def mlp_up_body(
    step, row_steps, mixed, tokens, w_out, vecs, w_up, up_bias, cot, resid, normed, act, slope,
    g_down, held,
):
    @pl.when(step < row_steps)
    def _():
        value = tokens[...].astype(F32) + dot(mixed[...], w_out[...]) + vecs[0:1]
        resid[...] = value
        low = (row_stats(value)[0] * vecs[1:2] + vecs[2:3]).astype(BF)
        normed[...] = low
        held[pl.ds(step * ROW_TILE, ROW_TILE), :] = low

    @pl.when(step >= row_steps)
    def _():
        rows = held.shape[0]

        for row in range(0, rows, ROW_TILE):
            part = pl.ds(row, ROW_TILE)
            upward = dot(held[part, :], w_up[...]) + up_bias[...]
            cdf = 0.5 * (1.0 + lax.erf(upward * ROOT_HALF))
            pdf = jnp.exp(-0.5 * upward * upward) * PDF_SCALE
            act[part, :] = (upward * cdf).astype(BF)
            slope[part, :] = (cdf + upward * pdf).astype(BF)
        g_down[...] = dot(act[...], cot[...], TN).astype(BF)


def mlp_up_kernel(row_steps, *refs):
    mlp_up_body(pl.program_id(0), row_steps, *refs)


def mlp_up_gather_kernel(row_steps, *refs):
    ins, shard, outs, full = refs[:7], refs[7], refs[8:13], refs[13]
    held, send, recv, own = refs[14:]
    step = pl.program_id(0)
    place = Place()
    pl.when(step == 0)(lambda: greet(place.partners))
    cols = shard.shape[1] // 4
    pieces = [
        Gather(place, shard, full, pl.ds(k * cols, cols), send.at[k], recv.at[k], own.at[k])
        for k in range(4)
    ]
    run_stages(pieces, step, (0, 4, 7, 9, 11))
    mlp_up_body(step, row_steps, *ins, *outs, held)
    pl.when(step == pl.num_programs(0) - 1)(lambda: run_rest(pieces, 5))


def mlp_up(mixed, tokens, w_out, vecs, w_up, up_bias, cot, shard=None):
    rows, width = tokens.shape
    hidden = w_up.shape[1]
    row_steps, ff_steps = rows // ROW_TILE, hidden // FF_TILE
    at_row = lambda s: (jnp.minimum(s, row_steps - 1), 0)
    at_col = lambda s: (0, jnp.maximum(s - row_steps, 0))
    at_ff = lambda s: (jnp.maximum(s - row_steps, 0), 0)
    const = lambda s: (0, 0)
    hbm = pl.BlockSpec(memory_space=pl.ANY)
    tall = pl.BlockSpec((rows, FF_TILE), at_col)
    in_specs = [
        pl.BlockSpec((ROW_TILE, width), at_row),
        pl.BlockSpec((ROW_TILE, width), at_row),
        pl.BlockSpec((width, width), const),
        pl.BlockSpec((8, width), const),
        pl.BlockSpec((width, FF_TILE), at_col),
        pl.BlockSpec((1, FF_TILE), at_col),
        pl.BlockSpec((rows, width), const),
    ]
    out_specs = [
        pl.BlockSpec((ROW_TILE, width), at_row),
        pl.BlockSpec((ROW_TILE, width), at_row),
        tall,
        tall,
        pl.BlockSpec((FF_TILE, width), at_ff),
    ]
    out_shape = [
        jax.ShapeDtypeStruct((rows, width), F32),
        jax.ShapeDtypeStruct((rows, width), BF),
        jax.ShapeDtypeStruct((rows, hidden), BF),
        jax.ShapeDtypeStruct((rows, hidden), BF),
        jax.ShapeDtypeStruct((hidden, width), BF),
    ]
    scratch = [pltpu.VMEM((rows, width), BF)]
    params = dict(vmem_limit_bytes=62 * 2**20)
    args = [mixed, tokens, w_out, vecs, w_up, up_bias, cot]
    kernel = mlp_up_kernel
    if shard is not None:
        kernel = mlp_up_gather_kernel
        in_specs += [hbm]
        out_specs += [hbm]
        out_shape += [jax.ShapeDtypeStruct((4, 2, 2, 2, *shard.shape), BF)]
        scratch += [
            pltpu.SemaphoreType.DMA((4, GATHER_SEMS)),
            pltpu.SemaphoreType.DMA((4, GATHER_SEMS)),
            pltpu.SemaphoreType.DMA((4,)),
        ]
        params |= dict(collective_id=5, has_side_effects=True)
        args += [shard]
    return pl.pallas_call(
        functools.partial(kernel, row_steps),
        grid=(row_steps + ff_steps,),
        in_specs=in_specs,
        out_specs=out_specs,
        out_shape=out_shape,
        scratch_shapes=scratch,
        compiler_params=pltpu.CompilerParams(**params),
        name="mlp_up",
    )(*args)


def mlp_back_body(
    step, ff_steps, act, slope, w_up, w_down, cot, normed, resid, mixed, w_out, vecs,
    g_up, up_sums, layer_out, dresid, dmixed, g_out, sums, total, dnormed, branches, dup,
):
    rows, width = cot.shape

    @pl.when(step == 0)
    def _():
        total[...] = jnp.zeros(total.shape, F32)
        dnormed[...] = jnp.zeros(dnormed.shape, F32)
        sums[...] = jnp.zeros(sums.shape, F32)

    @pl.when(step < ff_steps)
    def _():
        count = jnp.zeros(up_sums.shape, F32)
        for row in range(0, rows, ROW_TILE):
            part = pl.ds(row, ROW_TILE)
            total[part, :] += dot(act[part, :], w_down[...])
            dact = dot(cot[part, :], w_down[...], NT)
            low = (dact * slope[part, :].astype(F32)).astype(BF)
            dup[part, :] = low
            count += jnp.sum(low.astype(F32), axis=0, keepdims=True)
            dnormed[part, :] += dot(low, w_up[...], NT)
        up_sums[...] = count
        g_up[...] = dot(normed[...], dup[...], TN).astype(BF)

    @pl.when(step >= ff_steps)
    def _():
        part = pl.ds((step - ff_steps) * ROW_TILE, ROW_TILE)
        value = resid[...]
        scaled, inv_std = row_stats(value)
        upstream = dnormed[part, :]
        above = cot[part, :].astype(F32)
        through = upstream * vecs[1:2]
        inner = (
            through
            - jnp.mean(through, axis=1, keepdims=True)
            - scaled * jnp.mean(through * scaled, axis=1, keepdims=True)
        )
        grad = above + inv_std * inner
        dresid[...] = grad
        low = grad.astype(BF)
        branches[part, :] = low
        dmixed[...] = dot(low, w_out[...], NT).astype(BF)
        layer_out[...] = (value + total[part, :] + vecs[3:4]).astype(BF)
        sums[0:1] += jnp.sum(low.astype(F32), axis=0, keepdims=True)
        sums[1:2] += jnp.sum(upstream * scaled, axis=0, keepdims=True)
        sums[2:3] += jnp.sum(upstream, axis=0, keepdims=True)
        sums[3:4] += jnp.sum(above, axis=0, keepdims=True)

    @pl.when(step == pl.num_programs(0) - 1)
    def _():
        g_out[...] = dot(mixed[...], branches[...], TN).astype(BF)


def mlp_back_kernel(ff_steps, *refs):
    mlp_back_body(pl.program_id(0), ff_steps, *refs)


def mlp_back_scatter_kernel(ff_steps, *refs):
    ins, grad, outs, reduced, scratch, comm = (
        refs[:10], refs[10], refs[11:18], refs[18], refs[19:23], refs[23:],
    )
    step = pl.program_id(0)
    place = Place()
    pl.when(step == 0)(lambda: greet(place.partners))
    cols = reduced.shape[1] // 4
    pieces = []
    for k in range(4):
        here = pl.ds(k * cols, cols)
        bufs = comm[k * 8 : k * 8 + 8]
        pieces.append(
            Scatter(
                place, grad.at[:, :, :, :, :, here], *bufs[:5], reduced.at[:, here], bufs[5:]
            )
        )
    run_stages(pieces, step, (0, 1, 2, 4, 5, 7, 9))
    mlp_back_body(step, ff_steps, *ins, *outs, *scratch)

    @pl.when(step == pl.num_programs(0) - 1)
    def _():
        pieces[3].stage(4)


def mlp_back(act, slope, w_up, w_down, cot, normed, resid, mixed, w_out, vecs, grad=None):
    rows, width = cot.shape
    hidden = w_up.shape[1]
    row_steps, ff_steps = rows // ROW_TILE, hidden // FF_TILE
    at_row = lambda s: (jnp.maximum(s - ff_steps, 0), 0)
    at_col = lambda s: (0, jnp.minimum(s, ff_steps - 1))
    at_ff = lambda s: (jnp.minimum(s, ff_steps - 1), 0)
    const = lambda s: (0, 0)
    hbm, vmem = pl.BlockSpec(memory_space=pl.ANY), pl.BlockSpec(memory_space=pltpu.VMEM)
    once = lambda *shape: pl.BlockSpec(shape, const, pipeline_mode=pl.Buffered(1))
    tall = pl.BlockSpec((rows, FF_TILE), at_col)
    tile = pl.BlockSpec((ROW_TILE, width), at_row)
    in_specs = [
        tall, tall, pl.BlockSpec((width, FF_TILE), at_col), pl.BlockSpec((FF_TILE, width), at_ff),
        once(rows, width), once(rows, width), tile, once(rows, width), once(width, width),
        once(8, width),
    ]
    out_specs = [
        pl.BlockSpec((width, FF_TILE), at_col), pl.BlockSpec((1, FF_TILE), at_col), tile, tile,
        tile, once(width, width), once(8, width),
    ]
    out_shape = [
        jax.ShapeDtypeStruct((width, hidden), BF),
        jax.ShapeDtypeStruct((1, hidden), F32),
        jax.ShapeDtypeStruct((rows, width), BF),
        jax.ShapeDtypeStruct((rows, width), F32),
        jax.ShapeDtypeStruct((rows, width), BF),
        jax.ShapeDtypeStruct((width, width), BF),
        jax.ShapeDtypeStruct((8, width), F32),
    ]
    scratch = [
        pltpu.VMEM((rows, width), F32),
        pltpu.VMEM((rows, width), F32),
        pltpu.VMEM((rows, width), BF),
        pltpu.VMEM((rows, FF_TILE), BF),
    ]
    params = dict(vmem_limit_bytes=62 * 2**20)
    args = [act, slope, w_up, w_down, cot, normed, resid, mixed, w_out, vecs]
    kernel = mlp_back_kernel
    if grad is not None:
        kernel = mlp_back_scatter_kernel
        part = grad.shape[0] // 32
        in_specs += [hbm]
        out_specs += [vmem]
        out_shape += [jax.ShapeDtypeStruct((part, width), F32)]
        scratch += scatter_scratch(part, width // 4) * 4
        params |= dict(collective_id=6, has_side_effects=True)
        args += [blocks(grad)]
    return pl.pallas_call(
        functools.partial(kernel, ff_steps),
        grid=(row_steps + ff_steps,),
        in_specs=in_specs,
        out_specs=out_specs,
        out_shape=out_shape,
        scratch_shapes=scratch,
        compiler_params=pltpu.CompilerParams(**params),
        name="mlp_back",
    )(*args)


TILE = 64


class Total:
    def __init__(self, place, value, arrived, send, recv):
        p = place
        self.rounds = [p.zp, [p.xp, p.yp, p.far], [p.sib]]
        self.value, self.arrived, self.send, self.recv = value, arrived, send, recv

    def copies(self, i):
        slot = sum(len(targets) for targets in self.rounds[:i])
        return slot, [
            mesh_copy(
                self.value.at[i], self.arrived.at[slot + k], self.send.at[slot + k],
                self.recv.at[slot + k], to,
            )
            for k, to in enumerate(self.rounds[i])
        ]

    def stage(self, number):
        if number > 0:
            slot, copies = self.copies(number - 1)
            total = self.value[number - 1]
            for k, copy in enumerate(copies):
                copy.wait()
                total = total + self.arrived[slot + k]
            self.value[number] = total
        if number < len(self.rounds):
            for copy in self.copies(number)[1]:
                copy.start()


def last_body(
    step, n0_ref, normed, dq, dk, dv, dn, w_q, tokens, dresid, vecs, sums, up_sums, kv_sums,
    out, grads, padded, outgoing, incoming, send, recv, dqw, vector_out,
):
    rows = dq.shape[0]
    ext, width = normed.shape
    images = Images(n0_ref[0], rows, ext)
    bases = [images.base(span[0]) for span in images.spans]
    me, peers = lax.axis_index(AXIS), lax.axis_size(AXIS)
    wide = slice(TILE, TILE + WIN)

    def halo(way):
        return mesh_copy(
            outgoing if way else dn.at[0], incoming.at[way], send.at[way], recv.at[way],
            me + 1 if way else me - 1,
        )

    def column_sums(value):
        return jnp.sum(value.astype(F32), axis=0, keepdims=True)

    @pl.when(step == 0)
    def _():
        outgoing[...] = jnp.where(images.third, dn[2], dn[1])
        pl.when(me > 0)(lambda: halo(0).start())
        pl.when(me < peers - 1)(lambda: halo(1).start())
        vector_out[...] = jnp.zeros(vector_out.shape, F32)
        vector_out[0:2] = kv_sums[0:2]
        vector_out[4:8] = sums[0:4]
        for k in range(up_sums.shape[1] // width):
            vector_out[8 + k : 9 + k] = up_sums[:, k * width : (k + 1) * width]
        vector_out[2:3] = column_sums(dq[...])
        padded[...] = jnp.zeros(padded.shape, BF)

        @pl.when(me == 0)
        def _():
            incoming[1] = jnp.zeros(incoming.shape[1:], BF)

        @pl.when(me == peers - 1)
        def _():
            incoming[0] = jnp.zeros(incoming.shape[1:], BF)

        for col in range(0, width, ROW_TILE):
            cols = pl.ds(col, ROW_TILE)
            grads[0, cols, :] = dot(normed[pl.ds(RIM, rows), cols], dq[...], TN).astype(BF)

    for which, part in ((1, dk), (2, dv)):
        @pl.when(step == which)
        def _():
            for col in range(0, width, ROW_TILE):
                cols = pl.ds(col, ROW_TILE)
                total = None
                for seg, base in enumerate(bases):
                    term = dot(normed[pl.ds(base * 16, WIN), cols], part[seg], TN)
                    total = term if total is None else total + term
                grads[which, cols, :] = total.astype(BF)
            if which == 2:
                vector_out[3:4] = (
                    column_sums(dv[0]) + column_sums(dv[1]) + column_sums(dv[2])
                )

    @pl.when((step >= 3) & (step < 7))
    def _():
        part = pl.ds((step - 3) * ROW_TILE, ROW_TILE)
        upstream = dot(dq[part, :], w_q[...], NT)
        dqw[part, :] = upstream
        scaled = row_stats(tokens[...].astype(F32))[0]
        vector_out[0:1] += jnp.sum(upstream * scaled, axis=0, keepdims=True)
        vector_out[1:2] += jnp.sum(upstream, axis=0, keepdims=True)

    @pl.when(step == 7)
    def _():
        @pl.when(me > 0)
        def _():
            halo(0).wait_send()
            halo(1).wait_recv()

        @pl.when(me < peers - 1)
        def _():
            halo(1).wait_send()
            halo(0).wait_recv()

        none = jnp.zeros((WIN, width), F32)
        stop = jnp.where(images.third, images.spans[2][1], images.spans[1][1])
        cut = (stop > RIM + rows) & (me < peers - 1)
        after = jnp.where(cut, incoming[0].astype(F32), none)
        before = jnp.where(images.spans[0][0] < RIM, incoming[1].astype(F32), none)
        padded[0, wide] = (dn[0].astype(F32) + before).astype(BF)
        padded[1, wide] = (dn[1].astype(F32) + jnp.where(images.third, none, after)).astype(BF)
        padded[2, wide] = (dn[2].astype(F32) + jnp.where(images.third, after, none)).astype(BF)

    @pl.when(step >= 7)
    def _():
        upstream = dqw[pl.ds((step - 7) * ROW_TILE, ROW_TILE), :]
        places = []
        for k in range(ROW_TILE // TILE):
            total = upstream[k * TILE : (k + 1) * TILE]
            for seg, base in enumerate(bases):
                off = jnp.maximum(
                    (RIM + TILE) // 16 + (step - 7) * (ROW_TILE // 16) + k * (TILE // 16) - base, 0
                )
                off = jnp.minimum(off, (WIN + TILE) // 16) * 16
                total = total + padded[seg, pl.ds(off, TILE), :].astype(F32)
            places.append(total)
        upstream = jnp.concatenate(places, axis=0)
        scaled, inv_std = row_stats(tokens[...].astype(F32))
        through = upstream * vecs[0:1]
        inner = (
            through
            - jnp.mean(through, axis=1, keepdims=True)
            - scaled * jnp.mean(through * scaled, axis=1, keepdims=True)
        )
        out[...] = dresid[...] + inv_std * inner


LAST_STEPS = 11


def last_kernel(*refs):
    step = pl.program_id(0)
    me, peers = lax.axis_index(AXIS), lax.axis_size(AXIS)
    ins, (out, vector_out, grads_out), scratch = refs[:13], refs[13:16], refs[16:]
    grads, padded, outgoing, incoming, send, recv, dqw = scratch
    pl.when(step == 0)(lambda: greet([], me > 0, me < peers - 1))
    last_body(step, *ins, out, grads, padded, outgoing, incoming, send, recv, dqw, vector_out)

    @pl.when(step == LAST_STEPS - 1)
    def _():
        grads_out[...] = grads[...]


def last_scatter_kernel(*refs):
    step = pl.program_id(0)
    me, peers = lax.axis_index(AXIS), lax.axis_size(AXIS)
    ins, (out, vector_out, reduced, up_own), scratch = refs[:13], refs[13:17], refs[17:]
    grads, padded, outgoing, incoming, send, recv, dqw = scratch[:7]
    vectors, arrived, vec_send, vec_recv = scratch[7:11]
    comm = scratch[11:]
    place = Place()
    pl.when(step == 0)(
        lambda: greet([*place.partners, place.far], me > 0, me < peers - 1)
    )
    pieces = [
        Scatter(
            place, grads.at[k], *comm[k * 8 : k * 8 + 5], reduced.at[:, pl.ds(k * UNIT, UNIT)],
            comm[k * 8 + 5 : k * 8 + 8], k == 0,
        )
        for k in range(3)
    ]
    total = Total(place, vectors, arrived, vec_send, vec_recv)
    part = vector_out.shape[1]
    for i in range(4):
        pl.when(step == 7 + i)(functools.partial(total.stage, i))
    run_stages(pieces, step, (1, 2, 3, 7, 8, 9))
    last_body(
        step, *ins, out, Flat(grads), padded, outgoing, incoming, send, recv, dqw, vectors.at[0]
    )

    @pl.when(step == LAST_STEPS - 1)
    def _():
        own, up = vectors[3, :8, :part], vectors[3, 8:9, :128]
        for k in range(1, peers):
            own = jnp.where(me == k, vectors[3, :8, k * part : (k + 1) * part], own)
            row, col = 8 + k // 8, k % 8 * 128
            up = jnp.where(me == k, vectors[3, row : row + 1, col : col + 128], up)
        vector_out[...] = own
        up_own[...] = up
        pieces[2].stage(4)


class Flat:
    def __init__(self, ref):
        self.ref = ref

    def __setitem__(self, index, value):
        k, rows, _ = index
        part = self.ref.shape[5]
        count = rows.size // part
        first = rows.start // part
        for i in range(0, count, 8):
            block = value[i * part : (i + 8) * part].reshape(2, 2, 2, part, value.shape[1])
            self.ref[k, (first + i) // 8] = block


def last(
    n0, normed, dq, dk, dv, dn, w_qkv, tokens, dresid, vecs, sums, up_sums, kv_sums, plan
):
    rows, width = dq.shape
    ext = normed.shape[0]
    peers = lax.axis_size(AXIS)
    const = lambda s: (0, 0)
    once = lambda *shape: pl.BlockSpec(
        shape, lambda s: (0,) * len(shape), pipeline_mode=pl.Buffered(1)
    )
    tile = pl.BlockSpec((ROW_TILE, width), lambda s: (jnp.maximum(s - 7, 0), 0))
    twice = pl.BlockSpec(
        (ROW_TILE, width), lambda s: (jnp.where(s < 7, jnp.maximum(s - 3, 0), s - 7), 0)
    )
    vmem = pl.BlockSpec(memory_space=pltpu.VMEM)
    in_specs = [
        pl.BlockSpec(memory_space=pltpu.SMEM),
        once(ext, width), once(rows, width), once(3, WIN, width), once(3, WIN, width),
        once(3, WIN, width), once(width, width), twice, tile, once(*vecs.shape), once(8, width),
        once(*up_sums.shape), once(8, width),
    ]
    vector_rows = 16
    shared = [
        pltpu.VMEM((3, WIN + 2 * TILE, width), BF),
        pltpu.VMEM((WIN, width), BF),
        pltpu.VMEM((2, WIN, width), BF),
        pltpu.SemaphoreType.DMA((2,)),
        pltpu.SemaphoreType.DMA((2,)),
        pltpu.VMEM((rows, width), F32),
    ]
    if plan:
        part = width // peers
        kernel, collective = last_scatter_kernel, 3
        scratch = [pltpu.VMEM((3, 4, 2, 2, 2, part, width), BF)] + shared + [
            pltpu.VMEM((4, vector_rows, width), F32),
            pltpu.VMEM((7, vector_rows, width), F32),
            pltpu.SemaphoreType.DMA((7,)),
            pltpu.SemaphoreType.DMA((7,)),
        ] + scatter_scratch(part, UNIT, tilt=True) + scatter_scratch(part, UNIT) * 2
        third_out = jax.ShapeDtypeStruct((part, 3 * width), F32)
        vector_shapes = [(8, part), (1, 128)]
    else:
        kernel, collective = last_kernel, 4
        scratch = [pltpu.VMEM((3, width, width), BF)] + shared
        third_out = jax.ShapeDtypeStruct((3, width, width), BF)
        vector_shapes = [(vector_rows, width)]
    return pl.pallas_call(
        kernel,
        grid=(LAST_STEPS,),
        in_specs=in_specs,
        out_specs=[tile, once(*vector_shapes[0]), once(*third_out.shape)]
        + [once(*v) for v in vector_shapes[1:]],
        out_shape=[
            jax.ShapeDtypeStruct((rows, width), F32),
            jax.ShapeDtypeStruct(vector_shapes[0], F32),
            third_out,
            *(jax.ShapeDtypeStruct(v, F32) for v in vector_shapes[1:]),
        ],
        scratch_shapes=scratch,
        compiler_params=pltpu.CompilerParams(
            vmem_limit_bytes=61 * 2**20, collective_id=collective, has_side_effects=True
        ),
        name="last",
    )(n0, normed, dq, dk, dv, dn, w_qkv, tokens, dresid, vecs, sums, up_sums, kv_sums)


def shifted(value, by):
    peers = lax.axis_size(AXIS)
    pairs = [(i, i + by) for i in range(peers) if 0 <= i + by < peers]
    return lax.ppermute(value, AXIS, pairs)


def gathered(value):
    return lax.all_gather(value, AXIS, axis=0, tiled=True)


def scattered(value):
    return lax.psum_scatter(value, AXIS, scatter_dimension=0, tiled=True)


def local(
    tokens,
    image_ids,
    cotangent,
    norm1_gain,
    norm1_shift,
    qkv_weight,
    query_bias,
    value_bias,
    out_weight,
    out_bias,
    norm2_gain,
    norm2_shift,
    up_weight,
    up_bias,
    down_weight,
    down_bias,
):
    rows, width = tokens.shape
    me = lax.axis_index(AXIS)
    peers = lax.axis_size(AXIS)
    ext = -(-(rows + 2 * RIM + 64) // 128) * 128
    vectors = [
        norm1_gain, norm1_shift, query_bias, value_bias, out_bias, norm2_gain, norm2_shift,
        down_bias,
    ]
    part = norm1_gain.shape[0]
    block_plan = peers == 32
    if block_plan:
        lane = lax.broadcasted_iota(jnp.int32, (1, 128), 1) // part
        spread = jnp.tile(jnp.stack(vectors), (1, 128 // part))
        spread = jnp.where(lane == me % (128 // part), spread, jnp.zeros_like(spread))
        vec = jnp.concatenate(
            [spread, up_bias[None], jnp.zeros((VEC_ROWS - 9, 128), BF)], axis=0
        )
        (
            queries, key_value, normed_ext, scaled_ext, w_qkv, vectors, u_bias, vecs, n0
        ) = first(tokens, qkv_weight, vec, image_ids.reshape(-1, 128), ext)
        u_bias = u_bias[0]
    else:
        n0 = jnp.sum((image_ids == image_ids[0]).astype(jnp.int32)).reshape(1)
        gathered_vec = gathered(jnp.concatenate([*vectors, up_bias])[None]).astype(F32)
        gain1, shift1, q_bias, v_bias, o_bias, gain2, shift2, d_bias = (
            gathered_vec[:, i * part : (i + 1) * part].reshape(-1) for i in range(8)
        )
        u_bias = gathered_vec[:, 8 * part :].reshape(-1)
        none = [jnp.zeros_like(d_bias)] * 4
        vecs = jnp.stack([o_bias, gain2, shift2, d_bias] + none)
        vectors = jnp.stack([gain1] + none * 3 + none[:3])
        w_qkv, w_out, w_up, w_down = map(
            gathered, (qkv_weight, out_weight, up_weight, down_weight)
        )
        low_rim = shifted(tokens[rows - RIM :], 1)
        high_rim = shifted(tokens[:RIM], -1)
        pad = jnp.zeros((ext - rows - 2 * RIM, width), BF)
        tokens_ext = jnp.concatenate([low_rim, tokens, high_rim, pad], axis=0).astype(F32)
        scaled_ext = row_stats(tokens_ext)[0]
        normed_ext = (scaled_ext * gain1 + shift1).astype(BF)
        scaled_ext = scaled_ext.astype(BF)
        normed_low = normed_ext[RIM : RIM + rows]
        queries = (dot(normed_low, w_qkv[:, :width]) + q_bias).astype(BF)
        key_value = (
            dot(normed_ext, w_qkv[:, width:])
            + jnp.concatenate([jnp.zeros_like(v_bias), v_bias])
        ).astype(BF)
    if block_plan:
        mixed_low, lse, w_out, w_up = attend(
            n0, queries, key_value, (out_weight, up_weight)
        )
        w_out, w_up = w_out.reshape(width, -1), w_up.reshape(width, -1)
    else:
        mixed_low, lse = attend(n0, queries, key_value)

    args = (mixed_low, tokens, w_out, vecs, w_up, u_bias[None], cotangent)
    if block_plan:
        resid, normed_two, act, slope, grad_down, w_down = mlp_up(*args, down_weight)
        w_down = w_down.reshape(-1, width)
    else:
        resid, normed_two, act, slope, grad_down = mlp_up(*args)
    args = (act, slope, w_up, w_down, cotangent, normed_two, resid, mixed_low, w_out, vecs)
    if block_plan:
        grad_up, up_sums, layer_out, dresid, dmixed_low, grad_out, sums, r_down = mlp_back(
            *args, grad_down
        )
    else:
        grad_up, up_sums, layer_out, dresid, dmixed_low, grad_out, sums = mlp_back(*args)
        r_down = scattered(grad_down).astype(F32)
    if block_plan:
        dquery, dkey, dvalue, dnormed, kv_sums, r_out, r_up = attend_back(
            n0, queries, key_value, dmixed_low, lse, w_qkv, scaled_ext, (grad_out, grad_up)
        )
    else:
        dquery, dkey, dvalue, dnormed, kv_sums = attend_back(
            n0, queries, key_value, dmixed_low, lse, w_qkv, scaled_ext
        )
        r_out, r_up = (scattered(v).astype(F32) for v in (grad_out, grad_up))
    grad_tokens, totals, r_qkv, *up_own = last(
        n0, normed_ext, dquery, dkey, dvalue, dnormed, w_qkv, tokens, dresid, vectors, sums,
        up_sums, kv_sums, block_plan,
    )
    if block_plan:
        owned, up_own = totals, up_own[0][0]
    else:
        totals = lax.psum(totals, AXIS)
        r_qkv = jnp.concatenate([scattered(v) for v in r_qkv], axis=1).astype(F32)
        owned = lax.dynamic_slice_in_dim(totals[:8], me * part, part, 1)
        size = u_bias.shape[0] // peers
        up_rows = totals[8 : 8 + u_bias.shape[0] // width].reshape(-1)
        up_own = lax.dynamic_slice_in_dim(up_rows, me * size, size)
    g = [owned[i] for i in range(8)] + [up_own]
    return (
        layer_out, grad_tokens, g[0], g[1], r_qkv, g[2], g[3], r_out, g[4], g[5], g[6], r_up,
        g[8], r_down, g[7],
    )


def solution(mesh):
    row, vec = P(AXIS, None), P(AXIS)
    return jax.shard_map(
        local,
        mesh=mesh,
        in_specs=(
            row, vec, row, vec, vec, row, vec, vec, row, vec, vec, vec, row, vec, row, vec,
        ),
        out_specs=(
            row, row, vec, vec, row, vec, vec, row, vec, vec, vec, row, vec, row, vec,
        ),
        check_vma=False,
    )
```

```python
import functools
import math

import jax
import jax.numpy as jnp
from jax import lax
from jax.experimental import pallas as pl
from jax.experimental.pallas import tpu as pltpu
from jax.sharding import PartitionSpec as P

HDIM = 64
IMG = 577
RIM = IMG - 1
WIN = 592
QB = 128
EPS = 1e-06
NEG = -1e30
AXIS = "fsdp"
BF = jnp.bfloat16
F32 = jnp.float32
NT = (((1,), (1,)), ((), ()))
TN = (((0,), (0,)), ((), ()))
NN = (((1,), (0,)), ((), ()))


def dot(a, b, dims=NN):
    return lax.dot_general(a, b, dims, preferred_element_type=F32)


def stacked(block):
    lane = lax.broadcasted_iota(jnp.int32, block.shape, 1)
    zero = jnp.zeros_like(block)
    return jnp.concatenate(
        [jnp.where(lane < HDIM, block, zero), jnp.where(lane >= HDIM, block, zero)], axis=0
    )


def unstacked(wide):
    return jnp.concatenate([wide[:HDIM, :QB], wide[HDIM:, QB:]], axis=0).T


def key_mask(low, high):
    row = lax.broadcasted_iota(jnp.int32, (WIN, QB), 0)
    bias = jnp.where((row >= low) & (row < high), 0.0, NEG)
    return jnp.concatenate([bias, bias], axis=1)


def mesh_copy(src, dst, send_sem, recv_sem, to):
    return pltpu.make_async_remote_copy(
        src_ref=src,
        dst_ref=dst,
        send_sem=send_sem,
        recv_sem=recv_sem,
        device_id=(to,),
        device_id_type=pl.DeviceIdType.MESH,
    )


class Place:
    def __init__(self):
        me = lax.axis_index(AXIS)
        self.c, self.x, self.y, self.z = me % 2, me // 2 % 2, me // 4 % 2, me // 8
        self.sib = self.at(self.z, self.y, self.x, 1 - self.c)
        self.xp = self.at(self.z, self.y, 1 - self.x, self.c)
        self.yp = self.at(self.z, 1 - self.y, self.x, self.c)
        self.zp = [self.at((self.z + k) % 4, self.y, self.x, self.c) for k in (1, 2, 3)]
        self.far = self.at(self.z, 1 - self.y, 1 - self.x, self.c)
        self.partners = [self.sib, self.xp, self.yp, *self.zp]

    @staticmethod
    def at(z, y, x, c):
        return ((z * 2 + y) * 2 + x) * 2 + c


def greet(partners, before=None, after=None):
    barrier = pltpu.get_barrier_semaphore()

    def hello(to):
        pl.semaphore_signal(
            barrier, inc=1, device_id=(to,), device_id_type=pl.DeviceIdType.MESH
        )

    for to in partners:
        hello(to)
    if before is None:
        pl.semaphore_wait(barrier, len(partners))
        return
    me = lax.axis_index(AXIS)
    pl.when(before)(lambda: hello(me - 1))
    pl.when(after)(lambda: hello(me + 1))
    pl.semaphore_wait(
        barrier, len(partners) + before.astype(jnp.int32) + after.astype(jnp.int32)
    )


class Gather:
    def __init__(self, place, shard, full, cols, send, recv, own, tilt=False):
        self.shard, self.own = shard.at[:, cols], own
        p, rows = place, shard.shape[0]
        half = rows // 2

        def block(y, x, part=slice(None)):
            return full.at[:, y, x, p.c, part, cols]

        mine = full.at[p.z, p.y, p.x, p.c, :, cols]
        self.local = lambda: pltpu.make_async_copy(self.shard, mine, own)

        def copy(i, src, dst, to):
            return lambda: mesh_copy(src, dst, send.at[i], recv.at[i], to)

        same = lambda i, ref, to: copy(i, ref, ref, to)
        first, second = pl.ds(0, half), pl.ds(half, half)
        self.z = [copy(i, self.shard, mine, to) for i, to in enumerate(p.zp)]
        self.xy = [same(3, block(p.y, p.x), p.xp), same(4, block(p.y, p.x), p.yp)]
        self.far = [
            same(5, block(p.y, 1 - p.x, first), p.yp),
            same(6, block(1 - p.y, p.x, second), p.xp),
        ]
        if tilt:
            self.far = [same(5, block(p.y, 1 - p.x), p.yp)]
        self.pair = [
            same(7, block(p.y, p.x), p.sib),
            same(8, block(p.y, 1 - p.x), p.sib),
            same(9, block(1 - p.y, p.x), p.sib),
            same(10, block(1 - p.y, 1 - p.x), p.sib),
        ]

    def stage(self, number):
        if number == 0:
            self.local().start()
            for c in self.z:
                c().start()
        elif number == 1:
            self.local().wait()
            for c in self.z:
                c().wait()
            for c in (*self.xy, self.pair[0]):
                c().start()
        elif number == 2:
            for c in self.xy:
                c().wait()
            for c in (*self.far, self.pair[1], self.pair[2]):
                c().start()
        elif number == 3:
            for c in self.far:
                c().wait()
            self.pair[3]().start()
        else:
            for c in self.pair:
                c().wait()


GATHER_SEMS = 11


class Column:
    def __init__(self, place, shard, column, send, recv, own):
        mine = column.at[place.z]
        self.local = lambda: pltpu.make_async_copy(shard, mine, own)
        self.z = [
            lambda i=i, to=to: mesh_copy(shard, mine, send.at[i], recv.at[i], to)
            for i, to in enumerate(place.zp)
        ]

    def start(self):
        self.local().start()
        for c in self.z:
            c().start()

    def wait(self):
        self.local().wait()
        for c in self.z:
            c().wait()


def column_scratch(count):
    return [
        pltpu.SemaphoreType.DMA((count, 3)),
        pltpu.SemaphoreType.DMA((count, 3)),
        pltpu.SemaphoreType.DMA((count,)),
    ]


class GatherRest:
    def __init__(self, place, column, full, cols, send, recv, own):
        p, half = place, column.shape[1] // 2
        first, second = pl.ds(0, half), pl.ds(half, half)
        held = column.at[:, :, cols]

        def block(y, x, part=slice(None)):
            return full.at[:, y, x, p.c, part, cols]

        def copy(i, src, dst, to):
            return lambda: mesh_copy(src, dst, send.at[i], recv.at[i], to)

        same = lambda i, ref, to: copy(i, ref, ref, to)
        mine = block(p.y, p.x)
        self.local = lambda: pltpu.make_async_copy(held, mine, own)
        self.xy = [copy(0, held, mine, p.xp), copy(1, held, mine, p.yp)]
        self.far = [
            same(2, block(p.y, 1 - p.x, first), p.yp),
            same(3, block(1 - p.y, p.x, second), p.xp),
        ]
        self.pair = [
            copy(4, held, mine, p.sib),
            same(5, block(p.y, 1 - p.x), p.sib),
            same(6, block(1 - p.y, p.x), p.sib),
            same(7, block(1 - p.y, 1 - p.x), p.sib),
        ]

    def stage(self, number):
        if number == 0:
            for c in (*self.xy, self.pair[0], self.local):
                c().start()
        elif number == 1:
            for c in self.xy:
                c().wait()
            for c in (*self.far, self.pair[1], self.pair[2]):
                c().start()
        elif number == 2:
            for c in self.far:
                c().wait()
            self.pair[3]().start()
        elif number == 3:
            for c in (*self.pair, self.local):
                c().wait()


def gather_rest(place, arrays, send, recv, own):
    pieces = []
    for column, full in arrays:
        unit = UNIT * 32 // column.shape[1]
        for at in range(0, column.shape[2], unit):
            i = len(pieces)
            pieces.append(
                GatherRest(
                    place, column, full, pl.ds(at, unit), send.at[i], recv.at[i], own.at[i]
                )
            )
    return pieces


def run_stages(pieces, step, steps):
    for at in sorted(set(steps)):
        todo = [
            (q, pieces[tick - q])
            for tick, when in enumerate(steps)
            if when == at
            for q in range(5)
            if 0 <= tick - q < len(pieces)
        ]

        @pl.when(step == at)
        def _():
            for q, piece in todo:
                piece.stage(q)


def run_rest(pieces, ticks):
    for tick in range(ticks, len(pieces) + 4):
        for q in range(5):
            if 0 <= tick - q < len(pieces):
                pieces[tick - q].stage(q)


class Scatter:
    def __init__(self, place, grad, held, from_pair, far, side, line, out, sems, tilt=False):
        self.tilt = tilt
        self.p, self.out = place, out
        self.held, self.from_pair, self.far, self.side, self.line = held, from_pair, far, side, line
        p, rows = place, held.shape[3]
        self.half = rows // 2
        own, send, recv = sems
        first, second = pl.ds(0, self.half), pl.ds(self.half, self.half)

        def copy(i, src, dst, to):
            return lambda: mesh_copy(src, dst, send.at[i], recv.at[i], to)

        self.load = lambda: pltpu.make_async_copy(grad.at[:, :, :, p.c], held, own)
        self.to_pair = copy(0, grad.at[:, :, :, 1 - p.c], from_pair, p.sib)
        self.to_far = [
            copy(1, held.at[:, 1 - p.y, 1 - p.x, first], far.at[0], p.xp),
            copy(2, held.at[:, 1 - p.y, 1 - p.x, second], far.at[1], p.yp),
        ]
        if tilt:
            self.to_far = [copy(1, held.at[:, 1 - p.y, 1 - p.x], far, p.yp)]
        self.to_side = [
            copy(3, held.at[:, p.y, 1 - p.x], side.at[0], p.xp),
            copy(4, held.at[:, 1 - p.y, p.x], side.at[1], p.yp),
        ]
        self.to_line = [
            copy(5 + k, held.at[(p.z + k + 1) % 4, p.y, p.x], line.at[k], to)
            for k, to in enumerate(p.zp)
        ]

    def stage(self, number):
        p, half = self.p, self.half
        held, far, side, line = self.held, self.far, self.side, self.line
        if number == 0:
            self.load().start()
            self.to_pair().start()
        elif number == 1:
            self.load().wait()
            self.to_pair().wait()

            @pl.loop(0, 4)
            def _(z):
                for y in range(2):
                    for x in range(2):
                        held[z, y, x] = held[z, y, x] + self.from_pair[z, y, x]

            for c in self.to_far:
                c().start()
        elif number == 2:
            for c in self.to_far:
                c().wait()

            @pl.loop(0, 4)
            def _(z):
                if self.tilt:
                    held[z, p.y, 1 - p.x] = (
                        held[z, p.y, 1 - p.x].astype(F32) + far[z].astype(F32)
                    ).astype(held.dtype)
                    return
                held[z, 1 - p.y, p.x, :half] = (
                    held[z, 1 - p.y, p.x, :half].astype(F32) + far[0, z].astype(F32)
                ).astype(held.dtype)
                held[z, p.y, 1 - p.x, half:] = (
                    held[z, p.y, 1 - p.x, half:].astype(F32) + far[1, z].astype(F32)
                ).astype(held.dtype)

            for c in self.to_side:
                c().start()
        elif number == 3:
            for c in self.to_side:
                c().wait()

            @pl.loop(0, 4)
            def _(z):
                held[z, p.y, p.x] = (
                    held[z, p.y, p.x].astype(F32)
                    + side[0, z].astype(F32)
                    + side[1, z].astype(F32)
                ).astype(held.dtype)

            for c in self.to_line:
                c().start()
        else:
            for c in self.to_line:
                c().wait()
            self.out[...] = (
                held[p.z, p.y, p.x].astype(F32)
                + line[0].astype(F32)
                + line[1].astype(F32)
                + line[2].astype(F32)
            )


SCATTER_SEMS = 8
UNIT = 1024


def scatter_scratch(rows, cols, dtype=BF, tilt=False):
    return [
        pltpu.VMEM((4, 2, 2, rows, cols), dtype),
        pltpu.VMEM((4, 2, 2, rows, cols), dtype),
        pltpu.VMEM((4, rows, cols) if tilt else (2, 4, rows // 2, cols), dtype),
        pltpu.VMEM((2, 4, rows, cols), dtype),
        pltpu.VMEM((3, rows, cols), dtype),
        pltpu.SemaphoreType.DMA,
        pltpu.SemaphoreType.DMA((SCATTER_SEMS,)),
        pltpu.SemaphoreType.DMA((SCATTER_SEMS,)),
    ]


def blocks(value):
    return value.reshape(4, 2, 2, 2, value.shape[0] // 32, value.shape[1])


VEC_ROWS = 16


def first_body(
    rows, tokens, wide, vec, ids, w_out_shard, w_up_shard, q_out, kv_out, normed_out, scaled_out, w_out, vecs_out,
    bias_out, mlp_out, n0_out, out_column, up_column, near, normed, scaled, weights, gathered_vec, queries, pairs, send, recv,
    own, halo_send, halo_recv, load, store, col_send, col_recv, col_own,
):
    place = Place()
    me, peers = lax.axis_index(AXIS), lax.axis_size(AXIS)
    greet(place.partners, me > 0, me < peers - 1)
    width = near.shape[1]
    mine = pl.ds(RIM, rows)

    def halo(way):
        if way == 0:
            src, dst, to = tokens.at[pl.ds(0, RIM)], near.at[pl.ds(RIM + rows, RIM)], me - 1
        else:
            src, dst, to = tokens.at[pl.ds(rows - RIM, RIM)], near.at[pl.ds(0, RIM)], me + 1
        return mesh_copy(src, dst, halo_send.at[way], halo_recv.at[way], to)

    pieces = [
        Gather(
            place, vec, gathered_vec, pl.ds(0, vec.shape[1]), send.at[0], recv.at[0], own.at[0],
            True,
        )
    ]
    for i, k in enumerate((1, 2, 0)):
        pieces.append(
            Gather(
                place, wide, weights, pl.ds(k * UNIT, UNIT), send.at[i + 1], recv.at[i + 1],
                own.at[i + 1],
            )
        )
    g_vec, g_k, g_v, g_q = pieces
    columns = [
        Column(place, shard, column, col_send.at[i], col_recv.at[i], col_own.at[i])
        for i, (shard, column) in enumerate(((w_out_shard, out_column), (w_up_shard, up_column)))
    ]
    own_copy = pltpu.make_async_copy(tokens, near.at[mine], load)
    own_copy.start()
    g_vec.stage(0)
    g_k.stage(0)
    pl.when(me > 0)(lambda: halo(0).start())
    pl.when(me < peers - 1)(lambda: halo(1).start())
    n0_out[0] = jnp.sum((ids[...] == ids[0:1, 0:1]).astype(jnp.int32))
    near[pl.ds(2 * RIM + rows, near.shape[0] - rows - 2 * RIM), :] = jnp.zeros(
        (near.shape[0] - rows - 2 * RIM, width), BF
    )

    @pl.when(me == 0)
    def _():
        near[pl.ds(0, RIM), :] = jnp.zeros((RIM, width), BF)

    @pl.when(me == peers - 1)
    def _():
        near[pl.ds(RIM + rows, RIM), :] = jnp.zeros((RIM, width), BF)

    g_vec.stage(1)
    g_k.stage(1)
    g_v.stage(0)
    g_vec.stage(2)
    g_vec.stage(3)
    g_vec.stage(4)
    table = []
    for z in range(4):
        for y in range(2):
            group = [gathered_vec[z, y, x, c].astype(F32) for x in range(2) for c in range(2)]
            table.append(group[0] + group[1] + group[2] + group[3])
            for x in range(2):
                for c in range(2):
                    at = ((z * 2 + y) * 2 + x) * 2 + c
                    bias_out[:, at * 128 : (at + 1) * 128] = group[x * 2 + c][8:9]
    vecs = jnp.concatenate(table, axis=1)
    vecs_out[...] = vecs
    mlp_out[...] = vecs[4:12]
    gain, shift = vecs[0:1], vecs[1:2]
    q_bias, v_bias = vecs[2:3], vecs[3:4]

    def norm(first, count):
        part = pl.ds(first, count)
        value = row_stats(near[part, :].astype(F32))[0]
        scaled[part, :] = value.astype(BF)
        normed[part, :] = (value * gain + shift).astype(BF)

    own_copy.wait()
    for row in range(RIM, RIM + rows, 256):
        norm(row, 256)
    g_k.stage(2)
    g_v.stage(1)
    g_q.stage(0)
    g_k.stage(3)
    g_v.stage(2)
    g_q.stage(1)
    for column in columns:
        column.start()
    g_k.stage(4)

    def full(k):
        return weights[:, :, :, :, :, pl.ds(k * UNIT, UNIT)].reshape(width, UNIT)

    def project(target, k, first, stop, bias, at):
        matrix = full(k)
        for row in range(first, stop, 256):
            size = min(256, stop - row)
            value = dot(normed[pl.ds(row, size), :], matrix)
            value = value if bias is None else value + bias
            target[pl.ds(row - at[0], size), pl.ds(at[1], UNIT)] = value.astype(BF)

    last_row = near.shape[0]
    project(pairs, 1, RIM, RIM + rows, None, (0, 0))
    g_v.stage(3)
    g_q.stage(2)

    @pl.when(me > 0)
    def _():
        halo(0).wait_send()
        halo(1).wait_recv()

    @pl.when(me < peers - 1)
    def _():
        halo(1).wait_send()
        halo(0).wait_recv()

    for row in range(0, RIM, 192):
        norm(row, 192)
    for row in range(RIM + rows, last_row, 176):
        norm(row, 176)
    normed_copy = pltpu.make_async_copy(normed, normed_out, store.at[0])
    normed_copy.start()
    scaled_copy = pltpu.make_async_copy(scaled, scaled_out, store.at[5])
    scaled_copy.start()
    project(pairs, 1, 0, RIM, None, (0, 0))
    project(pairs, 1, RIM + rows, last_row, None, (0, 0))
    k_copy = pltpu.make_async_copy(
        pairs.at[:, pl.ds(0, UNIT)], kv_out.at[:, pl.ds(0, UNIT)], store.at[1]
    )
    k_copy.start()
    g_v.stage(4)
    g_q.stage(3)
    project(pairs, 2, 0, last_row, v_bias, (0, UNIT))
    v_copy = pltpu.make_async_copy(
        pairs.at[:, pl.ds(UNIT, UNIT)], kv_out.at[:, pl.ds(UNIT, UNIT)], store.at[2]
    )
    v_copy.start()
    g_q.stage(4)
    w_copy = pltpu.make_async_copy(weights, w_out, store.at[3])
    w_copy.start()
    project(queries, 0, RIM, RIM + rows, q_bias, (RIM, 0))
    q_copy = pltpu.make_async_copy(queries, q_out, store.at[4])
    q_copy.start()
    for column in columns:
        column.wait()
    for copy in (normed_copy, scaled_copy, k_copy, v_copy, w_copy, q_copy):
        copy.wait()


def first(tokens, wide, vec, ids, shards, ext):
    rows, width = tokens.shape
    part = wide.shape[0]
    hbm, vmem = pl.BlockSpec(memory_space=pl.ANY), pl.BlockSpec(memory_space=pltpu.VMEM)
    queries, key_value, normed, scaled, w_qkv, vecs, bias, mlp_vecs, n0, *columns = pl.pallas_call(
        functools.partial(first_body, rows),
        in_specs=[hbm] * 3 + [vmem] + [hbm] * 2,
        out_specs=[hbm] * 5 + [vmem] * 3 + [pl.BlockSpec(memory_space=pltpu.SMEM)] + [hbm] * 2,
        out_shape=[
            jax.ShapeDtypeStruct((rows, width), BF),
            jax.ShapeDtypeStruct((ext, 2 * width), BF),
            jax.ShapeDtypeStruct((ext, width), BF),
            jax.ShapeDtypeStruct((ext, width), BF),
            jax.ShapeDtypeStruct((4, 2, 2, 2, *wide.shape), BF),
            jax.ShapeDtypeStruct((VEC_ROWS, width), F32),
            jax.ShapeDtypeStruct((1, 32 * 128), F32),
            jax.ShapeDtypeStruct((8, width), F32),
            jax.ShapeDtypeStruct((1,), jnp.int32),
            *(jax.ShapeDtypeStruct((4, *v.shape), BF) for v in shards),
        ],
        scratch_shapes=[
            pltpu.VMEM((ext, width), BF),
            pltpu.VMEM((ext, width), BF),
            pltpu.VMEM((ext, width), BF),
            pltpu.VMEM((4, 2, 2, 2, *wide.shape), BF),
            pltpu.VMEM((4, 2, 2, 2, *vec.shape), BF),
            pltpu.VMEM((rows, width), BF),
            pltpu.VMEM((ext, 2 * width), BF),
            pltpu.SemaphoreType.DMA((4, GATHER_SEMS)),
            pltpu.SemaphoreType.DMA((4, GATHER_SEMS)),
            pltpu.SemaphoreType.DMA((4,)),
            pltpu.SemaphoreType.DMA((2,)),
            pltpu.SemaphoreType.DMA((2,)),
            pltpu.SemaphoreType.DMA,
            pltpu.SemaphoreType.DMA((6,)),
            *column_scratch(2),
        ],
        compiler_params=pltpu.CompilerParams(
            collective_id=0, has_side_effects=True, vmem_limit_bytes=62 * 2**20
        ),
        name="first",
    )(tokens, wide, vec, ids, *shards)
    w_qkv = w_qkv.reshape(width, wide.shape[1])
    return queries, key_value, normed, scaled, w_qkv, vecs, bias, mlp_vecs, n0, columns


ITEMS = 10
BACK_GROUP = 5
GROUP = 5


class Images:
    def __init__(self, n0, rows, ext):
        self.n0, self.n1, self.rows, self.ext = n0, n0 + IMG, rows, ext
        me, peers = lax.axis_index(AXIS), lax.axis_size(AXIS)
        limit = jnp.where(me == peers - 1, RIM + rows, 2 * RIM + rows)
        start0 = jnp.where(me == 0, RIM, n0 - 1)
        start1 = RIM + n0
        start2 = start1 + IMG
        self.spans = (
            (start0, start1),
            (start1, jnp.minimum(start1 + IMG, limit)),
            (start2, jnp.minimum(start2 + IMG, limit)),
        )
        one = lambda flag: jnp.where(flag, 1, 0)
        self.b0, self.b1 = lax.div(n0, QB), lax.div(self.n1, QB)
        self.d0 = one(self.b0 * QB != n0)
        self.d1 = one((self.n1 < rows) & (self.b1 * QB != self.n1))
        self.third = self.n1 < rows
        self.end0 = lax.div(n0 - 1, QB)
        self.end1 = lax.div(self.n1 - 1, QB) + self.d0
        self.one = one

    def base(self, start):
        return jnp.minimum(lax.div(start, 16), (self.ext - WIN) // 16)

    def segment(self, item):
        return self.one(item > self.end0) + self.one(item > self.end1)

    def item(self, item):
        blk = (
            item
            - self.d0 * self.one(item > self.b0)
            - self.d1 * self.one(item > self.b1 + self.d0)
        )
        used = blk < self.rows // QB
        blk = jnp.minimum(blk, self.rows // QB - 1)
        seg = self.segment(item)
        choose = lambda i: jnp.where(
            seg == 0, self.spans[0][i], jnp.where(seg == 1, self.spans[1][i], self.spans[2][i])
        )
        start, stop = choose(0), choose(1)
        base = self.base(start) * 16
        row0 = blk * QB
        low = jnp.maximum(start - RIM - row0, 0)
        high = jnp.where(used, jnp.minimum(stop - RIM - row0, QB), 0)
        return blk, row0, base, start - base, stop - base, low, high

    def of_block(self, blk):
        at0 = self.d0 * self.one(blk == self.b0)
        at1 = self.d1 * self.one(blk == self.b1)
        first = blk + self.d0 * self.one(blk > self.b0) + self.d1 * self.one(blk > self.b1)
        split = jnp.where(at0 == 1, self.n0, jnp.where(at1 == 1, self.n1, self.rows)) - blk * QB
        return first, first + at0 + at1, split


def attend_body(n0_ref, q_ref, k_ref, v_ref, out_ref, lse_ref, parts, parts_lse):
    rows = q_ref.shape[0]
    images = Images(n0_ref[0], rows, k_ref.shape[0])

    def scores_of(item):
        _, row0, base, low, high, _, _ = images.item(item)
        queries = stacked(q_ref[pl.ds(row0, QB), :]) * jnp.asarray(0.125, BF)
        scores = dot(k_ref[pl.ds(base, WIN), :], queries, NT)
        return scores + key_mask(low, high), base

    def softmax_of(scores):
        top = jnp.max(scores, axis=0, keepdims=True)
        terms = jnp.exp(scores - top)
        total = jnp.sum(terms, axis=0, keepdims=True)
        return terms.astype(BF), top, total

    @pl.loop(0, ITEMS // GROUP)
    def _(step):
        items = [step * GROUP + g for g in range(GROUP)]
        scored = [scores_of(item) for item in items]
        soft = [softmax_of(scores) for scores, _ in scored]
        mixed = [
            dot(v_ref[pl.ds(base, WIN), :], terms, TN) / total
            for (_, base), (terms, _, total) in zip(scored, soft)
        ]
        for item, value, (_, top, total) in zip(items, mixed, soft):
            parts[item] = unstacked(value)
            parts_lse[item] = jnp.broadcast_to(top + jnp.log(total), parts_lse.shape[1:])

    for blk in range(rows // QB):
        first, last, split = images.of_block(blk)
        row = lax.broadcasted_iota(jnp.int32, (QB, 2 * HDIM), 0)
        out_ref[pl.ds(blk * QB, QB), :] = jnp.where(
            row < split, parts[first], parts[last]
        ).astype(BF)
        lane = lax.broadcasted_iota(jnp.int32, parts_lse.shape[1:], 1) % QB
        lse_ref[0, pl.ds(blk, 1), :] = jnp.where(
            lane < split, parts_lse[first], parts_lse[last]
        )[:1]


def attend_kernel(n0_ref, q_ref, k_ref, v_ref, out_ref, lse_ref, parts, parts_lse):
    attend_body(n0_ref, q_ref, k_ref, v_ref, out_ref, lse_ref, parts, parts_lse)


def attend_gather_kernel(
    n0_ref, q_ref, k_ref, v_ref, c_out, c_up, w_down, out_ref, lse_ref, full_out, full_up,
    c_down, parts, parts_lse, send, recv, own, *column_sems,
):
    tick = pl.program_id(0)
    place = Place()
    column = Column(place, w_down, c_down, *(v.at[0] for v in column_sems))

    @pl.when(tick == 0)
    def _():
        greet(place.partners)

    pieces = gather_rest(place, ((c_out, full_out), (c_up, full_up)), send, recv, own)
    run_stages(pieces, tick, range(7))
    pl.when(tick == 0)(column.start)
    attend_body(n0_ref, q_ref, k_ref, v_ref, out_ref, lse_ref, parts, parts_lse)

    @pl.when(tick == 7)
    def _():
        run_rest(pieces, 7)
        column.wait()


def attend(n0, queries, key_value, columns=None, shard=None):
    rows, width = queries.shape
    pairs = width // (2 * HDIM)
    ext = key_value.shape[0]
    hbm = pl.BlockSpec(memory_space=pl.ANY)
    in_specs = [
        pl.BlockSpec(memory_space=pltpu.SMEM),
        pl.BlockSpec((rows, 2 * HDIM), lambda p: (0, p)),
        pl.BlockSpec((ext, 2 * HDIM), lambda p: (0, p)),
        pl.BlockSpec((ext, 2 * HDIM), lambda p: (0, pairs + p)),
    ]
    out_specs = [
        pl.BlockSpec((rows, 2 * HDIM), lambda p: (0, p)),
        pl.BlockSpec((1, rows // QB, 2 * QB), lambda p: (p, 0, 0)),
    ]
    out_shape = [
        jax.ShapeDtypeStruct((rows, width), BF),
        jax.ShapeDtypeStruct((pairs, rows // QB, 2 * QB), F32),
    ]
    scratch = [
        pltpu.VMEM((ITEMS, QB, 2 * HDIM), F32),
        pltpu.VMEM((ITEMS, 8, 2 * QB), F32),
    ]
    params = dict(vmem_limit_bytes=62 * 2**20)
    args = [n0, queries, key_value, key_value]
    kernel = attend_kernel
    if columns is not None:
        kernel = attend_gather_kernel
        in_specs += [hbm] * 3
        out_specs += [hbm] * 3
        out_shape += [jax.ShapeDtypeStruct((4, 2, 2, 2, *v.shape[1:]), BF) for v in columns]
        out_shape += [jax.ShapeDtypeStruct((4, *shard.shape), BF)]
        count = sum(v.shape[1] * v.shape[2] for v in columns) // (32 * UNIT)
        scratch += [
            pltpu.SemaphoreType.DMA((count, 8)),
            pltpu.SemaphoreType.DMA((count, 8)),
            pltpu.SemaphoreType.DMA((count,)),
            *column_scratch(1),
        ]
        params |= dict(collective_id=1, has_side_effects=True)
        args += [*columns, shard]
    return pl.pallas_call(
        kernel,
        grid=(pairs,),
        in_specs=in_specs,
        out_specs=out_specs,
        out_shape=out_shape,
        scratch_shapes=scratch,
        compiler_params=pltpu.CompilerParams(**params),
        name="attend",
    )(*args)


def attend_back_body(
    pair, n0_ref, q_ref, k_ref, v_ref, up_ref, lse_ref, wk_ref, wv_ref, scaled_ref, dq_ref, dk_ref, dv_ref,
    dn_ref, sums_ref, slots, parts, total,
):
    rows = q_ref.shape[0]
    images = Images(n0_ref[0], rows, k_ref.shape[0])

    @pl.when(pair == 0)
    def _():
        slots[0] = jnp.zeros(slots.shape[1:], F32)
        total[...] = jnp.zeros(total.shape, F32)

    lane = lax.broadcasted_iota(jnp.int32, (1, 2 * QB), 1) % QB

    def begin(item):
        blk, row0, base, low, high, first, stop = images.item(item)
        queries = stacked(q_ref[pl.ds(row0, QB), :]) * jnp.asarray(0.125, BF)
        upstream = stacked(up_ref[pl.ds(row0, QB), :])
        here = (lane >= first) & (lane < stop)
        lse = jnp.where(here, lse_ref[0, pl.ds(blk, 1), :], -NEG)
        scores = dot(k_ref[pl.ds(base, WIN), :], queries, NT)
        dprobs = dot(v_ref[pl.ds(base, WIN), :], upstream, NT)
        return base, queries, upstream, scores + key_mask(low, high), lse, dprobs

    def middle(scores, lse, dprobs):
        probs = jnp.exp(scores - lse)
        row_dot = jnp.sum(probs * dprobs, axis=0, keepdims=True)
        return probs.astype(BF), (probs * (dprobs - row_dot)).astype(BF)

    def finish(item, base, queries, upstream, probs, dscores):
        keep = (item > 0) & (images.segment(item) == images.segment(item - 1))
        old = jnp.where(keep, slots[item], jnp.zeros(slots.shape[1:], F32))
        slots[item + 1, :, : 2 * HDIM] = old[:, : 2 * HDIM] + dot(dscores, queries)
        slots[item + 1, :, 2 * HDIM :] = old[:, 2 * HDIM :] + dot(probs, upstream)
        parts[item] = unstacked(dot(k_ref[pl.ds(base, WIN), :], dscores, TN)) * 0.125

    @pl.loop(0, ITEMS // BACK_GROUP)
    def _(step):
        items = [step * BACK_GROUP + g for g in range(BACK_GROUP)]
        begun = [begin(items[0])]
        done = []
        for g in range(BACK_GROUP + 1):
            if g + 1 < BACK_GROUP:
                begun.append(begin(items[g + 1]))
            if g < BACK_GROUP:
                done.append(middle(*begun[g][3:]))
            if g > 0:
                finish(items[g - 1], *begun[g - 1][:3], *done[g - 1])

    for blk in range(rows // QB):
        first, last, split = images.of_block(blk)
        row = lax.broadcasted_iota(jnp.int32, (QB, 2 * HDIM), 0)
        dq_ref[pl.ds(blk * QB, QB), :] = jnp.where(
            row < split, parts[first], parts[last]
        ).astype(BF)
    ends = (
        images.end0 + 1,
        jnp.minimum(images.end1, (rows - 1) // QB + images.d0) + 1,
        jnp.where(images.third, ITEMS, 0),
    )
    weights = jnp.concatenate([wk_ref[...], wv_ref[...]], axis=1)
    for seg, end in enumerate(ends):
        both = slots[end].astype(BF)
        dk_ref[seg] = both[:, : 2 * HDIM]
        dv_ref[seg] = both[:, 2 * HDIM :]
        total[seg] += dot(both, weights, NT)

    @pl.when(pair == pl.num_programs(0) - 1)
    def _():
        dn_ref[...] = total[...].astype(BF)
        sums_ref[...] = jnp.zeros(sums_ref.shape, F32)
        for seg, span in enumerate(images.spans):
            window = scaled_ref[pl.ds(images.base(span[0]) * 16, WIN), :].astype(F32)
            sums_ref[0:1] += jnp.sum(total[seg] * window, axis=0, keepdims=True)
            sums_ref[1:2] += jnp.sum(total[seg], axis=0, keepdims=True)


def attend_back_kernel(*refs):
    attend_back_body(pl.program_id(0), *refs)


def attend_back_scatter_kernel(*refs):
    base, (g_out, g_up), rest = refs[:9], refs[9:11], refs[11:]
    outs, (r_out, r_up), scratch = rest[:5], rest[5:7], rest[7:]
    mine, comm = scratch[:3], scratch[3:]
    pair = pl.program_id(0)
    place = Place()
    pl.when(pair == 0)(lambda: greet(place.partners))
    pieces = []
    for grad, out in ((g_out, r_out), (g_up, r_up)):
        for k in range(grad.shape[5] // UNIT):
            cols = pl.ds(k * UNIT, UNIT)
            bufs = comm[len(pieces) * 8 : len(pieces) * 8 + 8]
            pieces.append(
                Scatter(
                    place, grad.at[:, :, :, :, :, cols], *bufs[:5], out.at[:, cols], bufs[5:]
                )
            )
    run_stages(pieces, pair, range(8))
    attend_back_body(pair, *base, *outs, *mine)

    @pl.when(pair == pl.num_programs(0) - 1)
    def _():
        pieces[-1].stage(4)


def attend_back(n0, queries, key_value, upstream, lse, w_qkv, scaled, grads=None):
    rows, width = queries.shape
    pairs = width // (2 * HDIM)
    ext = key_value.shape[0]
    hbm, vmem = pl.BlockSpec(memory_space=pl.ANY), pl.BlockSpec(memory_space=pltpu.VMEM)
    own = pl.BlockSpec((rows, 2 * HDIM), lambda p: (0, p))
    windows = pl.BlockSpec((3, WIN, 2 * HDIM), lambda p: (0, 0, p))
    in_specs = [
        pl.BlockSpec(memory_space=pltpu.SMEM),
        own,
        pl.BlockSpec((ext, 2 * HDIM), lambda p: (0, p)),
        pl.BlockSpec((ext, 2 * HDIM), lambda p: (0, pairs + p)),
        own,
        pl.BlockSpec((1, rows // QB, 2 * QB), lambda p: (p, 0, 0)),
        pl.BlockSpec((width, 2 * HDIM), lambda p: (0, pairs + p)),
        pl.BlockSpec((width, 2 * HDIM), lambda p: (0, 2 * pairs + p)),
        pl.BlockSpec((ext, width), lambda p: (0, 0), pipeline_mode=pl.Buffered(1)),
    ]
    out_specs = [
        own, windows, windows,
        pl.BlockSpec((3, WIN, width), lambda p: (0, 0, 0), pipeline_mode=pl.Buffered(1)),
        pl.BlockSpec((8, width), lambda p: (0, 0)),
    ]
    out_shape = [jax.ShapeDtypeStruct((rows, width), BF)]
    out_shape += [jax.ShapeDtypeStruct((3, WIN, width), BF)] * 3
    out_shape += [jax.ShapeDtypeStruct((8, width), F32)]
    scratch = [
        pltpu.VMEM((ITEMS + 1, WIN, 4 * HDIM), F32),
        pltpu.VMEM((ITEMS, QB, 2 * HDIM), F32),
        pltpu.VMEM((3, WIN, width), F32),
    ]
    args = [n0, queries, key_value, key_value, upstream, lse, w_qkv, w_qkv, scaled]
    kernel, params = attend_back_kernel, dict(vmem_limit_bytes=62 * 2**20)
    if grads is not None:
        kernel = attend_back_scatter_kernel
        params |= dict(collective_id=2, has_side_effects=True)
        args += map(blocks, grads)
        in_specs += [hbm] * 2
        out_specs += [vmem] * 2
        out_shape += [jax.ShapeDtypeStruct((v.shape[0] // 32, v.shape[1]), F32) for v in grads]
        for v in grads:
            scratch += scatter_scratch(v.shape[0] // 32, UNIT) * (v.shape[1] // UNIT)
    return pl.pallas_call(
        kernel,
        grid=(pairs,),
        in_specs=in_specs,
        out_specs=out_specs,
        out_shape=out_shape,
        scratch_shapes=scratch,
        compiler_params=pltpu.CompilerParams(**params),
        name="attend_back",
    )(*args)


ROW_TILE = 256
FF_TILE = 512
ROOT_HALF = 1.0 / math.sqrt(2.0)
PDF_SCALE = 1.0 / math.sqrt(2.0 * math.pi)


def row_stats(value):
    mean = jnp.mean(value, axis=1, keepdims=True)
    center = value - mean
    inv_std = lax.rsqrt(jnp.mean(center * center, axis=1, keepdims=True) + EPS)
    return center * inv_std, inv_std


def mlp_up_body(
    step, row_steps, mixed, tokens, w_out, vecs, w_up, up_bias, cot, resid, normed, act, slope,
    g_down, held,
):
    @pl.when(step < row_steps)
    def _():
        value = tokens[...].astype(F32) + dot(mixed[...], w_out[...]) + vecs[0:1]
        resid[...] = value
        low = (row_stats(value)[0] * vecs[1:2] + vecs[2:3]).astype(BF)
        normed[...] = low
        held[pl.ds(step * ROW_TILE, ROW_TILE), :] = low

    @pl.when(step >= row_steps)
    def _():
        rows = held.shape[0]

        for row in range(0, rows, ROW_TILE):
            part = pl.ds(row, ROW_TILE)
            upward = dot(held[part, :], w_up[...]) + up_bias[...]
            cdf = 0.5 * (1.0 + lax.erf(upward * ROOT_HALF))
            pdf = jnp.exp(-0.5 * upward * upward) * PDF_SCALE
            act[part, :] = (upward * cdf).astype(BF)
            slope[part, :] = (cdf + upward * pdf).astype(BF)
        g_down[...] = dot(act[...], cot[...], TN).astype(BF)


def mlp_up_kernel(row_steps, *refs):
    mlp_up_body(pl.program_id(0), row_steps, *refs)


def mlp_up_gather_kernel(row_steps, *refs):
    ins, shard, outs, full = refs[:7], refs[7], refs[8:13], refs[13]
    held, send, recv, own = refs[14:]
    step = pl.program_id(0)
    place = Place()
    pl.when(step == 0)(lambda: greet(place.partners))
    pieces = gather_rest(place, ((shard, full),), send, recv, own)
    run_stages(pieces, step, (0, 4, 6, 8, 10))
    mlp_up_body(step, row_steps, *ins, *outs, held)
    pl.when(step == pl.num_programs(0) - 1)(lambda: run_rest(pieces, 5))


def mlp_up(mixed, tokens, w_out, vecs, w_up, up_bias, cot, shard=None):
    rows, width = tokens.shape
    hidden = w_up.shape[1]
    row_steps, ff_steps = rows // ROW_TILE, hidden // FF_TILE
    at_row = lambda s: (jnp.minimum(s, row_steps - 1), 0)
    at_col = lambda s: (0, jnp.maximum(s - row_steps, 0))
    at_ff = lambda s: (jnp.maximum(s - row_steps, 0), 0)
    const = lambda s: (0, 0)
    hbm = pl.BlockSpec(memory_space=pl.ANY)
    tall = pl.BlockSpec((rows, FF_TILE), at_col)
    in_specs = [
        pl.BlockSpec((ROW_TILE, width), at_row),
        pl.BlockSpec((ROW_TILE, width), at_row),
        pl.BlockSpec((width, width), const),
        pl.BlockSpec((8, width), const),
        pl.BlockSpec((width, FF_TILE), at_col),
        pl.BlockSpec((1, FF_TILE), at_col),
        pl.BlockSpec((rows, width), const),
    ]
    out_specs = [
        pl.BlockSpec((ROW_TILE, width), at_row),
        pl.BlockSpec((ROW_TILE, width), at_row),
        tall,
        tall,
        pl.BlockSpec((FF_TILE, width), at_ff),
    ]
    out_shape = [
        jax.ShapeDtypeStruct((rows, width), F32),
        jax.ShapeDtypeStruct((rows, width), BF),
        jax.ShapeDtypeStruct((rows, hidden), BF),
        jax.ShapeDtypeStruct((rows, hidden), BF),
        jax.ShapeDtypeStruct((hidden, width), BF),
    ]
    scratch = [pltpu.VMEM((rows, width), BF)]
    params = dict(vmem_limit_bytes=62 * 2**20)
    args = [mixed, tokens, w_out, vecs, w_up, up_bias, cot]
    kernel = mlp_up_kernel
    if shard is not None:
        kernel = mlp_up_gather_kernel
        in_specs += [hbm]
        out_specs += [hbm]
        out_shape += [jax.ShapeDtypeStruct((4, 2, 2, 2, *shard.shape[1:]), BF)]
        scratch += [
            pltpu.SemaphoreType.DMA((4, 8)),
            pltpu.SemaphoreType.DMA((4, 8)),
            pltpu.SemaphoreType.DMA((4,)),
        ]
        params |= dict(collective_id=5, has_side_effects=True)
        args += [shard]
    return pl.pallas_call(
        functools.partial(kernel, row_steps),
        grid=(row_steps + ff_steps,),
        in_specs=in_specs,
        out_specs=out_specs,
        out_shape=out_shape,
        scratch_shapes=scratch,
        compiler_params=pltpu.CompilerParams(**params),
        name="mlp_up",
    )(*args)


def mlp_back_body(
    step, ff_steps, act, slope, w_up, w_down, cot, normed, resid, mixed, w_out, vecs,
    g_up, up_sums, layer_out, dresid, dmixed, g_out, sums, total, dnormed, branches, dup,
):
    rows, width = cot.shape

    @pl.when(step == 0)
    def _():
        total[...] = jnp.zeros(total.shape, F32)
        dnormed[...] = jnp.zeros(dnormed.shape, F32)
        sums[...] = jnp.zeros(sums.shape, F32)

    @pl.when(step < ff_steps)
    def _():
        count = jnp.zeros(up_sums.shape, F32)
        for row in range(0, rows, ROW_TILE):
            part = pl.ds(row, ROW_TILE)
            total[part, :] += dot(act[part, :], w_down[...])
            dact = dot(cot[part, :], w_down[...], NT)
            low = (dact * slope[part, :].astype(F32)).astype(BF)
            dup[part, :] = low
            count += jnp.sum(low.astype(F32), axis=0, keepdims=True)
            dnormed[part, :] += dot(low, w_up[...], NT)
        up_sums[...] = count
        g_up[...] = dot(normed[...], dup[...], TN).astype(BF)

    @pl.when(step >= ff_steps)
    def _():
        part = pl.ds((step - ff_steps) * ROW_TILE, ROW_TILE)
        value = resid[...]
        scaled, inv_std = row_stats(value)
        upstream = dnormed[part, :]
        above = cot[part, :].astype(F32)
        through = upstream * vecs[1:2]
        inner = (
            through
            - jnp.mean(through, axis=1, keepdims=True)
            - scaled * jnp.mean(through * scaled, axis=1, keepdims=True)
        )
        grad = above + inv_std * inner
        dresid[...] = grad
        low = grad.astype(BF)
        branches[part, :] = low
        dmixed[...] = dot(low, w_out[...], NT).astype(BF)
        layer_out[...] = (value + total[part, :] + vecs[3:4]).astype(BF)
        sums[0:1] += jnp.sum(low.astype(F32), axis=0, keepdims=True)
        sums[1:2] += jnp.sum(upstream * scaled, axis=0, keepdims=True)
        sums[2:3] += jnp.sum(upstream, axis=0, keepdims=True)
        sums[3:4] += jnp.sum(above, axis=0, keepdims=True)

    @pl.when(step == pl.num_programs(0) - 1)
    def _():
        g_out[...] = dot(mixed[...], branches[...], TN).astype(BF)


def mlp_back_kernel(ff_steps, *refs):
    mlp_back_body(pl.program_id(0), ff_steps, *refs)


def mlp_back_scatter_kernel(ff_steps, *refs):
    ins, grad, outs, reduced, scratch, comm = (
        refs[:10], refs[10], refs[11:18], refs[18], refs[19:23], refs[23:],
    )
    step = pl.program_id(0)
    place = Place()
    pl.when(step == 0)(lambda: greet(place.partners))
    cols = reduced.shape[1] // 4
    pieces = []
    for k in range(4):
        here = pl.ds(k * cols, cols)
        bufs = comm[k * 8 : k * 8 + 8]
        pieces.append(
            Scatter(
                place, grad.at[:, :, :, :, :, here], *bufs[:5], reduced.at[:, here], bufs[5:]
            )
        )
    run_stages(pieces, step, (0, 1, 2, 4, 5, 7, 9))
    mlp_back_body(step, ff_steps, *ins, *outs, *scratch)

    @pl.when(step == pl.num_programs(0) - 1)
    def _():
        pieces[3].stage(4)


def mlp_back(act, slope, w_up, w_down, cot, normed, resid, mixed, w_out, vecs, grad=None):
    rows, width = cot.shape
    hidden = w_up.shape[1]
    row_steps, ff_steps = rows // ROW_TILE, hidden // FF_TILE
    at_row = lambda s: (jnp.maximum(s - ff_steps, 0), 0)
    at_col = lambda s: (0, jnp.minimum(s, ff_steps - 1))
    at_ff = lambda s: (jnp.minimum(s, ff_steps - 1), 0)
    const = lambda s: (0, 0)
    hbm, vmem = pl.BlockSpec(memory_space=pl.ANY), pl.BlockSpec(memory_space=pltpu.VMEM)
    once = lambda *shape: pl.BlockSpec(shape, const, pipeline_mode=pl.Buffered(1))
    tall = pl.BlockSpec((rows, FF_TILE), at_col)
    tile = pl.BlockSpec((ROW_TILE, width), at_row)
    in_specs = [
        tall, tall, pl.BlockSpec((width, FF_TILE), at_col), pl.BlockSpec((FF_TILE, width), at_ff),
        once(rows, width), once(rows, width), tile, once(rows, width), once(width, width),
        once(8, width),
    ]
    out_specs = [
        pl.BlockSpec((width, FF_TILE), at_col), pl.BlockSpec((1, FF_TILE), at_col), tile, tile,
        tile, once(width, width), once(8, width),
    ]
    out_shape = [
        jax.ShapeDtypeStruct((width, hidden), BF),
        jax.ShapeDtypeStruct((1, hidden), F32),
        jax.ShapeDtypeStruct((rows, width), BF),
        jax.ShapeDtypeStruct((rows, width), F32),
        jax.ShapeDtypeStruct((rows, width), BF),
        jax.ShapeDtypeStruct((width, width), BF),
        jax.ShapeDtypeStruct((8, width), F32),
    ]
    scratch = [
        pltpu.VMEM((rows, width), F32),
        pltpu.VMEM((rows, width), F32),
        pltpu.VMEM((rows, width), BF),
        pltpu.VMEM((rows, FF_TILE), BF),
    ]
    params = dict(vmem_limit_bytes=62 * 2**20)
    args = [act, slope, w_up, w_down, cot, normed, resid, mixed, w_out, vecs]
    kernel = mlp_back_kernel
    if grad is not None:
        kernel = mlp_back_scatter_kernel
        part = grad.shape[0] // 32
        in_specs += [hbm]
        out_specs += [vmem]
        out_shape += [jax.ShapeDtypeStruct((part, width), F32)]
        scratch += scatter_scratch(part, width // 4) * 4
        params |= dict(collective_id=6, has_side_effects=True)
        args += [blocks(grad)]
    return pl.pallas_call(
        functools.partial(kernel, ff_steps),
        grid=(row_steps + ff_steps,),
        in_specs=in_specs,
        out_specs=out_specs,
        out_shape=out_shape,
        scratch_shapes=scratch,
        compiler_params=pltpu.CompilerParams(**params),
        name="mlp_back",
    )(*args)


TILE = 64


class Total:
    def __init__(self, place, value, arrived, send, recv):
        p = place
        self.rounds = [p.zp, [p.xp, p.yp, p.far], [p.sib]]
        self.value, self.arrived, self.send, self.recv = value, arrived, send, recv

    def copies(self, i):
        slot = sum(len(targets) for targets in self.rounds[:i])
        return slot, [
            mesh_copy(
                self.value.at[i], self.arrived.at[slot + k], self.send.at[slot + k],
                self.recv.at[slot + k], to,
            )
            for k, to in enumerate(self.rounds[i])
        ]

    def stage(self, number):
        if number > 0:
            slot, copies = self.copies(number - 1)
            total = self.value[number - 1]
            for k, copy in enumerate(copies):
                copy.wait()
                total = total + self.arrived[slot + k]
            self.value[number] = total
        if number < len(self.rounds):
            for copy in self.copies(number)[1]:
                copy.start()


def last_body(
    step, n0_ref, normed, dq, dk, dv, dn, w_q, tokens, dresid, vecs, sums, up_sums, kv_sums,
    out, grads, padded, outgoing, incoming, send, recv, dqw, vector_out,
):
    rows = dq.shape[0]
    ext, width = normed.shape
    images = Images(n0_ref[0], rows, ext)
    bases = [images.base(span[0]) for span in images.spans]
    me, peers = lax.axis_index(AXIS), lax.axis_size(AXIS)
    wide = slice(TILE, TILE + WIN)

    def halo(way):
        return mesh_copy(
            outgoing if way else dn.at[0], incoming.at[way], send.at[way], recv.at[way],
            me + 1 if way else me - 1,
        )

    def column_sums(value):
        return jnp.sum(value.astype(F32), axis=0, keepdims=True)

    @pl.when(step == 0)
    def _():
        outgoing[...] = jnp.where(images.third, dn[2], dn[1])
        pl.when(me > 0)(lambda: halo(0).start())
        pl.when(me < peers - 1)(lambda: halo(1).start())
        vector_out[...] = jnp.zeros(vector_out.shape, F32)
        vector_out[0:2] = kv_sums[0:2]
        vector_out[4:8] = sums[0:4]
        for k in range(up_sums.shape[1] // width):
            vector_out[8 + k : 9 + k] = up_sums[:, k * width : (k + 1) * width]
        vector_out[2:3] = column_sums(dq[...])
        padded[...] = jnp.zeros(padded.shape, BF)

        @pl.when(me == 0)
        def _():
            incoming[1] = jnp.zeros(incoming.shape[1:], BF)

        @pl.when(me == peers - 1)
        def _():
            incoming[0] = jnp.zeros(incoming.shape[1:], BF)

        for col in range(0, width, ROW_TILE):
            cols = pl.ds(col, ROW_TILE)
            grads[0, cols, :] = dot(normed[pl.ds(RIM, rows), cols], dq[...], TN).astype(BF)

    for which, part in ((1, dk), (2, dv)):
        @pl.when(step == which)
        def _():
            for col in range(0, width, ROW_TILE):
                cols = pl.ds(col, ROW_TILE)
                total = None
                for seg, base in enumerate(bases):
                    term = dot(normed[pl.ds(base * 16, WIN), cols], part[seg], TN)
                    total = term if total is None else total + term
                grads[which, cols, :] = total.astype(BF)
            if which == 2:
                vector_out[3:4] = (
                    column_sums(dv[0]) + column_sums(dv[1]) + column_sums(dv[2])
                )

    @pl.when((step >= 3) & (step < 7))
    def _():
        part = pl.ds((step - 3) * ROW_TILE, ROW_TILE)
        upstream = dot(dq[part, :], w_q[...], NT)
        dqw[part, :] = upstream
        scaled = row_stats(tokens[...].astype(F32))[0]
        vector_out[0:1] += jnp.sum(upstream * scaled, axis=0, keepdims=True)
        vector_out[1:2] += jnp.sum(upstream, axis=0, keepdims=True)

    @pl.when(step == 7)
    def _():
        @pl.when(me > 0)
        def _():
            halo(0).wait_send()
            halo(1).wait_recv()

        @pl.when(me < peers - 1)
        def _():
            halo(1).wait_send()
            halo(0).wait_recv()

        none = jnp.zeros((WIN, width), F32)
        stop = jnp.where(images.third, images.spans[2][1], images.spans[1][1])
        cut = (stop > RIM + rows) & (me < peers - 1)
        after = jnp.where(cut, incoming[0].astype(F32), none)
        before = jnp.where(images.spans[0][0] < RIM, incoming[1].astype(F32), none)
        padded[0, wide] = (dn[0].astype(F32) + before).astype(BF)
        padded[1, wide] = (dn[1].astype(F32) + jnp.where(images.third, none, after)).astype(BF)
        padded[2, wide] = (dn[2].astype(F32) + jnp.where(images.third, after, none)).astype(BF)

    @pl.when(step >= 7)
    def _():
        upstream = dqw[pl.ds((step - 7) * ROW_TILE, ROW_TILE), :]
        places = []
        for k in range(ROW_TILE // TILE):
            total = upstream[k * TILE : (k + 1) * TILE]
            for seg, base in enumerate(bases):
                off = jnp.maximum(
                    (RIM + TILE) // 16 + (step - 7) * (ROW_TILE // 16) + k * (TILE // 16) - base, 0
                )
                off = jnp.minimum(off, (WIN + TILE) // 16) * 16
                total = total + padded[seg, pl.ds(off, TILE), :].astype(F32)
            places.append(total)
        upstream = jnp.concatenate(places, axis=0)
        scaled, inv_std = row_stats(tokens[...].astype(F32))
        through = upstream * vecs[0:1]
        inner = (
            through
            - jnp.mean(through, axis=1, keepdims=True)
            - scaled * jnp.mean(through * scaled, axis=1, keepdims=True)
        )
        out[...] = dresid[...] + inv_std * inner


LAST_STEPS = 11


def last_kernel(*refs):
    step = pl.program_id(0)
    me, peers = lax.axis_index(AXIS), lax.axis_size(AXIS)
    ins, (out, vector_out, grads_out), scratch = refs[:13], refs[13:16], refs[16:]
    grads, padded, outgoing, incoming, send, recv, dqw = scratch
    pl.when(step == 0)(lambda: greet([], me > 0, me < peers - 1))
    last_body(step, *ins, out, grads, padded, outgoing, incoming, send, recv, dqw, vector_out)

    @pl.when(step == LAST_STEPS - 1)
    def _():
        grads_out[...] = grads[...]


def last_scatter_kernel(*refs):
    step = pl.program_id(0)
    me, peers = lax.axis_index(AXIS), lax.axis_size(AXIS)
    ins, (out, vector_out, reduced, up_own), scratch = refs[:13], refs[13:17], refs[17:]
    grads, padded, outgoing, incoming, send, recv, dqw = scratch[:7]
    vectors, arrived, vec_send, vec_recv = scratch[7:11]
    comm = scratch[11:]
    place = Place()
    pl.when(step == 0)(
        lambda: greet([*place.partners, place.far], me > 0, me < peers - 1)
    )
    pieces = [
        Scatter(
            place, grads.at[k], *comm[k * 8 : k * 8 + 5], reduced.at[:, pl.ds(k * UNIT, UNIT)],
            comm[k * 8 + 5 : k * 8 + 8], k == 0,
        )
        for k in range(3)
    ]
    total = Total(place, vectors, arrived, vec_send, vec_recv)
    part = vector_out.shape[1]
    for i in range(4):
        pl.when(step == 7 + i)(functools.partial(total.stage, i))
    run_stages(pieces, step, (1, 2, 3, 7, 8, 9))
    last_body(
        step, *ins, out, Flat(grads), padded, outgoing, incoming, send, recv, dqw, vectors.at[0]
    )

    @pl.when(step == LAST_STEPS - 1)
    def _():
        own, up = vectors[3, :8, :part], vectors[3, 8:9, :128]
        for k in range(1, peers):
            own = jnp.where(me == k, vectors[3, :8, k * part : (k + 1) * part], own)
            row, col = 8 + k // 8, k % 8 * 128
            up = jnp.where(me == k, vectors[3, row : row + 1, col : col + 128], up)
        vector_out[...] = own
        up_own[...] = up
        pieces[2].stage(4)


class Flat:
    def __init__(self, ref):
        self.ref = ref

    def __setitem__(self, index, value):
        k, rows, _ = index
        part = self.ref.shape[5]
        count = rows.size // part
        first = rows.start // part
        for i in range(0, count, 8):
            block = value[i * part : (i + 8) * part].reshape(2, 2, 2, part, value.shape[1])
            self.ref[k, (first + i) // 8] = block


def last(
    n0, normed, dq, dk, dv, dn, w_qkv, tokens, dresid, vecs, sums, up_sums, kv_sums, plan
):
    rows, width = dq.shape
    ext = normed.shape[0]
    peers = lax.axis_size(AXIS)
    const = lambda s: (0, 0)
    once = lambda *shape: pl.BlockSpec(
        shape, lambda s: (0,) * len(shape), pipeline_mode=pl.Buffered(1)
    )
    tile = pl.BlockSpec((ROW_TILE, width), lambda s: (jnp.maximum(s - 7, 0), 0))
    twice = pl.BlockSpec(
        (ROW_TILE, width), lambda s: (jnp.where(s < 7, jnp.maximum(s - 3, 0), s - 7), 0)
    )
    vmem = pl.BlockSpec(memory_space=pltpu.VMEM)
    in_specs = [
        pl.BlockSpec(memory_space=pltpu.SMEM),
        once(ext, width), once(rows, width), once(3, WIN, width), once(3, WIN, width),
        once(3, WIN, width), once(width, width), twice, tile, once(*vecs.shape), once(8, width),
        once(*up_sums.shape), once(8, width),
    ]
    vector_rows = 16
    shared = [
        pltpu.VMEM((3, WIN + 2 * TILE, width), BF),
        pltpu.VMEM((WIN, width), BF),
        pltpu.VMEM((2, WIN, width), BF),
        pltpu.SemaphoreType.DMA((2,)),
        pltpu.SemaphoreType.DMA((2,)),
        pltpu.VMEM((rows, width), F32),
    ]
    if plan:
        part = width // peers
        kernel, collective = last_scatter_kernel, 3
        scratch = [pltpu.VMEM((3, 4, 2, 2, 2, part, width), BF)] + shared + [
            pltpu.VMEM((4, vector_rows, width), F32),
            pltpu.VMEM((7, vector_rows, width), F32),
            pltpu.SemaphoreType.DMA((7,)),
            pltpu.SemaphoreType.DMA((7,)),
        ] + scatter_scratch(part, UNIT, tilt=True) + scatter_scratch(part, UNIT) * 2
        third_out = jax.ShapeDtypeStruct((part, 3 * width), F32)
        vector_shapes = [(8, part), (1, 128)]
    else:
        kernel, collective = last_kernel, 4
        scratch = [pltpu.VMEM((3, width, width), BF)] + shared
        third_out = jax.ShapeDtypeStruct((3, width, width), BF)
        vector_shapes = [(vector_rows, width)]
    return pl.pallas_call(
        kernel,
        grid=(LAST_STEPS,),
        in_specs=in_specs,
        out_specs=[tile, once(*vector_shapes[0]), once(*third_out.shape)]
        + [once(*v) for v in vector_shapes[1:]],
        out_shape=[
            jax.ShapeDtypeStruct((rows, width), F32),
            jax.ShapeDtypeStruct(vector_shapes[0], F32),
            third_out,
            *(jax.ShapeDtypeStruct(v, F32) for v in vector_shapes[1:]),
        ],
        scratch_shapes=scratch,
        compiler_params=pltpu.CompilerParams(
            vmem_limit_bytes=61 * 2**20, collective_id=collective, has_side_effects=True
        ),
        name="last",
    )(n0, normed, dq, dk, dv, dn, w_qkv, tokens, dresid, vecs, sums, up_sums, kv_sums)


def shifted(value, by):
    peers = lax.axis_size(AXIS)
    pairs = [(i, i + by) for i in range(peers) if 0 <= i + by < peers]
    return lax.ppermute(value, AXIS, pairs)


def gathered(value):
    return lax.all_gather(value, AXIS, axis=0, tiled=True)


def scattered(value):
    return lax.psum_scatter(value, AXIS, scatter_dimension=0, tiled=True)


def local(
    tokens,
    image_ids,
    cotangent,
    norm1_gain,
    norm1_shift,
    qkv_weight,
    query_bias,
    value_bias,
    out_weight,
    out_bias,
    norm2_gain,
    norm2_shift,
    up_weight,
    up_bias,
    down_weight,
    down_bias,
):
    rows, width = tokens.shape
    me = lax.axis_index(AXIS)
    peers = lax.axis_size(AXIS)
    ext = -(-(rows + 2 * RIM + 64) // 128) * 128
    vectors = [
        norm1_gain, norm1_shift, query_bias, value_bias, out_bias, norm2_gain, norm2_shift,
        down_bias,
    ]
    part = norm1_gain.shape[0]
    block_plan = peers == 32
    if block_plan:
        lane = lax.broadcasted_iota(jnp.int32, (1, 128), 1) // part
        spread = jnp.tile(jnp.stack(vectors), (1, 128 // part))
        spread = jnp.where(lane == me % (128 // part), spread, jnp.zeros_like(spread))
        vec = jnp.concatenate(
            [spread, up_bias[None], jnp.zeros((VEC_ROWS - 9, 128), BF)], axis=0
        )
        (
            queries, key_value, normed_ext, scaled_ext, w_qkv, vectors, u_bias, vecs, n0, columns
        ) = first(
            tokens, qkv_weight, vec, image_ids.reshape(-1, 128), (out_weight, up_weight), ext
        )
        u_bias = u_bias[0]
    else:
        n0 = jnp.sum((image_ids == image_ids[0]).astype(jnp.int32)).reshape(1)
        gathered_vec = gathered(jnp.concatenate([*vectors, up_bias])[None]).astype(F32)
        gain1, shift1, q_bias, v_bias, o_bias, gain2, shift2, d_bias = (
            gathered_vec[:, i * part : (i + 1) * part].reshape(-1) for i in range(8)
        )
        u_bias = gathered_vec[:, 8 * part :].reshape(-1)
        none = [jnp.zeros_like(d_bias)] * 4
        vecs = jnp.stack([o_bias, gain2, shift2, d_bias] + none)
        vectors = jnp.stack([gain1] + none * 3 + none[:3])
        w_qkv, w_out, w_up, w_down = map(
            gathered, (qkv_weight, out_weight, up_weight, down_weight)
        )
        low_rim = shifted(tokens[rows - RIM :], 1)
        high_rim = shifted(tokens[:RIM], -1)
        pad = jnp.zeros((ext - rows - 2 * RIM, width), BF)
        tokens_ext = jnp.concatenate([low_rim, tokens, high_rim, pad], axis=0).astype(F32)
        scaled_ext = row_stats(tokens_ext)[0]
        normed_ext = (scaled_ext * gain1 + shift1).astype(BF)
        scaled_ext = scaled_ext.astype(BF)
        normed_low = normed_ext[RIM : RIM + rows]
        queries = (dot(normed_low, w_qkv[:, :width]) + q_bias).astype(BF)
        key_value = (
            dot(normed_ext, w_qkv[:, width:])
            + jnp.concatenate([jnp.zeros_like(v_bias), v_bias])
        ).astype(BF)
    if block_plan:
        mixed_low, lse, w_out, w_up, down_column = attend(
            n0, queries, key_value, columns, down_weight
        )
        w_out, w_up = w_out.reshape(width, -1), w_up.reshape(width, -1)
    else:
        mixed_low, lse = attend(n0, queries, key_value)

    args = (mixed_low, tokens, w_out, vecs, w_up, u_bias[None], cotangent)
    if block_plan:
        resid, normed_two, act, slope, grad_down, w_down = mlp_up(*args, down_column)
        w_down = w_down.reshape(-1, width)
    else:
        resid, normed_two, act, slope, grad_down = mlp_up(*args)
    args = (act, slope, w_up, w_down, cotangent, normed_two, resid, mixed_low, w_out, vecs)
    if block_plan:
        grad_up, up_sums, layer_out, dresid, dmixed_low, grad_out, sums, r_down = mlp_back(
            *args, grad_down
        )
    else:
        grad_up, up_sums, layer_out, dresid, dmixed_low, grad_out, sums = mlp_back(*args)
        r_down = scattered(grad_down).astype(F32)
    if block_plan:
        dquery, dkey, dvalue, dnormed, kv_sums, r_out, r_up = attend_back(
            n0, queries, key_value, dmixed_low, lse, w_qkv, scaled_ext, (grad_out, grad_up)
        )
    else:
        dquery, dkey, dvalue, dnormed, kv_sums = attend_back(
            n0, queries, key_value, dmixed_low, lse, w_qkv, scaled_ext
        )
        r_out, r_up = (scattered(v).astype(F32) for v in (grad_out, grad_up))
    grad_tokens, totals, r_qkv, *up_own = last(
        n0, normed_ext, dquery, dkey, dvalue, dnormed, w_qkv, tokens, dresid, vectors, sums,
        up_sums, kv_sums, block_plan,
    )
    if block_plan:
        owned, up_own = totals, up_own[0][0]
    else:
        totals = lax.psum(totals, AXIS)
        r_qkv = jnp.concatenate([scattered(v) for v in r_qkv], axis=1).astype(F32)
        owned = lax.dynamic_slice_in_dim(totals[:8], me * part, part, 1)
        size = u_bias.shape[0] // peers
        up_rows = totals[8 : 8 + u_bias.shape[0] // width].reshape(-1)
        up_own = lax.dynamic_slice_in_dim(up_rows, me * size, size)
    g = [owned[i] for i in range(8)] + [up_own]
    return (
        layer_out, grad_tokens, g[0], g[1], r_qkv, g[2], g[3], r_out, g[4], g[5], g[6], r_up,
        g[8], r_down, g[7],
    )


def solution(mesh):
    row, vec = P(AXIS, None), P(AXIS)
    return jax.shard_map(
        local,
        mesh=mesh,
        in_specs=(
            row, vec, row, vec, vec, row, vec, vec, row, vec, vec, vec, row, vec, row, vec,
        ),
        out_specs=(
            row, row, vec, vec, row, vec, vec, row, vec, vec, vec, row, vec, row, vec,
        ),
        check_vma=False,
    )
```

```python
import functools
import math

import jax
import jax.numpy as jnp
from jax import lax
from jax.experimental import pallas as pl
from jax.experimental.pallas import tpu as pltpu
from jax.sharding import PartitionSpec as P

HDIM = 64
IMG = 577
RIM = IMG - 1
WIN = 592
QB = 128
EPS = 1e-06
NEG = -1e30
AXIS = "fsdp"
BF = jnp.bfloat16
F32 = jnp.float32
NT = (((1,), (1,)), ((), ()))
TN = (((0,), (0,)), ((), ()))
NN = (((1,), (0,)), ((), ()))


def dot(a, b, dims=NN):
    return lax.dot_general(a, b, dims, preferred_element_type=F32)


def stacked(block):
    lane = lax.broadcasted_iota(jnp.int32, block.shape, 1)
    zero = jnp.zeros_like(block)
    return jnp.concatenate(
        [jnp.where(lane < HDIM, block, zero), jnp.where(lane >= HDIM, block, zero)], axis=0
    )


def unstacked(wide):
    return jnp.concatenate([wide[:HDIM, :QB], wide[HDIM:, QB:]], axis=0).T


def key_mask(low, high):
    row = lax.broadcasted_iota(jnp.int32, (WIN, QB), 0)
    bias = jnp.where((row >= low) & (row < high), 0.0, NEG)
    return jnp.concatenate([bias, bias], axis=1)


def mesh_copy(src, dst, send_sem, recv_sem, to):
    return pltpu.make_async_remote_copy(
        src_ref=src,
        dst_ref=dst,
        send_sem=send_sem,
        recv_sem=recv_sem,
        device_id=(to,),
        device_id_type=pl.DeviceIdType.MESH,
    )


class Place:
    def __init__(self):
        me = lax.axis_index(AXIS)
        self.c, self.x, self.y, self.z = me % 2, me // 2 % 2, me // 4 % 2, me // 8
        self.sib = self.at(self.z, self.y, self.x, 1 - self.c)
        self.xp = self.at(self.z, self.y, 1 - self.x, self.c)
        self.yp = self.at(self.z, 1 - self.y, self.x, self.c)
        self.zp = [self.at((self.z + k) % 4, self.y, self.x, self.c) for k in (1, 2, 3)]
        self.far = self.at(self.z, 1 - self.y, 1 - self.x, self.c)
        self.partners = [self.sib, self.xp, self.yp, *self.zp]

    @staticmethod
    def at(z, y, x, c):
        return ((z * 2 + y) * 2 + x) * 2 + c


def greet(partners, before=None, after=None):
    barrier = pltpu.get_barrier_semaphore()

    def hello(to):
        pl.semaphore_signal(
            barrier, inc=1, device_id=(to,), device_id_type=pl.DeviceIdType.MESH
        )

    for to in partners:
        hello(to)
    if before is None:
        pl.semaphore_wait(barrier, len(partners))
        return
    me = lax.axis_index(AXIS)
    pl.when(before)(lambda: hello(me - 1))
    pl.when(after)(lambda: hello(me + 1))
    pl.semaphore_wait(
        barrier, len(partners) + before.astype(jnp.int32) + after.astype(jnp.int32)
    )


class Gather:
    def __init__(self, place, shard, full, cols, send, recv, own, tilt=False):
        self.shard, self.own = shard.at[:, cols], own
        p, rows = place, shard.shape[0]
        half = rows // 2

        def block(y, x, part=slice(None)):
            return full.at[:, y, x, p.c, part, cols]

        mine = full.at[p.z, p.y, p.x, p.c, :, cols]
        self.local = lambda: pltpu.make_async_copy(self.shard, mine, own)

        def copy(i, src, dst, to):
            return lambda: mesh_copy(src, dst, send.at[i], recv.at[i], to)

        same = lambda i, ref, to: copy(i, ref, ref, to)
        first, second = pl.ds(0, half), pl.ds(half, half)
        self.z = [copy(i, self.shard, mine, to) for i, to in enumerate(p.zp)]
        self.xy = [same(3, block(p.y, p.x), p.xp), same(4, block(p.y, p.x), p.yp)]
        self.far = [
            same(5, block(p.y, 1 - p.x, first), p.yp),
            same(6, block(1 - p.y, p.x, second), p.xp),
        ]
        if tilt:
            self.far = [same(5, block(p.y, 1 - p.x), p.yp)]
        self.pair = [
            same(7, block(p.y, p.x), p.sib),
            same(8, block(p.y, 1 - p.x), p.sib),
            same(9, block(1 - p.y, p.x), p.sib),
            same(10, block(1 - p.y, 1 - p.x), p.sib),
        ]

    def stage(self, number):
        if number == 0:
            self.local().start()
            for c in self.z:
                c().start()
        elif number == 1:
            self.local().wait()
            for c in self.z:
                c().wait()
            for c in (*self.xy, self.pair[0]):
                c().start()
        elif number == 2:
            for c in self.xy:
                c().wait()
            for c in (*self.far, self.pair[1], self.pair[2]):
                c().start()
        elif number == 3:
            for c in self.far:
                c().wait()
            self.pair[3]().start()
        else:
            for c in self.pair:
                c().wait()


GATHER_SEMS = 11


class Column:
    def __init__(self, place, shard, column, send, recv, own):
        mine = column.at[place.z]
        self.local = lambda: pltpu.make_async_copy(shard, mine, own)
        self.z = [
            lambda i=i, to=to: mesh_copy(shard, mine, send.at[i], recv.at[i], to)
            for i, to in enumerate(place.zp)
        ]

    def start(self):
        self.local().start()
        for c in self.z:
            c().start()

    def wait(self):
        self.local().wait()
        for c in self.z:
            c().wait()


def column_scratch(count):
    return [
        pltpu.SemaphoreType.DMA((count, 3)),
        pltpu.SemaphoreType.DMA((count, 3)),
        pltpu.SemaphoreType.DMA((count,)),
    ]


class GatherRest:
    def __init__(self, place, column, full, cols, send, recv, own):
        p, half = place, column.shape[1] // 2
        first, second = pl.ds(0, half), pl.ds(half, half)
        held = column.at[:, :, cols]

        def block(y, x, part=slice(None)):
            return full.at[:, y, x, p.c, part, cols]

        def copy(i, src, dst, to):
            return lambda: mesh_copy(src, dst, send.at[i], recv.at[i], to)

        same = lambda i, ref, to: copy(i, ref, ref, to)
        mine = block(p.y, p.x)
        self.local = lambda: pltpu.make_async_copy(held, mine, own)
        self.xy = [copy(0, held, mine, p.xp), copy(1, held, mine, p.yp)]
        self.far = [
            same(2, block(p.y, 1 - p.x, first), p.yp),
            same(3, block(1 - p.y, p.x, second), p.xp),
        ]
        self.pair = [
            copy(4, held, mine, p.sib),
            same(5, block(p.y, 1 - p.x), p.sib),
            same(6, block(1 - p.y, p.x), p.sib),
            same(7, block(1 - p.y, 1 - p.x), p.sib),
        ]

    def stage(self, number):
        if number == 0:
            for c in (*self.xy, self.pair[0], self.local):
                c().start()
        elif number == 1:
            for c in self.xy:
                c().wait()
            for c in (*self.far, self.pair[1], self.pair[2]):
                c().start()
        elif number == 2:
            for c in self.far:
                c().wait()
            self.pair[3]().start()
        elif number == 3:
            for c in (*self.pair, self.local):
                c().wait()


def gather_rest(place, arrays, send, recv, own):
    pieces = []
    for column, full in arrays:
        unit = UNIT * 32 // column.shape[1]
        for at in range(0, column.shape[2], unit):
            i = len(pieces)
            pieces.append(
                GatherRest(
                    place, column, full, pl.ds(at, unit), send.at[i], recv.at[i], own.at[i]
                )
            )
    return pieces


def run_stages(pieces, step, steps):
    for at in sorted(set(steps)):
        todo = [
            (q, pieces[tick - q])
            for tick, when in enumerate(steps)
            if when == at
            for q in range(5)
            if 0 <= tick - q < len(pieces)
        ]

        @pl.when(step == at)
        def _():
            for q, piece in todo:
                piece.stage(q)


def run_rest(pieces, ticks):
    for tick in range(ticks, len(pieces) + 4):
        for q in range(5):
            if 0 <= tick - q < len(pieces):
                pieces[tick - q].stage(q)


class Scatter:
    def __init__(self, place, grad, held, from_pair, far, side, line, out, sems, tilt=False):
        self.tilt = tilt
        self.p, self.out = place, out
        self.held, self.from_pair, self.far, self.side, self.line = held, from_pair, far, side, line
        p, rows = place, held.shape[3]
        self.half = rows // 2
        own, send, recv = sems
        first, second = pl.ds(0, self.half), pl.ds(self.half, self.half)

        def copy(i, src, dst, to):
            return lambda: mesh_copy(src, dst, send.at[i], recv.at[i], to)

        self.load = lambda: pltpu.make_async_copy(grad.at[:, :, :, p.c], held, own)
        self.to_pair = copy(0, grad.at[:, :, :, 1 - p.c], from_pair, p.sib)
        self.to_far = [
            copy(1, held.at[:, 1 - p.y, 1 - p.x, first], far.at[0], p.xp),
            copy(2, held.at[:, 1 - p.y, 1 - p.x, second], far.at[1], p.yp),
        ]
        if tilt:
            self.to_far = [copy(1, held.at[:, 1 - p.y, 1 - p.x], far, p.yp)]
        self.to_side = [
            copy(3, held.at[:, p.y, 1 - p.x], side.at[0], p.xp),
            copy(4, held.at[:, 1 - p.y, p.x], side.at[1], p.yp),
        ]
        self.to_line = [
            copy(5 + k, held.at[(p.z + k + 1) % 4, p.y, p.x], line.at[k], to)
            for k, to in enumerate(p.zp)
        ]

    def stage(self, number):
        p, half = self.p, self.half
        held, far, side, line = self.held, self.far, self.side, self.line
        if number == 0:
            self.load().start()
            self.to_pair().start()
        elif number == 1:
            self.load().wait()
            self.to_pair().wait()

            @pl.loop(0, 4)
            def _(z):
                for y in range(2):
                    for x in range(2):
                        held[z, y, x] = held[z, y, x] + self.from_pair[z, y, x]

            for c in self.to_far:
                c().start()
        elif number == 2:
            for c in self.to_far:
                c().wait()

            @pl.loop(0, 4)
            def _(z):
                if self.tilt:
                    held[z, p.y, 1 - p.x] = (
                        held[z, p.y, 1 - p.x].astype(F32) + far[z].astype(F32)
                    ).astype(held.dtype)
                    return
                held[z, 1 - p.y, p.x, :half] = (
                    held[z, 1 - p.y, p.x, :half].astype(F32) + far[0, z].astype(F32)
                ).astype(held.dtype)
                held[z, p.y, 1 - p.x, half:] = (
                    held[z, p.y, 1 - p.x, half:].astype(F32) + far[1, z].astype(F32)
                ).astype(held.dtype)

            for c in self.to_side:
                c().start()
        elif number == 3:
            for c in self.to_side:
                c().wait()

            @pl.loop(0, 4)
            def _(z):
                held[z, p.y, p.x] = (
                    held[z, p.y, p.x].astype(F32)
                    + side[0, z].astype(F32)
                    + side[1, z].astype(F32)
                ).astype(held.dtype)

            for c in self.to_line:
                c().start()
        else:
            for c in self.to_line:
                c().wait()
            self.out[...] = (
                held[p.z, p.y, p.x].astype(F32)
                + line[0].astype(F32)
                + line[1].astype(F32)
                + line[2].astype(F32)
            )


SCATTER_SEMS = 8
UNIT = 1024


def scatter_scratch(rows, cols, dtype=BF, tilt=False):
    return [
        pltpu.VMEM((4, 2, 2, rows, cols), dtype),
        pltpu.VMEM((4, 2, 2, rows, cols), dtype),
        pltpu.VMEM((4, rows, cols) if tilt else (2, 4, rows // 2, cols), dtype),
        pltpu.VMEM((2, 4, rows, cols), dtype),
        pltpu.VMEM((3, rows, cols), dtype),
        pltpu.SemaphoreType.DMA,
        pltpu.SemaphoreType.DMA((SCATTER_SEMS,)),
        pltpu.SemaphoreType.DMA((SCATTER_SEMS,)),
    ]


def blocks(value):
    return value.reshape(4, 2, 2, 2, value.shape[0] // 32, value.shape[1])


VEC_ROWS = 16


def first_body(
    rows, tokens, wide, vec, ids, w_out_shard, w_up_shard, q_out, kv_out, normed_out, scaled_out, w_out, vecs_out,
    bias_out, mlp_out, n0_out, out_column, up_column, near, normed, scaled, weights, gathered_vec, queries, pairs, send, recv,
    own, halo_send, halo_recv, load, store, col_send, col_recv, col_own,
):
    place = Place()
    me, peers = lax.axis_index(AXIS), lax.axis_size(AXIS)
    greet(place.partners, me > 0, me < peers - 1)
    width = near.shape[1]
    mine = pl.ds(RIM, rows)

    def halo(way):
        if way == 0:
            src, dst, to = tokens.at[pl.ds(0, RIM)], near.at[pl.ds(RIM + rows, RIM)], me - 1
        else:
            src, dst, to = tokens.at[pl.ds(rows - RIM, RIM)], near.at[pl.ds(0, RIM)], me + 1
        return mesh_copy(src, dst, halo_send.at[way], halo_recv.at[way], to)

    pieces = [
        Gather(
            place, vec, gathered_vec, pl.ds(0, vec.shape[1]), send.at[0], recv.at[0], own.at[0],
            True,
        )
    ]
    for i, k in enumerate((1, 2, 0)):
        pieces.append(
            Gather(
                place, wide, weights, pl.ds(k * UNIT, UNIT), send.at[i + 1], recv.at[i + 1],
                own.at[i + 1],
            )
        )
    g_vec, g_k, g_v, g_q = pieces
    columns = [
        Column(place, shard, column, col_send.at[i], col_recv.at[i], col_own.at[i])
        for i, (shard, column) in enumerate(((w_out_shard, out_column), (w_up_shard, up_column)))
    ]
    own_copy = pltpu.make_async_copy(tokens, near.at[mine], load)
    own_copy.start()
    g_vec.stage(0)
    g_k.stage(0)
    pl.when(me > 0)(lambda: halo(0).start())
    pl.when(me < peers - 1)(lambda: halo(1).start())
    n0_out[0] = jnp.sum((ids[...] == ids[0:1, 0:1]).astype(jnp.int32))
    near[pl.ds(2 * RIM + rows, near.shape[0] - rows - 2 * RIM), :] = jnp.zeros(
        (near.shape[0] - rows - 2 * RIM, width), BF
    )

    @pl.when(me == 0)
    def _():
        near[pl.ds(0, RIM), :] = jnp.zeros((RIM, width), BF)

    @pl.when(me == peers - 1)
    def _():
        near[pl.ds(RIM + rows, RIM), :] = jnp.zeros((RIM, width), BF)

    g_vec.stage(1)
    g_k.stage(1)
    g_v.stage(0)
    g_vec.stage(2)
    g_vec.stage(3)
    g_vec.stage(4)
    table = []
    for z in range(4):
        for y in range(2):
            group = [gathered_vec[z, y, x, c].astype(F32) for x in range(2) for c in range(2)]
            table.append(group[0] + group[1] + group[2] + group[3])
            for x in range(2):
                for c in range(2):
                    at = ((z * 2 + y) * 2 + x) * 2 + c
                    bias_out[:, at * 128 : (at + 1) * 128] = group[x * 2 + c][8:9]
    vecs = jnp.concatenate(table, axis=1)
    vecs_out[...] = vecs
    mlp_out[...] = vecs[4:12]
    gain, shift = vecs[0:1], vecs[1:2]
    q_bias, v_bias = vecs[2:3], vecs[3:4]

    def norm(first, count):
        part = pl.ds(first, count)
        value = row_stats(near[part, :].astype(F32))[0]
        scaled[part, :] = value.astype(BF)
        normed[part, :] = (value * gain + shift).astype(BF)

    own_copy.wait()
    for row in range(RIM, RIM + rows, 256):
        norm(row, 256)
    g_k.stage(2)
    g_v.stage(1)
    g_q.stage(0)
    for column in columns:
        column.start()
    g_k.stage(3)
    g_v.stage(2)
    g_q.stage(1)
    g_k.stage(4)

    def full(k):
        return weights[:, :, :, :, :, pl.ds(k * UNIT, UNIT)].reshape(width, UNIT)

    def project(target, k, first, stop, bias, at):
        matrix = full(k)
        for row in range(first, stop, 256):
            size = min(256, stop - row)
            value = dot(normed[pl.ds(row, size), :], matrix)
            value = value if bias is None else value + bias
            target[pl.ds(row - at[0], size), pl.ds(at[1], UNIT)] = value.astype(BF)

    last_row = near.shape[0]
    project(pairs, 1, RIM, RIM + rows, None, (0, 0))
    g_v.stage(3)
    g_q.stage(2)

    @pl.when(me > 0)
    def _():
        halo(0).wait_send()
        halo(1).wait_recv()

    @pl.when(me < peers - 1)
    def _():
        halo(1).wait_send()
        halo(0).wait_recv()

    for row in range(0, RIM, 192):
        norm(row, 192)
    for row in range(RIM + rows, last_row, 176):
        norm(row, 176)
    normed_copy = pltpu.make_async_copy(normed, normed_out, store.at[0])
    normed_copy.start()
    scaled_copy = pltpu.make_async_copy(scaled, scaled_out, store.at[5])
    scaled_copy.start()
    project(pairs, 1, 0, RIM, None, (0, 0))
    project(pairs, 1, RIM + rows, last_row, None, (0, 0))
    k_copy = pltpu.make_async_copy(
        pairs.at[:, pl.ds(0, UNIT)], kv_out.at[:, pl.ds(0, UNIT)], store.at[1]
    )
    k_copy.start()
    g_v.stage(4)
    g_q.stage(3)
    project(pairs, 2, 0, last_row, v_bias, (0, UNIT))
    v_copy = pltpu.make_async_copy(
        pairs.at[:, pl.ds(UNIT, UNIT)], kv_out.at[:, pl.ds(UNIT, UNIT)], store.at[2]
    )
    v_copy.start()
    g_q.stage(4)
    w_copy = pltpu.make_async_copy(weights, w_out, store.at[3])
    w_copy.start()
    project(queries, 0, RIM, RIM + rows, q_bias, (RIM, 0))
    q_copy = pltpu.make_async_copy(queries, q_out, store.at[4])
    q_copy.start()
    for column in columns:
        column.wait()
    for copy in (normed_copy, scaled_copy, k_copy, v_copy, w_copy, q_copy):
        copy.wait()


def first(tokens, wide, vec, ids, shards, ext):
    rows, width = tokens.shape
    part = wide.shape[0]
    hbm, vmem = pl.BlockSpec(memory_space=pl.ANY), pl.BlockSpec(memory_space=pltpu.VMEM)
    queries, key_value, normed, scaled, w_qkv, vecs, bias, mlp_vecs, n0, *columns = pl.pallas_call(
        functools.partial(first_body, rows),
        in_specs=[hbm] * 3 + [vmem] + [hbm] * 2,
        out_specs=[hbm] * 5 + [vmem] * 3 + [pl.BlockSpec(memory_space=pltpu.SMEM)] + [hbm] * 2,
        out_shape=[
            jax.ShapeDtypeStruct((rows, width), BF),
            jax.ShapeDtypeStruct((ext, 2 * width), BF),
            jax.ShapeDtypeStruct((ext, width), BF),
            jax.ShapeDtypeStruct((ext, width), BF),
            jax.ShapeDtypeStruct((4, 2, 2, 2, *wide.shape), BF),
            jax.ShapeDtypeStruct((VEC_ROWS, width), F32),
            jax.ShapeDtypeStruct((1, 32 * 128), F32),
            jax.ShapeDtypeStruct((8, width), F32),
            jax.ShapeDtypeStruct((1,), jnp.int32),
            *(jax.ShapeDtypeStruct((4, *v.shape), BF) for v in shards),
        ],
        scratch_shapes=[
            pltpu.VMEM((ext, width), BF),
            pltpu.VMEM((ext, width), BF),
            pltpu.VMEM((ext, width), BF),
            pltpu.VMEM((4, 2, 2, 2, *wide.shape), BF),
            pltpu.VMEM((4, 2, 2, 2, *vec.shape), BF),
            pltpu.VMEM((rows, width), BF),
            pltpu.VMEM((ext, 2 * width), BF),
            pltpu.SemaphoreType.DMA((4, GATHER_SEMS)),
            pltpu.SemaphoreType.DMA((4, GATHER_SEMS)),
            pltpu.SemaphoreType.DMA((4,)),
            pltpu.SemaphoreType.DMA((2,)),
            pltpu.SemaphoreType.DMA((2,)),
            pltpu.SemaphoreType.DMA,
            pltpu.SemaphoreType.DMA((6,)),
            *column_scratch(2),
        ],
        compiler_params=pltpu.CompilerParams(
            collective_id=0, has_side_effects=True, vmem_limit_bytes=62 * 2**20
        ),
        name="first",
    )(tokens, wide, vec, ids, *shards)
    w_qkv = w_qkv.reshape(width, wide.shape[1])
    return queries, key_value, normed, scaled, w_qkv, vecs, bias, mlp_vecs, n0, columns


ITEMS = 10
BACK_GROUP = 5
GROUP = 5


class Images:
    def __init__(self, n0, rows, ext):
        self.n0, self.n1, self.rows, self.ext = n0, n0 + IMG, rows, ext
        me, peers = lax.axis_index(AXIS), lax.axis_size(AXIS)
        limit = jnp.where(me == peers - 1, RIM + rows, 2 * RIM + rows)
        start0 = jnp.where(me == 0, RIM, n0 - 1)
        start1 = RIM + n0
        start2 = start1 + IMG
        self.spans = (
            (start0, start1),
            (start1, jnp.minimum(start1 + IMG, limit)),
            (start2, jnp.minimum(start2 + IMG, limit)),
        )
        one = lambda flag: jnp.where(flag, 1, 0)
        self.b0, self.b1 = lax.div(n0, QB), lax.div(self.n1, QB)
        self.d0 = one(self.b0 * QB != n0)
        self.d1 = one((self.n1 < rows) & (self.b1 * QB != self.n1))
        self.third = self.n1 < rows
        self.end0 = lax.div(n0 - 1, QB)
        self.end1 = lax.div(self.n1 - 1, QB) + self.d0
        self.one = one

    def base(self, start):
        return jnp.minimum(lax.div(start, 16), (self.ext - WIN) // 16)

    def segment(self, item):
        return self.one(item > self.end0) + self.one(item > self.end1)

    def item(self, item):
        blk = (
            item
            - self.d0 * self.one(item > self.b0)
            - self.d1 * self.one(item > self.b1 + self.d0)
        )
        used = blk < self.rows // QB
        blk = jnp.minimum(blk, self.rows // QB - 1)
        seg = self.segment(item)
        choose = lambda i: jnp.where(
            seg == 0, self.spans[0][i], jnp.where(seg == 1, self.spans[1][i], self.spans[2][i])
        )
        start, stop = choose(0), choose(1)
        base = self.base(start) * 16
        row0 = blk * QB
        low = jnp.maximum(start - RIM - row0, 0)
        high = jnp.where(used, jnp.minimum(stop - RIM - row0, QB), 0)
        return blk, row0, base, start - base, stop - base, low, high

    def of_block(self, blk):
        at0 = self.d0 * self.one(blk == self.b0)
        at1 = self.d1 * self.one(blk == self.b1)
        first = blk + self.d0 * self.one(blk > self.b0) + self.d1 * self.one(blk > self.b1)
        split = jnp.where(at0 == 1, self.n0, jnp.where(at1 == 1, self.n1, self.rows)) - blk * QB
        return first, first + at0 + at1, split


def attend_body(n0_ref, q_ref, k_ref, v_ref, out_ref, lse_ref, parts, parts_lse):
    rows = q_ref.shape[0]
    images = Images(n0_ref[0], rows, k_ref.shape[0])

    def scores_of(item):
        _, row0, base, low, high, _, _ = images.item(item)
        queries = stacked(q_ref[pl.ds(row0, QB), :]) * jnp.asarray(0.125, BF)
        scores = dot(k_ref[pl.ds(base, WIN), :], queries, NT)
        return scores + key_mask(low, high), base

    def softmax_of(scores):
        top = jnp.max(scores, axis=0, keepdims=True)
        terms = jnp.exp(scores - top)
        total = jnp.sum(terms, axis=0, keepdims=True)
        return terms.astype(BF), top, total

    @pl.loop(0, ITEMS // GROUP)
    def _(step):
        items = [step * GROUP + g for g in range(GROUP)]
        scored = [scores_of(item) for item in items]
        soft = [softmax_of(scores) for scores, _ in scored]
        mixed = [
            dot(v_ref[pl.ds(base, WIN), :], terms, TN) / total
            for (_, base), (terms, _, total) in zip(scored, soft)
        ]
        for item, value, (_, top, total) in zip(items, mixed, soft):
            parts[item] = unstacked(value)
            parts_lse[item] = jnp.broadcast_to(top + jnp.log(total), parts_lse.shape[1:])

    for blk in range(rows // QB):
        first, last, split = images.of_block(blk)
        row = lax.broadcasted_iota(jnp.int32, (QB, 2 * HDIM), 0)
        out_ref[pl.ds(blk * QB, QB), :] = jnp.where(
            row < split, parts[first], parts[last]
        ).astype(BF)
        lane = lax.broadcasted_iota(jnp.int32, parts_lse.shape[1:], 1) % QB
        lse_ref[0, pl.ds(blk, 1), :] = jnp.where(
            lane < split, parts_lse[first], parts_lse[last]
        )[:1]


def attend_kernel(n0_ref, q_ref, k_ref, v_ref, out_ref, lse_ref, parts, parts_lse):
    attend_body(n0_ref, q_ref, k_ref, v_ref, out_ref, lse_ref, parts, parts_lse)


def attend_gather_kernel(
    n0_ref, q_ref, k_ref, v_ref, c_out, c_up, w_down, out_ref, lse_ref, full_out, full_up,
    c_down, parts, parts_lse, send, recv, own, *column_sems,
):
    tick = pl.program_id(0)
    place = Place()
    column = Column(place, w_down, c_down, *(v.at[0] for v in column_sems))

    @pl.when(tick == 0)
    def _():
        greet(place.partners)

    pieces = gather_rest(place, ((c_out, full_out), (c_up, full_up)), send, recv, own)
    run_stages(pieces, tick, range(7))
    pl.when(tick == 0)(column.start)
    attend_body(n0_ref, q_ref, k_ref, v_ref, out_ref, lse_ref, parts, parts_lse)

    @pl.when(tick == 7)
    def _():
        run_rest(pieces, 7)
        column.wait()


def attend(n0, queries, key_value, columns=None, shard=None):
    rows, width = queries.shape
    pairs = width // (2 * HDIM)
    ext = key_value.shape[0]
    hbm = pl.BlockSpec(memory_space=pl.ANY)
    in_specs = [
        pl.BlockSpec(memory_space=pltpu.SMEM),
        pl.BlockSpec((rows, 2 * HDIM), lambda p: (0, p)),
        pl.BlockSpec((ext, 2 * HDIM), lambda p: (0, p)),
        pl.BlockSpec((ext, 2 * HDIM), lambda p: (0, pairs + p)),
    ]
    out_specs = [
        pl.BlockSpec((rows, 2 * HDIM), lambda p: (0, p)),
        pl.BlockSpec((1, rows // QB, 2 * QB), lambda p: (p, 0, 0)),
    ]
    out_shape = [
        jax.ShapeDtypeStruct((rows, width), BF),
        jax.ShapeDtypeStruct((pairs, rows // QB, 2 * QB), F32),
    ]
    scratch = [
        pltpu.VMEM((ITEMS, QB, 2 * HDIM), F32),
        pltpu.VMEM((ITEMS, 8, 2 * QB), F32),
    ]
    params = dict(vmem_limit_bytes=62 * 2**20)
    args = [n0, queries, key_value, key_value]
    kernel = attend_kernel
    if columns is not None:
        kernel = attend_gather_kernel
        in_specs += [hbm] * 3
        out_specs += [hbm] * 3
        out_shape += [jax.ShapeDtypeStruct((4, 2, 2, 2, *v.shape[1:]), BF) for v in columns]
        out_shape += [jax.ShapeDtypeStruct((4, *shard.shape), BF)]
        count = sum(v.shape[1] * v.shape[2] for v in columns) // (32 * UNIT)
        scratch += [
            pltpu.SemaphoreType.DMA((count, 8)),
            pltpu.SemaphoreType.DMA((count, 8)),
            pltpu.SemaphoreType.DMA((count,)),
            *column_scratch(1),
        ]
        params |= dict(collective_id=1, has_side_effects=True)
        args += [*columns, shard]
    return pl.pallas_call(
        kernel,
        grid=(pairs,),
        in_specs=in_specs,
        out_specs=out_specs,
        out_shape=out_shape,
        scratch_shapes=scratch,
        compiler_params=pltpu.CompilerParams(**params),
        name="attend",
    )(*args)


def attend_back_body(
    pair, n0_ref, q_ref, k_ref, v_ref, up_ref, lse_ref, wk_ref, wv_ref, scaled_ref, dq_ref, dk_ref, dv_ref,
    dn_ref, sums_ref, slots, parts, total,
):
    rows = q_ref.shape[0]
    images = Images(n0_ref[0], rows, k_ref.shape[0])

    @pl.when(pair == 0)
    def _():
        slots[0] = jnp.zeros(slots.shape[1:], F32)
        total[...] = jnp.zeros(total.shape, F32)

    lane = lax.broadcasted_iota(jnp.int32, (1, 2 * QB), 1) % QB

    def begin(item):
        blk, row0, base, low, high, first, stop = images.item(item)
        queries = stacked(q_ref[pl.ds(row0, QB), :]) * jnp.asarray(0.125, BF)
        upstream = stacked(up_ref[pl.ds(row0, QB), :])
        here = (lane >= first) & (lane < stop)
        lse = jnp.where(here, lse_ref[0, pl.ds(blk, 1), :], -NEG)
        scores = dot(k_ref[pl.ds(base, WIN), :], queries, NT)
        dprobs = dot(v_ref[pl.ds(base, WIN), :], upstream, NT)
        return base, queries, upstream, scores + key_mask(low, high), lse, dprobs

    def middle(scores, lse, dprobs):
        probs = jnp.exp(scores - lse)
        row_dot = jnp.sum(probs * dprobs, axis=0, keepdims=True)
        return probs.astype(BF), (probs * (dprobs - row_dot)).astype(BF)

    def finish(item, base, queries, upstream, probs, dscores):
        keep = (item > 0) & (images.segment(item) == images.segment(item - 1))
        old = jnp.where(keep, slots[item], jnp.zeros(slots.shape[1:], F32))
        slots[item + 1, :, : 2 * HDIM] = old[:, : 2 * HDIM] + dot(dscores, queries)
        slots[item + 1, :, 2 * HDIM :] = old[:, 2 * HDIM :] + dot(probs, upstream)
        parts[item] = unstacked(dot(k_ref[pl.ds(base, WIN), :], dscores, TN)) * 0.125

    @pl.loop(0, ITEMS // BACK_GROUP)
    def _(step):
        items = [step * BACK_GROUP + g for g in range(BACK_GROUP)]
        begun = [begin(items[0])]
        done = []
        for g in range(BACK_GROUP + 1):
            if g + 1 < BACK_GROUP:
                begun.append(begin(items[g + 1]))
            if g < BACK_GROUP:
                done.append(middle(*begun[g][3:]))
            if g > 0:
                finish(items[g - 1], *begun[g - 1][:3], *done[g - 1])

    for blk in range(rows // QB):
        first, last, split = images.of_block(blk)
        row = lax.broadcasted_iota(jnp.int32, (QB, 2 * HDIM), 0)
        dq_ref[pl.ds(blk * QB, QB), :] = jnp.where(
            row < split, parts[first], parts[last]
        ).astype(BF)
    ends = (
        images.end0 + 1,
        jnp.minimum(images.end1, (rows - 1) // QB + images.d0) + 1,
        jnp.where(images.third, ITEMS, 0),
    )
    weights = jnp.concatenate([wk_ref[...], wv_ref[...]], axis=1)
    for seg, end in enumerate(ends):
        both = slots[end].astype(BF)
        dk_ref[seg] = both[:, : 2 * HDIM]
        dv_ref[seg] = both[:, 2 * HDIM :]
        total[seg] += dot(both, weights, NT)

    @pl.when(pair == pl.num_programs(0) - 1)
    def _():
        dn_ref[...] = total[...].astype(BF)
        sums_ref[...] = jnp.zeros(sums_ref.shape, F32)
        for seg, span in enumerate(images.spans):
            window = scaled_ref[pl.ds(images.base(span[0]) * 16, WIN), :].astype(F32)
            sums_ref[0:1] += jnp.sum(total[seg] * window, axis=0, keepdims=True)
            sums_ref[1:2] += jnp.sum(total[seg], axis=0, keepdims=True)


def attend_back_kernel(*refs):
    attend_back_body(pl.program_id(0), *refs)


def attend_back_scatter_kernel(*refs):
    base, (g_out, g_up), rest = refs[:9], refs[9:11], refs[11:]
    outs, (r_out, r_up), scratch = rest[:5], rest[5:7], rest[7:]
    mine, comm = scratch[:3], scratch[3:]
    pair = pl.program_id(0)
    place = Place()
    pl.when(pair == 0)(lambda: greet(place.partners))
    pieces = []
    for grad, out in ((g_out, r_out), (g_up, r_up)):
        for k in range(grad.shape[5] // UNIT):
            cols = pl.ds(k * UNIT, UNIT)
            bufs = comm[len(pieces) * 8 : len(pieces) * 8 + 8]
            pieces.append(
                Scatter(
                    place, grad.at[:, :, :, :, :, cols], *bufs[:5], out.at[:, cols], bufs[5:]
                )
            )
    run_stages(pieces, pair, range(8))
    attend_back_body(pair, *base, *outs, *mine)

    @pl.when(pair == pl.num_programs(0) - 1)
    def _():
        pieces[-1].stage(4)


def attend_back(n0, queries, key_value, upstream, lse, w_qkv, scaled, grads=None):
    rows, width = queries.shape
    pairs = width // (2 * HDIM)
    ext = key_value.shape[0]
    hbm, vmem = pl.BlockSpec(memory_space=pl.ANY), pl.BlockSpec(memory_space=pltpu.VMEM)
    own = pl.BlockSpec((rows, 2 * HDIM), lambda p: (0, p))
    windows = pl.BlockSpec((3, WIN, 2 * HDIM), lambda p: (0, 0, p))
    in_specs = [
        pl.BlockSpec(memory_space=pltpu.SMEM),
        own,
        pl.BlockSpec((ext, 2 * HDIM), lambda p: (0, p)),
        pl.BlockSpec((ext, 2 * HDIM), lambda p: (0, pairs + p)),
        own,
        pl.BlockSpec((1, rows // QB, 2 * QB), lambda p: (p, 0, 0)),
        pl.BlockSpec((width, 2 * HDIM), lambda p: (0, pairs + p)),
        pl.BlockSpec((width, 2 * HDIM), lambda p: (0, 2 * pairs + p)),
        pl.BlockSpec((ext, width), lambda p: (0, 0), pipeline_mode=pl.Buffered(1)),
    ]
    out_specs = [
        own, windows, windows,
        pl.BlockSpec((3, WIN, width), lambda p: (0, 0, 0), pipeline_mode=pl.Buffered(1)),
        pl.BlockSpec((8, width), lambda p: (0, 0)),
    ]
    out_shape = [jax.ShapeDtypeStruct((rows, width), BF)]
    out_shape += [jax.ShapeDtypeStruct((3, WIN, width), BF)] * 3
    out_shape += [jax.ShapeDtypeStruct((8, width), F32)]
    scratch = [
        pltpu.VMEM((ITEMS + 1, WIN, 4 * HDIM), F32),
        pltpu.VMEM((ITEMS, QB, 2 * HDIM), F32),
        pltpu.VMEM((3, WIN, width), F32),
    ]
    args = [n0, queries, key_value, key_value, upstream, lse, w_qkv, w_qkv, scaled]
    kernel, params = attend_back_kernel, dict(vmem_limit_bytes=62 * 2**20)
    if grads is not None:
        kernel = attend_back_scatter_kernel
        params |= dict(collective_id=2, has_side_effects=True)
        args += map(blocks, grads)
        in_specs += [hbm] * 2
        out_specs += [vmem] * 2
        out_shape += [jax.ShapeDtypeStruct((v.shape[0] // 32, v.shape[1]), F32) for v in grads]
        for v in grads:
            scratch += scatter_scratch(v.shape[0] // 32, UNIT) * (v.shape[1] // UNIT)
    return pl.pallas_call(
        kernel,
        grid=(pairs,),
        in_specs=in_specs,
        out_specs=out_specs,
        out_shape=out_shape,
        scratch_shapes=scratch,
        compiler_params=pltpu.CompilerParams(**params),
        name="attend_back",
    )(*args)


ROW_TILE = 256
FF_TILE = 512
ROOT_HALF = 1.0 / math.sqrt(2.0)
PDF_SCALE = 1.0 / math.sqrt(2.0 * math.pi)


def row_stats(value):
    mean = jnp.mean(value, axis=1, keepdims=True)
    center = value - mean
    inv_std = lax.rsqrt(jnp.mean(center * center, axis=1, keepdims=True) + EPS)
    return center * inv_std, inv_std


def mlp_up_body(
    step, row_steps, mixed, tokens, w_out, vecs, w_up, up_bias, cot, resid, normed, act, slope,
    g_down, held,
):
    @pl.when(step < row_steps)
    def _():
        value = tokens[...].astype(F32) + dot(mixed[...], w_out[...]) + vecs[0:1]
        resid[...] = value
        low = (row_stats(value)[0] * vecs[1:2] + vecs[2:3]).astype(BF)
        normed[...] = low
        held[pl.ds(step * ROW_TILE, ROW_TILE), :] = low

    @pl.when(step >= row_steps)
    def _():
        rows = held.shape[0]

        for row in range(0, rows, ROW_TILE):
            part = pl.ds(row, ROW_TILE)
            upward = dot(held[part, :], w_up[...]) + up_bias[...]
            cdf = 0.5 * (1.0 + lax.erf(upward * ROOT_HALF))
            pdf = jnp.exp(-0.5 * upward * upward) * PDF_SCALE
            act[part, :] = (upward * cdf).astype(BF)
            slope[part, :] = (cdf + upward * pdf).astype(BF)
        g_down[...] = dot(act[...], cot[...], TN).astype(BF)


def mlp_up_kernel(row_steps, *refs):
    mlp_up_body(pl.program_id(0), row_steps, *refs)


def mlp_up_gather_kernel(row_steps, *refs):
    ins, shard, outs, full = refs[:7], refs[7], refs[8:13], refs[13]
    held, send, recv, own = refs[14:]
    step = pl.program_id(0)
    place = Place()
    pl.when(step == 0)(lambda: greet(place.partners))
    pieces = gather_rest(place, ((shard, full),), send, recv, own)
    run_stages(pieces, step, (0, 4, 6, 8, 10))
    mlp_up_body(step, row_steps, *ins, *outs, held)
    pl.when(step == pl.num_programs(0) - 1)(lambda: run_rest(pieces, 5))


def mlp_up(mixed, tokens, w_out, vecs, w_up, up_bias, cot, shard=None):
    rows, width = tokens.shape
    hidden = w_up.shape[1]
    row_steps, ff_steps = rows // ROW_TILE, hidden // FF_TILE
    at_row = lambda s: (jnp.minimum(s, row_steps - 1), 0)
    at_col = lambda s: (0, jnp.maximum(s - row_steps, 0))
    at_ff = lambda s: (jnp.maximum(s - row_steps, 0), 0)
    const = lambda s: (0, 0)
    hbm = pl.BlockSpec(memory_space=pl.ANY)
    tall = pl.BlockSpec((rows, FF_TILE), at_col)
    in_specs = [
        pl.BlockSpec((ROW_TILE, width), at_row),
        pl.BlockSpec((ROW_TILE, width), at_row),
        pl.BlockSpec((width, width), const),
        pl.BlockSpec((8, width), const),
        pl.BlockSpec((width, FF_TILE), at_col),
        pl.BlockSpec((1, FF_TILE), at_col),
        pl.BlockSpec((rows, width), const),
    ]
    out_specs = [
        pl.BlockSpec((ROW_TILE, width), at_row),
        pl.BlockSpec((ROW_TILE, width), at_row),
        tall,
        tall,
        pl.BlockSpec((FF_TILE, width), at_ff),
    ]
    out_shape = [
        jax.ShapeDtypeStruct((rows, width), F32),
        jax.ShapeDtypeStruct((rows, width), BF),
        jax.ShapeDtypeStruct((rows, hidden), BF),
        jax.ShapeDtypeStruct((rows, hidden), BF),
        jax.ShapeDtypeStruct((hidden, width), BF),
    ]
    scratch = [pltpu.VMEM((rows, width), BF)]
    params = dict(vmem_limit_bytes=62 * 2**20)
    args = [mixed, tokens, w_out, vecs, w_up, up_bias, cot]
    kernel = mlp_up_kernel
    if shard is not None:
        kernel = mlp_up_gather_kernel
        in_specs += [hbm]
        out_specs += [hbm]
        out_shape += [jax.ShapeDtypeStruct((4, 2, 2, 2, *shard.shape[1:]), BF)]
        scratch += [
            pltpu.SemaphoreType.DMA((4, 8)),
            pltpu.SemaphoreType.DMA((4, 8)),
            pltpu.SemaphoreType.DMA((4,)),
        ]
        params |= dict(collective_id=5, has_side_effects=True)
        args += [shard]
    return pl.pallas_call(
        functools.partial(kernel, row_steps),
        grid=(row_steps + ff_steps,),
        in_specs=in_specs,
        out_specs=out_specs,
        out_shape=out_shape,
        scratch_shapes=scratch,
        compiler_params=pltpu.CompilerParams(**params),
        name="mlp_up",
    )(*args)


def mlp_back_body(
    step, ff_steps, act, slope, w_up, w_down, cot, normed, resid, mixed, w_out, vecs,
    g_up, up_sums, layer_out, dresid, dmixed, g_out, sums, total, dnormed, branches, dup,
):
    rows, width = cot.shape

    @pl.when(step == 0)
    def _():
        total[...] = jnp.zeros(total.shape, F32)
        dnormed[...] = jnp.zeros(dnormed.shape, F32)
        sums[...] = jnp.zeros(sums.shape, F32)

    @pl.when(step < ff_steps)
    def _():
        count = jnp.zeros(up_sums.shape, F32)
        for row in range(0, rows, ROW_TILE):
            part = pl.ds(row, ROW_TILE)
            total[part, :] += dot(act[part, :], w_down[...])
            dact = dot(cot[part, :], w_down[...], NT)
            low = (dact * slope[part, :].astype(F32)).astype(BF)
            dup[part, :] = low
            count += jnp.sum(low.astype(F32), axis=0, keepdims=True)
            dnormed[part, :] += dot(low, w_up[...], NT)
        up_sums[...] = count
        g_up[...] = dot(normed[...], dup[...], TN).astype(BF)

    @pl.when(step >= ff_steps)
    def _():
        part = pl.ds((step - ff_steps) * ROW_TILE, ROW_TILE)
        value = resid[...]
        scaled, inv_std = row_stats(value)
        upstream = dnormed[part, :]
        above = cot[part, :].astype(F32)
        through = upstream * vecs[1:2]
        inner = (
            through
            - jnp.mean(through, axis=1, keepdims=True)
            - scaled * jnp.mean(through * scaled, axis=1, keepdims=True)
        )
        grad = above + inv_std * inner
        dresid[...] = grad
        low = grad.astype(BF)
        branches[part, :] = low
        dmixed[...] = dot(low, w_out[...], NT).astype(BF)
        layer_out[...] = (value + total[part, :] + vecs[3:4]).astype(BF)
        sums[0:1] += jnp.sum(low.astype(F32), axis=0, keepdims=True)
        sums[1:2] += jnp.sum(upstream * scaled, axis=0, keepdims=True)
        sums[2:3] += jnp.sum(upstream, axis=0, keepdims=True)
        sums[3:4] += jnp.sum(above, axis=0, keepdims=True)

    @pl.when(step == pl.num_programs(0) - 1)
    def _():
        g_out[...] = dot(mixed[...], branches[...], TN).astype(BF)


def mlp_back_kernel(ff_steps, *refs):
    mlp_back_body(pl.program_id(0), ff_steps, *refs)


def mlp_back_scatter_kernel(ff_steps, *refs):
    ins, grad, outs, reduced, scratch, comm = (
        refs[:10], refs[10], refs[11:18], refs[18], refs[19:23], refs[23:],
    )
    step = pl.program_id(0)
    place = Place()
    pl.when(step == 0)(lambda: greet(place.partners))
    cols = reduced.shape[1] // 4
    pieces = []
    for k in range(4):
        here = pl.ds(k * cols, cols)
        bufs = comm[k * 8 : k * 8 + 8]
        pieces.append(
            Scatter(
                place, grad.at[:, :, :, :, :, here], *bufs[:5], reduced.at[:, here], bufs[5:]
            )
        )
    run_stages(pieces, step, (0, 1, 2, 4, 5, 7, 9))
    mlp_back_body(step, ff_steps, *ins, *outs, *scratch)

    @pl.when(step == pl.num_programs(0) - 1)
    def _():
        pieces[3].stage(4)


def mlp_back(act, slope, w_up, w_down, cot, normed, resid, mixed, w_out, vecs, grad=None):
    rows, width = cot.shape
    hidden = w_up.shape[1]
    row_steps, ff_steps = rows // ROW_TILE, hidden // FF_TILE
    at_row = lambda s: (jnp.maximum(s - ff_steps, 0), 0)
    at_col = lambda s: (0, jnp.minimum(s, ff_steps - 1))
    at_ff = lambda s: (jnp.minimum(s, ff_steps - 1), 0)
    const = lambda s: (0, 0)
    hbm, vmem = pl.BlockSpec(memory_space=pl.ANY), pl.BlockSpec(memory_space=pltpu.VMEM)
    once = lambda *shape: pl.BlockSpec(shape, const, pipeline_mode=pl.Buffered(1))
    tall = pl.BlockSpec((rows, FF_TILE), at_col)
    tile = pl.BlockSpec((ROW_TILE, width), at_row)
    in_specs = [
        tall, tall, pl.BlockSpec((width, FF_TILE), at_col), pl.BlockSpec((FF_TILE, width), at_ff),
        once(rows, width), once(rows, width), tile, once(rows, width), once(width, width),
        once(8, width),
    ]
    out_specs = [
        pl.BlockSpec((width, FF_TILE), at_col), pl.BlockSpec((1, FF_TILE), at_col), tile, tile,
        tile, once(width, width), once(8, width),
    ]
    out_shape = [
        jax.ShapeDtypeStruct((width, hidden), BF),
        jax.ShapeDtypeStruct((1, hidden), F32),
        jax.ShapeDtypeStruct((rows, width), BF),
        jax.ShapeDtypeStruct((rows, width), F32),
        jax.ShapeDtypeStruct((rows, width), BF),
        jax.ShapeDtypeStruct((width, width), BF),
        jax.ShapeDtypeStruct((8, width), F32),
    ]
    scratch = [
        pltpu.VMEM((rows, width), F32),
        pltpu.VMEM((rows, width), F32),
        pltpu.VMEM((rows, width), BF),
        pltpu.VMEM((rows, FF_TILE), BF),
    ]
    params = dict(vmem_limit_bytes=62 * 2**20)
    args = [act, slope, w_up, w_down, cot, normed, resid, mixed, w_out, vecs]
    kernel = mlp_back_kernel
    if grad is not None:
        kernel = mlp_back_scatter_kernel
        part = grad.shape[0] // 32
        in_specs += [hbm]
        out_specs += [vmem]
        out_shape += [jax.ShapeDtypeStruct((part, width), F32)]
        scratch += scatter_scratch(part, width // 4) * 4
        params |= dict(collective_id=6, has_side_effects=True)
        args += [blocks(grad)]
    return pl.pallas_call(
        functools.partial(kernel, ff_steps),
        grid=(row_steps + ff_steps,),
        in_specs=in_specs,
        out_specs=out_specs,
        out_shape=out_shape,
        scratch_shapes=scratch,
        compiler_params=pltpu.CompilerParams(**params),
        name="mlp_back",
    )(*args)


TILE = 64


class Total:
    def __init__(self, place, value, arrived, send, recv):
        p = place
        self.rounds = [p.zp, [p.xp, p.yp, p.far], [p.sib]]
        self.value, self.arrived, self.send, self.recv = value, arrived, send, recv

    def copies(self, i):
        slot = sum(len(targets) for targets in self.rounds[:i])
        return slot, [
            mesh_copy(
                self.value.at[i], self.arrived.at[slot + k], self.send.at[slot + k],
                self.recv.at[slot + k], to,
            )
            for k, to in enumerate(self.rounds[i])
        ]

    def stage(self, number):
        if number > 0:
            slot, copies = self.copies(number - 1)
            total = self.value[number - 1]
            for k, copy in enumerate(copies):
                copy.wait()
                total = total + self.arrived[slot + k]
            self.value[number] = total
        if number < len(self.rounds):
            for copy in self.copies(number)[1]:
                copy.start()


def last_body(
    step, n0_ref, normed, dq, dk, dv, dn, w_q, tokens, dresid, vecs, sums, up_sums, kv_sums,
    out, grads, padded, outgoing, incoming, send, recv, dqw, vector_out,
):
    rows = dq.shape[0]
    ext, width = normed.shape
    images = Images(n0_ref[0], rows, ext)
    bases = [images.base(span[0]) for span in images.spans]
    me, peers = lax.axis_index(AXIS), lax.axis_size(AXIS)
    wide = slice(TILE, TILE + WIN)

    def halo(way):
        return mesh_copy(
            outgoing if way else dn.at[0], incoming.at[way], send.at[way], recv.at[way],
            me + 1 if way else me - 1,
        )

    def column_sums(value):
        return jnp.sum(value.astype(F32), axis=0, keepdims=True)

    @pl.when(step == 0)
    def _():
        outgoing[...] = jnp.where(images.third, dn[2], dn[1])
        pl.when(me > 0)(lambda: halo(0).start())
        pl.when(me < peers - 1)(lambda: halo(1).start())
        vector_out[...] = jnp.zeros(vector_out.shape, F32)
        vector_out[0:2] = kv_sums[0:2]
        vector_out[4:8] = sums[0:4]
        for k in range(up_sums.shape[1] // width):
            vector_out[8 + k : 9 + k] = up_sums[:, k * width : (k + 1) * width]
        vector_out[2:3] = column_sums(dq[...])
        padded[...] = jnp.zeros(padded.shape, BF)

        @pl.when(me == 0)
        def _():
            incoming[1] = jnp.zeros(incoming.shape[1:], BF)

        @pl.when(me == peers - 1)
        def _():
            incoming[0] = jnp.zeros(incoming.shape[1:], BF)

        for col in range(0, width, ROW_TILE):
            cols = pl.ds(col, ROW_TILE)
            grads[0, cols, :] = dot(normed[pl.ds(RIM, rows), cols], dq[...], TN).astype(BF)

    for which, part in ((1, dk), (2, dv)):
        @pl.when(step == which)
        def _():
            for col in range(0, width, ROW_TILE):
                cols = pl.ds(col, ROW_TILE)
                total = None
                for seg, base in enumerate(bases):
                    term = dot(normed[pl.ds(base * 16, WIN), cols], part[seg], TN)
                    total = term if total is None else total + term
                grads[which, cols, :] = total.astype(BF)
            if which == 2:
                vector_out[3:4] = (
                    column_sums(dv[0]) + column_sums(dv[1]) + column_sums(dv[2])
                )

    @pl.when((step >= 3) & (step < 7))
    def _():
        part = pl.ds((step - 3) * ROW_TILE, ROW_TILE)
        upstream = dot(dq[part, :], w_q[...], NT)
        dqw[part, :] = upstream
        scaled = row_stats(tokens[...].astype(F32))[0]
        vector_out[0:1] += jnp.sum(upstream * scaled, axis=0, keepdims=True)
        vector_out[1:2] += jnp.sum(upstream, axis=0, keepdims=True)

    @pl.when(step == 7)
    def _():
        @pl.when(me > 0)
        def _():
            halo(0).wait_send()
            halo(1).wait_recv()

        @pl.when(me < peers - 1)
        def _():
            halo(1).wait_send()
            halo(0).wait_recv()

        none = jnp.zeros((WIN, width), F32)
        stop = jnp.where(images.third, images.spans[2][1], images.spans[1][1])
        cut = (stop > RIM + rows) & (me < peers - 1)
        after = jnp.where(cut, incoming[0].astype(F32), none)
        before = jnp.where(images.spans[0][0] < RIM, incoming[1].astype(F32), none)
        padded[0, wide] = (dn[0].astype(F32) + before).astype(BF)
        padded[1, wide] = (dn[1].astype(F32) + jnp.where(images.third, none, after)).astype(BF)
        padded[2, wide] = (dn[2].astype(F32) + jnp.where(images.third, after, none)).astype(BF)

    @pl.when(step >= 7)
    def _():
        upstream = dqw[pl.ds((step - 7) * ROW_TILE, ROW_TILE), :]
        places = []
        for k in range(ROW_TILE // TILE):
            total = upstream[k * TILE : (k + 1) * TILE]
            for seg, base in enumerate(bases):
                off = jnp.maximum(
                    (RIM + TILE) // 16 + (step - 7) * (ROW_TILE // 16) + k * (TILE // 16) - base, 0
                )
                off = jnp.minimum(off, (WIN + TILE) // 16) * 16
                total = total + padded[seg, pl.ds(off, TILE), :].astype(F32)
            places.append(total)
        upstream = jnp.concatenate(places, axis=0)
        scaled, inv_std = row_stats(tokens[...].astype(F32))
        through = upstream * vecs[0:1]
        inner = (
            through
            - jnp.mean(through, axis=1, keepdims=True)
            - scaled * jnp.mean(through * scaled, axis=1, keepdims=True)
        )
        out[...] = dresid[...] + inv_std * inner


LAST_STEPS = 11


def last_kernel(*refs):
    step = pl.program_id(0)
    me, peers = lax.axis_index(AXIS), lax.axis_size(AXIS)
    ins, (out, vector_out, grads_out), scratch = refs[:13], refs[13:16], refs[16:]
    grads, padded, outgoing, incoming, send, recv, dqw = scratch
    pl.when(step == 0)(lambda: greet([], me > 0, me < peers - 1))
    last_body(step, *ins, out, grads, padded, outgoing, incoming, send, recv, dqw, vector_out)

    @pl.when(step == LAST_STEPS - 1)
    def _():
        grads_out[...] = grads[...]


def last_scatter_kernel(*refs):
    step = pl.program_id(0)
    me, peers = lax.axis_index(AXIS), lax.axis_size(AXIS)
    ins, (out, vector_out, reduced, up_own), scratch = refs[:13], refs[13:17], refs[17:]
    grads, padded, outgoing, incoming, send, recv, dqw = scratch[:7]
    vectors, arrived, vec_send, vec_recv = scratch[7:11]
    comm = scratch[11:]
    place = Place()
    pl.when(step == 0)(
        lambda: greet([*place.partners, place.far], me > 0, me < peers - 1)
    )
    pieces = [
        Scatter(
            place, grads.at[k], *comm[k * 8 : k * 8 + 5], reduced.at[:, pl.ds(k * UNIT, UNIT)],
            comm[k * 8 + 5 : k * 8 + 8], k == 0,
        )
        for k in range(3)
    ]
    total = Total(place, vectors, arrived, vec_send, vec_recv)
    part = vector_out.shape[1]
    for i in range(4):
        pl.when(step == 7 + i)(functools.partial(total.stage, i))
    run_stages(pieces, step, (1, 2, 3, 7, 8, 9))
    last_body(
        step, *ins, out, Flat(grads), padded, outgoing, incoming, send, recv, dqw, vectors.at[0]
    )

    @pl.when(step == LAST_STEPS - 1)
    def _():
        own, up = vectors[3, :8, :part], vectors[3, 8:9, :128]
        for k in range(1, peers):
            own = jnp.where(me == k, vectors[3, :8, k * part : (k + 1) * part], own)
            row, col = 8 + k // 8, k % 8 * 128
            up = jnp.where(me == k, vectors[3, row : row + 1, col : col + 128], up)
        vector_out[...] = own
        up_own[...] = up
        pieces[2].stage(4)


class Flat:
    def __init__(self, ref):
        self.ref = ref

    def __setitem__(self, index, value):
        k, rows, _ = index
        part = self.ref.shape[5]
        count = rows.size // part
        first = rows.start // part
        for i in range(0, count, 8):
            block = value[i * part : (i + 8) * part].reshape(2, 2, 2, part, value.shape[1])
            self.ref[k, (first + i) // 8] = block


def last(
    n0, normed, dq, dk, dv, dn, w_qkv, tokens, dresid, vecs, sums, up_sums, kv_sums, plan
):
    rows, width = dq.shape
    ext = normed.shape[0]
    peers = lax.axis_size(AXIS)
    const = lambda s: (0, 0)
    once = lambda *shape: pl.BlockSpec(
        shape, lambda s: (0,) * len(shape), pipeline_mode=pl.Buffered(1)
    )
    tile = pl.BlockSpec((ROW_TILE, width), lambda s: (jnp.maximum(s - 7, 0), 0))
    twice = pl.BlockSpec(
        (ROW_TILE, width), lambda s: (jnp.where(s < 7, jnp.maximum(s - 3, 0), s - 7), 0)
    )
    vmem = pl.BlockSpec(memory_space=pltpu.VMEM)
    in_specs = [
        pl.BlockSpec(memory_space=pltpu.SMEM),
        once(ext, width), once(rows, width), once(3, WIN, width), once(3, WIN, width),
        once(3, WIN, width), once(width, width), twice, tile, once(*vecs.shape), once(8, width),
        once(*up_sums.shape), once(8, width),
    ]
    vector_rows = 16
    shared = [
        pltpu.VMEM((3, WIN + 2 * TILE, width), BF),
        pltpu.VMEM((WIN, width), BF),
        pltpu.VMEM((2, WIN, width), BF),
        pltpu.SemaphoreType.DMA((2,)),
        pltpu.SemaphoreType.DMA((2,)),
        pltpu.VMEM((rows, width), F32),
    ]
    if plan:
        part = width // peers
        kernel, collective = last_scatter_kernel, 3
        scratch = [pltpu.VMEM((3, 4, 2, 2, 2, part, width), BF)] + shared + [
            pltpu.VMEM((4, vector_rows, width), F32),
            pltpu.VMEM((7, vector_rows, width), F32),
            pltpu.SemaphoreType.DMA((7,)),
            pltpu.SemaphoreType.DMA((7,)),
        ] + scatter_scratch(part, UNIT, tilt=True) + scatter_scratch(part, UNIT) * 2
        third_out = jax.ShapeDtypeStruct((part, 3 * width), F32)
        vector_shapes = [(8, part), (1, 128)]
    else:
        kernel, collective = last_kernel, 4
        scratch = [pltpu.VMEM((3, width, width), BF)] + shared
        third_out = jax.ShapeDtypeStruct((3, width, width), BF)
        vector_shapes = [(vector_rows, width)]
    return pl.pallas_call(
        kernel,
        grid=(LAST_STEPS,),
        in_specs=in_specs,
        out_specs=[tile, once(*vector_shapes[0]), once(*third_out.shape)]
        + [once(*v) for v in vector_shapes[1:]],
        out_shape=[
            jax.ShapeDtypeStruct((rows, width), F32),
            jax.ShapeDtypeStruct(vector_shapes[0], F32),
            third_out,
            *(jax.ShapeDtypeStruct(v, F32) for v in vector_shapes[1:]),
        ],
        scratch_shapes=scratch,
        compiler_params=pltpu.CompilerParams(
            vmem_limit_bytes=61 * 2**20, collective_id=collective, has_side_effects=True
        ),
        name="last",
    )(n0, normed, dq, dk, dv, dn, w_qkv, tokens, dresid, vecs, sums, up_sums, kv_sums)


def shifted(value, by):
    peers = lax.axis_size(AXIS)
    pairs = [(i, i + by) for i in range(peers) if 0 <= i + by < peers]
    return lax.ppermute(value, AXIS, pairs)


def gathered(value):
    return lax.all_gather(value, AXIS, axis=0, tiled=True)


def scattered(value):
    return lax.psum_scatter(value, AXIS, scatter_dimension=0, tiled=True)


def local(
    tokens,
    image_ids,
    cotangent,
    norm1_gain,
    norm1_shift,
    qkv_weight,
    query_bias,
    value_bias,
    out_weight,
    out_bias,
    norm2_gain,
    norm2_shift,
    up_weight,
    up_bias,
    down_weight,
    down_bias,
):
    rows, width = tokens.shape
    me = lax.axis_index(AXIS)
    peers = lax.axis_size(AXIS)
    ext = -(-(rows + 2 * RIM + 64) // 128) * 128
    vectors = [
        norm1_gain, norm1_shift, query_bias, value_bias, out_bias, norm2_gain, norm2_shift,
        down_bias,
    ]
    part = norm1_gain.shape[0]
    block_plan = peers == 32
    if block_plan:
        lane = lax.broadcasted_iota(jnp.int32, (1, 128), 1) // part
        spread = jnp.tile(jnp.stack(vectors), (1, 128 // part))
        spread = jnp.where(lane == me % (128 // part), spread, jnp.zeros_like(spread))
        vec = jnp.concatenate(
            [spread, up_bias[None], jnp.zeros((VEC_ROWS - 9, 128), BF)], axis=0
        )
        (
            queries, key_value, normed_ext, scaled_ext, w_qkv, vectors, u_bias, vecs, n0, columns
        ) = first(
            tokens, qkv_weight, vec, image_ids.reshape(-1, 128), (out_weight, up_weight), ext
        )
        u_bias = u_bias[0]
    else:
        n0 = jnp.sum((image_ids == image_ids[0]).astype(jnp.int32)).reshape(1)
        gathered_vec = gathered(jnp.concatenate([*vectors, up_bias])[None]).astype(F32)
        gain1, shift1, q_bias, v_bias, o_bias, gain2, shift2, d_bias = (
            gathered_vec[:, i * part : (i + 1) * part].reshape(-1) for i in range(8)
        )
        u_bias = gathered_vec[:, 8 * part :].reshape(-1)
        none = [jnp.zeros_like(d_bias)] * 4
        vecs = jnp.stack([o_bias, gain2, shift2, d_bias] + none)
        vectors = jnp.stack([gain1] + none * 3 + none[:3])
        w_qkv, w_out, w_up, w_down = map(
            gathered, (qkv_weight, out_weight, up_weight, down_weight)
        )
        low_rim = shifted(tokens[rows - RIM :], 1)
        high_rim = shifted(tokens[:RIM], -1)
        pad = jnp.zeros((ext - rows - 2 * RIM, width), BF)
        tokens_ext = jnp.concatenate([low_rim, tokens, high_rim, pad], axis=0).astype(F32)
        scaled_ext = row_stats(tokens_ext)[0]
        normed_ext = (scaled_ext * gain1 + shift1).astype(BF)
        scaled_ext = scaled_ext.astype(BF)
        normed_low = normed_ext[RIM : RIM + rows]
        queries = (dot(normed_low, w_qkv[:, :width]) + q_bias).astype(BF)
        key_value = (
            dot(normed_ext, w_qkv[:, width:])
            + jnp.concatenate([jnp.zeros_like(v_bias), v_bias])
        ).astype(BF)
    if block_plan:
        mixed_low, lse, w_out, w_up, down_column = attend(
            n0, queries, key_value, columns, down_weight
        )
        w_out, w_up = w_out.reshape(width, -1), w_up.reshape(width, -1)
    else:
        mixed_low, lse = attend(n0, queries, key_value)

    args = (mixed_low, tokens, w_out, vecs, w_up, u_bias[None], cotangent)
    if block_plan:
        resid, normed_two, act, slope, grad_down, w_down = mlp_up(*args, down_column)
        w_down = w_down.reshape(-1, width)
    else:
        resid, normed_two, act, slope, grad_down = mlp_up(*args)
    args = (act, slope, w_up, w_down, cotangent, normed_two, resid, mixed_low, w_out, vecs)
    if block_plan:
        grad_up, up_sums, layer_out, dresid, dmixed_low, grad_out, sums, r_down = mlp_back(
            *args, grad_down
        )
    else:
        grad_up, up_sums, layer_out, dresid, dmixed_low, grad_out, sums = mlp_back(*args)
        r_down = scattered(grad_down).astype(F32)
    if block_plan:
        dquery, dkey, dvalue, dnormed, kv_sums, r_out, r_up = attend_back(
            n0, queries, key_value, dmixed_low, lse, w_qkv, scaled_ext, (grad_out, grad_up)
        )
    else:
        dquery, dkey, dvalue, dnormed, kv_sums = attend_back(
            n0, queries, key_value, dmixed_low, lse, w_qkv, scaled_ext
        )
        r_out, r_up = (scattered(v).astype(F32) for v in (grad_out, grad_up))
    grad_tokens, totals, r_qkv, *up_own = last(
        n0, normed_ext, dquery, dkey, dvalue, dnormed, w_qkv, tokens, dresid, vectors, sums,
        up_sums, kv_sums, block_plan,
    )
    if block_plan:
        owned, up_own = totals, up_own[0][0]
    else:
        totals = lax.psum(totals, AXIS)
        r_qkv = jnp.concatenate([scattered(v) for v in r_qkv], axis=1).astype(F32)
        owned = lax.dynamic_slice_in_dim(totals[:8], me * part, part, 1)
        size = u_bias.shape[0] // peers
        up_rows = totals[8 : 8 + u_bias.shape[0] // width].reshape(-1)
        up_own = lax.dynamic_slice_in_dim(up_rows, me * size, size)
    g = [owned[i] for i in range(8)] + [up_own]
    return (
        layer_out, grad_tokens, g[0], g[1], r_qkv, g[2], g[3], r_out, g[4], g[5], g[6], r_up,
        g[8], r_down, g[7],
    )


def solution(mesh):
    row, vec = P(AXIS, None), P(AXIS)
    return jax.shard_map(
        local,
        mesh=mesh,
        in_specs=(
            row, vec, row, vec, vec, row, vec, vec, row, vec, vec, vec, row, vec, row, vec,
        ),
        out_specs=(
            row, row, vec, vec, row, vec, vec, row, vec, vec, vec, row, vec, row, vec,
        ),
        check_vma=False,
    )
```
